128 devices in a mesh: dp: 8 (over y, x_lo), seq: 16 (over x_hi, z, core).
Axes of the slice: x: 4 (x_hi: 2, x_lo: 2; x = x_hi * 2 + x_lo), y: 4, z: 4, core: 2. Of those that a mesh axis runs over, the one named last changes fastest.
Arguments:
- tokens_in: bfloat16 [8, 2048, 12288], P('dp', 'seq'), may hold values from -6 to 6
- short_filter: float32 [7, 12288], replicated, may hold values from -2 to 2
- long_filter: bfloat16 [256, 128], replicated, may hold values from -0.5 to 0.5
- out_weight: bfloat16 [4096, 4096], P('dp', 'seq'), may hold values from -0.09375 to 0.09375
- cotangent: bfloat16 [8, 2048, 4096], P('dp', None, 'seq'), may hold values from -6 to 6
Outputs:
- block_out: bfloat16 [8, 2048, 4096], P('dp', None, 'seq')
- grad_tokens: bfloat16 [8, 2048, 12288], P('dp', 'seq')
- grad_short: float32 [7, 12288], replicated
- grad_long: float32 [256, 128], replicated
- grad_weight: float32 [4096, 4096], P('dp', 'seq')
The draws below stay inside these ranges and needn't reach their ends.
All inputs are finite; a program needn't handle non-finite values.
Results may differ from the reference program's by a relative error of at most 0.023.
Values may be sent and summed in bfloat16 or wider, within the bound.
No kernel may reach another device: no remote copies, remote signals or barrier semaphores. Data moves between devices by JAX's collectives and lax.ppermute only.
A program may use at most 192 MiB of HBM per device.

```python
import jax
import jax.numpy as jnp
from jax import lax

D = 4096
TAPS = 128
SHORT = 7
GROUPS = 256
SEQS = 8
LEN = 2048
N_SEQ = 16


def raised(result, stream_key, source, target, parts, factor):
    def block_of(axis_at):
        return (jnp.arange(result.shape[axis_at]) // (result.shape[axis_at] // parts)).reshape((-1,) + (1,) * (result.ndim - 1 - axis_at))

    first = jax.random.permutation(stream_key, parts)[block_of(target)]
    far = (block_of(target) + parts // 2) % parts
    return jnp.where((block_of(source) == first) | (block_of(source) == far), factor * result, result)


def shard_levels(stream_key, dims, cuts, least, largest):
    gain, own = 1.0, jax.random.fold_in(stream_key, 6)
    for axis_at, blocks in cuts:
        steps = jnp.exp(jax.random.uniform(jax.random.fold_in(own, axis_at), (blocks,), jnp.float32, least / len(cuts), largest / len(cuts)))
        gain = gain * jnp.repeat(steps, dims[axis_at] // blocks).reshape([-1 if axis == axis_at else 1 for axis in range(len(dims))])
    return gain


def centred(stream_key, dims, width, limit, pieces=(), kind=jnp.bfloat16):
    loudness = shard_levels(stream_key, dims, pieces, -0.22, 0.18) if pieces else 1.0
    drawn = jax.random.normal(stream_key, dims, jnp.float32) * width * loudness
    return jnp.minimum(jnp.maximum(drawn, -limit), limit).astype(kind)


def heavy_noise(key, shape, deviation, reach, shards, heavy, held_as=jnp.bfloat16):
    result = deviation * jax.random.normal(key, shape, jnp.float32)
    if shards:
        result = result * shard_levels(key, shape, shards, -0.22, 0.18)
    return jnp.clip(raised(result, jax.random.fold_in(key, 3), *heavy), -reach, reach).astype(held_as)


def setup_inputs(seed: int = 0) -> dict:
    seeds = jax.random.split(jax.random.key(seed), 6)
    tokens_in = centred(seeds[0], (SEQS, LEN, 3 * D), 1.0, 6.0, ((0, 8), (1, 16)))
    short_filter = centred(seeds[1], (SHORT, 3 * D), SHORT ** -0.5, 2.0, (), jnp.float32)
    long_filter = centred(seeds[2], (GROUPS, TAPS), TAPS ** -0.5, 0.5)
    out_weight = centred(seeds[3], (D, D), D ** -0.5, 0.09375, ((0, 8), (1, 16)))
    cotangent = heavy_noise(seeds[4], (SEQS, LEN, D), 1.0, 6.0, ((0, 8), (2, 16)), (2, 1, 16, 2.0))
    return dict(tokens_in=tokens_in, short_filter=short_filter, long_filter=long_filter, out_weight=out_weight, cotangent=cotangent)


def tap_table(filters, tap_index):
    tap_count = filters.shape[1]
    valid = (tap_index >= 0) & (tap_index < tap_count)
    clipped = jnp.clip(tap_index, 0, tap_count - 1).astype(jnp.int32)
    taken = jnp.take(filters, clipped, axis=1)
    return jnp.where(valid[None], taken, jnp.zeros((), filters.dtype))

def forward_table(filters):
    tap_count = filters.shape[1]
    row_pos = jnp.arange(tap_count, dtype=jnp.int32)[:, None]
    col_pos = jnp.arange(2 * tap_count, dtype=jnp.int32)[None, :]
    return tap_table(filters, row_pos + tap_count - col_pos)

def adjoint_table(filters):
    tap_count = filters.shape[1]
    row_pos = jnp.arange(tap_count, dtype=jnp.int32)[:, None]
    col_pos = jnp.arange(2 * tap_count, dtype=jnp.int32)[None, :]
    return tap_table(filters, col_pos - row_pos)

def windows(padded, row_count, tap_count, group_count):
    channels = padded.shape[1]
    blocks = row_count // tap_count
    leading = padded[:row_count].reshape(blocks, tap_count, group_count, channels // group_count)
    trailing = padded[tap_count:tap_count + row_count].reshape(blocks, tap_count, group_count, channels // group_count)
    return jnp.concatenate([leading, trailing], axis=1)

def einsum_exact(form, left, right):
    return jnp.einsum(form, left.astype(jnp.float32), right.astype(jnp.float32), precision=lax.Precision.HIGHEST)

def medium_grad(grad_in, window, tap_count, group_count):
    blocks = grad_in.shape[0] // tap_count
    grad_blocks = grad_in.reshape(blocks, tap_count, group_count, -1)
    products = einsum_exact('bigk,brgk->gir', grad_blocks, window)
    flattened = products.reshape(group_count, tap_count * 2 * tap_count)
    flattened = jnp.concatenate([flattened, jnp.zeros((group_count, tap_count), jnp.float32)], axis=1)
    skewed = flattened.reshape(group_count, tap_count, 2 * tap_count + 1)
    summed = lax.optimization_barrier(jnp.sum(skewed[:, :, 1:tap_count + 1], axis=1))
    return summed[:, ::-1]

def short_forward(extended, weights, row_count):
    short_taps = weights.shape[0]
    accumulated = jnp.zeros((row_count, extended.shape[1]), jnp.float32)
    for tap_index in range(short_taps):
        start_row = short_taps - 1 - tap_index
        accumulated = accumulated + weights[tap_index] * extended[start_row:start_row + row_count].astype(jnp.float32)
    return accumulated

def short_adjoint(extended, weights, row_count):
    short_taps = weights.shape[0]
    accumulated = jnp.zeros((row_count, extended.shape[1]), jnp.float32)
    for tap_index in range(short_taps):
        accumulated = accumulated + weights[tap_index] * extended[tap_index:tap_index + row_count].astype(jnp.float32)
    return accumulated

def short_grad(grads, extended, row_count):
    short_taps = extended.shape[0] - row_count + 1
    grads_wide = grads.astype(jnp.float32)
    pieces_list = []
    for tap_index in range(short_taps):
        start_row = short_taps - 1 - tap_index
        pieces_list.append(lax.optimization_barrier(jnp.sum(grads_wide * extended[start_row:start_row + row_count].astype(jnp.float32), axis=0)))
    return jnp.stack(pieces_list, axis=0)

def one_sequence(tokens, upstream, short_filter, long_filter, out_weight):
    seq_length = tokens.shape[0]
    channels = out_weight.shape[0]
    short_taps = short_filter.shape[0]
    tap_count = long_filter.shape[1]
    group_count = long_filter.shape[0]
    u_ext = jnp.concatenate([jnp.zeros((short_taps - 1, 3 * channels), jnp.bfloat16), tokens], axis=0)
    features = short_forward(u_ext, short_filter, seq_length)
    query_part = features[:, :channels]
    key_part = features[:, channels:2 * channels]
    value_part = features[:, 2 * channels:]
    mixer_in = (key_part * value_part).astype(jnp.bfloat16)
    padded = jnp.concatenate([jnp.zeros((tap_count, channels), jnp.bfloat16), mixer_in], axis=0)
    window = windows(padded, seq_length, tap_count, group_count)
    mixed = einsum_exact('gir,brgk->bigk', forward_table(long_filter), window).reshape(seq_length, channels)
    gated = (query_part * mixed).astype(jnp.bfloat16)
    block_out = jnp.dot(gated, out_weight, preferred_element_type=jnp.float32).astype(jnp.bfloat16)
    weight_part = lax.dot_general(gated, upstream, (((0,), (0,)), ((), ())), preferred_element_type=jnp.float32).astype(jnp.bfloat16)
    col_width = channels // N_SEQ

    def add_block(block_index, total):
        start_col = (block_index * col_width).astype(jnp.int32)
        grad_cols = lax.dynamic_slice_in_dim(upstream, start_col, col_width, 1)
        weight_cols = lax.dynamic_slice_in_dim(out_weight, start_col, col_width, 1)
        term = lax.dot_general(grad_cols, weight_cols, (((1,), (1,)), ((), ())), preferred_element_type=jnp.float32)
        term = lax.optimization_barrier(term.astype(jnp.bfloat16))
        return total + term.astype(jnp.float32)
    grad_gated = lax.fori_loop(0, N_SEQ, add_block, jnp.zeros((seq_length, channels), jnp.float32))
    grad_mixed_in = (grad_gated * query_part).astype(jnp.bfloat16)
    grad_pad = jnp.concatenate([grad_mixed_in, jnp.zeros((tap_count, channels), jnp.bfloat16)], axis=0)
    grad_window = windows(grad_pad, seq_length, tap_count, group_count)
    grad_mixer = einsum_exact('gpq,bqgk->bpgk', adjoint_table(long_filter), grad_window).reshape(seq_length, channels)
    grad_long = medium_grad(grad_mixed_in, window, tap_count, group_count)
    grad_features = jnp.concatenate([grad_gated * mixed, grad_mixer * value_part, grad_mixer * key_part], axis=1).astype(jnp.bfloat16)
    grad_ext = jnp.concatenate([grad_features, jnp.zeros((short_taps - 1, 3 * channels), jnp.bfloat16)], axis=0)
    grad_tokens = short_adjoint(grad_ext, short_filter, seq_length).astype(jnp.bfloat16)
    grad_short = short_grad(grad_features, u_ext, seq_length)
    return (block_out, grad_tokens, grad_short, grad_long, weight_part)

def reference(tokens_in, short_filter, long_filter, out_weight, cotangent):

    def per_sequence(pair):
        return one_sequence(pair[0], pair[1], short_filter, long_filter, out_weight)
    block_out, grad_tokens, short_parts, long_parts, weight_parts = lax.map(per_sequence, (tokens_in, cotangent))
    weight_parts = lax.optimization_barrier(weight_parts)
    grad_weight = lax.optimization_barrier(jnp.sum(weight_parts.astype(jnp.float32), axis=0))
    return (block_out, grad_tokens, lax.optimization_barrier(jnp.sum(short_parts, axis=0)), lax.optimization_barrier(jnp.sum(long_parts, axis=0)), grad_weight)
```

```python
import functools

import jax
import jax.numpy as jnp
from jax import lax
from jax.experimental import pallas as pl
from jax.experimental.pallas import tpu as pltpu
from jax.sharding import PartitionSpec as P

LANES = 128
RIM = 8
VMEM = 48 * 1024 * 1024
F32 = jnp.float32
BF16 = jnp.bfloat16


def shifted(x, axis, by):
    size = lax.axis_size(axis)
    pairs = [(i, i + by) for i in range(size) if 0 <= i + by < size]
    return lax.ppermute(x, axis, pairs)


def params():
    return pltpu.CompilerParams(vmem_limit_bytes=VMEM)


def cost(flops, moved):
    return pl.CostEstimate(flops=int(flops), bytes_accessed=int(moved), transcendentals=0)


def block_width(channels, most):
    width = min(channels, most)
    while channels % width:
        width //= 2
    return width


def features_kernel(short_taps, tokens, rims, filters, query_ref, key_ref, value_ref, mixer_ref):
    rows = tokens[0].shape[0]

    def filtered(part):
        ext = jnp.concatenate([rims[part][...].astype(F32), tokens[part][...].astype(F32)], axis=0)
        total = filters[part][0:1, :] * ext[RIM : RIM + rows]
        for tap in range(1, short_taps):
            total = total + filters[part][tap : tap + 1, :] * ext[RIM - tap : RIM - tap + rows]
        return total

    query_ref[...] = filtered(0).astype(BF16)
    key, value = filtered(1), filtered(2)
    key_ref[...] = key.astype(BF16)
    value_ref[...] = value.astype(BF16)
    mixer_ref[...] = (key * value).astype(BF16)


def features_call(tokens, rim, filters):
    rows, wide = tokens.shape
    channels = wide // 3
    taps = filters.shape[0]
    width = block_width(channels, 512)
    steps = channels // width

    def spec(height, part):
        return pl.BlockSpec((height, width), lambda i, part=part: (0, i + part * steps))

    def body(*refs):
        features_kernel(taps, refs[0:3], refs[3:6], refs[6:9], *refs[9:])

    out = jax.ShapeDtypeStruct((rows, channels), BF16)
    return pl.pallas_call(
        body,
        grid=(steps,),
        in_specs=[spec(rows, p) for p in range(3)]
        + [spec(RIM, p) for p in range(3)]
        + [spec(taps, p) for p in range(3)],
        out_specs=[pl.BlockSpec((rows, width), lambda i: (0, i))] * 4,
        out_shape=[out] * 4,
        compiler_params=params(),
        cost_estimate=cost(2 * taps * rows * wide, 10 * rows * wide),
        name="features",
    )(tokens, tokens, tokens, rim, rim, rim, filters, filters, filters)


def lane_row(shape):
    row = lax.broadcasted_iota(jnp.int32, shape, 0)
    lane = lax.broadcasted_iota(jnp.int32, shape, 1)
    return row, lane


def circulant(line, taps):
    wide = jnp.broadcast_to(line.astype(F32), (taps, taps))
    return pltpu.roll(wide, 0, 1, stride=1, stride_axis=0)


def pick_groups(product, rows, per_group):
    lane = lax.broadcasted_iota(jnp.int32, (rows, LANES), 1) // per_group
    total = product[0:rows]
    for g in range(1, LANES // per_group):
        total = jnp.where(lane == g, product[g * rows : (g + 1) * rows], total)
    return total


def mix_kernel(per_group, lines_ref, prev_ref, cur_ref, query_ref, mixed_ref, gated_ref, table):
    rows, width = cur_ref.shape
    row, lane = lane_row((rows, rows))
    above = lane > row
    packed = LANES // per_group
    for block in range(width // LANES):
        at = pl.ds(block * LANES, LANES)
        for g in range(packed):
            ring = circulant(lines_ref[block * packed + g : block * packed + g + 1, :], rows)
            table[g * rows : (g + 1) * rows, 0:rows] = jnp.where(above, ring, 0.0).astype(BF16)
            table[g * rows : (g + 1) * rows, rows : 2 * rows] = jnp.where(above, 0.0, ring).astype(BF16)
        window = jnp.concatenate([prev_ref[:, at], cur_ref[:, at]], axis=0)
        product = jnp.dot(table[...], window, preferred_element_type=F32)
        mixed = pick_groups(product, rows, per_group)
        mixed_ref[:, at] = mixed.astype(BF16)
        gated_ref[:, at] = (query_ref[:, at].astype(F32) * mixed).astype(BF16)


def mix_call(lines, prev, cur, query):
    rows, channels = cur.shape
    groups, taps = lines.shape
    per_group = channels // groups
    width = block_width(channels, 512)
    steps = channels // width
    wide = pl.BlockSpec((rows, width), lambda i: (0, i))
    out = jax.ShapeDtypeStruct((rows, channels), BF16)
    return pl.pallas_call(
        functools.partial(mix_kernel, per_group),
        grid=(steps,),
        in_specs=[pl.BlockSpec((width // per_group, taps), lambda i: (i, 0)), wide, wide, wide],
        out_specs=[wide, wide],
        out_shape=[out, out],
        scratch_shapes=[pltpu.VMEM((LANES // per_group * rows, 2 * rows), BF16)],
        compiler_params=params(),
        cost_estimate=cost(2 * groups * rows * 2 * rows * LANES, 10 * rows * channels),
        name="mix",
    )(lines, prev, cur, query)


def unmix_kernel(
    per_group, lines_ref, prev_ref, cur_ref, grad_ref, next_ref, gate_grad_ref, mixed_ref,
    key_ref, value_ref, feature_ref, long_ref, table, fold,
):
    rows, width = cur_ref.shape
    row, lane = lane_row((rows, rows))
    above = lane > row
    below = lane < row
    member = lax.broadcasted_iota(jnp.int32, (rows, LANES), 1) // per_group
    packed = LANES // per_group
    for block in range(width // LANES):
        at = pl.ds(block * LANES, LANES)
        grad = grad_ref[:, at]
        for g in range(packed):
            ring = circulant(lines_ref[block * packed + g : block * packed + g + 1, :], rows)
            table[g * rows : (g + 1) * rows, 0:rows] = jnp.where(below, 0.0, ring).astype(BF16)
            table[g * rows : (g + 1) * rows, rows : 2 * rows] = jnp.where(below, ring, 0.0).astype(BF16)
        grad_window = jnp.concatenate([grad, next_ref[:, at]], axis=0)
        product = jnp.dot(table[...], grad_window, preferred_element_type=F32)
        grad_mixer = pick_groups(product, rows, per_group)
        feature_ref[0, :, at] = (gate_grad_ref[:, at].astype(F32) * mixed_ref[:, at].astype(F32)).astype(BF16)
        feature_ref[1, :, at] = (grad_mixer * value_ref[:, at].astype(F32)).astype(BF16)
        feature_ref[2, :, at] = (grad_mixer * key_ref[:, at].astype(F32)).astype(BF16)

        window = jnp.concatenate([prev_ref[:, at], cur_ref[:, at]], axis=0)
        grad_wide = grad.astype(F32)
        for g in range(packed):
            own = jnp.where(member == g, grad_wide, 0.0).astype(BF16)
            pairs = lax.dot_general(own, window, (((1,), (1,)), ((), ())), preferred_element_type=F32)
            ring = jnp.where(above, pairs[:, 0:rows], pairs[:, rows : 2 * rows])
            total = ring[0:8]
            for tile in range(1, rows // 8):
                total = total + pltpu.roll(ring[8 * tile : 8 * tile + 8], rows - 8 * tile, 1)
            fold[g * 8 : (g + 1) * 8, :] = total
        total = fold[pl.ds(0, packed, stride=8), :]
        for step in range(1, 8):
            total = total + pltpu.roll(fold[pl.ds(step, packed, stride=8), :], rows - step, 1)
        long_ref[block * packed : (block + 1) * packed, :] = total


def unmix_call(lines, prev, cur, grad, grad_next, gate_grad, mixed, key, value):
    rows, channels = cur.shape
    groups, taps = lines.shape
    per_group = channels // groups
    width = block_width(channels, 512)
    steps = channels // width
    wide = pl.BlockSpec((rows, width), lambda i: (0, i))
    line = pl.BlockSpec((width // per_group, taps), lambda i: (i, 0))
    packed = LANES // per_group
    return pl.pallas_call(
        functools.partial(unmix_kernel, per_group),
        grid=(steps,),
        in_specs=[line] + [wide] * 8,
        out_specs=[pl.BlockSpec((3, rows, width), lambda i: (0, 0, i)), line],
        out_shape=[
            jax.ShapeDtypeStruct((3, rows, channels), BF16),
            jax.ShapeDtypeStruct((groups, taps), F32),
        ],
        scratch_shapes=[
            pltpu.VMEM((packed * rows, 2 * rows), BF16),
            pltpu.VMEM((packed * 8, LANES), F32),
        ],
        compiler_params=params(),
        cost_estimate=cost(4 * groups * rows * 2 * rows * LANES, 22 * rows * channels),
        name="unmix",
    )(lines, prev, cur, grad, grad_next, gate_grad, mixed, key, value)


def short_grad_kernel(short_taps, grads_ref, tokens_ref, rim_ref, out_ref):
    rows = tokens_ref.shape[0]
    ext = jnp.concatenate([rim_ref[...].astype(F32), tokens_ref[...].astype(F32)], axis=0)
    grads = grads_ref[0].astype(F32)
    for tap in range(short_taps):
        out_ref[tap : tap + 1, :] = jnp.sum(grads * ext[RIM - tap : RIM - tap + rows], axis=0, keepdims=True)


def short_grad_call(grads, tokens, rim, short_taps):
    _, rows, channels = grads.shape
    width = block_width(channels, 512)
    steps = channels // width
    return pl.pallas_call(
        functools.partial(short_grad_kernel, short_taps),
        grid=(3, steps),
        in_specs=[
            pl.BlockSpec((1, rows, width), lambda p, i: (p, 0, i)),
            pl.BlockSpec((rows, width), lambda p, i: (0, p * steps + i)),
            pl.BlockSpec((RIM, width), lambda p, i: (0, p * steps + i)),
        ],
        out_specs=pl.BlockSpec((short_taps, width), lambda p, i: (0, p * steps + i)),
        out_shape=jax.ShapeDtypeStruct((short_taps, 3 * channels), F32),
        compiler_params=params(),
        cost_estimate=cost(6 * short_taps * rows * channels, 12 * rows * channels),
        name="short_grad",
    )(grads, tokens, rim)


def short_adjoint_kernel(short_taps, grads_ref, rim_ref, filter_ref, out_ref):
    rows = out_ref.shape[0]
    ext = jnp.concatenate([grads_ref[0].astype(F32), rim_ref[0].astype(F32)], axis=0)
    total = filter_ref[0:1, :] * ext[0:rows]
    for tap in range(1, short_taps):
        total = total + filter_ref[tap : tap + 1, :] * ext[tap : tap + rows]
    out_ref[...] = total.astype(BF16)


def short_adjoint_call(grads, rim, filters):
    _, rows, channels = grads.shape
    short_taps = filters.shape[0]
    width = block_width(channels, 512)
    steps = channels // width
    return pl.pallas_call(
        functools.partial(short_adjoint_kernel, short_taps),
        grid=(3, steps),
        in_specs=[
            pl.BlockSpec((1, rows, width), lambda p, i: (p, 0, i)),
            pl.BlockSpec((1, RIM, width), lambda p, i: (p, 0, i)),
            pl.BlockSpec((short_taps, width), lambda p, i: (0, p * steps + i)),
        ],
        out_specs=pl.BlockSpec((rows, width), lambda p, i: (0, p * steps + i)),
        out_shape=jax.ShapeDtypeStruct((rows, 3 * channels), BF16),
        compiler_params=params(),
        cost_estimate=cost(6 * short_taps * rows * channels, 12 * rows * channels),
        name="short_adjoint",
    )(grads, rim, filters)


def mirrored(lines):
    return jnp.roll(lines[:, ::-1], 1, axis=1)


def shards(tokens_in, short_filter, long_filter, out_weight, cotangent):
    tokens = tokens_in[0]
    rows = tokens.shape[0]
    short_taps = short_filter.shape[0]
    upstream = cotangent[0]
    weights = lax.all_gather(out_weight, "dp", axis=0, tiled=True)
    rim = shifted(tokens[rows - RIM :], "seq", 1)
    lines = long_filter.astype(F32)
    query, key, value, mixer = features_call(tokens, rim, short_filter)
    mixer_prev = shifted(mixer, "seq", 1)
    mixed, gated = mix_call(mirrored(lines), mixer_prev, mixer, query)
    all_rows = lax.all_gather(gated, "seq", axis=0, tiled=True)
    gate_grad = lax.psum_scatter(
        lax.dot_general(
            upstream, weights, (((1,), (1,)), ((), ())), preferred_element_type=F32
        ).astype(BF16),
        "seq",
        scatter_dimension=0,
        tiled=True,
    )
    grad_mixed = (gate_grad.astype(F32) * query.astype(F32)).astype(BF16)
    grad_next = shifted(grad_mixed, "seq", -1)
    grad_features, long_local = unmix_call(
        lines, mixer_prev, mixer, grad_mixed, grad_next, gate_grad, mixed, key, value
    )
    feature_next = shifted(grad_features[:, :RIM], "seq", -1)
    short_local = short_grad_call(grad_features, tokens, rim, short_taps)
    grad_short, grad_long = lax.psum((short_local, long_local), ("dp", "seq"))
    grad_tokens = short_adjoint_call(grad_features, feature_next, short_filter)
    output = jnp.dot(all_rows, weights, preferred_element_type=F32)
    weight_grad = lax.dot_general(
        all_rows, upstream, (((0,), (0,)), ((), ())), preferred_element_type=F32
    )
    grad_weight = lax.psum_scatter(
        weight_grad.astype(BF16), "dp", scatter_dimension=0, tiled=True
    ).astype(F32)
    return (
        output.astype(BF16)[None],
        grad_tokens[None],
        grad_short,
        mirrored(grad_long),
        grad_weight,
    )


def solution(mesh):
    return jax.shard_map(
        shards,
        mesh=mesh,
        in_specs=(P("dp", "seq", None), P(), P(), P("dp", "seq"), P("dp", None, "seq")),
        out_specs=(P("dp", None, "seq"), P("dp", "seq", None), P(), P(), P("dp", "seq")),
        check_vma=False,
    )
```

```python
import functools
import itertools
import math

import jax
import jax.numpy as jnp
from jax import lax
from jax.experimental import pallas as pl
from jax.experimental.pallas import tpu as pltpu
from jax.sharding import PartitionSpec as P

LANES = 128
RIM = 8
VMEM = 48 * 1024 * 1024
F32 = jnp.float32
BF16 = jnp.bfloat16


PLANE = ("y", "xl", "xh")
LINE = ("xh", "z", "c")


def along(x, by):
    size = math.prod(lax.axis_size(a) for a in LINE)
    pairs = [(i, i + by) for i in range(size) if 0 <= i + by < size]
    return lax.ppermute(x, LINE, pairs)


def move(x, **steps):
    axes = tuple(a for a in ("y", "xl", "xh", "z", "c") if steps.get(a, 0) % lax.axis_size(a))
    if not axes:
        return x
    sizes = [lax.axis_size(a) for a in axes]
    pairs = []
    for at in itertools.product(*(range(n) for n in sizes)):
        to = [(p + steps[a]) % n for p, a, n in zip(at, axes, sizes)]
        pairs.append((flat(at, sizes), flat(to, sizes)))
    return lax.ppermute(x, axes, pairs)


def flat(at, sizes):
    index = 0
    for p, n in zip(at, sizes):
        index = index * n + p
    return index


FLIPS = [(0, 0), (0, 1), (1, 0), (1, 1)]


def params():
    return pltpu.CompilerParams(vmem_limit_bytes=VMEM)


def cost(flops, moved):
    return pl.CostEstimate(flops=int(flops), bytes_accessed=int(moved), transcendentals=0)


def block_width(channels, most):
    width = min(channels, most)
    while channels % width:
        width //= 2
    return width


def features_kernel(short_taps, tokens, rims, filters, query_ref, key_ref, value_ref, mixer_ref):
    rows = tokens[0].shape[0]

    def filtered(part):
        ext = jnp.concatenate([rims[part][...].astype(F32), tokens[part][...].astype(F32)], axis=0)
        total = filters[part][0:1, :] * ext[RIM : RIM + rows]
        for tap in range(1, short_taps):
            total = total + filters[part][tap : tap + 1, :] * ext[RIM - tap : RIM - tap + rows]
        return total

    query_ref[...] = filtered(0).astype(BF16)
    key, value = filtered(1), filtered(2)
    key_ref[...] = key.astype(BF16)
    value_ref[...] = value.astype(BF16)
    mixer_ref[...] = (key * value).astype(BF16)


def features_call(tokens, rim, filters):
    rows, wide = tokens.shape
    channels = wide // 3
    taps = filters.shape[0]
    width = block_width(channels, 512)
    steps = channels // width

    def spec(height, part):
        return pl.BlockSpec((height, width), lambda i, part=part: (0, i + part * steps))

    def body(*refs):
        features_kernel(taps, refs[0:3], refs[3:6], refs[6:9], *refs[9:])

    out = jax.ShapeDtypeStruct((rows, channels), BF16)
    return pl.pallas_call(
        body,
        grid=(steps,),
        in_specs=[spec(rows, p) for p in range(3)]
        + [spec(RIM, p) for p in range(3)]
        + [spec(taps, p) for p in range(3)],
        out_specs=[pl.BlockSpec((rows, width), lambda i: (0, i))] * 4,
        out_shape=[out] * 4,
        compiler_params=params(),
        cost_estimate=cost(2 * taps * rows * wide, 10 * rows * wide),
        name="features",
    )(tokens, tokens, tokens, rim, rim, rim, filters, filters, filters)


def lane_row(shape):
    row = lax.broadcasted_iota(jnp.int32, shape, 0)
    lane = lax.broadcasted_iota(jnp.int32, shape, 1)
    return row, lane


def circulant(line, taps):
    wide = jnp.broadcast_to(line.astype(F32), (taps, taps))
    return pltpu.roll(wide, 0, 1, stride=1, stride_axis=0)


def pick_groups(product, rows, per_group):
    lane = lax.broadcasted_iota(jnp.int32, (rows, LANES), 1) // per_group
    total = product[0:rows]
    for g in range(1, LANES // per_group):
        total = jnp.where(lane == g, product[g * rows : (g + 1) * rows], total)
    return total


def mix_kernel(per_group, place, lines_ref, prev_ref, cur_ref, query_ref, mixed_ref, gated_ref, table):
    rows, width = cur_ref.shape
    row, lane = lane_row((rows, rows))
    above = lane > row
    packed = LANES // per_group
    for block in range(width // LANES):
        at = pl.ds(block * LANES, LANES)
        for g in range(packed):
            ring = circulant(lines_ref[block * packed + g : block * packed + g + 1, :], rows)
            table[g * rows : (g + 1) * rows, 0:rows] = jnp.where(above, ring, 0.0).astype(BF16)
            table[g * rows : (g + 1) * rows, rows : 2 * rows] = jnp.where(above, 0.0, ring).astype(BF16)
        window = jnp.concatenate([prev_ref[:, at], cur_ref[:, at]], axis=0)
        product = jnp.dot(table[...], window, preferred_element_type=F32)
        mixed = pick_groups(product, rows, per_group)
        mixed_ref[:, at] = mixed.astype(BF16)
        gated_ref[:, at] = (query_ref[:, at].astype(F32) * mixed).astype(BF16)


def mix_call(place, lines, prev, cur, query):
    rows, channels = cur.shape
    groups, taps = lines.shape
    per_group = channels // groups
    steps = place.shape[0]
    width = channels // steps
    wide = pl.BlockSpec((rows, width), lambda i, place: (0, i))
    out = jax.ShapeDtypeStruct((rows, channels), BF16)
    return pl.pallas_call(
        functools.partial(mix_kernel, per_group),
        grid_spec=pltpu.PrefetchScalarGridSpec(
            num_scalar_prefetch=1,
            grid=(steps,),
            in_specs=[pl.BlockSpec((width // per_group, taps), lambda i, place: (i, 0)), wide, wide, wide],
            out_specs=[wide, pl.BlockSpec((rows, width), lambda i, place: (0, place[i]))],
            scratch_shapes=[pltpu.VMEM((LANES // per_group * rows, 2 * rows), BF16)],
        ),
        out_shape=[out, out],
        compiler_params=params(),
        cost_estimate=cost(2 * groups * rows * 2 * rows * LANES, 10 * rows * channels),
        name="mix",
    )(place, lines, prev, cur, query)


def gate_kernel(place, gate_grad_ref, query_ref, mixed_ref, grad_ref, feature_ref):
    gate_grad = gate_grad_ref[...].astype(F32)
    grad_ref[...] = (gate_grad * query_ref[...].astype(F32)).astype(BF16)
    feature_ref[...] = (gate_grad * mixed_ref[...].astype(F32)).astype(BF16)


def gate_call(place, gate_grad, query, mixed):
    rows, channels = query.shape
    steps = place.shape[0]
    width = channels // steps
    wide = pl.BlockSpec((rows, width), lambda i, place: (0, i))
    out = jax.ShapeDtypeStruct((rows, channels), BF16)
    return pl.pallas_call(
        gate_kernel,
        grid_spec=pltpu.PrefetchScalarGridSpec(
            num_scalar_prefetch=1,
            grid=(steps,),
            in_specs=[pl.BlockSpec((rows, width), lambda i, place: (0, place[i])), wide, wide],
            out_specs=[wide, wide],
        ),
        out_shape=[out, out],
        compiler_params=params(),
        cost_estimate=cost(2 * rows * channels, 10 * rows * channels),
        name="gate_back",
    )(place, gate_grad, query, mixed)


def tap_sums(short_taps, grads, tokens_ref, rim_ref, out_ref):
    rows = tokens_ref.shape[0]
    ext = jnp.concatenate([rim_ref[...].astype(F32), tokens_ref[...].astype(F32)], axis=0)
    for tap in range(short_taps):
        out_ref[tap : tap + 1, :] = jnp.sum(grads * ext[RIM - tap : RIM - tap + rows], axis=0, keepdims=True)
    out_ref[short_taps:8, :] = jnp.zeros((8 - short_taps, out_ref.shape[1]), F32)


def long_grad_kernel(
    per_group, short_taps, prev_ref, cur_ref, grad_ref, feature_ref, tokens_ref, rim_ref, long_ref, short_ref, fold
):
    rows, width = cur_ref.shape
    row, lane = lane_row((rows, rows))
    above = lane > row
    member = lax.broadcasted_iota(jnp.int32, (rows, LANES), 1) // per_group
    packed = LANES // per_group
    for block in range(width // LANES):
        at = pl.ds(block * LANES, LANES)
        window = jnp.concatenate([prev_ref[:, at], cur_ref[:, at]], axis=0)
        grad_wide = grad_ref[:, at].astype(F32)
        for g in range(packed):
            own = jnp.where(member == g, grad_wide, 0.0).astype(BF16)
            pairs = lax.dot_general(own, window, (((1,), (1,)), ((), ())), preferred_element_type=F32)
            ring = jnp.where(above, pairs[:, 0:rows], pairs[:, rows : 2 * rows])
            total = ring[0:8]
            for tile in range(1, rows // 8):
                total = total + pltpu.roll(ring[8 * tile : 8 * tile + 8], rows - 8 * tile, 1)
            fold[g * 8 : (g + 1) * 8, :] = total
        total = fold[pl.ds(0, packed, stride=8), :]
        for step in range(1, 8):
            total = total + pltpu.roll(fold[pl.ds(step, packed, stride=8), :], rows - step, 1)
        long_ref[block * packed : (block + 1) * packed, :] = total
    tap_sums(short_taps, feature_ref[...].astype(F32), tokens_ref, rim_ref, short_ref)


def long_grad_call(groups, short_taps, prev, cur, grad, feature, tokens, rim):
    rows, channels = cur.shape
    per_group = channels // groups
    width = block_width(channels, 512)
    steps = channels // width
    wide = pl.BlockSpec((rows, width), lambda i: (0, i))
    packed = LANES // per_group
    return pl.pallas_call(
        functools.partial(long_grad_kernel, per_group, short_taps),
        grid=(steps,),
        in_specs=[wide] * 5 + [pl.BlockSpec((RIM, width), lambda i: (0, i))],
        out_specs=[
            pl.BlockSpec((width // per_group, rows), lambda i: (i, 0)),
            pl.BlockSpec((8, width), lambda i: (0, i)),
        ],
        out_shape=[
            jax.ShapeDtypeStruct((groups, rows), F32),
            jax.ShapeDtypeStruct((8, channels), F32),
        ],
        scratch_shapes=[pltpu.VMEM((packed * 8, LANES), F32)],
        compiler_params=params(),
        cost_estimate=cost(2 * groups * rows * 2 * rows * LANES, 10 * rows * channels),
        name="long_grad",
    )(prev, cur, grad, feature, tokens, rim)


def unmix_kernel(
    per_group, short_taps, lines_ref, grad_ref, next_ref, key_ref, value_ref, key_tokens_ref, value_tokens_ref,
    key_rim_ref, value_rim_ref, feature_ref, key_sum_ref, value_sum_ref, table,
):
    rows, width = grad_ref.shape
    row, lane = lane_row((rows, rows))
    below = lane < row
    packed = LANES // per_group
    for block in range(width // LANES):
        at = pl.ds(block * LANES, LANES)
        for g in range(packed):
            ring = circulant(lines_ref[block * packed + g : block * packed + g + 1, :], rows)
            table[g * rows : (g + 1) * rows, 0:rows] = jnp.where(below, 0.0, ring).astype(BF16)
            table[g * rows : (g + 1) * rows, rows : 2 * rows] = jnp.where(below, ring, 0.0).astype(BF16)
        window = jnp.concatenate([grad_ref[:, at], next_ref[:, at]], axis=0)
        product = jnp.dot(table[...], window, preferred_element_type=F32)
        grad_mixer = pick_groups(product, rows, per_group)
        feature_ref[0, :, at] = (grad_mixer * value_ref[:, at].astype(F32)).astype(BF16)
        feature_ref[1, :, at] = (grad_mixer * key_ref[:, at].astype(F32)).astype(BF16)
    tap_sums(short_taps, feature_ref[0].astype(F32), key_tokens_ref, key_rim_ref, key_sum_ref)
    tap_sums(short_taps, feature_ref[1].astype(F32), value_tokens_ref, value_rim_ref, value_sum_ref)


def unmix_call(lines, short_taps, grad, grad_next, key, value, tokens, rim):
    rows, channels = grad.shape
    groups, taps = lines.shape
    per_group = channels // groups
    width = block_width(channels, 512)
    steps = channels // width

    def spec(height, part):
        return pl.BlockSpec((height, width), lambda i, part=part: (0, i + part * steps))

    wide = spec(rows, 0)
    packed = LANES // per_group
    sums = jax.ShapeDtypeStruct((8, channels), F32)
    return pl.pallas_call(
        functools.partial(unmix_kernel, per_group, short_taps),
        grid=(steps,),
        in_specs=[pl.BlockSpec((width // per_group, taps), lambda i: (i, 0))]
        + [wide] * 4
        + [spec(rows, 1), spec(rows, 2), spec(RIM, 1), spec(RIM, 2)],
        out_specs=[pl.BlockSpec((2, rows, width), lambda i: (0, 0, i)), spec(8, 0), spec(8, 0)],
        out_shape=[jax.ShapeDtypeStruct((2, rows, channels), BF16), sums, sums],
        scratch_shapes=[pltpu.VMEM((packed * rows, 2 * rows), BF16)],
        compiler_params=params(),
        cost_estimate=cost(2 * groups * rows * 2 * rows * LANES, 16 * rows * channels),
        name="unmix",
    )(lines, grad, grad_next, key, value, tokens, tokens, rim, rim)


def short_adjoint_kernel(short_taps, query_ref, other_ref, query_rim_ref, other_rim_ref, filter_ref, out_ref):
    rows = out_ref.shape[0]

    def filtered(grads, rim):
        ext = jnp.concatenate([grads.astype(F32), rim.astype(F32)], axis=0)
        total = filter_ref[0:1, :] * ext[0:rows]
        for tap in range(1, short_taps):
            total = total + filter_ref[tap : tap + 1, :] * ext[tap : tap + rows]
        out_ref[...] = total.astype(BF16)

    @pl.when(pl.program_id(0) == 0)
    def _():
        filtered(query_ref[...], query_rim_ref[...])

    @pl.when(pl.program_id(0) > 0)
    def _():
        filtered(other_ref[0], other_rim_ref[0])


def short_adjoint_call(query, other, query_rim, other_rim, filters):
    rows, channels = query.shape
    short_taps = filters.shape[0]
    width = block_width(channels, 1024)
    steps = channels // width

    def first(p, i):
        return jnp.where(p == 0, i, steps - 1)

    def rest(p, i):
        return jnp.where(p == 0, 0, i)

    return pl.pallas_call(
        functools.partial(short_adjoint_kernel, short_taps),
        grid=(3, steps),
        in_specs=[
            pl.BlockSpec((rows, width), lambda p, i: (0, first(p, i))),
            pl.BlockSpec((1, rows, width), lambda p, i: (jnp.maximum(p - 1, 0), 0, rest(p, i))),
            pl.BlockSpec((RIM, width), lambda p, i: (0, first(p, i))),
            pl.BlockSpec((1, RIM, width), lambda p, i: (jnp.maximum(p - 1, 0), 0, rest(p, i))),
            pl.BlockSpec((short_taps, width), lambda p, i: (0, p * steps + i)),
        ],
        out_specs=pl.BlockSpec((rows, width), lambda p, i: (0, p * steps + i)),
        out_shape=jax.ShapeDtypeStruct((rows, 3 * channels), BF16),
        compiler_params=params(),
        cost_estimate=cost(6 * short_taps * rows * channels, 12 * rows * channels),
        name="short_adjoint",
    )(query, other, query_rim, other_rim, filters)


def spread_kernel(place, query_ref, key_ref, value_ref, long_ref, out_ref):
    steps = query_ref.shape[1] // LANES
    for part, ref in enumerate((query_ref, key_ref, value_ref)):
        for i in range(steps):
            out_ref[place[part * steps + i]] = ref[:, i * LANES : (i + 1) * LANES]
    for i in range(long_ref.shape[0] // 8):
        out_ref[place[3 * steps + i]] = long_ref[8 * i : 8 * i + 8, :]


def collect_kernel(place, tiles_ref, short_ref, long_ref):
    short_taps, wide = short_ref.shape
    steps = wide // LANES
    for i in range(steps):
        short_ref[:, i * LANES : (i + 1) * LANES] = tiles_ref[place[i]][0:short_taps, :]
    for i in range(long_ref.shape[0] // 8):
        long_ref[8 * i : 8 * i + 8, :] = tiles_ref[place[steps + i]]


def in_vmem():
    return pl.BlockSpec(memory_space=pltpu.VMEM)


def total_over_devices(places, query_sum, key_sum, value_sum, long_sum, short_taps):
    ny, nz = lax.axis_size("y"), lax.axis_size("z")
    channels = query_sum.shape[1]
    count = 3 * channels // LANES + long_sum.shape[0] // 8
    tiles = pl.pallas_call(
        spread_kernel,
        in_specs=[pl.BlockSpec(memory_space=pltpu.SMEM)] + [in_vmem()] * 4,
        out_specs=in_vmem(),
        out_shape=jax.ShapeDtypeStruct((count, 8, LANES), F32),
        compiler_params=params(),
        name="spread",
    )(places, query_sum, key_sum, value_sum, long_sum)
    half = count // 2
    part = tiles[:half] + move(tiles[half:], c=1)
    size = half // nz
    part = sum([move(part[d * size : (d + 1) * size], z=d) for d in range(1, nz)], part[:size])
    whole = paired_sum([part] + [move(part, y=d) for d in range(1, ny)])
    whole = paired_sum([move(whole, xl=a, xh=b) for a, b in FLIPS])
    line = jnp.concatenate([move(whole, z=-d) for d in range(nz)], axis=0)
    tiles = jnp.concatenate([line, move(line, c=1)], axis=0)
    groups, taps = long_sum.shape
    return pl.pallas_call(
        collect_kernel,
        in_specs=[pl.BlockSpec(memory_space=pltpu.SMEM), in_vmem()],
        out_specs=[in_vmem(), in_vmem()],
        out_shape=[
            jax.ShapeDtypeStruct((short_taps, 3 * channels), F32),
            jax.ShapeDtypeStruct((groups, taps), F32),
        ],
        compiler_params=params(),
        name="collect",
    )(places, tiles)


def paired_sum(terms):
    half = len(terms) // 2
    if half == 0:
        return terms[0]
    return paired_sum([terms[i] + terms[i + half] for i in range(half)])


def gather_near(shard):
    ny = lax.axis_size("y")
    half = shard.shape[0] // 2
    top, bottom = shard[:half], shard[half:]
    return (
        jnp.stack([move(top, xl=a, xh=b) for a, b in FLIPS]),
        jnp.stack([move(bottom, y=d) for d in range(ny)]),
    )


def gather_far(wide_top, tall_bottom):
    ny = lax.axis_size("y")
    return (
        [move(wide_top, y=d) for d in range(ny)],
        [move(tall_bottom, xl=a, xh=b) for a, b in FLIPS],
    )


def piece_rows(tops, bottoms, step):
    rows = []
    for a in range(2):
        rows.append(jnp.concatenate([tops[step][2 * a + b] for b in range(2)], axis=1))
        rows.append(jnp.concatenate([bottoms[2 * a + b][step] for b in range(2)], axis=1))
    return rows


def gate_matmul_kernel(ny, *refs):
    cotangent_ref, tops, bottoms, out_ref = refs[0], refs[1 : 1 + ny], refs[1 + ny : 5 + ny], refs[5 + ny]
    left = cotangent_ref[...]
    at = 0
    for step in range(ny):
        for right in piece_rows(tops, bottoms, step):
            size = right.shape[0]
            out_ref[:, at : at + size] = lax.dot_general(
                left, right, (((1,), (1,)), ((), ())), preferred_element_type=F32
            ).astype(BF16)
            at += size


def whole(x):
    return pl.BlockSpec(x.shape, lambda *_, n=x.ndim: (0,) * n)


def gate_matmul(cotangents, tops, bottoms):
    rows, depth = cotangents.shape
    ny = len(tops)
    channels = 4 * ny * tops[0].shape[1]
    height = rows // 2
    return pl.pallas_call(
        functools.partial(gate_matmul_kernel, ny),
        grid=(rows // height,),
        in_specs=[pl.BlockSpec((height, depth), lambda i: (i, 0))] + [whole(x) for x in (*tops, *bottoms)],
        out_specs=pl.BlockSpec((height, channels), lambda i: (i, 0)),
        out_shape=jax.ShapeDtypeStruct((rows, channels), BF16),
        compiler_params=params(),
        cost_estimate=cost(2 * rows * depth * channels, 2 * (rows + depth) * channels),
        name="gate_matmul",
    )(cotangents, *tops, *bottoms)


def project_kernel(ny, *refs):
    rows_ref, turned_ref, tops, bottoms = refs[0], refs[1], refs[2 : 2 + ny], refs[2 + ny : 6 + ny]
    own_ref, other_ref = refs[6 + ny : 8 + ny]
    top_grads, bottom_grads = refs[8 + ny : 8 + 2 * ny], refs[8 + 2 * ny : 12 + 2 * ny]
    total = refs[12 + 2 * ny]
    step = pl.program_id(0)
    width = own_ref.shape[1]
    size = tops[0].shape[1]
    grads = jnp.dot(turned_ref[...], rows_ref[...], preferred_element_type=F32).astype(BF16)
    for a in range(2):
        for b in range(2):
            at = (2 * a + 1) * size
            bottom_grads[2 * a + b][step] = grads[b * width : (b + 1) * width, at : at + size]
    for d in range(ny):

        @pl.when(step == d)
        def _(d=d):
            for a in range(2):
                for b in range(2):
                    at = 2 * a * size
                    top_grads[d][2 * a + b] = grads[b * width : (b + 1) * width, at : at + size]
            right = jnp.concatenate(piece_rows(tops, bottoms, d), axis=0)
            product = jnp.dot(rows_ref[...], right, preferred_element_type=F32)
            if d == 0:
                total[...] = product
            else:
                total[...] += product

    @pl.when(step == ny - 1)
    def _():
        own_ref[...] = total[:, :width].astype(BF16)
        other_ref[...] = total[:, width:].astype(BF16)


def project(all_rows, turned, tops, bottoms):
    rows, channels = all_rows.shape
    ny = len(tops)
    size = tops[0].shape[1]
    width = turned.shape[0] // 2
    half = jax.ShapeDtypeStruct((rows, width), BF16)
    outs = (
        [half, half]
        + [jax.ShapeDtypeStruct((4, width, size), BF16)] * ny
        + [jax.ShapeDtypeStruct((ny, width, size), BF16)] * 4
    )
    results = pl.pallas_call(
        functools.partial(project_kernel, ny),
        grid=(ny,),
        in_specs=[pl.BlockSpec((rows, channels // ny), lambda i: (0, i)), whole(turned)]
        + [whole(x) for x in (*tops, *bottoms)],
        out_specs=[whole(x) for x in outs],
        out_shape=outs,
        scratch_shapes=[pltpu.VMEM((rows, 2 * width), F32)],
        compiler_params=params(),
        cost_estimate=cost(8 * rows * width * channels, 2 * (rows + 4 * width) * channels),
        name="project",
    )(all_rows, turned, *tops, *bottoms)
    return results[0], results[1], results[2 : 2 + ny], results[2 + ny :]


def plane_scatter_sum(top_grads, bottom_grads):
    ny = len(top_grads)

    def added(terms):
        total = terms[0].astype(F32)
        for term in terms[1:]:
            total = total + term.astype(F32)
        return total

    top = added([move(top_grads[d], y=-d) for d in range(ny)]).astype(BF16)
    bottom = added([move(bottom_grads[f], xl=a, xh=b) for f, (a, b) in enumerate(FLIPS)]).astype(BF16)
    top = added([move(top[f], xl=a, xh=b) for f, (a, b) in enumerate(FLIPS)])
    bottom = added([move(bottom[d], y=-d) for d in range(ny)])
    return jnp.concatenate([top, bottom], axis=1).T


def mirrored(lines):
    return jnp.roll(lines[:, ::-1], 1, axis=1)


def shards(tokens_in, short_filter, long_filter, out_weight, cotangent):
    ny, nz = lax.axis_size("y"), lax.axis_size("z")
    y, xl, xh, z, c = (lax.axis_index(a) for a in ("y", "xl", "xh", "z", "c"))
    tokens = tokens_in[0]
    rows, wide = tokens.shape
    channels = wide // 3
    short_taps = short_filter.shape[0]
    groups = long_filter.shape[0]
    upstream = cotangent[0]
    length, columns = upstream.shape
    span = length // 2

    block = jnp.arange(2 * ny, dtype=jnp.int32)
    place = ((y - block // 2) % ny) * 2 + (block + xl) % 2
    size = 3 * channels // LANES + groups // 8
    each = size // (2 * nz)
    tile = jnp.arange(size, dtype=jnp.int32)
    places = ((tile // (nz * each) + c) % 2 * nz + (tile // each - z) % nz) * each + tile % each

    wide_top, tall_bottom = gather_near(out_weight)
    mine = lax.dynamic_slice_in_dim(upstream, xh * span, span, 0)
    others = move(lax.dynamic_slice_in_dim(upstream, (1 - xh) * span, span, 0), xh=1)
    cotangents = jnp.concatenate([mine, others], axis=1)

    rim = along(tokens[rows - RIM :], 1)
    lines = long_filter.astype(F32)
    query, key, value, mixer = features_call(tokens, rim, short_filter)
    mixer_prev = along(mixer, 1)
    mixer_prev, wide_top, tall_bottom = lax.optimization_barrier((mixer_prev, wide_top, tall_bottom))
    tops, bottoms = gather_far(wide_top, tall_bottom)
    mixed, gated = mix_call(place, mirrored(lines), mixer_prev, mixer, query)

    partial = gate_matmul(cotangents, tops, bottoms)
    gate_grad = lax.psum_scatter(partial, ("z", "c"), scatter_dimension=0, tiled=True)
    all_rows = lax.all_gather(gated, ("z", "c"), axis=0, tiled=True)

    grad_mixed, query_grad = gate_call(place, gate_grad, query, mixed)
    grad_next = along(grad_mixed, -1)
    query_next = along(query_grad[:RIM], -1)
    long_sum, query_sum = long_grad_call(
        groups, short_taps, mixer_prev, mixer, grad_mixed, query_grad, tokens, rim
    )
    other_grads, key_sum, value_sum = unmix_call(
        lines, short_taps, grad_mixed, grad_next, key, value, tokens, rim
    )
    other_next = along(other_grads[:, :RIM], -1)
    grad_short, grad_long = total_over_devices(places, query_sum, key_sum, value_sum, long_sum, short_taps)
    grad_tokens = short_adjoint_call(query_grad, other_grads, query_next, other_next, short_filter)

    own, other, top_grads, bottom_grads = project(all_rows, cotangents.T, tops, bottoms)
    grad_weight = plane_scatter_sum(top_grads, bottom_grads)
    theirs = move(other, xh=1)
    output = jnp.where(xh == 0, jnp.concatenate([own, theirs], axis=0), jnp.concatenate([theirs, own], axis=0))
    return output[None], grad_tokens[None], grad_short, mirrored(grad_long), grad_weight


def solution(mesh):
    dp, seq = mesh.shape["dp"], mesh.shape["seq"]
    grid = jax.sharding.Mesh(mesh.devices.reshape(dp // 2, 2, 2, seq // 4, 2), ("y", "xl", "xh", "z", "c"))
    rows, line = ("y", "xl"), ("xh", "z", "c")
    return jax.shard_map(
        shards,
        mesh=grid,
        in_specs=(P(rows, line, None), P(), P(), P(rows, line), P(rows, None, line)),
        out_specs=(P(rows, None, line), P(rows, line, None), P(), P(), P(rows, line)),
        check_vma=False,
    )
```

```python
import functools
import itertools
import math

import jax
import jax.numpy as jnp
from jax import lax
from jax.experimental import pallas as pl
from jax.experimental.pallas import tpu as pltpu
from jax.sharding import PartitionSpec as P

LANES = 128
RIM = 8
MIB = 1024 * 1024
F32 = jnp.float32
BF16 = jnp.bfloat16


PLANE = ("y", "xl", "xh")
LINE = ("xh", "z", "c")


def along(x, by):
    size = math.prod(lax.axis_size(a) for a in LINE)
    pairs = [(i, i + by) for i in range(size) if 0 <= i + by < size]
    return lax.ppermute(x, LINE, pairs)


def move(x, **steps):
    axes = tuple(a for a in ("y", "xl", "xh", "z", "c") if steps.get(a, 0) % lax.axis_size(a))
    if not axes:
        return x
    sizes = [lax.axis_size(a) for a in axes]
    pairs = []
    for at in itertools.product(*(range(n) for n in sizes)):
        to = [(p + steps[a]) % n for p, a, n in zip(at, axes, sizes)]
        pairs.append((flat(at, sizes), flat(to, sizes)))
    return lax.ppermute(x, axes, pairs)


def flat(at, sizes):
    index = 0
    for p, n in zip(at, sizes):
        index = index * n + p
    return index


FLIPS = [(0, 0), (0, 1), (1, 0), (1, 1)]


def params(mib=16):
    return pltpu.CompilerParams(vmem_limit_bytes=mib * MIB)


def cost(flops, moved):
    return pl.CostEstimate(flops=int(flops), bytes_accessed=int(moved), transcendentals=0)


def block_width(channels, most):
    width = min(channels, most)
    while channels % width:
        width //= 2
    return width


def features_kernel(short_taps, tokens, rims, filters, query_ref, key_ref, value_ref, mixer_ref):
    rows = tokens[0].shape[0]

    def filtered(part):
        ext = jnp.concatenate([rims[part][...].astype(F32), tokens[part][...].astype(F32)], axis=0)
        total = filters[part][0:1, :] * ext[RIM : RIM + rows]
        for tap in range(1, short_taps):
            total = total + filters[part][tap : tap + 1, :] * ext[RIM - tap : RIM - tap + rows]
        return total

    query_ref[...] = filtered(0).astype(BF16)
    key, value = filtered(1), filtered(2)
    key_ref[...] = key.astype(BF16)
    value_ref[...] = value.astype(BF16)
    mixer_ref[...] = (key * value).astype(BF16)


def features_call(tokens, rim, filters):
    rows, wide = tokens.shape
    channels = wide // 3
    taps = filters.shape[0]
    width = block_width(channels, 512)
    steps = channels // width

    def spec(height, part):
        return pl.BlockSpec((height, width), lambda i, part=part: (0, i + part * steps))

    def body(*refs):
        features_kernel(taps, refs[0:3], refs[3:6], refs[6:9], *refs[9:])

    out = jax.ShapeDtypeStruct((rows, channels), BF16)
    return pl.pallas_call(
        body,
        grid=(steps,),
        in_specs=[spec(rows, p) for p in range(3)]
        + [spec(RIM, p) for p in range(3)]
        + [spec(taps, p) for p in range(3)],
        out_specs=[pl.BlockSpec((rows, width), lambda i: (0, i))] * 4,
        out_shape=[out] * 4,
        compiler_params=params(),
        cost_estimate=cost(0, rows * wide),
        name="features",
    )(tokens, tokens, tokens, rim, rim, rim, filters, filters, filters)


def lane_row(shape):
    row = lax.broadcasted_iota(jnp.int32, shape, 0)
    lane = lax.broadcasted_iota(jnp.int32, shape, 1)
    return row, lane


def circulant(line, taps):
    wide = jnp.broadcast_to(line.astype(F32), (taps, taps))
    return pltpu.roll(wide, 0, 1, stride=1, stride_axis=0)


def pick_groups(product, rows, per_group):
    lane = lax.broadcasted_iota(jnp.int32, (rows, LANES), 1) // per_group
    total = product[0:rows]
    for g in range(1, LANES // per_group):
        total = jnp.where(lane == g, product[g * rows : (g + 1) * rows], total)
    return total


def mix_kernel(per_group, place, lines_ref, prev_ref, cur_ref, query_ref, mixed_ref, gated_ref, table):
    rows, width = cur_ref.shape
    row, lane = lane_row((rows, rows))
    above = lane > row
    packed = LANES // per_group
    for block in range(width // LANES):
        at = pl.ds(block * LANES, LANES)
        for g in range(packed):
            ring = circulant(lines_ref[block * packed + g : block * packed + g + 1, :], rows)
            table[g * rows : (g + 1) * rows, 0:rows] = jnp.where(above, ring, 0.0).astype(BF16)
            table[g * rows : (g + 1) * rows, rows : 2 * rows] = jnp.where(above, 0.0, ring).astype(BF16)
        window = jnp.concatenate([prev_ref[:, at], cur_ref[:, at]], axis=0)
        product = jnp.dot(table[...], window, preferred_element_type=F32)
        mixed = pick_groups(product, rows, per_group)
        mixed_ref[:, at] = mixed.astype(BF16)
        gated_ref[:, at] = (query_ref[:, at].astype(F32) * mixed).astype(BF16)


def mix_call(place, lines, prev, cur, query):
    rows, channels = cur.shape
    groups, taps = lines.shape
    per_group = channels // groups
    steps = place.shape[0]
    width = channels // steps
    wide = pl.BlockSpec((rows, width), lambda i, place: (0, i))
    out = jax.ShapeDtypeStruct((rows, channels), BF16)
    return pl.pallas_call(
        functools.partial(mix_kernel, per_group),
        grid_spec=pltpu.PrefetchScalarGridSpec(
            num_scalar_prefetch=1,
            grid=(steps,),
            in_specs=[pl.BlockSpec((width // per_group, taps), lambda i, place: (i, 0)), wide, wide, wide],
            out_specs=[wide, pl.BlockSpec((rows, width), lambda i, place: (0, place[i]))],
            scratch_shapes=[pltpu.VMEM((LANES // per_group * rows, 2 * rows), BF16)],
        ),
        out_shape=[out, out],
        compiler_params=params(),
        cost_estimate=cost(0, 2 * rows * channels),
        name="mix",
    )(place, lines, prev, cur, query)


def gate_kernel(place, gate_grad_ref, query_ref, mixed_ref, grad_ref, feature_ref):
    gate_grad = gate_grad_ref[...].astype(F32)
    grad_ref[...] = (gate_grad * query_ref[...].astype(F32)).astype(BF16)
    feature_ref[...] = (gate_grad * mixed_ref[...].astype(F32)).astype(BF16)


def gate_call(place, gate_grad, query, mixed):
    rows, channels = query.shape
    steps = place.shape[0]
    width = channels // steps
    wide = pl.BlockSpec((rows, width), lambda i, place: (0, i))
    out = jax.ShapeDtypeStruct((rows, channels), BF16)
    return pl.pallas_call(
        gate_kernel,
        grid_spec=pltpu.PrefetchScalarGridSpec(
            num_scalar_prefetch=1,
            grid=(steps,),
            in_specs=[pl.BlockSpec((rows, width), lambda i, place: (0, place[i])), wide, wide],
            out_specs=[wide, wide],
        ),
        out_shape=[out, out],
        compiler_params=params(),
        cost_estimate=cost(2 * rows * channels, 10 * rows * channels),
        name="gate_back",
    )(place, gate_grad, query, mixed)


def tap_sums(short_taps, grads, tokens_ref, rim_ref, out_ref):
    rows = tokens_ref.shape[0]
    ext = jnp.concatenate([rim_ref[...].astype(F32), tokens_ref[...].astype(F32)], axis=0)
    for tap in range(short_taps):
        out_ref[tap : tap + 1, :] = jnp.sum(grads * ext[RIM - tap : RIM - tap + rows], axis=0, keepdims=True)
    out_ref[short_taps:8, :] = jnp.zeros((8 - short_taps, out_ref.shape[1]), F32)


def long_grad_kernel(
    per_group, short_taps, prev_ref, cur_ref, grad_ref, feature_ref, tokens_ref, rim_ref, long_ref, short_ref, fold
):
    rows, width = cur_ref.shape
    row, lane = lane_row((rows, rows))
    above = lane > row
    member = lax.broadcasted_iota(jnp.int32, (rows, LANES), 1) // per_group
    packed = LANES // per_group
    for block in range(width // LANES):
        at = pl.ds(block * LANES, LANES)
        window = jnp.concatenate([prev_ref[:, at], cur_ref[:, at]], axis=0)
        grad_wide = grad_ref[:, at].astype(F32)
        for g in range(packed):
            own = jnp.where(member == g, grad_wide, 0.0).astype(BF16)
            pairs = lax.dot_general(own, window, (((1,), (1,)), ((), ())), preferred_element_type=F32)
            ring = jnp.where(above, pairs[:, 0:rows], pairs[:, rows : 2 * rows])
            total = ring[0:8]
            for tile in range(1, rows // 8):
                total = total + pltpu.roll(ring[8 * tile : 8 * tile + 8], rows - 8 * tile, 1)
            fold[g * 8 : (g + 1) * 8, :] = total
        total = fold[pl.ds(0, packed, stride=8), :]
        for step in range(1, 8):
            total = total + pltpu.roll(fold[pl.ds(step, packed, stride=8), :], rows - step, 1)
        long_ref[block * packed : (block + 1) * packed, :] = total
    tap_sums(short_taps, feature_ref[...].astype(F32), tokens_ref, rim_ref, short_ref)


def long_grad_call(groups, short_taps, prev, cur, grad, feature, tokens, rim):
    rows, channels = cur.shape
    per_group = channels // groups
    width = block_width(channels, 512)
    steps = channels // width
    wide = pl.BlockSpec((rows, width), lambda i: (0, i))
    packed = LANES // per_group
    return pl.pallas_call(
        functools.partial(long_grad_kernel, per_group, short_taps),
        grid=(steps,),
        in_specs=[wide] * 5 + [pl.BlockSpec((RIM, width), lambda i: (0, i))],
        out_specs=[
            pl.BlockSpec((width // per_group, rows), lambda i: (i, 0)),
            pl.BlockSpec((8, width), lambda i: (0, i)),
        ],
        out_shape=[
            jax.ShapeDtypeStruct((groups, rows), F32),
            jax.ShapeDtypeStruct((8, channels), F32),
        ],
        scratch_shapes=[pltpu.VMEM((packed * 8, LANES), F32)],
        compiler_params=params(),
        cost_estimate=cost(2 * groups * rows * 2 * rows * LANES, 10 * rows * channels),
        name="long_grad",
    )(prev, cur, grad, feature, tokens, rim)


def unmix_kernel(
    per_group, short_taps, lines_ref, grad_ref, next_ref, key_ref, value_ref, key_tokens_ref, value_tokens_ref,
    key_rim_ref, value_rim_ref, feature_ref, key_sum_ref, value_sum_ref, table,
):
    rows, width = grad_ref.shape
    row, lane = lane_row((rows, rows))
    below = lane < row
    packed = LANES // per_group
    for block in range(width // LANES):
        at = pl.ds(block * LANES, LANES)
        for g in range(packed):
            ring = circulant(lines_ref[block * packed + g : block * packed + g + 1, :], rows)
            table[g * rows : (g + 1) * rows, 0:rows] = jnp.where(below, 0.0, ring).astype(BF16)
            table[g * rows : (g + 1) * rows, rows : 2 * rows] = jnp.where(below, ring, 0.0).astype(BF16)
        window = jnp.concatenate([grad_ref[:, at], next_ref[:, at]], axis=0)
        product = jnp.dot(table[...], window, preferred_element_type=F32)
        grad_mixer = pick_groups(product, rows, per_group)
        feature_ref[0, :, at] = (grad_mixer * value_ref[:, at].astype(F32)).astype(BF16)
        feature_ref[1, :, at] = (grad_mixer * key_ref[:, at].astype(F32)).astype(BF16)
    tap_sums(short_taps, feature_ref[0].astype(F32), key_tokens_ref, key_rim_ref, key_sum_ref)
    tap_sums(short_taps, feature_ref[1].astype(F32), value_tokens_ref, value_rim_ref, value_sum_ref)


def unmix_call(lines, short_taps, grad, grad_next, key, value, tokens, rim):
    rows, channels = grad.shape
    groups, taps = lines.shape
    per_group = channels // groups
    width = block_width(channels, 512)
    steps = channels // width

    def spec(height, part):
        return pl.BlockSpec((height, width), lambda i, part=part: (0, i + part * steps))

    wide = spec(rows, 0)
    packed = LANES // per_group
    sums = jax.ShapeDtypeStruct((8, channels), F32)
    return pl.pallas_call(
        functools.partial(unmix_kernel, per_group, short_taps),
        grid=(steps,),
        in_specs=[pl.BlockSpec((width // per_group, taps), lambda i: (i, 0))]
        + [wide] * 4
        + [spec(rows, 1), spec(rows, 2), spec(RIM, 1), spec(RIM, 2)],
        out_specs=[pl.BlockSpec((2, rows, width), lambda i: (0, 0, i)), spec(8, 0), spec(8, 0)],
        out_shape=[jax.ShapeDtypeStruct((2, rows, channels), BF16), sums, sums],
        scratch_shapes=[pltpu.VMEM((packed * rows, 2 * rows), BF16)],
        compiler_params=params(),
        cost_estimate=cost(2 * groups * rows * 2 * rows * LANES, 16 * rows * channels),
        name="unmix",
    )(lines, grad, grad_next, key, value, tokens, tokens, rim, rim)


def short_adjoint_kernel(short_taps, grads_ref, rim_ref, filter_ref, *refs):
    out_ref = refs[-1]
    rows = out_ref.shape[0]
    ext = jnp.concatenate([grads_ref[0].astype(F32), rim_ref[0].astype(F32)], axis=0)
    total = filter_ref[0:1, :] * ext[0:rows]
    for tap in range(1, short_taps):
        total = total + filter_ref[tap : tap + 1, :] * ext[tap : tap + rows]
    out_ref[...] = total.astype(BF16)


def short_adjoint_call(grads, rim, filters, first, out):
    parts, rows, channels = grads.shape
    short_taps = filters.shape[0]
    width = block_width(channels, 1024)
    steps = channels // width
    result = pl.BlockSpec((rows, width), lambda p, i: (0, (p + first) * steps + i))
    given = [] if out is None else [out]
    return pl.pallas_call(
        functools.partial(short_adjoint_kernel, short_taps),
        grid=(parts, steps),
        in_specs=[
            pl.BlockSpec((1, rows, width), lambda p, i: (p, 0, i)),
            pl.BlockSpec((1, RIM, width), lambda p, i: (p, 0, i)),
            pl.BlockSpec((short_taps, width), lambda p, i: (0, (p + first) * steps + i)),
        ]
        + [pl.BlockSpec(memory_space=pl.ANY)] * len(given),
        out_specs=result,
        out_shape=jax.ShapeDtypeStruct((rows, 3 * channels), BF16),
        input_output_aliases={3: 0} if given else {},
        compiler_params=params(),
        cost_estimate=cost(2 * parts * short_taps * rows * channels, 4 * parts * rows * channels),
        name="short_adjoint",
    )(grads, rim, filters, *given)


def spread_kernel(place, query_ref, key_ref, value_ref, long_ref, out_ref):
    steps = query_ref.shape[1] // LANES
    for part, ref in enumerate((query_ref, key_ref, value_ref)):
        for i in range(steps):
            out_ref[place[part * steps + i]] = ref[:, i * LANES : (i + 1) * LANES]
    for i in range(long_ref.shape[0] // 8):
        out_ref[place[3 * steps + i]] = long_ref[8 * i : 8 * i + 8, :]


def collect_kernel(place, tiles_ref, short_ref, long_ref):
    short_taps, wide = short_ref.shape
    steps = wide // LANES
    for i in range(steps):
        short_ref[:, i * LANES : (i + 1) * LANES] = tiles_ref[place[i]][0:short_taps, :]
    for i in range(long_ref.shape[0] // 8):
        long_ref[8 * i : 8 * i + 8, :] = tiles_ref[place[steps + i]]


def in_vmem():
    return pl.BlockSpec(memory_space=pltpu.VMEM)


def total_over_devices(places, query_sum, key_sum, value_sum, long_sum, short_taps):
    ny, nz = lax.axis_size("y"), lax.axis_size("z")
    channels = query_sum.shape[1]
    count = 3 * channels // LANES + long_sum.shape[0] // 8
    tiles = pl.pallas_call(
        spread_kernel,
        in_specs=[pl.BlockSpec(memory_space=pltpu.SMEM)] + [in_vmem()] * 4,
        out_specs=in_vmem(),
        out_shape=jax.ShapeDtypeStruct((count, 8, LANES), F32),
        compiler_params=params(),
        name="spread",
    )(places, query_sum, key_sum, value_sum, long_sum)
    half = count // 2
    part = tiles[:half] + move(tiles[half:], c=1)
    size = half // nz
    part = sum([move(part[d * size : (d + 1) * size], z=d) for d in range(1, nz)], part[:size])
    whole = paired_sum([part] + [move(part, y=d) for d in range(1, ny)])
    whole = paired_sum([move(whole, xl=a, xh=b) for a, b in FLIPS])
    line = jnp.concatenate([move(whole, z=-d) for d in range(nz)], axis=0)
    tiles = jnp.concatenate([line, move(line, c=1)], axis=0)
    groups, taps = long_sum.shape
    return pl.pallas_call(
        collect_kernel,
        in_specs=[pl.BlockSpec(memory_space=pltpu.SMEM), in_vmem()],
        out_specs=[in_vmem(), in_vmem()],
        out_shape=[
            jax.ShapeDtypeStruct((short_taps, 3 * channels), F32),
            jax.ShapeDtypeStruct((groups, taps), F32),
        ],
        compiler_params=params(),
        name="collect",
    )(places, tiles)


def paired_sum(terms):
    half = len(terms) // 2
    if half == 0:
        return terms[0]
    return paired_sum([terms[i] + terms[i + half] for i in range(half)])


def gather_near(shard):
    ny = lax.axis_size("y")
    half = shard.shape[0] // 2
    top, bottom = shard[:half], shard[half:]
    return (
        jnp.stack([move(top, xl=a, xh=b) for a, b in FLIPS]),
        jnp.stack([move(bottom, y=d) for d in range(ny)]),
    )


def gather_far(wide_top, tall_bottom):
    ny = lax.axis_size("y")
    return (
        [move(wide_top, y=d) for d in range(ny)],
        [move(tall_bottom, xl=a, xh=b) for a, b in FLIPS],
    )


def piece_rows(tops, bottoms, step):
    rows = []
    for a in range(2):
        rows.append(jnp.concatenate([tops[step][2 * a + b] for b in range(2)], axis=1))
        rows.append(jnp.concatenate([bottoms[2 * a + b][step] for b in range(2)], axis=1))
    return rows


def gate_matmul_kernel(ny, *refs):
    cotangent_ref, tops, bottoms, out_ref = refs[0], refs[1 : 1 + ny], refs[1 + ny : 5 + ny], refs[5 + ny]
    left = cotangent_ref[...]
    at = 0
    for step in range(ny):
        for right in piece_rows(tops, bottoms, step):
            size = right.shape[0]
            out_ref[:, at : at + size] = lax.dot_general(
                left, right, (((1,), (1,)), ((), ())), preferred_element_type=F32
            ).astype(BF16)
            at += size


def whole(x):
    return pl.BlockSpec(x.shape, lambda *_, n=x.ndim: (0,) * n)


def gate_matmul(cotangents, tops, bottoms):
    rows, depth = cotangents.shape
    ny = len(tops)
    channels = 4 * ny * tops[0].shape[1]
    height = rows // 2
    return pl.pallas_call(
        functools.partial(gate_matmul_kernel, ny),
        grid=(rows // height,),
        in_specs=[pl.BlockSpec((height, depth), lambda i: (i, 0))] + [whole(x) for x in (*tops, *bottoms)],
        out_specs=pl.BlockSpec((height, channels), lambda i: (i, 0)),
        out_shape=jax.ShapeDtypeStruct((rows, channels), BF16),
        compiler_params=params(32),
        cost_estimate=cost(2 * rows * depth * channels, 2 * (rows + depth) * channels),
        name="gate_matmul",
    )(cotangents, *tops, *bottoms)


def project_kernel(ny, count, place, *refs):
    pieces, refs = refs[:count], refs[count - 1 :]
    turned_ref, tops, bottoms = refs[1], refs[2 : 2 + ny], refs[2 + ny : 6 + ny]
    own_ref, other_ref = refs[6 + ny : 8 + ny]
    top_grads, bottom_grads = refs[8 + ny : 8 + 2 * ny], refs[8 + 2 * ny : 12 + 2 * ny]
    total, turned = refs[12 + 2 * ny :]
    step = pl.program_id(0)
    height = pieces[0].shape[0]
    blocks = total.shape[0] // height

    @pl.when(step == 0)
    def _():
        for j in range(blocks):
            at = pl.multiple_of(place[j] * height, height)
            turned[:, j * height : (j + 1) * height] = turned_ref[:, pl.ds(at, height)]

    rows = jnp.concatenate([p[...] for p in pieces], axis=0)
    width = own_ref.shape[1]
    size = tops[0].shape[1]
    grads = jnp.dot(turned[...], rows, preferred_element_type=F32).astype(BF16)
    for a in range(2):
        for b in range(2):
            at = (2 * a + 1) * size
            bottom_grads[2 * a + b][step] = grads[b * width : (b + 1) * width, at : at + size]
    for d in range(ny):

        @pl.when(step == d)
        def _(d=d):
            for a in range(2):
                for b in range(2):
                    at = 2 * a * size
                    top_grads[d][2 * a + b] = grads[b * width : (b + 1) * width, at : at + size]
            right = jnp.concatenate(piece_rows(tops, bottoms, d), axis=0)
            product = jnp.dot(rows, right, preferred_element_type=F32)
            if d == 0:
                total[...] = product
            else:
                total[...] += product

    @pl.when(step == ny - 1)
    def _():
        for j in range(blocks):
            at = pl.ds(pl.multiple_of(place[j] * height, height), height)
            own_ref[at, :] = total[j * height : (j + 1) * height, :width].astype(BF16)
            other_ref[at, :] = total[j * height : (j + 1) * height, width:].astype(BF16)


def line_gather(x):
    half = x.shape[0] // 2
    before, after = move(x, z=1), move(x, z=-1)
    far = [move(before[:half], z=1), move(after[half:], z=-1)]
    pieces = [x, before, after, *far]
    return pieces + [move(p, c=1) for p in pieces]


def project(place, pieces, turned, tops, bottoms):
    rows = sum(p.shape[0] for p in pieces)
    channels = pieces[0].shape[1]
    ny = len(tops)
    size = tops[0].shape[1]
    width = turned.shape[0] // 2
    half = jax.ShapeDtypeStruct((rows, width), BF16)
    outs = (
        [half, half]
        + [jax.ShapeDtypeStruct((4, width, size), BF16)] * ny
        + [jax.ShapeDtypeStruct((ny, width, size), BF16)] * 4
    )
    results = pl.pallas_call(
        functools.partial(project_kernel, ny, len(pieces)),
        grid_spec=pltpu.PrefetchScalarGridSpec(
            num_scalar_prefetch=1,
            grid=(ny,),
            in_specs=[pl.BlockSpec((p.shape[0], channels // ny), lambda i, place: (0, i)) for p in pieces]
            + [whole(turned)]
            + [whole(x) for x in (*tops, *bottoms)],
            out_specs=[whole(x) for x in outs],
            scratch_shapes=[pltpu.VMEM((rows, 2 * width), F32), pltpu.VMEM(turned.shape, BF16)],
        ),
        out_shape=outs,
        compiler_params=params(40),
        cost_estimate=cost(8 * rows * width * channels, 2 * (rows + 4 * width) * channels),
        name="project",
    )(place, *pieces, turned, *tops, *bottoms)
    return results[0], results[1], results[2 : 2 + ny], results[2 + ny :]


def plane_scatter_sum(top_grads, bottom_grads):
    ny = len(top_grads)

    def added(terms):
        total = terms[0].astype(F32)
        for term in terms[1:]:
            total = total + term.astype(F32)
        return total

    top = added([move(top_grads[d], y=-d) for d in range(ny)]).astype(BF16)
    bottom = added([move(bottom_grads[f], xl=a, xh=b) for f, (a, b) in enumerate(FLIPS)]).astype(BF16)
    top = added([move(top[f], xl=a, xh=b) for f, (a, b) in enumerate(FLIPS)])
    bottom = added([move(bottom[d], y=-d) for d in range(ny)])
    return jnp.concatenate([top, bottom], axis=1).T


def mirrored(lines):
    return jnp.roll(lines[:, ::-1], 1, axis=1)


def shards(tokens_in, short_filter, long_filter, out_weight, cotangent):
    ny, nz = lax.axis_size("y"), lax.axis_size("z")
    y, xl, xh, z, c = (lax.axis_index(a) for a in ("y", "xl", "xh", "z", "c"))
    tokens = tokens_in[0]
    rows, wide = tokens.shape
    channels = wide // 3
    short_taps = short_filter.shape[0]
    groups = long_filter.shape[0]
    upstream = cotangent[0]
    length, columns = upstream.shape
    span = length // 2

    block = jnp.arange(2 * ny, dtype=jnp.int32)
    place = ((y - block // 2) % ny) * 2 + (block + xl) % 2
    step = jnp.arange(2 * nz, dtype=jnp.int32)
    near = jnp.array([0, -1, 1, 2], jnp.int32)[step % nz]
    row_place = (z + near) % nz * 2 + (step // nz + c) % 2
    size = 3 * channels // LANES + groups // 8
    each = size // (2 * nz)
    tile = jnp.arange(size, dtype=jnp.int32)
    places = ((tile // (nz * each) + c) % 2 * nz + (tile // each - z) % nz) * each + tile % each

    rim = along(tokens[rows - RIM :], 1)
    rim, out_weight = lax.optimization_barrier((rim, out_weight))
    wide_top, tall_bottom = gather_near(out_weight)
    mine = lax.dynamic_slice_in_dim(upstream, xh * span, span, 0)
    others = move(lax.dynamic_slice_in_dim(upstream, (1 - xh) * span, span, 0), xh=1)
    cotangents = jnp.concatenate([mine, others], axis=1)

    lines = long_filter.astype(F32)
    query, key, value, mixer = features_call(tokens, rim, short_filter)
    mixer, wide_top, tall_bottom = lax.optimization_barrier((mixer, wide_top, tall_bottom))
    tops, bottoms = gather_far(wide_top, tall_bottom)
    mixer_prev = along(mixer, 1)
    mixed, gated = mix_call(place, mirrored(lines), mixer_prev, mixer, query)
    cotangents, gated = lax.optimization_barrier((cotangents, gated))
    partial = gate_matmul(cotangents, tops, bottoms)
    gate_grad = lax.psum_scatter(partial, ("z", "c"), scatter_dimension=0, tiled=True)
    pieces = line_gather(gated)

    grad_mixed, query_grad = gate_call(place, gate_grad, query, mixed)
    grad_next = along(grad_mixed, -1)
    query_next = along(query_grad[:RIM], -1)
    grad_tokens = short_adjoint_call(query_grad[None], query_next[None], short_filter, 0, None)
    long_sum, query_sum = long_grad_call(
        groups, short_taps, mixer_prev, mixer, grad_mixed, query_grad, tokens, rim
    )
    other_grads, key_sum, value_sum = unmix_call(
        lines, short_taps, grad_mixed, grad_next, key, value, tokens, rim
    )
    other_next = along(other_grads[:, :RIM], -1)
    grad_short, grad_long = total_over_devices(places, query_sum, key_sum, value_sum, long_sum, short_taps)
    grad_tokens = short_adjoint_call(other_grads, other_next, short_filter, 1, grad_tokens)

    own, other, top_grads, bottom_grads = project(row_place, pieces, cotangents.T, tops, bottoms)
    grad_weight = plane_scatter_sum(top_grads, bottom_grads)
    theirs = move(other, xh=1)
    output = jnp.where(xh == 0, jnp.concatenate([own, theirs], axis=0), jnp.concatenate([theirs, own], axis=0))
    return output[None], grad_tokens[None], grad_short, mirrored(grad_long), grad_weight


def solution(mesh):
    dp, seq = mesh.shape["dp"], mesh.shape["seq"]
    grid = jax.sharding.Mesh(mesh.devices.reshape(dp // 2, 2, 2, seq // 4, 2), ("y", "xl", "xh", "z", "c"))
    rows, line = ("y", "xl"), ("xh", "z", "c")
    return jax.shard_map(
        shards,
        mesh=grid,
        in_specs=(P(rows, line, None), P(), P(), P(rows, line), P(rows, None, line)),
        out_specs=(P(rows, None, line), P(rows, line, None), P(), P(), P(rows, line)),
        check_vma=False,
    )
```

```python
import functools
import itertools
import math

import jax
import jax.numpy as jnp
from jax import lax
from jax.experimental import pallas as pl
from jax.experimental.pallas import tpu as pltpu
from jax.sharding import PartitionSpec as P

LANES = 128
RIM = 8
MIB = 1024 * 1024
F32 = jnp.float32
BF16 = jnp.bfloat16


PLANE = ("y", "xl", "xh")
LINE = ("xh", "z", "c")


def along(x, by):
    size = math.prod(lax.axis_size(a) for a in LINE)
    pairs = [(i, i + by) for i in range(size) if 0 <= i + by < size]
    return lax.ppermute(x, LINE, pairs)


def move(x, **steps):
    axes = tuple(a for a in ("y", "xl", "xh", "z", "c") if steps.get(a, 0) % lax.axis_size(a))
    if not axes:
        return x
    sizes = [lax.axis_size(a) for a in axes]
    pairs = []
    for at in itertools.product(*(range(n) for n in sizes)):
        to = [(p + steps[a]) % n for p, a, n in zip(at, axes, sizes)]
        pairs.append((flat(at, sizes), flat(to, sizes)))
    return lax.ppermute(x, axes, pairs)


def flat(at, sizes):
    index = 0
    for p, n in zip(at, sizes):
        index = index * n + p
    return index


FLIPS = [(0, 0), (0, 1), (1, 0), (1, 1)]


def params(mib=16):
    return pltpu.CompilerParams(vmem_limit_bytes=mib * MIB)


def cost(flops, moved):
    return pl.CostEstimate(flops=int(flops), bytes_accessed=int(moved), transcendentals=0)


def block_width(channels, most):
    width = min(channels, most)
    while channels % width:
        width //= 2
    return width


def features_kernel(short_taps, tokens, rims, filters, query_ref, key_ref, value_ref, mixer_ref):
    rows = tokens[0].shape[0]

    def filtered(part):
        ext = jnp.concatenate([rims[part][...].astype(F32), tokens[part][...].astype(F32)], axis=0)
        total = filters[part][0:1, :] * ext[RIM : RIM + rows]
        for tap in range(1, short_taps):
            total = total + filters[part][tap : tap + 1, :] * ext[RIM - tap : RIM - tap + rows]
        return total

    query_ref[...] = filtered(0).astype(BF16)
    key, value = filtered(1), filtered(2)
    key_ref[...] = key.astype(BF16)
    value_ref[...] = value.astype(BF16)
    mixer_ref[...] = (key * value).astype(BF16)


def features_call(tokens, rim, filters):
    rows, wide = tokens.shape
    channels = wide // 3
    taps = filters.shape[0]
    width = block_width(channels, 512)
    steps = channels // width

    def spec(height, part):
        return pl.BlockSpec((height, width), lambda i, part=part: (0, i + part * steps))

    def body(*refs):
        features_kernel(taps, refs[0:3], refs[3:6], refs[6:9], *refs[9:])

    out = jax.ShapeDtypeStruct((rows, channels), BF16)
    return pl.pallas_call(
        body,
        grid=(steps,),
        in_specs=[spec(rows, p) for p in range(3)]
        + [spec(RIM, p) for p in range(3)]
        + [spec(taps, p) for p in range(3)],
        out_specs=[pl.BlockSpec((rows, width), lambda i: (0, i))] * 4,
        out_shape=[out] * 4,
        compiler_params=params(),
        cost_estimate=cost(0, rows * wide),
        name="features",
    )(tokens, tokens, tokens, rim, rim, rim, filters, filters, filters)


def lane_row(shape):
    row = lax.broadcasted_iota(jnp.int32, shape, 0)
    lane = lax.broadcasted_iota(jnp.int32, shape, 1)
    return row, lane


def mirror(size):
    row, lane = lane_row((size, size))
    return jnp.where((row + lane) % size == 0, 1.0, 0.0)


def circulant(line, taps):
    wide = jnp.broadcast_to(line.astype(F32), (taps, taps))
    return pltpu.roll(wide, 0, 1, stride=1, stride_axis=0)


def pick_groups(product, rows, per_group):
    lane = lax.broadcasted_iota(jnp.int32, (rows, LANES), 1) // per_group
    total = product[0:rows]
    for g in range(1, LANES // per_group):
        total = jnp.where(lane == g, product[g * rows : (g + 1) * rows], total)
    return total


def mix_kernel(per_group, place, lines_ref, prev_ref, cur_ref, query_ref, mixed_ref, gated_ref, table):
    rows, width = cur_ref.shape
    row, lane = lane_row((rows, rows))
    above = lane > row
    packed = LANES // per_group
    lines = jnp.dot(lines_ref[...].astype(BF16), mirror(rows).astype(BF16), preferred_element_type=F32)
    for block in range(width // LANES):
        at = pl.ds(block * LANES, LANES)
        for g in range(packed):
            ring = circulant(lines[block * packed + g : block * packed + g + 1, :], rows)
            table[g * rows : (g + 1) * rows, 0:rows] = jnp.where(above, ring, 0.0).astype(BF16)
            table[g * rows : (g + 1) * rows, rows : 2 * rows] = jnp.where(above, 0.0, ring).astype(BF16)
        window = jnp.concatenate([prev_ref[:, at], cur_ref[:, at]], axis=0)
        product = jnp.dot(table[...], window, preferred_element_type=F32)
        mixed = pick_groups(product, rows, per_group)
        mixed_ref[:, at] = mixed.astype(BF16)
        gated_ref[:, at] = (query_ref[:, at].astype(F32) * mixed).astype(BF16)


def mix_call(place, lines, prev, cur, query):
    rows, channels = cur.shape
    groups, taps = lines.shape
    per_group = channels // groups
    steps = place.shape[0]
    width = channels // steps
    wide = pl.BlockSpec((rows, width), lambda i, place: (0, i))
    out = jax.ShapeDtypeStruct((rows, channels), BF16)
    return pl.pallas_call(
        functools.partial(mix_kernel, per_group),
        grid_spec=pltpu.PrefetchScalarGridSpec(
            num_scalar_prefetch=1,
            grid=(steps,),
            in_specs=[pl.BlockSpec((width // per_group, taps), lambda i, place: (i, 0)), wide, wide, wide],
            out_specs=[wide, pl.BlockSpec((rows, width), lambda i, place: (0, place[i]))],
            scratch_shapes=[pltpu.VMEM((LANES // per_group * rows, 2 * rows), BF16)],
        ),
        out_shape=[out, out],
        compiler_params=params(),
        cost_estimate=cost(0, 2 * rows * channels),
        name="mix",
    )(place, lines, prev, cur, query)


def gate_kernel(place, gate_grad_ref, query_ref, mixed_ref, grad_ref, feature_ref):
    gate_grad = gate_grad_ref[...].astype(F32)
    grad_ref[...] = (gate_grad * query_ref[...].astype(F32)).astype(BF16)
    feature_ref[...] = (gate_grad * mixed_ref[...].astype(F32)).astype(BF16)


def gate_call(place, gate_grad, query, mixed):
    rows, channels = query.shape
    steps = place.shape[0]
    width = channels // steps
    wide = pl.BlockSpec((rows, width), lambda i, place: (0, i))
    out = jax.ShapeDtypeStruct((rows, channels), BF16)
    return pl.pallas_call(
        gate_kernel,
        grid_spec=pltpu.PrefetchScalarGridSpec(
            num_scalar_prefetch=1,
            grid=(steps,),
            in_specs=[pl.BlockSpec((rows, width), lambda i, place: (0, place[i])), wide, wide],
            out_specs=[wide, wide],
        ),
        out_shape=[out, out],
        compiler_params=params(),
        cost_estimate=cost(2 * rows * channels, 10 * rows * channels),
        name="gate_back",
    )(place, gate_grad, query, mixed)


def tap_sums(short_taps, grads, tokens_ref, rim_ref, out_ref):
    rows = tokens_ref.shape[0]
    ext = jnp.concatenate([rim_ref[...].astype(F32), tokens_ref[...].astype(F32)], axis=0)
    for tap in range(short_taps):
        out_ref[tap : tap + 1, :] = jnp.sum(grads * ext[RIM - tap : RIM - tap + rows], axis=0, keepdims=True)
    out_ref[short_taps:8, :] = jnp.zeros((8 - short_taps, out_ref.shape[1]), F32)


def long_grad_kernel(
    per_group, short_taps, prev_ref, cur_ref, grad_ref, feature_ref, tokens_ref, rim_ref, long_ref, short_ref, fold
):
    rows, width = cur_ref.shape
    row, lane = lane_row((rows, rows))
    above = lane > row
    member = lax.broadcasted_iota(jnp.int32, (rows, LANES), 1) // per_group
    packed = LANES // per_group
    sums = []
    for block in range(width // LANES):
        at = pl.ds(block * LANES, LANES)
        window = jnp.concatenate([prev_ref[:, at], cur_ref[:, at]], axis=0)
        grad_wide = grad_ref[:, at].astype(F32)
        for g in range(packed):
            own = jnp.where(member == g, grad_wide, 0.0).astype(BF16)
            pairs = lax.dot_general(own, window, (((1,), (1,)), ((), ())), preferred_element_type=F32)
            ring = jnp.where(above, pairs[:, 0:rows], pairs[:, rows : 2 * rows])
            total = ring[0:8]
            for tile in range(1, rows // 8):
                total = total + pltpu.roll(ring[8 * tile : 8 * tile + 8], rows - 8 * tile, 1)
            fold[g * 8 : (g + 1) * 8, :] = total
        total = fold[pl.ds(0, packed, stride=8), :]
        for step in range(1, 8):
            total = total + pltpu.roll(fold[pl.ds(step, packed, stride=8), :], rows - step, 1)
        sums.append(total)
    long_ref[...] = jnp.dot(
        jnp.concatenate(sums, axis=0), mirror(rows), precision=lax.Precision.HIGHEST, preferred_element_type=F32
    )
    tap_sums(short_taps, feature_ref[...].astype(F32), tokens_ref, rim_ref, short_ref)


def long_grad_call(groups, short_taps, prev, cur, grad, feature, tokens, rim):
    rows, channels = cur.shape
    per_group = channels // groups
    width = block_width(channels, 512)
    steps = channels // width
    wide = pl.BlockSpec((rows, width), lambda i: (0, i))
    packed = LANES // per_group
    return pl.pallas_call(
        functools.partial(long_grad_kernel, per_group, short_taps),
        grid=(steps,),
        in_specs=[wide] * 5 + [pl.BlockSpec((RIM, width), lambda i: (0, i))],
        out_specs=[
            pl.BlockSpec((width // per_group, rows), lambda i: (i, 0)),
            pl.BlockSpec((8, width), lambda i: (0, i)),
        ],
        out_shape=[
            jax.ShapeDtypeStruct((groups, rows), F32),
            jax.ShapeDtypeStruct((8, channels), F32),
        ],
        scratch_shapes=[pltpu.VMEM((packed * 8, LANES), F32)],
        compiler_params=params(),
        cost_estimate=cost(2 * groups * rows * 2 * rows * LANES, 10 * rows * channels),
        name="long_grad",
    )(prev, cur, grad, feature, tokens, rim)


def unmix_kernel(
    per_group, short_taps, lines_ref, grad_ref, next_ref, key_ref, value_ref, key_tokens_ref, value_tokens_ref,
    key_rim_ref, value_rim_ref, feature_ref, key_sum_ref, value_sum_ref, table,
):
    rows, width = grad_ref.shape
    row, lane = lane_row((rows, rows))
    below = lane < row
    packed = LANES // per_group
    for block in range(width // LANES):
        at = pl.ds(block * LANES, LANES)
        for g in range(packed):
            ring = circulant(lines_ref[block * packed + g : block * packed + g + 1, :], rows)
            table[g * rows : (g + 1) * rows, 0:rows] = jnp.where(below, 0.0, ring).astype(BF16)
            table[g * rows : (g + 1) * rows, rows : 2 * rows] = jnp.where(below, ring, 0.0).astype(BF16)
        window = jnp.concatenate([grad_ref[:, at], next_ref[:, at]], axis=0)
        product = jnp.dot(table[...], window, preferred_element_type=F32)
        grad_mixer = pick_groups(product, rows, per_group)
        feature_ref[0, :, at] = (grad_mixer * value_ref[:, at].astype(F32)).astype(BF16)
        feature_ref[1, :, at] = (grad_mixer * key_ref[:, at].astype(F32)).astype(BF16)
    tap_sums(short_taps, feature_ref[0].astype(F32), key_tokens_ref, key_rim_ref, key_sum_ref)
    tap_sums(short_taps, feature_ref[1].astype(F32), value_tokens_ref, value_rim_ref, value_sum_ref)


def unmix_call(lines, short_taps, grad, grad_next, key, value, tokens, rim):
    rows, channels = grad.shape
    groups, taps = lines.shape
    per_group = channels // groups
    width = block_width(channels, 512)
    steps = channels // width

    def spec(height, part):
        return pl.BlockSpec((height, width), lambda i, part=part: (0, i + part * steps))

    wide = spec(rows, 0)
    packed = LANES // per_group
    sums = jax.ShapeDtypeStruct((8, channels), F32)
    return pl.pallas_call(
        functools.partial(unmix_kernel, per_group, short_taps),
        grid=(steps,),
        in_specs=[pl.BlockSpec((width // per_group, taps), lambda i: (i, 0))]
        + [wide] * 4
        + [spec(rows, 1), spec(rows, 2), spec(RIM, 1), spec(RIM, 2)],
        out_specs=[pl.BlockSpec((2, rows, width), lambda i: (0, 0, i)), spec(8, 0), spec(8, 0)],
        out_shape=[jax.ShapeDtypeStruct((2, rows, channels), BF16), sums, sums],
        scratch_shapes=[pltpu.VMEM((packed * rows, 2 * rows), BF16)],
        compiler_params=params(),
        cost_estimate=cost(2 * groups * rows * 2 * rows * LANES, 16 * rows * channels),
        name="unmix",
    )(lines, grad, grad_next, key, value, tokens, tokens, rim, rim)


def short_adjoint_kernel(short_taps, grads_ref, rim_ref, filter_ref, *refs):
    out_ref = refs[-1]
    rows = out_ref.shape[0]
    ext = jnp.concatenate([grads_ref[0].astype(F32), rim_ref[0].astype(F32)], axis=0)
    total = filter_ref[0:1, :] * ext[0:rows]
    for tap in range(1, short_taps):
        total = total + filter_ref[tap : tap + 1, :] * ext[tap : tap + rows]
    out_ref[...] = total.astype(BF16)


def short_adjoint_call(grads, rim, filters, first, out):
    parts, rows, channels = grads.shape
    short_taps = filters.shape[0]
    width = block_width(channels, 1024)
    steps = channels // width
    result = pl.BlockSpec((rows, width), lambda p, i: (0, (p + first) * steps + i))
    given = [] if out is None else [out]
    return pl.pallas_call(
        functools.partial(short_adjoint_kernel, short_taps),
        grid=(parts, steps),
        in_specs=[
            pl.BlockSpec((1, rows, width), lambda p, i: (p, 0, i)),
            pl.BlockSpec((1, RIM, width), lambda p, i: (p, 0, i)),
            pl.BlockSpec((short_taps, width), lambda p, i: (0, (p + first) * steps + i)),
        ]
        + [pl.BlockSpec(memory_space=pl.ANY)] * len(given),
        out_specs=result,
        out_shape=jax.ShapeDtypeStruct((rows, 3 * channels), BF16),
        input_output_aliases={3: 0} if given else {},
        compiler_params=params(),
        cost_estimate=cost(2 * parts * short_taps * rows * channels, 4 * parts * rows * channels),
        name="short_adjoint",
    )(grads, rim, filters, *given)


def spread_kernel(place, query_ref, key_ref, value_ref, long_ref, own_ref, other_ref):
    steps = query_ref.shape[1] // LANES
    half = own_ref.shape[0]
    tiles = [ref[:, i * LANES : (i + 1) * LANES] for ref in (query_ref, key_ref, value_ref) for i in range(steps)]
    tiles += [long_ref[8 * i : 8 * i + 8, :] for i in range(long_ref.shape[0] // 8)]
    first = place[0] < half

    @pl.when(first)
    def _():
        for i in range(half):
            own_ref[place[i]] = tiles[i]
            other_ref[place[half + i] - half] = tiles[half + i]

    @pl.when(jnp.logical_not(first))
    def _():
        for i in range(half):
            other_ref[place[i] - half] = tiles[i]
            own_ref[place[half + i]] = tiles[half + i]


def collect_kernel(place, *refs):
    parts, short_ref, long_ref, tiles_ref = refs[:-3], refs[-3], refs[-2], refs[-1]
    short_taps, wide = short_ref.shape
    steps = wide // LANES
    size = parts[0].shape[0]
    for i, part in enumerate(parts):
        tiles_ref[i * size : (i + 1) * size] = part[...]
    for i in range(steps):
        short_ref[:, i * LANES : (i + 1) * LANES] = tiles_ref[place[i]][0:short_taps, :]
    for i in range(long_ref.shape[0] // 8):
        long_ref[8 * i : 8 * i + 8, :] = tiles_ref[place[steps + i]]


def in_vmem():
    return pl.BlockSpec(memory_space=pltpu.VMEM)


def total_over_devices(spread_to, collect_from, query_sum, key_sum, value_sum, long_sum, short_taps):
    ny, nz = lax.axis_size("y"), lax.axis_size("z")
    channels = query_sum.shape[1]
    count = 3 * channels // LANES + long_sum.shape[0] // 8
    half = jax.ShapeDtypeStruct((count // 2, 8, LANES), F32)
    own, other = pl.pallas_call(
        spread_kernel,
        in_specs=[pl.BlockSpec(memory_space=pltpu.SMEM)] + [in_vmem()] * 4,
        out_specs=[in_vmem()] * 2,
        out_shape=[half] * 2,
        compiler_params=params(),
        name="spread",
    )(spread_to, query_sum, key_sum, value_sum, long_sum)
    part = own + move(other, c=1)
    size = count // 2 // nz
    part = sum([move(part[d * size : (d + 1) * size], z=d) for d in range(1, nz)], part[:size])
    whole = paired_sum([part] + [move(part, y=d) for d in range(1, ny)])
    whole = paired_sum([move(whole, xl=a, xh=b) for a, b in FLIPS])
    line = jnp.concatenate([whole, move(whole, c=1)], axis=0)
    lines = [move(line, z=-d) for d in range(nz)]
    groups, taps = long_sum.shape
    return pl.pallas_call(
        collect_kernel,
        in_specs=[pl.BlockSpec(memory_space=pltpu.SMEM)] + [in_vmem()] * nz,
        out_specs=[in_vmem(), in_vmem()],
        scratch_shapes=[pltpu.VMEM((count, 8, LANES), F32)],
        out_shape=[
            jax.ShapeDtypeStruct((short_taps, 3 * channels), F32),
            jax.ShapeDtypeStruct((groups, taps), F32),
        ],
        compiler_params=params(),
        name="collect",
    )(collect_from, *lines)


def paired_sum(terms):
    half = len(terms) // 2
    if half == 0:
        return terms[0]
    return paired_sum([terms[i] + terms[i + half] for i in range(half)])


def gather_near(shard):
    ny = lax.axis_size("y")
    half = shard.shape[0] // 2
    top, bottom = shard[:half], shard[half:]
    return (
        jnp.stack([move(top, xl=a, xh=b) for a, b in FLIPS]),
        jnp.stack([move(bottom, y=d) for d in range(ny)]),
    )


def gather_far(wide_top, tall_bottom):
    ny = lax.axis_size("y")
    return (
        [move(wide_top, y=d) for d in range(ny)],
        [move(tall_bottom, xl=a, xh=b) for a, b in FLIPS],
    )


def piece_rows(tops, bottoms, step):
    rows = []
    for a in range(2):
        rows.append(jnp.concatenate([tops[step][2 * a + b] for b in range(2)], axis=1))
        rows.append(jnp.concatenate([bottoms[2 * a + b][step] for b in range(2)], axis=1))
    return rows


def gate_matmul_kernel(ny, *refs):
    cotangent_ref, tops, bottoms, out_ref = refs[0], refs[1 : 1 + ny], refs[1 + ny : 5 + ny], refs[5 + ny]
    left = cotangent_ref[...]
    at = 0
    for step in range(ny):
        for right in piece_rows(tops, bottoms, step):
            size = right.shape[0]
            out_ref[:, at : at + size] = lax.dot_general(
                left, right, (((1,), (1,)), ((), ())), preferred_element_type=F32
            ).astype(BF16)
            at += size


def whole(x):
    return pl.BlockSpec(x.shape, lambda *_, n=x.ndim: (0,) * n)


def gate_matmul(cotangents, tops, bottoms):
    rows, depth = cotangents.shape
    ny = len(tops)
    channels = 4 * ny * tops[0].shape[1]
    height = rows // 2
    return pl.pallas_call(
        functools.partial(gate_matmul_kernel, ny),
        grid=(rows // height,),
        in_specs=[pl.BlockSpec((height, depth), lambda i: (i, 0))] + [whole(x) for x in (*tops, *bottoms)],
        out_specs=pl.BlockSpec((height, channels), lambda i: (i, 0)),
        out_shape=jax.ShapeDtypeStruct((rows, channels), BF16),
        compiler_params=params(32),
        cost_estimate=cost(2 * rows * depth * channels, 2 * (rows + depth) * channels),
        name="gate_matmul",
    )(cotangents, *tops, *bottoms)


def project_kernel(ny, *refs):
    rows_ref, turned_ref, tops, bottoms = refs[0], refs[1], refs[2 : 2 + ny], refs[2 + ny : 6 + ny]
    own_ref, other_ref = refs[6 + ny : 8 + ny]
    top_grads, bottom_grads = refs[8 + ny : 8 + 2 * ny], refs[8 + 2 * ny : 12 + 2 * ny]
    total = refs[12 + 2 * ny]
    step = pl.program_id(0)
    rows = rows_ref[...]
    width = own_ref.shape[1]
    size = tops[0].shape[1]
    grads = jnp.dot(turned_ref[...], rows, preferred_element_type=F32).astype(BF16)
    for a in range(2):
        for b in range(2):
            at = (2 * a + 1) * size
            bottom_grads[2 * a + b][step] = grads[b * width : (b + 1) * width, at : at + size]
    for d in range(ny):

        @pl.when(step == d)
        def _(d=d):
            for a in range(2):
                for b in range(2):
                    at = 2 * a * size
                    top_grads[d][2 * a + b] = grads[b * width : (b + 1) * width, at : at + size]
            right = jnp.concatenate(piece_rows(tops, bottoms, d), axis=0)
            product = jnp.dot(rows, right, preferred_element_type=F32)
            if d == 0:
                total[...] = product
            else:
                total[...] += product

    @pl.when(step == ny - 1)
    def _():
        own_ref[...] = total[:, :width].astype(BF16)
        other_ref[...] = total[:, width:].astype(BF16)


def project(all_rows, turned, tops, bottoms):
    rows, channels = all_rows.shape
    ny = len(tops)
    size = tops[0].shape[1]
    width = turned.shape[0] // 2
    half = jax.ShapeDtypeStruct((rows, width), BF16)
    outs = (
        [half, half]
        + [jax.ShapeDtypeStruct((4, width, size), BF16)] * ny
        + [jax.ShapeDtypeStruct((ny, width, size), BF16)] * 4
    )
    results = pl.pallas_call(
        functools.partial(project_kernel, ny),
        grid=(ny,),
        in_specs=[pl.BlockSpec((rows, channels // ny), lambda i: (0, i)), whole(turned)]
        + [whole(x) for x in (*tops, *bottoms)],
        out_specs=[whole(x) for x in outs],
        out_shape=outs,
        scratch_shapes=[pltpu.VMEM((rows, 2 * width), F32)],
        compiler_params=params(40),
        cost_estimate=cost(8 * rows * width * channels, 2 * (rows + 4 * width) * channels),
        name="project",
    )(all_rows, turned, *tops, *bottoms)
    return results[0], results[1], results[2 : 2 + ny], results[2 + ny :]


def plane_scatter_sum(top_grads, bottom_grads):
    ny = len(top_grads)

    def added(terms):
        total = terms[0].astype(F32)
        for term in terms[1:]:
            total = total + term.astype(F32)
        return total

    top = added([move(top_grads[d], y=-d) for d in range(ny)]).astype(BF16)
    bottom = added([move(bottom_grads[f], xl=a, xh=b) for f, (a, b) in enumerate(FLIPS)]).astype(BF16)
    top = added([move(top[f], xl=a, xh=b) for f, (a, b) in enumerate(FLIPS)])
    bottom = added([move(bottom[d], y=-d) for d in range(ny)])
    return jnp.concatenate([top, bottom], axis=1).T


def shards(tokens_in, short_filter, long_filter, out_weight, cotangent):
    ny, nz = lax.axis_size("y"), lax.axis_size("z")
    y, xl, xh, z, c = (lax.axis_index(a) for a in ("y", "xl", "xh", "z", "c"))
    tokens = tokens_in[0]
    rows, wide = tokens.shape
    channels = wide // 3
    short_taps = short_filter.shape[0]
    groups = long_filter.shape[0]
    upstream = cotangent[0]
    length, columns = upstream.shape
    span = length // 2

    block = jnp.arange(2 * ny, dtype=jnp.int32)
    place = ((y - block // 2) % ny) * 2 + (block + xl) % 2
    size = 3 * channels // LANES + groups // 8
    each = size // (2 * nz)
    tile = jnp.arange(size, dtype=jnp.int32)
    core_step, z_step = (tile // (nz * each) + c) % 2, (tile // each - z) % nz
    spread_to = (core_step * nz + z_step) * each + tile % each
    collect_from = (z_step * 2 + core_step) * each + tile % each

    rim = along(tokens[rows - RIM :], 1)
    mine = lax.dynamic_slice_in_dim(upstream, xh * span, span, 0)
    others = move(lax.dynamic_slice_in_dim(upstream, (1 - xh) * span, span, 0), xh=1)
    query, key, value, mixer = features_call(tokens, rim, short_filter)
    mixer, others, out_weight = lax.optimization_barrier((mixer, others, out_weight))
    mixer_prev = along(mixer, 1)
    wide_top, tall_bottom = gather_near(out_weight)
    lines = long_filter.astype(F32)
    mixed, gated = mix_call(place, lines, mixer_prev, mixer, query)
    gated, wide_top, tall_bottom = lax.optimization_barrier((gated, wide_top, tall_bottom))
    all_rows = lax.all_gather(gated, ("z", "c"), axis=0, tiled=True)
    tops, bottoms = gather_far(wide_top, tall_bottom)
    cotangents = jnp.concatenate([mine, others], axis=1)
    partial = gate_matmul(cotangents, tops, bottoms)
    partial, all_rows = lax.optimization_barrier((partial, all_rows))
    gate_grad = lax.psum_scatter(partial, ("z", "c"), scatter_dimension=0, tiled=True)

    own, other, top_grads, bottom_grads = project(all_rows, cotangents.T, tops, bottoms)
    grad_weight = plane_scatter_sum(top_grads, bottom_grads)
    theirs = move(other, xh=1)
    output = jnp.where(xh == 0, jnp.concatenate([own, theirs], axis=0), jnp.concatenate([theirs, own], axis=0))
    gate_grad, grad_weight, output = lax.optimization_barrier((gate_grad, grad_weight, output))

    grad_mixed, query_grad = gate_call(place, gate_grad, query, mixed)
    grad_next = along(grad_mixed, -1)
    query_next = along(query_grad[:RIM], -1)
    grad_tokens = short_adjoint_call(query_grad[None], query_next[None], short_filter, 0, None)
    long_sum, query_sum = long_grad_call(
        groups, short_taps, mixer_prev, mixer, grad_mixed, query_grad, tokens, rim
    )
    other_grads, key_sum, value_sum = unmix_call(
        lines, short_taps, grad_mixed, grad_next, key, value, tokens, rim
    )
    other_next = along(other_grads[:, :RIM], -1)
    grad_short, grad_long = total_over_devices(
        spread_to, collect_from, query_sum, key_sum, value_sum, long_sum, short_taps
    )
    grad_tokens = short_adjoint_call(other_grads, other_next, short_filter, 1, grad_tokens)
    return output[None], grad_tokens[None], grad_short, grad_long, grad_weight


def solution(mesh):
    dp, seq = mesh.shape["dp"], mesh.shape["seq"]
    grid = jax.sharding.Mesh(mesh.devices.reshape(dp // 2, 2, 2, seq // 4, 2), ("y", "xl", "xh", "z", "c"))
    rows, line = ("y", "xl"), ("xh", "z", "c")
    return jax.shard_map(
        shards,
        mesh=grid,
        in_specs=(P(rows, line, None), P(), P(), P(rows, line), P(rows, None, line)),
        out_specs=(P(rows, None, line), P(rows, line, None), P(), P(), P(rows, line)),
        check_vma=False,
    )
```

```python
import functools
import itertools
import math

import jax
import jax.numpy as jnp
from jax import lax
from jax.experimental import pallas as pl
from jax.experimental.pallas import tpu as pltpu
from jax.sharding import PartitionSpec as P

LANES = 128
RIM = 8
MIB = 1024 * 1024
F32 = jnp.float32
BF16 = jnp.bfloat16


PLANE = ("y", "xl", "xh")
LINE = ("xh", "z", "c")


def along(x, by):
    size = math.prod(lax.axis_size(a) for a in LINE)
    pairs = [(i, i + by) for i in range(size) if 0 <= i + by < size]
    return lax.ppermute(x, LINE, pairs)


def move(x, **steps):
    axes = tuple(a for a in ("y", "xl", "xh", "z", "c") if steps.get(a, 0) % lax.axis_size(a))
    if not axes:
        return x
    sizes = [lax.axis_size(a) for a in axes]
    pairs = []
    for at in itertools.product(*(range(n) for n in sizes)):
        to = [(p + steps[a]) % n for p, a, n in zip(at, axes, sizes)]
        pairs.append((flat(at, sizes), flat(to, sizes)))
    return lax.ppermute(x, axes, pairs)


def flat(at, sizes):
    index = 0
    for p, n in zip(at, sizes):
        index = index * n + p
    return index


FLIPS = [(0, 0), (0, 1), (1, 0), (1, 1)]


def params(mib=16):
    return pltpu.CompilerParams(vmem_limit_bytes=mib * MIB)


def hbm_call(kernel, *, out_shape, loose=(), **options):
    single = not isinstance(out_shape, (list, tuple))
    shapes = [out_shape] if single else out_shape
    placed = [pltpu.HBM(x.shape, x.dtype) for x in shapes]
    call = pl.pallas_call(kernel, out_shape=placed[0] if single else placed, **options)

    def run(*args):
        held = [x if i in loose else pltpu.with_memory_space_constraint(x, pltpu.HBM) for i, x in enumerate(args)]
        return call(*held)

    return run


def cost(flops, moved):
    return pl.CostEstimate(flops=int(flops), bytes_accessed=int(moved), transcendentals=0)


def block_width(channels, most):
    width = min(channels, most)
    while channels % width:
        width //= 2
    return width


def features_kernel(short_taps, tokens, rims, filters, query_ref, key_ref, value_ref, mixer_ref):
    rows = tokens[0].shape[0]

    def filtered(part):
        ext = jnp.concatenate([rims[part][...].astype(F32), tokens[part][...].astype(F32)], axis=0)
        total = filters[part][0:1, :] * ext[RIM : RIM + rows]
        for tap in range(1, short_taps):
            total = total + filters[part][tap : tap + 1, :] * ext[RIM - tap : RIM - tap + rows]
        return total

    query_ref[...] = filtered(0).astype(BF16)
    key, value = filtered(1), filtered(2)
    key_ref[...] = key.astype(BF16)
    value_ref[...] = value.astype(BF16)
    mixer_ref[...] = (key * value).astype(BF16)


def features_call(tokens, rim, filters):
    rows, wide = tokens.shape
    channels = wide // 3
    taps = filters.shape[0]
    width = block_width(channels, 512)
    steps = channels // width

    def spec(height, part):
        return pl.BlockSpec((height, width), lambda i, part=part: (0, i + part * steps))

    def body(*refs):
        features_kernel(taps, refs[0:3], refs[3:6], refs[6:9], *refs[9:])

    out = jax.ShapeDtypeStruct((rows, channels), BF16)
    return hbm_call(
        body,
        loose=(3, 4, 5),
        grid=(steps,),
        in_specs=[spec(rows, p) for p in range(3)]
        + [spec(RIM, p) for p in range(3)]
        + [spec(taps, p) for p in range(3)],
        out_specs=[pl.BlockSpec((rows, width), lambda i: (0, i))] * 4,
        out_shape=[out] * 4,
        compiler_params=params(),
        cost_estimate=cost(0, rows * wide),
        name="features",
    )(tokens, tokens, tokens, rim, rim, rim, filters, filters, filters)


def lane_row(shape):
    row = lax.broadcasted_iota(jnp.int32, shape, 0)
    lane = lax.broadcasted_iota(jnp.int32, shape, 1)
    return row, lane


def mirror(size):
    row, lane = lane_row((size, size))
    return jnp.where((row + lane) % size == 0, 1.0, 0.0)


def circulant(line, taps):
    wide = jnp.broadcast_to(line.astype(F32), (taps, taps))
    return pltpu.roll(wide, 0, 1, stride=1, stride_axis=0)


def pick_groups(product, rows, per_group):
    lane = lax.broadcasted_iota(jnp.int32, (rows, LANES), 1) // per_group
    total = product[0:rows]
    for g in range(1, LANES // per_group):
        total = jnp.where(lane == g, product[g * rows : (g + 1) * rows], total)
    return total


def mix_kernel(per_group, place, lines_ref, prev_ref, cur_ref, query_ref, mixed_ref, gated_ref, table):
    rows, width = cur_ref.shape
    row, lane = lane_row((rows, rows))
    above = lane > row
    packed = LANES // per_group
    lines = jnp.dot(lines_ref[...].astype(BF16), mirror(rows).astype(BF16), preferred_element_type=F32)
    for block in range(width // LANES):
        at = pl.ds(block * LANES, LANES)
        for g in range(packed):
            ring = circulant(lines[block * packed + g : block * packed + g + 1, :], rows)
            table[g * rows : (g + 1) * rows, 0:rows] = jnp.where(above, ring, 0.0).astype(BF16)
            table[g * rows : (g + 1) * rows, rows : 2 * rows] = jnp.where(above, 0.0, ring).astype(BF16)
        window = jnp.concatenate([prev_ref[:, at], cur_ref[:, at]], axis=0)
        product = jnp.dot(table[...], window, preferred_element_type=F32)
        mixed = pick_groups(product, rows, per_group)
        mixed_ref[:, at] = mixed.astype(BF16)
        gated_ref[:, at] = (query_ref[:, at].astype(F32) * mixed).astype(BF16)


def mix_call(place, lines, prev, cur, query):
    rows, channels = cur.shape
    groups, taps = lines.shape
    per_group = channels // groups
    steps = place.shape[0]
    width = channels // steps
    wide = pl.BlockSpec((rows, width), lambda i, place: (0, i))
    out = jax.ShapeDtypeStruct((rows, channels), BF16)
    return hbm_call(
        functools.partial(mix_kernel, per_group),
        loose=(0, 1, 2),
        grid_spec=pltpu.PrefetchScalarGridSpec(
            num_scalar_prefetch=1,
            grid=(steps,),
            in_specs=[pl.BlockSpec((width // per_group, taps), lambda i, place: (i, 0)), wide, wide, wide],
            out_specs=[wide, pl.BlockSpec((rows, width), lambda i, place: (0, place[i]))],
            scratch_shapes=[pltpu.VMEM((LANES // per_group * rows, 2 * rows), BF16)],
        ),
        out_shape=[out, out],
        compiler_params=params(),
        cost_estimate=cost(0, 2 * rows * channels),
        name="mix",
    )(place, lines, prev, cur, query)


def gate_kernel(place, gate_grad_ref, query_ref, mixed_ref, grad_ref, feature_ref):
    gate_grad = gate_grad_ref[...].astype(F32)
    grad_ref[...] = (gate_grad * query_ref[...].astype(F32)).astype(BF16)
    feature_ref[...] = (gate_grad * mixed_ref[...].astype(F32)).astype(BF16)


def gate_call(place, gate_grad, query, mixed):
    rows, channels = query.shape
    steps = place.shape[0]
    width = channels // steps
    wide = pl.BlockSpec((rows, width), lambda i, place: (0, i))
    out = jax.ShapeDtypeStruct((rows, channels), BF16)
    return hbm_call(
        gate_kernel,
        loose=(0,),
        grid_spec=pltpu.PrefetchScalarGridSpec(
            num_scalar_prefetch=1,
            grid=(steps,),
            in_specs=[pl.BlockSpec((rows, width), lambda i, place: (0, place[i])), wide, wide],
            out_specs=[wide, wide],
        ),
        out_shape=[out, out],
        compiler_params=params(),
        cost_estimate=cost(2 * rows * channels, 10 * rows * channels),
        name="gate_back",
    )(place, gate_grad, query, mixed)


def tap_sums(short_taps, grads, tokens_ref, rim_ref, out_ref):
    rows = tokens_ref.shape[0]
    ext = jnp.concatenate([rim_ref[...].astype(F32), tokens_ref[...].astype(F32)], axis=0)
    for tap in range(short_taps):
        out_ref[tap : tap + 1, :] = jnp.sum(grads * ext[RIM - tap : RIM - tap + rows], axis=0, keepdims=True)
    out_ref[short_taps:8, :] = jnp.zeros((8 - short_taps, out_ref.shape[1]), F32)


def long_grad_kernel(
    per_group, short_taps, prev_ref, cur_ref, grad_ref, feature_ref, tokens_ref, rim_ref, long_ref, short_ref, fold
):
    rows, width = cur_ref.shape
    row, lane = lane_row((rows, rows))
    above = lane > row
    member = lax.broadcasted_iota(jnp.int32, (rows, LANES), 1) // per_group
    packed = LANES // per_group
    sums = []
    for block in range(width // LANES):
        at = pl.ds(block * LANES, LANES)
        window = jnp.concatenate([prev_ref[:, at], cur_ref[:, at]], axis=0)
        grad_wide = grad_ref[:, at].astype(F32)
        for g in range(packed):
            own = jnp.where(member == g, grad_wide, 0.0).astype(BF16)
            pairs = lax.dot_general(own, window, (((1,), (1,)), ((), ())), preferred_element_type=F32)
            ring = jnp.where(above, pairs[:, 0:rows], pairs[:, rows : 2 * rows])
            total = ring[0:8]
            for tile in range(1, rows // 8):
                total = total + pltpu.roll(ring[8 * tile : 8 * tile + 8], rows - 8 * tile, 1)
            fold[g * 8 : (g + 1) * 8, :] = total
        total = fold[pl.ds(0, packed, stride=8), :]
        for step in range(1, 8):
            total = total + pltpu.roll(fold[pl.ds(step, packed, stride=8), :], rows - step, 1)
        sums.append(total)
    long_ref[...] = jnp.dot(
        jnp.concatenate(sums, axis=0), mirror(rows), precision=lax.Precision.HIGHEST, preferred_element_type=F32
    )
    tap_sums(short_taps, feature_ref[...].astype(F32), tokens_ref, rim_ref, short_ref)


def long_grad_call(groups, short_taps, prev, cur, grad, feature, tokens, rim):
    rows, channels = cur.shape
    per_group = channels // groups
    width = block_width(channels, 512)
    steps = channels // width
    wide = pl.BlockSpec((rows, width), lambda i: (0, i))
    packed = LANES // per_group
    return hbm_call(
        functools.partial(long_grad_kernel, per_group, short_taps),
        grid=(steps,),
        in_specs=[wide] * 5 + [pl.BlockSpec((RIM, width), lambda i: (0, i))],
        out_specs=[
            pl.BlockSpec((width // per_group, rows), lambda i: (i, 0)),
            pl.BlockSpec((8, width), lambda i: (0, i)),
        ],
        out_shape=[
            jax.ShapeDtypeStruct((groups, rows), F32),
            jax.ShapeDtypeStruct((8, channels), F32),
        ],
        scratch_shapes=[pltpu.VMEM((packed * 8, LANES), F32)],
        compiler_params=params(),
        cost_estimate=cost(2 * groups * rows * 2 * rows * LANES, 10 * rows * channels),
        name="long_grad",
    )(prev, cur, grad, feature, tokens, rim)


def unmix_kernel(
    per_group, short_taps, lines_ref, grad_ref, next_ref, key_ref, value_ref, key_tokens_ref, value_tokens_ref,
    key_rim_ref, value_rim_ref, feature_ref, key_sum_ref, value_sum_ref, table,
):
    rows, width = grad_ref.shape
    row, lane = lane_row((rows, rows))
    below = lane < row
    packed = LANES // per_group
    for block in range(width // LANES):
        at = pl.ds(block * LANES, LANES)
        for g in range(packed):
            ring = circulant(lines_ref[block * packed + g : block * packed + g + 1, :], rows)
            table[g * rows : (g + 1) * rows, 0:rows] = jnp.where(below, 0.0, ring).astype(BF16)
            table[g * rows : (g + 1) * rows, rows : 2 * rows] = jnp.where(below, ring, 0.0).astype(BF16)
        window = jnp.concatenate([grad_ref[:, at], next_ref[:, at]], axis=0)
        product = jnp.dot(table[...], window, preferred_element_type=F32)
        grad_mixer = pick_groups(product, rows, per_group)
        feature_ref[0, :, at] = (grad_mixer * value_ref[:, at].astype(F32)).astype(BF16)
        feature_ref[1, :, at] = (grad_mixer * key_ref[:, at].astype(F32)).astype(BF16)
    tap_sums(short_taps, feature_ref[0].astype(F32), key_tokens_ref, key_rim_ref, key_sum_ref)
    tap_sums(short_taps, feature_ref[1].astype(F32), value_tokens_ref, value_rim_ref, value_sum_ref)


def unmix_call(lines, short_taps, grad, grad_next, key, value, tokens, rim):
    rows, channels = grad.shape
    groups, taps = lines.shape
    per_group = channels // groups
    width = block_width(channels, 512)
    steps = channels // width

    def spec(height, part):
        return pl.BlockSpec((height, width), lambda i, part=part: (0, i + part * steps))

    wide = spec(rows, 0)
    packed = LANES // per_group
    sums = jax.ShapeDtypeStruct((8, channels), F32)
    return hbm_call(
        functools.partial(unmix_kernel, per_group, short_taps),
        loose=(0, 2),
        grid=(steps,),
        in_specs=[pl.BlockSpec((width // per_group, taps), lambda i: (i, 0))]
        + [wide] * 4
        + [spec(rows, 1), spec(rows, 2), spec(RIM, 1), spec(RIM, 2)],
        out_specs=[pl.BlockSpec((2, rows, width), lambda i: (0, 0, i)), spec(8, 0), spec(8, 0)],
        out_shape=[jax.ShapeDtypeStruct((2, rows, channels), BF16), sums, sums],
        scratch_shapes=[pltpu.VMEM((packed * rows, 2 * rows), BF16)],
        compiler_params=params(),
        cost_estimate=cost(2 * groups * rows * 2 * rows * LANES, 16 * rows * channels),
        name="unmix",
    )(lines, grad, grad_next, key, value, tokens, tokens, rim, rim)


def short_adjoint_kernel(short_taps, grads_ref, rim_ref, filter_ref, *refs):
    out_ref = refs[-1]
    rows = out_ref.shape[0]
    ext = jnp.concatenate([grads_ref[0].astype(F32), rim_ref[0].astype(F32)], axis=0)
    total = filter_ref[0:1, :] * ext[0:rows]
    for tap in range(1, short_taps):
        total = total + filter_ref[tap : tap + 1, :] * ext[tap : tap + rows]
    out_ref[...] = total.astype(BF16)


def short_adjoint_call(grads, rim, filters, first, out):
    parts, rows, channels = grads.shape
    short_taps = filters.shape[0]
    width = block_width(channels, 1024)
    steps = channels // width
    result = pl.BlockSpec((rows, width), lambda p, i: (0, (p + first) * steps + i))
    given = [] if out is None else [out]
    return hbm_call(
        functools.partial(short_adjoint_kernel, short_taps),
        loose=(1,),
        grid=(parts, steps),
        in_specs=[
            pl.BlockSpec((1, rows, width), lambda p, i: (p, 0, i)),
            pl.BlockSpec((1, RIM, width), lambda p, i: (p, 0, i)),
            pl.BlockSpec((short_taps, width), lambda p, i: (0, (p + first) * steps + i)),
        ]
        + [pl.BlockSpec(memory_space=pl.ANY)] * len(given),
        out_specs=result,
        out_shape=jax.ShapeDtypeStruct((rows, 3 * channels), BF16),
        input_output_aliases={3: 0} if given else {},
        compiler_params=params(),
        cost_estimate=cost(2 * parts * short_taps * rows * channels, 4 * parts * rows * channels),
        name="short_adjoint",
    )(grads, rim, filters, *given)


def spread_kernel(place, query_ref, key_ref, value_ref, long_ref, own_ref, other_ref):
    steps = query_ref.shape[1] // LANES
    half = own_ref.shape[0]
    tiles = [ref[:, i * LANES : (i + 1) * LANES] for ref in (query_ref, key_ref, value_ref) for i in range(steps)]
    tiles += [long_ref[8 * i : 8 * i + 8, :] for i in range(long_ref.shape[0] // 8)]
    first = place[0] < half

    @pl.when(first)
    def _():
        for i in range(half):
            own_ref[place[i]] = tiles[i]
            other_ref[place[half + i] - half] = tiles[half + i]

    @pl.when(jnp.logical_not(first))
    def _():
        for i in range(half):
            other_ref[place[i] - half] = tiles[i]
            own_ref[place[half + i]] = tiles[half + i]


def collect_kernel(place, *refs):
    parts, short_ref, long_ref, tiles_ref = refs[:-3], refs[-3], refs[-2], refs[-1]
    short_taps, wide = short_ref.shape
    steps = wide // LANES
    size = parts[0].shape[0]
    for i, part in enumerate(parts):
        tiles_ref[i * size : (i + 1) * size] = part[...]
    for i in range(steps):
        short_ref[:, i * LANES : (i + 1) * LANES] = tiles_ref[place[i]][0:short_taps, :]
    for i in range(long_ref.shape[0] // 8):
        long_ref[8 * i : 8 * i + 8, :] = tiles_ref[place[steps + i]]


def in_vmem():
    return pl.BlockSpec(memory_space=pltpu.VMEM)


def total_over_devices(spread_to, collect_from, query_sum, key_sum, value_sum, long_sum, short_taps):
    ny, nz = lax.axis_size("y"), lax.axis_size("z")
    channels = query_sum.shape[1]
    count = 3 * channels // LANES + long_sum.shape[0] // 8
    half = jax.ShapeDtypeStruct((count // 2, 8, LANES), F32)
    own, other = pl.pallas_call(
        spread_kernel,
        in_specs=[pl.BlockSpec(memory_space=pltpu.SMEM)] + [in_vmem()] * 4,
        out_specs=[in_vmem()] * 2,
        out_shape=[half] * 2,
        compiler_params=params(),
        name="spread",
    )(spread_to, query_sum, key_sum, value_sum, long_sum)
    part = own + move(other, c=1)
    size = count // 2 // nz
    part = sum([move(part[d * size : (d + 1) * size], z=d) for d in range(1, nz)], part[:size])
    whole = paired_sum([part] + [move(part, y=d) for d in range(1, ny)])
    whole = paired_sum([move(whole, xl=a, xh=b) for a, b in FLIPS])
    line = jnp.concatenate([whole, move(whole, c=1)], axis=0)
    lines = [move(line, z=-d) for d in range(nz)]
    groups, taps = long_sum.shape
    return pl.pallas_call(
        collect_kernel,
        in_specs=[pl.BlockSpec(memory_space=pltpu.SMEM)] + [in_vmem()] * nz,
        out_specs=[in_vmem(), in_vmem()],
        scratch_shapes=[pltpu.VMEM((count, 8, LANES), F32)],
        out_shape=[
            jax.ShapeDtypeStruct((short_taps, 3 * channels), F32),
            jax.ShapeDtypeStruct((groups, taps), F32),
        ],
        compiler_params=params(),
        name="collect",
    )(collect_from, *lines)


def paired_sum(terms):
    half = len(terms) // 2
    if half == 0:
        return terms[0]
    return paired_sum([terms[i] + terms[i + half] for i in range(half)])


def gather_near(shard):
    ny = lax.axis_size("y")
    half = shard.shape[0] // 2
    top, bottom = shard[:half], shard[half:]
    return (
        jnp.stack([move(top, xl=a, xh=b) for a, b in FLIPS]),
        jnp.stack([move(bottom, y=d) for d in range(ny)]),
    )


def gather_far(wide_top, tall_bottom):
    ny = lax.axis_size("y")
    return (
        [move(wide_top, y=d) for d in range(ny)],
        [move(tall_bottom, xl=a, xh=b) for a, b in FLIPS],
    )


def piece_rows(tops, bottoms, step):
    rows = []
    for a in range(2):
        rows.append(jnp.concatenate([tops[step][2 * a + b] for b in range(2)], axis=1))
        rows.append(jnp.concatenate([bottoms[2 * a + b][step] for b in range(2)], axis=1))
    return rows


def gate_matmul_kernel(ny, *refs):
    cotangent_ref, tops, bottoms, out_ref = refs[0], refs[1 : 1 + ny], refs[1 + ny : 5 + ny], refs[5 + ny]
    left = cotangent_ref[...]
    at = 0
    for step in range(ny):
        for right in piece_rows(tops, bottoms, step):
            size = right.shape[0]
            out_ref[:, at : at + size] = lax.dot_general(
                left, right, (((1,), (1,)), ((), ())), preferred_element_type=F32
            ).astype(BF16)
            at += size


def whole(x):
    return pl.BlockSpec(x.shape, lambda *_, n=x.ndim: (0,) * n)


def gate_matmul(cotangents, tops, bottoms):
    rows, depth = cotangents.shape
    ny = len(tops)
    channels = 4 * ny * tops[0].shape[1]
    height = rows // 2
    return hbm_call(
        functools.partial(gate_matmul_kernel, ny),
        loose=range(5 + ny),
        grid=(rows // height,),
        in_specs=[pl.BlockSpec((height, depth), lambda i: (i, 0))] + [whole(x) for x in (*tops, *bottoms)],
        out_specs=pl.BlockSpec((height, channels), lambda i: (i, 0)),
        out_shape=jax.ShapeDtypeStruct((rows, channels), BF16),
        compiler_params=params(32),
        cost_estimate=cost(2 * rows * depth * channels, 2 * (rows + depth) * channels),
        name="gate_matmul",
    )(cotangents, *tops, *bottoms)


def project_kernel(ny, *refs):
    rows_ref, turned_ref, tops, bottoms = refs[0], refs[1], refs[2 : 2 + ny], refs[2 + ny : 6 + ny]
    own_ref, other_ref = refs[6 + ny : 8 + ny]
    top_grads, bottom_grads = refs[8 + ny : 8 + 2 * ny], refs[8 + 2 * ny : 12 + 2 * ny]
    total = refs[12 + 2 * ny]
    step = pl.program_id(0)
    rows = rows_ref[...]
    width = own_ref.shape[1]
    size = tops[0].shape[1]
    grads = jnp.dot(turned_ref[...], rows, preferred_element_type=F32).astype(BF16)
    for a in range(2):
        for b in range(2):
            at = (2 * a + 1) * size
            bottom_grads[2 * a + b][step] = grads[b * width : (b + 1) * width, at : at + size]
    for d in range(ny):

        @pl.when(step == d)
        def _(d=d):
            for a in range(2):
                for b in range(2):
                    at = 2 * a * size
                    top_grads[d][2 * a + b] = grads[b * width : (b + 1) * width, at : at + size]
            right = jnp.concatenate(piece_rows(tops, bottoms, d), axis=0)
            product = jnp.dot(rows, right, preferred_element_type=F32)
            if d == 0:
                total[...] = product
            else:
                total[...] += product

    @pl.when(step == ny - 1)
    def _():
        own_ref[...] = total[:, :width].astype(BF16)
        other_ref[...] = total[:, width:].astype(BF16)


def project(all_rows, turned, tops, bottoms):
    rows, channels = all_rows.shape
    ny = len(tops)
    size = tops[0].shape[1]
    width = turned.shape[0] // 2
    half = jax.ShapeDtypeStruct((rows, width), BF16)
    outs = (
        [half, half]
        + [jax.ShapeDtypeStruct((4, width, size), BF16)] * ny
        + [jax.ShapeDtypeStruct((ny, width, size), BF16)] * 4
    )
    results = hbm_call(
        functools.partial(project_kernel, ny),
        loose=range(1, 6 + ny),
        grid=(ny,),
        in_specs=[pl.BlockSpec((rows, channels // ny), lambda i: (0, i)), whole(turned)]
        + [whole(x) for x in (*tops, *bottoms)],
        out_specs=[whole(x) for x in outs],
        out_shape=outs,
        scratch_shapes=[pltpu.VMEM((rows, 2 * width), F32)],
        compiler_params=params(40),
        cost_estimate=cost(8 * rows * width * channels, 2 * (rows + 4 * width) * channels),
        name="project",
    )(all_rows, turned, *tops, *bottoms)
    return results[0], results[1], results[2 : 2 + ny], results[2 + ny :]


def plane_scatter_sum(top_grads, bottom_grads):
    ny = len(top_grads)

    def added(terms):
        total = terms[0].astype(F32)
        for term in terms[1:]:
            total = total + term.astype(F32)
        return total

    top = added([move(top_grads[d], y=-d) for d in range(ny)]).astype(BF16)
    bottom = added([move(bottom_grads[f], xl=a, xh=b) for f, (a, b) in enumerate(FLIPS)]).astype(BF16)
    top = added([move(top[f], xl=a, xh=b) for f, (a, b) in enumerate(FLIPS)])
    bottom = added([move(bottom[d], y=-d) for d in range(ny)])
    return jnp.concatenate([top, bottom], axis=1).T


def shards(tokens_in, short_filter, long_filter, out_weight, cotangent):
    ny, nz = lax.axis_size("y"), lax.axis_size("z")
    y, xl, xh, z, c = (lax.axis_index(a) for a in ("y", "xl", "xh", "z", "c"))
    tokens = tokens_in[0]
    rows, wide = tokens.shape
    channels = wide // 3
    short_taps = short_filter.shape[0]
    groups = long_filter.shape[0]
    upstream = cotangent[0]
    length, columns = upstream.shape
    span = length // 2

    block = jnp.arange(2 * ny, dtype=jnp.int32)
    place = ((y - block // 2) % ny) * 2 + (block + xl) % 2
    size = 3 * channels // LANES + groups // 8
    each = size // (2 * nz)
    tile = jnp.arange(size, dtype=jnp.int32)
    core_step, z_step = (tile // (nz * each) + c) % 2, (tile // each - z) % nz
    spread_to = (core_step * nz + z_step) * each + tile % each
    collect_from = (z_step * 2 + core_step) * each + tile % each

    rim = along(tokens[rows - RIM :], 1)
    lines = long_filter.astype(F32)
    query, key, value, mixer = features_call(tokens, rim, short_filter)
    mixer_prev = along(mixer, 1)
    mixed, gated = mix_call(place, lines, mixer_prev, mixer, query)
    gated, out_weight, upstream = lax.optimization_barrier((gated, out_weight, upstream))
    all_rows = lax.all_gather(gated, ("z", "c"), axis=0, tiled=True)
    wide_top, tall_bottom = gather_near(out_weight)
    tops, bottoms = gather_far(wide_top, tall_bottom)
    mine = lax.dynamic_slice_in_dim(upstream, xh * span, span, 0)
    others = move(lax.dynamic_slice_in_dim(upstream, (1 - xh) * span, span, 0), xh=1)
    cotangents = jnp.concatenate([mine, others], axis=1)
    partial = gate_matmul(cotangents, tops, bottoms)
    partial, all_rows = lax.optimization_barrier((partial, all_rows))
    gate_grad = lax.psum_scatter(partial, ("z", "c"), scatter_dimension=0, tiled=True)

    own, other, top_grads, bottom_grads = project(all_rows, cotangents.T, tops, bottoms)
    grad_weight = plane_scatter_sum(top_grads, bottom_grads)
    theirs = move(other, xh=1)
    output = jnp.where(xh == 0, jnp.concatenate([own, theirs], axis=0), jnp.concatenate([theirs, own], axis=0))
    gate_grad, grad_weight, output = lax.optimization_barrier((gate_grad, grad_weight, output))

    grad_mixed, query_grad = gate_call(place, gate_grad, query, mixed)
    grad_next = along(grad_mixed, -1)
    query_next = along(query_grad[:RIM], -1)
    grad_tokens = short_adjoint_call(query_grad[None], query_next[None], short_filter, 0, None)
    long_sum, query_sum = long_grad_call(
        groups, short_taps, mixer_prev, mixer, grad_mixed, query_grad, tokens, rim
    )
    other_grads, key_sum, value_sum = unmix_call(
        lines, short_taps, grad_mixed, grad_next, key, value, tokens, rim
    )
    other_next = along(other_grads[:, :RIM], -1)
    grad_short, grad_long = total_over_devices(
        spread_to, collect_from, query_sum, key_sum, value_sum, long_sum, short_taps
    )
    grad_tokens = short_adjoint_call(other_grads, other_next, short_filter, 1, grad_tokens)
    return output[None], grad_tokens[None], grad_short, grad_long, grad_weight


def solution(mesh):
    dp, seq = mesh.shape["dp"], mesh.shape["seq"]
    grid = jax.sharding.Mesh(mesh.devices.reshape(dp // 2, 2, 2, seq // 4, 2), ("y", "xl", "xh", "z", "c"))
    rows, line = ("y", "xl"), ("xh", "z", "c")
    return jax.shard_map(
        shards,
        mesh=grid,
        in_specs=(P(rows, line, None), P(), P(), P(rows, line), P(rows, None, line)),
        out_specs=(P(rows, None, line), P(rows, line, None), P(), P(), P(rows, line)),
        check_vma=False,
    )
```

```python
import functools
import itertools
import math

import jax
import jax.numpy as jnp
from jax import lax
from jax.experimental import pallas as pl
from jax.experimental.pallas import tpu as pltpu
from jax.sharding import PartitionSpec as P

LANES = 128
RIM = 8
MIB = 1024 * 1024
WIDTH = 1024
F32 = jnp.float32
BF16 = jnp.bfloat16


PLANE = ("y", "xl", "xh")
LINE = ("xh", "z", "c")


def along(x, by):
    size = math.prod(lax.axis_size(a) for a in LINE)
    pairs = [(i, i + by) for i in range(size) if 0 <= i + by < size]
    return lax.ppermute(x, LINE, pairs)


def move(x, **steps):
    axes = tuple(a for a in ("y", "xl", "xh", "z", "c") if steps.get(a, 0) % lax.axis_size(a))
    if not axes:
        return x
    sizes = [lax.axis_size(a) for a in axes]
    pairs = []
    for at in itertools.product(*(range(n) for n in sizes)):
        to = [(p + steps[a]) % n for p, a, n in zip(at, axes, sizes)]
        pairs.append((flat(at, sizes), flat(to, sizes)))
    return lax.ppermute(x, axes, pairs)


def flat(at, sizes):
    index = 0
    for p, n in zip(at, sizes):
        index = index * n + p
    return index


FLIPS = [(0, 0), (0, 1), (1, 0), (1, 1)]


def params(mib=16):
    return pltpu.CompilerParams(vmem_limit_bytes=mib * MIB)


def hbm_call(kernel, *, out_shape, loose=(), **options):
    single = not isinstance(out_shape, (list, tuple))
    shapes = [out_shape] if single else out_shape
    placed = [pltpu.HBM(x.shape, x.dtype) if x.size * x.dtype.itemsize > 256 * 1024 else x for x in shapes]
    call = pl.pallas_call(kernel, out_shape=placed[0] if single else placed, **options)

    def run(*args):
        held = [x if i in loose else pltpu.with_memory_space_constraint(x, pltpu.HBM) for i, x in enumerate(args)]
        return call(*held)

    return run


def cost(flops, moved):
    return pl.CostEstimate(flops=int(flops), bytes_accessed=int(moved), transcendentals=0)


def block_width(channels, most):
    width = min(channels, most)
    while channels % width:
        width //= 2
    return width


def extend(ext, rim, rows_of, at):
    ext[0:RIM, :] = rim[:, at].astype(F32)
    ext[RIM:, :] = rows_of.astype(F32)


def features_kernel(short_taps, tokens, rims, filters, query_ref, key_ref, value_ref, mixer_ref, ext):
    rows, width = tokens[0].shape

    def filtered(part, block, at):
        own = ext.at[(3 * block + part) % ext.shape[0]]
        extend(own, rims[part], tokens[part][:, at], at)
        taps = filters[part][:, at]
        total = taps[0:1] * own[RIM : RIM + rows, :]
        for tap in range(1, short_taps):
            total = total + taps[tap : tap + 1] * own[RIM - tap : RIM - tap + rows, :]
        return total

    for block in range(width // LANES):
        at = pl.ds(block * LANES, LANES)
        query_ref[:, at] = filtered(0, block, at).astype(BF16)
        key, value = filtered(1, block, at), filtered(2, block, at)
        key_ref[:, at] = key.astype(BF16)
        value_ref[:, at] = value.astype(BF16)
        mixer_ref[:, at] = (key * value).astype(BF16)


def features_call(tokens, rim, filters):
    rows, wide = tokens.shape
    channels = wide // 3
    taps = filters.shape[0]
    width = block_width(channels, WIDTH)
    steps = channels // width

    def spec(height, part):
        return pl.BlockSpec((height, width), lambda i, part=part: (0, i + part * steps))

    def body(*refs):
        features_kernel(taps, refs[0:3], refs[3:6], refs[6:9], *refs[9:])

    out = jax.ShapeDtypeStruct((rows, channels), BF16)
    return hbm_call(
        body,
        loose=(3, 4, 5),
        grid=(steps,),
        in_specs=[spec(rows, p) for p in range(3)]
        + [spec(RIM, p) for p in range(3)]
        + [spec(taps, p) for p in range(3)],
        out_specs=[pl.BlockSpec((rows, width), lambda i: (0, i))] * 4,
        out_shape=[out] * 4,
        scratch_shapes=[pltpu.VMEM((6, RIM + rows, LANES), F32)],
        compiler_params=params(),
        cost_estimate=cost(0, rows * wide),
        name="features",
    )(tokens, tokens, tokens, rim, rim, rim, filters, filters, filters)


def lane_row(shape):
    row = lax.broadcasted_iota(jnp.int32, shape, 0)
    lane = lax.broadcasted_iota(jnp.int32, shape, 1)
    return row, lane


def mirror(size):
    row, lane = lane_row((size, size))
    both = row + lane
    return jnp.where((both == 0) | (both == size), 1.0, 0.0)


def circulant(line, taps):
    wide = jnp.broadcast_to(line.astype(F32), (taps, taps))
    return pltpu.roll(wide, 0, 1, stride=1, stride_axis=0)


def pick_groups(product, rows, per_group):
    lane = lax.broadcasted_iota(jnp.int32, (rows, LANES), 1)
    total = product[0:rows]
    for g in range(1, LANES // per_group):
        total = jnp.where(lane >= g * per_group, product[g * rows : (g + 1) * rows], total)
    return total


def mix_kernel(per_group, lines_ref, prev_ref, cur_ref, query_ref, mixed_ref, gated_ref, table, lines):
    rows, width = cur_ref.shape
    row, lane = lane_row((rows, rows))
    above = lane > row
    packed = LANES // per_group
    lines[...] = jnp.dot(lines_ref[...].astype(BF16), mirror(rows).astype(BF16), preferred_element_type=F32)
    for block in range(width // LANES):
        at = pl.ds(block * LANES, LANES)
        own = table.at[block % 2]
        for g in range(packed):
            ring = circulant(lines[block * packed + g : block * packed + g + 1, :], rows)
            own[g * rows : (g + 1) * rows, 0:rows] = jnp.where(above, ring, 0.0).astype(BF16)
            own[g * rows : (g + 1) * rows, rows : 2 * rows] = jnp.where(above, 0.0, ring).astype(BF16)
        window = jnp.concatenate([prev_ref[:, at], cur_ref[:, at]], axis=0)
        product = jnp.dot(own[...], window, preferred_element_type=F32)
        mixed = pick_groups(product, rows, per_group)
        mixed_ref[:, at] = mixed.astype(BF16)
        gated_ref[:, at] = (query_ref[:, at].astype(F32) * mixed).astype(BF16)


def mix_call(lines, prev, cur, query):
    rows, channels = cur.shape
    groups, taps = lines.shape
    per_group = channels // groups
    width = block_width(channels, WIDTH)
    steps = channels // width
    wide = pl.BlockSpec((rows, width), lambda i: (0, i))
    out = jax.ShapeDtypeStruct((rows, channels), BF16)
    return hbm_call(
        functools.partial(mix_kernel, per_group),
        loose=(0, 1),
        grid=(steps,),
        in_specs=[pl.BlockSpec((width // per_group, taps), lambda i: (i, 0)), wide, wide, wide],
        out_specs=[wide, wide],
        out_shape=[out, out],
        scratch_shapes=[
            pltpu.VMEM((2, LANES // per_group * rows, 2 * rows), BF16),
            pltpu.VMEM((width // per_group, taps), F32),
        ],
        compiler_params=params(),
        cost_estimate=cost(0, 2 * rows * channels),
        name="mix",
    )(lines, prev, cur, query)


def gate_kernel(place, gate_grad_ref, query_ref, mixed_ref, grad_ref, feature_ref):
    width = query_ref.shape[1] // place.shape[0]
    for i in range(place.shape[0]):
        at = pl.ds(i * width, width)
        gate_grad = gate_grad_ref[:, pl.ds(pl.multiple_of(place[i] * width, width), width)].astype(F32)
        grad_ref[:, at] = (gate_grad * query_ref[:, at].astype(F32)).astype(BF16)
        feature_ref[:, at] = (gate_grad * mixed_ref[:, at].astype(F32)).astype(BF16)


def gate_call(place, gate_grad, query, mixed):
    rows, channels = query.shape
    out = jax.ShapeDtypeStruct((rows, channels), BF16)
    return hbm_call(
        gate_kernel,
        loose=(0,),
        grid_spec=pltpu.PrefetchScalarGridSpec(
            num_scalar_prefetch=1,
            grid=(2,),
            in_specs=[pl.BlockSpec((rows // 2, channels), lambda i, place: (i, 0))] * 3,
            out_specs=[pl.BlockSpec((rows // 2, channels), lambda i, place: (i, 0))] * 2,
        ),
        out_shape=[out, out],
        compiler_params=params(),
        cost_estimate=cost(2 * rows * channels, 10 * rows * channels),
        name="gate_back",
    )(place, gate_grad, query, mixed)


def tap_sums(short_taps, grad, tokens_ref, rim_ref, out_ref, at, ext):
    rows = tokens_ref.shape[0]
    extend(ext, rim_ref, tokens_ref[:, at], at)
    grad = grad.astype(F32)
    for tap in range(short_taps):
        out_ref[tap : tap + 1, at] = jnp.sum(grad * ext[RIM - tap : RIM - tap + rows, :], axis=0, keepdims=True)
    out_ref[short_taps:8, at] = jnp.zeros((8 - short_taps, LANES), F32)


def long_grad_kernel(
    per_group, short_taps, prev_ref, cur_ref, grad_ref, feature_ref, tokens_ref, rim_ref, long_ref, short_ref, fold, masked, ext
):
    rows, width = cur_ref.shape
    row, lane = lane_row((rows, rows))
    above = lane > row
    member = lax.broadcasted_iota(jnp.int32, (rows, LANES), 1)
    packed = LANES // per_group
    sums = []
    for block in range(width // LANES):
        at = pl.ds(block * LANES, LANES)
        window = jnp.concatenate([prev_ref[:, at], cur_ref[:, at]], axis=0)
        grad_wide = grad_ref[:, at].astype(F32)
        own = masked.at[block % 2]
        for g in range(packed):
            own[g * rows : (g + 1) * rows, :] = jnp.where((member >= g * per_group) & (member < (g + 1) * per_group), grad_wide, 0.0).astype(BF16)
        pairs = lax.dot_general(own[...], window, (((1,), (1,)), ((), ())), preferred_element_type=F32)
        for g in range(packed):
            pair = pairs[g * rows : (g + 1) * rows]
            ring = jnp.where(above, pair[:, 0:rows], pair[:, rows : 2 * rows])
            total = ring[0:8]
            for tile in range(1, rows // 8):
                total = total + pltpu.roll(ring[8 * tile : 8 * tile + 8], rows - 8 * tile, 1)
            fold[block % 2, g * 8 : (g + 1) * 8, :] = total
        total = fold[block % 2, pl.ds(0, packed, stride=8), :]
        for step in range(1, 8):
            total = total + pltpu.roll(fold[block % 2, pl.ds(step, packed, stride=8), :], rows - step, 1)
        sums.append(total)
        tap_sums(short_taps, feature_ref[:, at], tokens_ref, rim_ref, short_ref, at, ext.at[block % 2])
    long_ref[...] = jnp.dot(
        jnp.concatenate(sums, axis=0), mirror(rows), precision=lax.Precision.HIGHEST, preferred_element_type=F32
    )


def long_grad_call(groups, short_taps, prev, cur, grad, feature, tokens, rim):
    rows, channels = cur.shape
    per_group = channels // groups
    width = block_width(channels, WIDTH)
    steps = channels // width
    wide = pl.BlockSpec((rows, width), lambda i: (0, i))
    packed = LANES // per_group
    return hbm_call(
        functools.partial(long_grad_kernel, per_group, short_taps),
        grid=(steps,),
        in_specs=[wide] * 5 + [pl.BlockSpec((RIM, width), lambda i: (0, i))],
        out_specs=[
            pl.BlockSpec((width // per_group, rows), lambda i: (i, 0)),
            pl.BlockSpec((8, width), lambda i: (0, i)),
        ],
        out_shape=[
            jax.ShapeDtypeStruct((groups, rows), F32),
            jax.ShapeDtypeStruct((8, channels), F32),
        ],
        scratch_shapes=[
            pltpu.VMEM((2, packed * 8, LANES), F32),
            pltpu.VMEM((2, packed * rows, LANES), BF16),
            pltpu.VMEM((2, RIM + rows, LANES), F32),
        ],
        compiler_params=params(),
        cost_estimate=cost(2 * groups * rows * 2 * rows * LANES, 10 * rows * channels),
        name="long_grad",
    )(prev, cur, grad, feature, tokens, rim)


def unmix_kernel(
    per_group, short_taps, lines_ref, grad_ref, next_ref, key_ref, value_ref, key_tokens_ref, value_tokens_ref,
    key_rim_ref, value_rim_ref, feature_ref, key_sum_ref, value_sum_ref, table, ext,
):
    rows, width = grad_ref.shape
    row, lane = lane_row((rows, rows))
    below = lane < row
    packed = LANES // per_group
    for block in range(width // LANES):
        at = pl.ds(block * LANES, LANES)
        own = table.at[block % 2]
        for g in range(packed):
            ring = circulant(lines_ref[block * packed + g : block * packed + g + 1, :], rows)
            own[g * rows : (g + 1) * rows, 0:rows] = jnp.where(below, 0.0, ring).astype(BF16)
            own[g * rows : (g + 1) * rows, rows : 2 * rows] = jnp.where(below, ring, 0.0).astype(BF16)
        window = jnp.concatenate([grad_ref[:, at], next_ref[:, at]], axis=0)
        product = jnp.dot(own[...], window, preferred_element_type=F32)
        grad_mixer = pick_groups(product, rows, per_group)
        key_grad = (grad_mixer * value_ref[:, at].astype(F32)).astype(BF16)
        value_grad = (grad_mixer * key_ref[:, at].astype(F32)).astype(BF16)
        feature_ref[0, :, at] = key_grad
        feature_ref[1, :, at] = value_grad
        slot = 2 * (block % 2)
        tap_sums(short_taps, key_grad, key_tokens_ref, key_rim_ref, key_sum_ref, at, ext.at[slot])
        tap_sums(short_taps, value_grad, value_tokens_ref, value_rim_ref, value_sum_ref, at, ext.at[slot + 1])


def unmix_call(lines, short_taps, grad, grad_next, key, value, tokens, rim):
    rows, channels = grad.shape
    groups, taps = lines.shape
    per_group = channels // groups
    width = block_width(channels, WIDTH)
    steps = channels // width

    def spec(height, part):
        return pl.BlockSpec((height, width), lambda i, part=part: (0, i + part * steps))

    wide = spec(rows, 0)
    packed = LANES // per_group
    sums = jax.ShapeDtypeStruct((8, channels), F32)
    return hbm_call(
        functools.partial(unmix_kernel, per_group, short_taps),
        loose=(0, 2),
        grid=(steps,),
        in_specs=[pl.BlockSpec((width // per_group, taps), lambda i: (i, 0))]
        + [wide] * 4
        + [spec(rows, 1), spec(rows, 2), spec(RIM, 1), spec(RIM, 2)],
        out_specs=[pl.BlockSpec((2, rows, width), lambda i: (0, 0, i)), spec(8, 0), spec(8, 0)],
        out_shape=[jax.ShapeDtypeStruct((2, rows, channels), BF16), sums, sums],
        scratch_shapes=[pltpu.VMEM((2, packed * rows, 2 * rows), BF16), pltpu.VMEM((4, RIM + rows, LANES), F32)],
        compiler_params=params(),
        cost_estimate=cost(2 * groups * rows * 2 * rows * LANES, 16 * rows * channels),
        name="unmix",
    )(lines, grad, grad_next, key, value, tokens, tokens, rim, rim)


def short_adjoint_kernel(short_taps, grads_ref, rim_ref, filter_ref, *refs):
    out_ref, ext = refs[-2:]
    rows, width = out_ref.shape
    for block in range(width // LANES):
        at = pl.ds(block * LANES, LANES)
        own = ext.at[block % 2]
        own[0:rows, :] = grads_ref[0, :, at].astype(F32)
        own[rows:, :] = rim_ref[0, :, at].astype(F32)
        taps = filter_ref[:, at]
        total = taps[0:1] * own[0:rows, :]
        for tap in range(1, short_taps):
            total = total + taps[tap : tap + 1] * own[tap : tap + rows, :]
        out_ref[:, at] = total.astype(BF16)


def short_adjoint_call(grads, rim, filters, first, out):
    parts, rows, channels = grads.shape
    short_taps = filters.shape[0]
    width = block_width(channels, 2 * WIDTH)
    steps = channels // width
    result = pl.BlockSpec((rows, width), lambda p, i: (0, (p + first) * steps + i))
    given = [] if out is None else [out]
    return hbm_call(
        functools.partial(short_adjoint_kernel, short_taps),
        loose=(1,),
        grid=(parts, steps),
        in_specs=[
            pl.BlockSpec((1, rows, width), lambda p, i: (p, 0, i)),
            pl.BlockSpec((1, RIM, width), lambda p, i: (p, 0, i)),
            pl.BlockSpec((short_taps, width), lambda p, i: (0, (p + first) * steps + i)),
        ]
        + [pl.BlockSpec(memory_space=pl.ANY)] * len(given),
        out_specs=result,
        out_shape=jax.ShapeDtypeStruct((rows, 3 * channels), BF16),
        input_output_aliases={3: 0} if given else {},
        scratch_shapes=[pltpu.VMEM((2, rows + RIM, LANES), F32)],
        compiler_params=params(),
        cost_estimate=cost(2 * parts * short_taps * rows * channels, 4 * parts * rows * channels),
        name="short_adjoint",
    )(grads, rim, filters, *given)


def spread_kernel(place, query_ref, key_ref, value_ref, long_ref, own_ref, other_ref):
    steps = query_ref.shape[1] // LANES
    half = own_ref.shape[0]
    tiles = [ref[:, i * LANES : (i + 1) * LANES] for ref in (query_ref, key_ref, value_ref) for i in range(steps)]
    tiles += [long_ref[8 * i : 8 * i + 8, :] for i in range(long_ref.shape[0] // 8)]
    first = place[0] < half

    @pl.when(first)
    def _():
        for i in range(half):
            own_ref[place[i]] = tiles[i]
            other_ref[place[half + i] - half] = tiles[half + i]

    @pl.when(jnp.logical_not(first))
    def _():
        for i in range(half):
            other_ref[place[i] - half] = tiles[i]
            own_ref[place[half + i]] = tiles[half + i]


def collect_kernel(place, *refs):
    parts, short_ref, long_ref, tiles_ref = refs[:-3], refs[-3], refs[-2], refs[-1]
    short_taps, wide = short_ref.shape
    steps = wide // LANES
    size = parts[0].shape[0]
    for i, part in enumerate(parts):
        tiles_ref[i * size : (i + 1) * size] = part[...]
    for i in range(steps):
        short_ref[:, i * LANES : (i + 1) * LANES] = tiles_ref[place[i]][0:short_taps, :]
    for i in range(long_ref.shape[0] // 8):
        long_ref[8 * i : 8 * i + 8, :] = tiles_ref[place[steps + i]]


def in_vmem():
    return pl.BlockSpec(memory_space=pltpu.VMEM)


def total_over_devices(spread_to, collect_from, query_sum, key_sum, value_sum, long_sum, short_taps):
    ny, nz = lax.axis_size("y"), lax.axis_size("z")
    channels = query_sum.shape[1]
    count = 3 * channels // LANES + long_sum.shape[0] // 8
    half = jax.ShapeDtypeStruct((count // 2, 8, LANES), F32)
    own, other = pl.pallas_call(
        spread_kernel,
        in_specs=[pl.BlockSpec(memory_space=pltpu.SMEM)] + [in_vmem()] * 4,
        out_specs=[in_vmem()] * 2,
        out_shape=[half] * 2,
        compiler_params=params(),
        name="spread",
    )(spread_to, query_sum, key_sum, value_sum, long_sum)
    part = own + move(other, c=1)
    size = count // 2 // nz
    part = sum([move(part[d * size : (d + 1) * size], z=d) for d in range(1, nz)], part[:size])
    whole = paired_sum([part] + [move(part, y=d) for d in range(1, ny)])
    whole = paired_sum([move(whole, xl=a, xh=b) for a, b in FLIPS])
    line = jnp.concatenate([whole, move(whole, c=1)], axis=0)
    lines = [move(line, z=-d) for d in range(nz)]
    groups, taps = long_sum.shape
    return pl.pallas_call(
        collect_kernel,
        in_specs=[pl.BlockSpec(memory_space=pltpu.SMEM)] + [in_vmem()] * nz,
        out_specs=[in_vmem(), in_vmem()],
        scratch_shapes=[pltpu.VMEM((count, 8, LANES), F32)],
        out_shape=[
            jax.ShapeDtypeStruct((short_taps, 3 * channels), F32),
            jax.ShapeDtypeStruct((groups, taps), F32),
        ],
        compiler_params=params(),
        name="collect",
    )(collect_from, *lines)


def paired_sum(terms):
    half = len(terms) // 2
    if half == 0:
        return terms[0]
    return paired_sum([terms[i] + terms[i + half] for i in range(half)])


def gather_near(shard):
    ny = lax.axis_size("y")
    half = shard.shape[0] // 2
    top, bottom = shard[:half], shard[half:]
    return [move(top, xl=a, xh=b) for a, b in FLIPS], [move(bottom, y=d) for d in range(ny)]


def gather_far(wide_top, tall_bottom):
    ny = lax.axis_size("y")
    wide_top, tall_bottom = jnp.stack(wide_top), jnp.stack(tall_bottom)
    return (
        [move(wide_top, y=d) for d in range(ny)],
        [move(tall_bottom, xl=a, xh=b) for a, b in FLIPS],
    )


def piece_rows(tops, bottoms, step):
    rows = []
    for a in range(2):
        rows.append(jnp.concatenate([tops[step][2 * a + b] for b in range(2)], axis=1))
        rows.append(jnp.concatenate([bottoms[2 * a + b][step] for b in range(2)], axis=1))
    return rows


def gate_matmul_kernel(ny, *refs):
    cotangent_ref, tops, bottoms, out_ref = refs[0], refs[1 : 1 + ny], refs[1 + ny : 5 + ny], refs[5 + ny]
    left = cotangent_ref[...]
    at = 0
    for step in range(ny):
        for right in piece_rows(tops, bottoms, step):
            size = right.shape[0]
            out_ref[:, at : at + size] = lax.dot_general(
                left, right, (((1,), (1,)), ((), ())), preferred_element_type=F32
            ).astype(BF16)
            at += size


def whole(x):
    return pl.BlockSpec(x.shape, lambda *_, n=x.ndim: (0,) * n)


def gate_matmul(cotangents, tops, bottoms):
    rows, depth = cotangents.shape
    ny = len(tops)
    channels = 4 * ny * tops[0].shape[1]
    height = rows // 2
    return hbm_call(
        functools.partial(gate_matmul_kernel, ny),
        loose=range(5 + ny),
        grid=(rows // height,),
        in_specs=[pl.BlockSpec((height, depth), lambda i: (i, 0))] + [whole(x) for x in (*tops, *bottoms)],
        out_specs=pl.BlockSpec((height, channels), lambda i: (i, 0)),
        out_shape=jax.ShapeDtypeStruct((rows, channels), BF16),
        compiler_params=params(32),
        cost_estimate=cost(2 * rows * depth * channels, 2 * (rows + depth) * channels),
        name="gate_matmul",
    )(cotangents, *tops, *bottoms)


def project_kernel(ny, origin, *refs):
    rows_ref, turned_ref, tops, bottoms = refs[0], refs[1], refs[2 : 2 + ny], refs[2 + ny : 6 + ny]
    own_ref, other_ref = refs[6 + ny : 8 + ny]
    top_grads, bottom_grads = refs[8 + ny : 8 + 2 * ny], refs[8 + 2 * ny : 12 + 2 * ny]
    total = refs[12 + 2 * ny]
    step = pl.program_id(0)
    height = rows_ref.shape[1] // 2
    rows = jnp.concatenate(
        [rows_ref[:, pl.ds(pl.multiple_of(origin[2 * step + a] % 2 * height, height), height)] for a in range(2)], axis=1
    )
    width = own_ref.shape[1]
    size = tops[0].shape[1]
    grads = jnp.dot(turned_ref[...], rows, preferred_element_type=F32).astype(BF16)
    for a in range(2):
        for b in range(2):
            at = (2 * a + 1) * size
            bottom_grads[2 * a + b][step] = grads[b * width : (b + 1) * width, at : at + size]
    for d in range(ny):

        @pl.when(step == d)
        def _(d=d):
            for a in range(2):
                for b in range(2):
                    at = 2 * a * size
                    top_grads[d][2 * a + b] = grads[b * width : (b + 1) * width, at : at + size]
            right = jnp.concatenate(piece_rows(tops, bottoms, d), axis=0)
            product = jnp.dot(rows, right, preferred_element_type=F32)
            if d == 0:
                total[...] = product
            else:
                total[...] += product

    @pl.when(step == ny - 1)
    def _():
        own_ref[...] = total[:, :width].astype(BF16)
        other_ref[...] = total[:, width:].astype(BF16)


def project(origin, all_rows, turned, tops, bottoms):
    rows, channels = all_rows.shape
    ny = len(tops)
    size = tops[0].shape[1]
    width = turned.shape[0] // 2
    half = jax.ShapeDtypeStruct((rows, width), BF16)
    outs = (
        [half, half]
        + [jax.ShapeDtypeStruct((4, width, size), BF16)] * ny
        + [jax.ShapeDtypeStruct((ny, width, size), BF16)] * 4
    )
    results = hbm_call(
        functools.partial(project_kernel, ny),
        loose=(0, *range(2, 7 + ny)),
        grid_spec=pltpu.PrefetchScalarGridSpec(
            num_scalar_prefetch=1,
            grid=(ny,),
            in_specs=[pl.BlockSpec((rows, channels // ny), lambda i, origin: (0, origin[2 * i] // 2)), whole(turned)]
            + [whole(x) for x in (*tops, *bottoms)],
            out_specs=[whole(x) for x in outs],
            scratch_shapes=[pltpu.VMEM((rows, 2 * width), F32)],
        ),
        out_shape=outs,
        compiler_params=params(40),
        cost_estimate=cost(8 * rows * width * channels, 2 * (rows + 4 * width) * channels),
        name="project",
    )(origin, all_rows, turned, *tops, *bottoms)
    return results[0], results[1], results[2 : 2 + ny], results[2 + ny :]


def plane_scatter_sum(top_grads, bottom_grads):
    ny = len(top_grads)

    def added(terms):
        total = terms[0].astype(F32)
        for term in terms[1:]:
            total = total + term.astype(F32)
        return total

    top = added([move(top_grads[d], y=-d) for d in range(ny)]).astype(BF16)
    bottom = added([move(bottom_grads[f], xl=a, xh=b) for f, (a, b) in enumerate(FLIPS)]).astype(BF16)
    top = added([move(top[f], xl=a, xh=b) for f, (a, b) in enumerate(FLIPS)])
    bottom = added([move(bottom[d], y=-d) for d in range(ny)])
    return jnp.concatenate([top, bottom], axis=1).T


def shards(tokens_in, short_filter, long_filter, out_weight, cotangent):
    ny, nz = lax.axis_size("y"), lax.axis_size("z")
    y, xl, xh, z, c = (lax.axis_index(a) for a in ("y", "xl", "xh", "z", "c"))
    tokens = tokens_in[0]
    rows, wide = tokens.shape
    channels = wide // 3
    short_taps = short_filter.shape[0]
    groups = long_filter.shape[0]
    upstream = cotangent[0]
    length, columns = upstream.shape
    span = length // 2

    block = jnp.arange(2 * ny, dtype=jnp.int32)
    place = ((y - block // 2) % ny) * 2 + (block + xl) % 2
    origin = place
    size = 3 * channels // LANES + groups // 8
    each = size // (2 * nz)
    tile = jnp.arange(size, dtype=jnp.int32)
    core_step, z_step = (tile // (nz * each) + c) % 2, (tile // each - z) % nz
    spread_to = (core_step * nz + z_step) * each + tile % each
    collect_from = (z_step * 2 + core_step) * each + tile % each

    rim = along(tokens[rows - RIM :], 1)
    lines = long_filter.astype(F32)
    query, key, value, mixer = features_call(tokens, rim, short_filter)
    mixer, out_weight = lax.optimization_barrier((mixer, out_weight))
    mixer_prev = along(mixer, 1)
    wide_top, tall_bottom = gather_near(out_weight)
    mixer_prev, wide_top, tall_bottom = lax.optimization_barrier((mixer_prev, wide_top, tall_bottom))
    mixed, gated = mix_call(lines, mixer_prev, mixer, query)
    mixed, wide_top, tall_bottom, upstream = lax.optimization_barrier((mixed, wide_top, tall_bottom, upstream))
    all_rows = lax.all_gather(gated, ("z", "c"), axis=0, tiled=True)
    tops, bottoms = gather_far(wide_top, tall_bottom)
    mine = lax.dynamic_slice_in_dim(upstream, xh * span, span, 0)
    others = move(lax.dynamic_slice_in_dim(upstream, (1 - xh) * span, span, 0), xh=1)
    cotangents = jnp.concatenate([mine, others], axis=1)
    partial = gate_matmul(cotangents, tops, bottoms)
    partial, all_rows = lax.optimization_barrier((partial, all_rows))
    gate_grad = lax.psum_scatter(partial, ("z", "c"), scatter_dimension=0, tiled=True)

    own, other, top_grads, bottom_grads = project(origin, all_rows, cotangents.T, tops, bottoms)
    grad_weight = plane_scatter_sum(top_grads, bottom_grads)
    theirs = move(other, xh=1)
    output = jnp.where(xh == 0, jnp.concatenate([own, theirs], axis=0), jnp.concatenate([theirs, own], axis=0))
    gate_grad, grad_weight, output = lax.optimization_barrier((gate_grad, grad_weight, output))

    grad_mixed, query_grad = gate_call(place, gate_grad, query, mixed)
    grad_next = along(grad_mixed, -1)
    query_next = along(query_grad[:RIM], -1)
    grad_tokens = short_adjoint_call(query_grad[None], query_next[None], short_filter, 0, None)
    long_sum, query_sum = long_grad_call(
        groups, short_taps, mixer_prev, mixer, grad_mixed, query_grad, tokens, rim
    )
    grad_next, grad_tokens, long_sum, query_sum = lax.optimization_barrier(
        (grad_next, grad_tokens, long_sum, query_sum)
    )
    other_grads, key_sum, value_sum = unmix_call(
        lines, short_taps, grad_mixed, grad_next, key, value, tokens, rim
    )
    other_next = along(other_grads[:, :RIM], -1)
    grad_short, grad_long = total_over_devices(
        spread_to, collect_from, query_sum, key_sum, value_sum, long_sum, short_taps
    )
    grad_tokens = short_adjoint_call(other_grads, other_next, short_filter, 1, grad_tokens)
    return output[None], grad_tokens[None], grad_short, grad_long, grad_weight


def solution(mesh):
    dp, seq = mesh.shape["dp"], mesh.shape["seq"]
    grid = jax.sharding.Mesh(mesh.devices.reshape(dp // 2, 2, 2, seq // 4, 2), ("y", "xl", "xh", "z", "c"))
    rows, line = ("y", "xl"), ("xh", "z", "c")
    return jax.shard_map(
        shards,
        mesh=grid,
        in_specs=(P(rows, line, None), P(), P(), P(rows, line), P(rows, None, line)),
        out_specs=(P(rows, None, line), P(rows, line, None), P(), P(), P(rows, line)),
        check_vma=False,
    )
```

```python
import functools
import itertools
import math

import jax
import jax.numpy as jnp
from jax import lax
from jax.experimental import pallas as pl
from jax.experimental.pallas import tpu as pltpu
from jax.sharding import PartitionSpec as P

LANES = 128
RIM = 8
MIB = 1024 * 1024
WIDTH = 1024
F32 = jnp.float32
BF16 = jnp.bfloat16


PLANE = ("y", "xl", "xh")
LINE = ("xh", "z", "c")


def along(x, by):
    size = math.prod(lax.axis_size(a) for a in LINE)
    pairs = [(i, i + by) for i in range(size) if 0 <= i + by < size]
    return lax.ppermute(x, LINE, pairs)


def move(x, **steps):
    axes = tuple(a for a in ("y", "xl", "xh", "z", "c") if steps.get(a, 0) % lax.axis_size(a))
    if not axes:
        return x
    sizes = [lax.axis_size(a) for a in axes]
    pairs = []
    for at in itertools.product(*(range(n) for n in sizes)):
        to = [(p + steps[a]) % n for p, a, n in zip(at, axes, sizes)]
        pairs.append((flat(at, sizes), flat(to, sizes)))
    return lax.ppermute(x, axes, pairs)


def flat(at, sizes):
    index = 0
    for p, n in zip(at, sizes):
        index = index * n + p
    return index


FLIPS = [(0, 0), (0, 1), (1, 0), (1, 1)]


def params(mib=16):
    return pltpu.CompilerParams(vmem_limit_bytes=mib * MIB)


def hbm_call(kernel, *, out_shape, loose=(), **options):
    single = not isinstance(out_shape, (list, tuple))
    shapes = [out_shape] if single else out_shape
    placed = [pltpu.HBM(x.shape, x.dtype) if x.size * x.dtype.itemsize > 256 * 1024 else x for x in shapes]
    call = pl.pallas_call(kernel, out_shape=placed[0] if single else placed, **options)

    def run(*args):
        held = [x if i in loose else pltpu.with_memory_space_constraint(x, pltpu.HBM) for i, x in enumerate(args)]
        return call(*held)

    return run


def cost(flops, moved):
    return pl.CostEstimate(flops=int(flops), bytes_accessed=int(moved), transcendentals=0)


def block_width(channels, most):
    width = min(channels, most)
    while channels % width:
        width //= 2
    return width


def extend(ext, rim, rows_of, at):
    ext[0:RIM, :] = rim[:, at].astype(F32)
    ext[RIM:, :] = rows_of.astype(F32)


def features_kernel(short_taps, tokens, rims, filters, query_ref, key_ref, value_ref, mixer_ref, ext):
    rows, width = tokens[0].shape

    def filtered(part, block, at):
        own = ext.at[(3 * block + part) % ext.shape[0]]
        extend(own, rims[part], tokens[part][:, at], at)
        taps = filters[part][:, at]
        total = taps[0:1] * own[RIM : RIM + rows, :]
        for tap in range(1, short_taps):
            total = total + taps[tap : tap + 1] * own[RIM - tap : RIM - tap + rows, :]
        return total

    for block in range(width // LANES):
        at = pl.ds(block * LANES, LANES)
        query_ref[:, at] = filtered(0, block, at).astype(BF16)
        key, value = filtered(1, block, at), filtered(2, block, at)
        key_ref[:, at] = key.astype(BF16)
        value_ref[:, at] = value.astype(BF16)
        mixer_ref[:, at] = (key * value).astype(BF16)


def features_call(tokens, rim, filters):
    rows, wide = tokens.shape
    channels = wide // 3
    taps = filters.shape[0]
    width = block_width(channels, WIDTH)
    steps = channels // width

    def spec(height, part):
        return pl.BlockSpec((height, width), lambda i, part=part: (0, i + part * steps))

    def body(*refs):
        features_kernel(taps, refs[0:3], refs[3:6], refs[6:9], *refs[9:])

    out = jax.ShapeDtypeStruct((rows, channels), BF16)
    return hbm_call(
        body,
        loose=(3, 4, 5),
        grid=(steps,),
        in_specs=[spec(rows, p) for p in range(3)]
        + [spec(RIM, p) for p in range(3)]
        + [spec(taps, p) for p in range(3)],
        out_specs=[pl.BlockSpec((rows, width), lambda i: (0, i))] * 4,
        out_shape=[out] * 4,
        scratch_shapes=[pltpu.VMEM((6, RIM + rows, LANES), F32)],
        compiler_params=params(),
        cost_estimate=cost(0, rows * wide),
        name="features",
    )(tokens, tokens, tokens, rim, rim, rim, filters, filters, filters)


def lane_row(shape):
    row = lax.broadcasted_iota(jnp.int32, shape, 0)
    lane = lax.broadcasted_iota(jnp.int32, shape, 1)
    return row, lane


def mirror(size):
    row, lane = lane_row((size, size))
    both = row + lane
    return jnp.where((both == 0) | (both == size), 1.0, 0.0)


def circulant(line, taps):
    wide = jnp.broadcast_to(line.astype(F32), (taps, taps))
    return pltpu.roll(wide, 0, 1, stride=1, stride_axis=0)


def pick_groups(product, rows, per_group):
    lane = lax.broadcasted_iota(jnp.int32, (rows, LANES), 1)
    total = product[0:rows]
    for g in range(1, LANES // per_group):
        total = jnp.where(lane >= g * per_group, product[g * rows : (g + 1) * rows], total)
    return total


def mix_kernel(per_group, lines_ref, prev_ref, cur_ref, query_ref, mixed_ref, gated_ref, table, lines):
    rows, width = cur_ref.shape
    row, lane = lane_row((rows, rows))
    above = lane > row
    packed = LANES // per_group
    lines[...] = jnp.dot(lines_ref[...].astype(BF16), mirror(rows).astype(BF16), preferred_element_type=F32)
    for block in range(width // LANES):
        at = pl.ds(block * LANES, LANES)
        own = table.at[block % 2]
        for g in range(packed):
            ring = circulant(lines[block * packed + g : block * packed + g + 1, :], rows)
            own[g * rows : (g + 1) * rows, 0:rows] = jnp.where(above, ring, 0.0).astype(BF16)
            own[g * rows : (g + 1) * rows, rows : 2 * rows] = jnp.where(above, 0.0, ring).astype(BF16)
        window = jnp.concatenate([prev_ref[:, at], cur_ref[:, at]], axis=0)
        product = jnp.dot(own[...], window, preferred_element_type=F32)
        mixed = pick_groups(product, rows, per_group)
        mixed_ref[:, at] = mixed.astype(BF16)
        gated_ref[:, at] = (query_ref[:, at].astype(F32) * mixed).astype(BF16)


def mix_call(lines, prev, cur, query):
    rows, channels = cur.shape
    groups, taps = lines.shape
    per_group = channels // groups
    width = block_width(channels, WIDTH)
    steps = channels // width
    wide = pl.BlockSpec((rows, width), lambda i: (0, i))
    out = jax.ShapeDtypeStruct((rows, channels), BF16)
    return hbm_call(
        functools.partial(mix_kernel, per_group),
        loose=(0, 1),
        grid=(steps,),
        in_specs=[pl.BlockSpec((width // per_group, taps), lambda i: (i, 0)), wide, wide, wide],
        out_specs=[wide, wide],
        out_shape=[out, out],
        scratch_shapes=[
            pltpu.VMEM((2, LANES // per_group * rows, 2 * rows), BF16),
            pltpu.VMEM((width // per_group, taps), F32),
        ],
        compiler_params=params(),
        cost_estimate=cost(0, 2 * rows * channels),
        name="mix",
    )(lines, prev, cur, query)


def gate_kernel(place, gate_grad_ref, query_ref, mixed_ref, grad_ref, feature_ref):
    width = query_ref.shape[1] // place.shape[0]
    for i in range(place.shape[0]):
        at = pl.ds(i * width, width)
        gate_grad = gate_grad_ref[:, pl.ds(pl.multiple_of(place[i] * width, width), width)].astype(F32)
        grad_ref[:, at] = (gate_grad * query_ref[:, at].astype(F32)).astype(BF16)
        feature_ref[:, at] = (gate_grad * mixed_ref[:, at].astype(F32)).astype(BF16)


def gate_call(place, gate_grad, query, mixed):
    rows, channels = query.shape
    out = jax.ShapeDtypeStruct((rows, channels), BF16)
    return hbm_call(
        gate_kernel,
        loose=(0,),
        grid_spec=pltpu.PrefetchScalarGridSpec(
            num_scalar_prefetch=1,
            grid=(2,),
            in_specs=[pl.BlockSpec((rows // 2, channels), lambda i, place: (i, 0))] * 3,
            out_specs=[pl.BlockSpec((rows // 2, channels), lambda i, place: (i, 0))] * 2,
        ),
        out_shape=[out, out],
        compiler_params=params(),
        cost_estimate=cost(2 * rows * channels, 10 * rows * channels),
        name="gate_back",
    )(place, gate_grad, query, mixed)


def tap_sums(short_taps, grad, tokens_ref, rim_ref, out_ref, at, ext):
    rows = tokens_ref.shape[0]
    extend(ext, rim_ref, tokens_ref[:, at], at)
    grad = grad.astype(F32)
    for tap in range(short_taps):
        out_ref[tap : tap + 1, at] = jnp.sum(grad * ext[RIM - tap : RIM - tap + rows, :], axis=0, keepdims=True)
    out_ref[short_taps:8, at] = jnp.zeros((8 - short_taps, LANES), F32)


def long_grad_kernel(
    per_group, short_taps, prev_ref, cur_ref, grad_ref, feature_ref, tokens_ref, rim_ref, long_ref, short_ref, fold, masked, ext
):
    rows, width = cur_ref.shape
    row, lane = lane_row((rows, rows))
    above = lane > row
    member = lax.broadcasted_iota(jnp.int32, (rows, LANES), 1)
    packed = LANES // per_group
    sums = []
    for block in range(width // LANES):
        at = pl.ds(block * LANES, LANES)
        window = jnp.concatenate([prev_ref[:, at], cur_ref[:, at]], axis=0)
        grad_wide = grad_ref[:, at].astype(F32)
        own = masked.at[block % 2]
        for g in range(packed):
            own[g * rows : (g + 1) * rows, :] = jnp.where((member >= g * per_group) & (member < (g + 1) * per_group), grad_wide, 0.0).astype(BF16)
        pairs = lax.dot_general(own[...], window, (((1,), (1,)), ((), ())), preferred_element_type=F32)
        for g in range(packed):
            pair = pairs[g * rows : (g + 1) * rows]
            ring = jnp.where(above, pair[:, 0:rows], pair[:, rows : 2 * rows])
            total = ring[0:8]
            for tile in range(1, rows // 8):
                total = total + pltpu.roll(ring[8 * tile : 8 * tile + 8], rows - 8 * tile, 1)
            fold[block % 2, g * 8 : (g + 1) * 8, :] = total
        total = fold[block % 2, pl.ds(0, packed, stride=8), :]
        for step in range(1, 8):
            total = total + pltpu.roll(fold[block % 2, pl.ds(step, packed, stride=8), :], rows - step, 1)
        sums.append(total)
        tap_sums(short_taps, feature_ref[:, at], tokens_ref, rim_ref, short_ref, at, ext.at[block % 2])
    long_ref[...] = jnp.dot(
        jnp.concatenate(sums, axis=0), mirror(rows), precision=lax.Precision.HIGHEST, preferred_element_type=F32
    )


def long_grad_call(groups, short_taps, prev, cur, grad, feature, tokens, rim):
    rows, channels = cur.shape
    per_group = channels // groups
    width = block_width(channels, WIDTH)
    steps = channels // width
    wide = pl.BlockSpec((rows, width), lambda i: (0, i))
    packed = LANES // per_group
    return hbm_call(
        functools.partial(long_grad_kernel, per_group, short_taps),
        grid=(steps,),
        in_specs=[wide] * 5 + [pl.BlockSpec((RIM, width), lambda i: (0, i))],
        out_specs=[
            pl.BlockSpec((width // per_group, rows), lambda i: (i, 0)),
            pl.BlockSpec((8, width), lambda i: (0, i)),
        ],
        out_shape=[
            jax.ShapeDtypeStruct((groups, rows), F32),
            jax.ShapeDtypeStruct((8, channels), F32),
        ],
        scratch_shapes=[
            pltpu.VMEM((2, packed * 8, LANES), F32),
            pltpu.VMEM((2, packed * rows, LANES), BF16),
            pltpu.VMEM((2, RIM + rows, LANES), F32),
        ],
        compiler_params=params(),
        cost_estimate=cost(2 * groups * rows * 2 * rows * LANES, 10 * rows * channels),
        name="long_grad",
    )(prev, cur, grad, feature, tokens, rim)


def unmix_kernel(
    per_group, short_taps, lines_ref, grad_ref, next_ref, key_ref, value_ref, key_tokens_ref, value_tokens_ref,
    key_rim_ref, value_rim_ref, feature_ref, key_sum_ref, value_sum_ref, table, ext,
):
    rows, width = grad_ref.shape
    row, lane = lane_row((rows, rows))
    below = lane < row
    packed = LANES // per_group
    for block in range(width // LANES):
        at = pl.ds(block * LANES, LANES)
        own = table.at[block % 2]
        for g in range(packed):
            ring = circulant(lines_ref[block * packed + g : block * packed + g + 1, :], rows)
            own[g * rows : (g + 1) * rows, 0:rows] = jnp.where(below, 0.0, ring).astype(BF16)
            own[g * rows : (g + 1) * rows, rows : 2 * rows] = jnp.where(below, ring, 0.0).astype(BF16)
        window = jnp.concatenate([grad_ref[:, at], next_ref[:, at]], axis=0)
        product = jnp.dot(own[...], window, preferred_element_type=F32)
        grad_mixer = pick_groups(product, rows, per_group)
        key_grad = (grad_mixer * value_ref[:, at].astype(F32)).astype(BF16)
        value_grad = (grad_mixer * key_ref[:, at].astype(F32)).astype(BF16)
        feature_ref[0, :, at] = key_grad
        feature_ref[1, :, at] = value_grad
        slot = 2 * (block % 2)
        tap_sums(short_taps, key_grad, key_tokens_ref, key_rim_ref, key_sum_ref, at, ext.at[slot])
        tap_sums(short_taps, value_grad, value_tokens_ref, value_rim_ref, value_sum_ref, at, ext.at[slot + 1])


def unmix_call(lines, short_taps, grad, grad_next, key, value, tokens, rim):
    rows, channels = grad.shape
    groups, taps = lines.shape
    per_group = channels // groups
    width = block_width(channels, WIDTH)
    steps = channels // width

    def spec(height, part):
        return pl.BlockSpec((height, width), lambda i, part=part: (0, i + part * steps))

    wide = spec(rows, 0)
    packed = LANES // per_group
    sums = jax.ShapeDtypeStruct((8, channels), F32)
    return hbm_call(
        functools.partial(unmix_kernel, per_group, short_taps),
        loose=(0, 2),
        grid=(steps,),
        in_specs=[pl.BlockSpec((width // per_group, taps), lambda i: (i, 0))]
        + [wide] * 4
        + [spec(rows, 1), spec(rows, 2), spec(RIM, 1), spec(RIM, 2)],
        out_specs=[pl.BlockSpec((2, rows, width), lambda i: (0, 0, i)), spec(8, 0), spec(8, 0)],
        out_shape=[jax.ShapeDtypeStruct((2, rows, channels), BF16), sums, sums],
        scratch_shapes=[pltpu.VMEM((2, packed * rows, 2 * rows), BF16), pltpu.VMEM((4, RIM + rows, LANES), F32)],
        compiler_params=params(),
        cost_estimate=cost(2 * groups * rows * 2 * rows * LANES, 16 * rows * channels),
        name="unmix",
    )(lines, grad, grad_next, key, value, tokens, tokens, rim, rim)


def short_adjoint_kernel(short_taps, grads_ref, rim_ref, filter_ref, *refs):
    out_ref, ext = refs[-2:]
    rows, width = out_ref.shape
    for block in range(width // LANES):
        at = pl.ds(block * LANES, LANES)
        own = ext.at[block % 2]
        own[0:rows, :] = grads_ref[0, :, at].astype(F32)
        own[rows:, :] = rim_ref[0, :, at].astype(F32)
        taps = filter_ref[:, at]
        total = taps[0:1] * own[0:rows, :]
        for tap in range(1, short_taps):
            total = total + taps[tap : tap + 1] * own[tap : tap + rows, :]
        out_ref[:, at] = total.astype(BF16)


def short_adjoint_call(grads, rim, filters, first, out):
    parts, rows, channels = grads.shape
    short_taps = filters.shape[0]
    width = block_width(channels, 2 * WIDTH)
    steps = channels // width
    result = pl.BlockSpec((rows, width), lambda p, i: (0, (p + first) * steps + i))
    given = [] if out is None else [out]
    return hbm_call(
        functools.partial(short_adjoint_kernel, short_taps),
        loose=(1,),
        grid=(parts, steps),
        in_specs=[
            pl.BlockSpec((1, rows, width), lambda p, i: (p, 0, i)),
            pl.BlockSpec((1, RIM, width), lambda p, i: (p + first, 0, i)),
            pl.BlockSpec((short_taps, width), lambda p, i: (0, (p + first) * steps + i)),
        ]
        + [pl.BlockSpec(memory_space=pl.ANY)] * len(given),
        out_specs=result,
        out_shape=jax.ShapeDtypeStruct((rows, 3 * channels), BF16),
        input_output_aliases={3: 0} if given else {},
        scratch_shapes=[pltpu.VMEM((2, rows + RIM, LANES), F32)],
        compiler_params=params(),
        cost_estimate=cost(2 * parts * short_taps * rows * channels, 4 * parts * rows * channels),
        name="short_adjoint",
    )(grads, rim, filters, *given)


def spread_kernel(place, query_ref, key_ref, value_ref, long_ref, own_ref, other_ref):
    steps = query_ref.shape[1] // LANES
    half = own_ref.shape[0]
    tiles = [ref[:, i * LANES : (i + 1) * LANES] for ref in (query_ref, key_ref, value_ref) for i in range(steps)]
    tiles += [long_ref[8 * i : 8 * i + 8, :] for i in range(long_ref.shape[0] // 8)]
    first = place[0] < half

    @pl.when(first)
    def _():
        for i in range(half):
            own_ref[place[i]] = tiles[i]
            other_ref[place[half + i] - half] = tiles[half + i]

    @pl.when(jnp.logical_not(first))
    def _():
        for i in range(half):
            other_ref[place[i] - half] = tiles[i]
            own_ref[place[half + i]] = tiles[half + i]


def collect_kernel(place, *refs):
    parts, short_ref, long_ref, tiles_ref = refs[:-3], refs[-3], refs[-2], refs[-1]
    short_taps, wide = short_ref.shape
    steps = wide // LANES
    size = parts[0].shape[0]
    for i, part in enumerate(parts):
        tiles_ref[i * size : (i + 1) * size] = part[...]
    for i in range(steps):
        short_ref[:, i * LANES : (i + 1) * LANES] = tiles_ref[place[i]][0:short_taps, :]
    for i in range(long_ref.shape[0] // 8):
        long_ref[8 * i : 8 * i + 8, :] = tiles_ref[place[steps + i]]


def in_vmem():
    return pl.BlockSpec(memory_space=pltpu.VMEM)


def total_over_devices(spread_to, collect_from, query_sum, key_sum, value_sum, long_sum, short_taps, beside):
    ny, nz = lax.axis_size("y"), lax.axis_size("z")
    channels = query_sum.shape[1]
    count = 3 * channels // LANES + long_sum.shape[0] // 8
    half = jax.ShapeDtypeStruct((count // 2, 8, LANES), F32)
    own, other = pl.pallas_call(
        spread_kernel,
        in_specs=[pl.BlockSpec(memory_space=pltpu.SMEM)] + [in_vmem()] * 4,
        out_specs=[in_vmem()] * 2,
        out_shape=[half] * 2,
        compiler_params=params(),
        name="spread",
    )(spread_to, query_sum, key_sum, value_sum, long_sum)
    part = own + move(other, c=1)
    size = count // 2 // nz
    part = sum([move(part[d * size : (d + 1) * size], z=d) for d in range(1, nz)], part[:size])
    terms, beside = lax.optimization_barrier(([part] + [move(part, y=d) for d in range(1, ny)], beside))
    whole = paired_sum(terms)
    whole = paired_sum([move(whole, xl=a, xh=b) for a, b in FLIPS])
    line = jnp.concatenate([whole, move(whole, c=1)], axis=0)
    lines = [move(line, z=-d) for d in range(nz)]
    groups, taps = long_sum.shape
    short, long = pl.pallas_call(
        collect_kernel,
        in_specs=[pl.BlockSpec(memory_space=pltpu.SMEM)] + [in_vmem()] * nz,
        out_specs=[in_vmem(), in_vmem()],
        scratch_shapes=[pltpu.VMEM((count, 8, LANES), F32)],
        out_shape=[
            jax.ShapeDtypeStruct((short_taps, 3 * channels), F32),
            jax.ShapeDtypeStruct((groups, taps), F32),
        ],
        compiler_params=params(),
        name="collect",
    )(collect_from, *lines)
    return short, long, beside


def paired_sum(terms):
    half = len(terms) // 2
    if half == 0:
        return terms[0]
    return paired_sum([terms[i] + terms[i + half] for i in range(half)])


def gather_near(shard):
    ny = lax.axis_size("y")
    half = shard.shape[0] // 2
    top, bottom = shard[:half], shard[half:]
    return [move(top, xl=a, xh=b) for a, b in FLIPS], [move(bottom, y=d) for d in range(ny)]


def gather_far(wide_top, tall_bottom):
    ny = lax.axis_size("y")
    wide_top, tall_bottom = jnp.stack(wide_top), jnp.stack(tall_bottom)
    return (
        [move(wide_top, y=d) for d in range(ny)],
        [move(tall_bottom, xl=a, xh=b) for a, b in FLIPS],
    )


def piece_rows(tops, bottoms, step):
    rows = []
    for a in range(2):
        rows.append(jnp.concatenate([tops[step][2 * a + b] for b in range(2)], axis=1))
        rows.append(jnp.concatenate([bottoms[2 * a + b][step] for b in range(2)], axis=1))
    return rows


def gate_matmul_kernel(ny, *refs):
    cotangent_ref, tops, bottoms, out_ref = refs[0], refs[1 : 1 + ny], refs[1 + ny : 5 + ny], refs[5 + ny]
    left = cotangent_ref[...]
    at = 0
    for step in range(ny):
        for right in piece_rows(tops, bottoms, step):
            size = right.shape[0]
            out_ref[:, at : at + size] = lax.dot_general(
                left, right, (((1,), (1,)), ((), ())), preferred_element_type=F32
            ).astype(BF16)
            at += size


def whole(x):
    return pl.BlockSpec(x.shape, lambda *_, n=x.ndim: (0,) * n)


def gate_matmul(cotangents, tops, bottoms):
    rows, depth = cotangents.shape
    ny = len(tops)
    channels = 4 * ny * tops[0].shape[1]
    height = rows // 2
    return hbm_call(
        functools.partial(gate_matmul_kernel, ny),
        loose=range(5 + ny),
        grid=(rows // height,),
        in_specs=[pl.BlockSpec((height, depth), lambda i: (i, 0))] + [whole(x) for x in (*tops, *bottoms)],
        out_specs=pl.BlockSpec((height, channels), lambda i: (i, 0)),
        out_shape=jax.ShapeDtypeStruct((rows, channels), BF16),
        compiler_params=params(32),
        cost_estimate=cost(2 * rows * depth * channels, 2 * (rows + depth) * channels),
        name="gate_matmul",
    )(cotangents, *tops, *bottoms)


def picked(origin, step, rows_ref):
    height = rows_ref.shape[1] // 2
    at = [pl.multiple_of(origin[2 * step + a] % 2 * height, height) for a in range(2)]
    return jnp.concatenate([rows_ref[:, pl.ds(x, height)] for x in at], axis=1)


def weight_grad_kernel(ny, origin, rows_ref, turned_ref, *refs):
    top_grads, bottom_grads = refs[:ny], refs[ny:]
    step = pl.program_id(0)
    size = bottom_grads[0].shape[2]
    width = bottom_grads[0].shape[1]
    rows = picked(origin, step, rows_ref)
    grads = jnp.dot(turned_ref[...], rows, preferred_element_type=F32).astype(BF16)
    for f in range(4):
        a, b = f // 2, f % 2
        at = (2 * a + 1) * size
        bottom_grads[f][step] = grads[b * width : (b + 1) * width, at : at + size]
    for d in range(ny):

        @pl.when(step == d)
        def _(d=d):
            for f in range(4):
                a, b = f // 2, f % 2
                at = 2 * a * size
                top_grads[d][f] = grads[b * width : (b + 1) * width, at : at + size]


def rows_of(origin, all_rows, ny):
    rows, channels = all_rows.shape
    return pl.BlockSpec((rows, channels // ny), lambda i, origin: (0, origin[2 * i] // 2))


def weight_grad(origin, all_rows, turned, ny):
    rows, channels = all_rows.shape
    size = channels // (4 * ny)
    width = turned.shape[0] // 2
    outs = [jax.ShapeDtypeStruct((4, width, size), BF16)] * ny + [jax.ShapeDtypeStruct((ny, width, size), BF16)] * 4
    results = hbm_call(
        functools.partial(weight_grad_kernel, ny),
        loose=(0, 2),
        grid_spec=pltpu.PrefetchScalarGridSpec(
            num_scalar_prefetch=1,
            grid=(ny,),
            in_specs=[rows_of(origin, all_rows, ny), whole(turned)],
            out_specs=[whole(x) for x in outs],
        ),
        out_shape=outs,
        compiler_params=params(40),
        cost_estimate=cost(4 * rows * width * channels, 2 * (rows + 2 * width) * channels),
        name="weight_grad",
    )(origin, all_rows, turned)
    return results[:ny], results[ny:]


def output_kernel(ny, origin, rows_ref, *refs):
    tops, bottoms, own_ref, other_ref, total = refs[:ny], refs[ny : ny + 4], refs[-3], refs[-2], refs[-1]
    step = pl.program_id(0)
    width = own_ref.shape[1]
    rows = picked(origin, step, rows_ref)
    for d in range(ny):

        @pl.when(step == d)
        def _(d=d):
            right = jnp.concatenate(piece_rows(tops, bottoms, d), axis=0)
            product = jnp.dot(rows, right, preferred_element_type=F32)
            if d == 0:
                total[...] = product
            else:
                total[...] += product

    @pl.when(step == ny - 1)
    def _():
        own_ref[...] = total[:, :width].astype(BF16)
        other_ref[...] = total[:, width:].astype(BF16)


def output_call(origin, all_rows, tops, bottoms):
    rows, channels = all_rows.shape
    ny = len(tops)
    width = tops[0].shape[2]
    half = jax.ShapeDtypeStruct((rows, width), BF16)
    return hbm_call(
        functools.partial(output_kernel, ny),
        loose=(0, *range(2, 6 + ny)),
        grid_spec=pltpu.PrefetchScalarGridSpec(
            num_scalar_prefetch=1,
            grid=(ny,),
            in_specs=[rows_of(origin, all_rows, ny)] + [whole(x) for x in (*tops, *bottoms)],
            out_specs=[whole(half)] * 2,
            scratch_shapes=[pltpu.VMEM((rows, 2 * width), F32)],
        ),
        out_shape=[half, half],
        compiler_params=params(32),
        cost_estimate=cost(4 * rows * width * channels, 2 * (rows + 2 * width) * channels),
        name="output",
    )(origin, all_rows, *tops, *bottoms)


def plane_scatter_sum(top_grads, bottom_grads):
    ny = len(top_grads)

    def added(terms):
        total = terms[0].astype(F32)
        for term in terms[1:]:
            total = total + term.astype(F32)
        return total

    top = added([move(top_grads[d], y=-d) for d in range(ny)]).astype(BF16)
    bottom = added([move(bottom_grads[f], xl=a, xh=b) for f, (a, b) in enumerate(FLIPS)]).astype(BF16)
    top = added([move(top[f], xl=a, xh=b) for f, (a, b) in enumerate(FLIPS)])
    bottom = added([move(bottom[d], y=-d) for d in range(ny)])
    return jnp.concatenate([top, bottom], axis=1).T


def shards(tokens_in, short_filter, long_filter, out_weight, cotangent):
    ny, nz = lax.axis_size("y"), lax.axis_size("z")
    y, xl, xh, z, c = (lax.axis_index(a) for a in ("y", "xl", "xh", "z", "c"))
    tokens = tokens_in[0]
    rows, wide = tokens.shape
    channels = wide // 3
    short_taps = short_filter.shape[0]
    groups = long_filter.shape[0]
    upstream = cotangent[0]
    length, columns = upstream.shape
    span = length // 2

    block = jnp.arange(2 * ny, dtype=jnp.int32)
    place = ((y - block // 2) % ny) * 2 + (block + xl) % 2
    origin = place
    size = 3 * channels // LANES + groups // 8
    each = size // (2 * nz)
    tile = jnp.arange(size, dtype=jnp.int32)
    core_step, z_step = (tile // (nz * each) + c) % 2, (tile // each - z) % nz
    spread_to = (core_step * nz + z_step) * each + tile % each
    collect_from = (z_step * 2 + core_step) * each + tile % each

    rim = along(tokens[rows - RIM :], 1)
    lines = long_filter.astype(F32)
    query, key, value, mixer = features_call(tokens, rim, short_filter)
    mixer, out_weight = lax.optimization_barrier((mixer, out_weight))
    mixer_prev = along(mixer, 1)
    wide_top, tall_bottom = gather_near(out_weight)
    mixer_prev, wide_top, tall_bottom = lax.optimization_barrier((mixer_prev, wide_top, tall_bottom))
    mixed, gated = mix_call(lines, mixer_prev, mixer, query)
    mixed, wide_top, tall_bottom, upstream = lax.optimization_barrier((mixed, wide_top, tall_bottom, upstream))
    all_rows = lax.all_gather(gated, ("z", "c"), axis=0, tiled=True)
    tops, bottoms = gather_far(wide_top, tall_bottom)
    mine = lax.dynamic_slice_in_dim(upstream, xh * span, span, 0)
    others = move(lax.dynamic_slice_in_dim(upstream, (1 - xh) * span, span, 0), xh=1)
    cotangents = jnp.concatenate([mine, others], axis=1)
    partial = gate_matmul(cotangents, tops, bottoms)
    partial, all_rows = lax.optimization_barrier((partial, all_rows))
    gate_grad = lax.psum_scatter(partial, ("z", "c"), scatter_dimension=0, tiled=True)

    top_grads, bottom_grads = weight_grad(origin, all_rows, cotangents.T, ny)
    own, other = output_call(origin, all_rows, tops, bottoms)
    grad_weight = plane_scatter_sum(top_grads, bottom_grads)
    theirs = move(other, xh=1)
    output = jnp.where(xh == 0, jnp.concatenate([own, theirs], axis=0), jnp.concatenate([theirs, own], axis=0))
    gate_grad, grad_weight, output = lax.optimization_barrier((gate_grad, grad_weight, output))

    grad_mixed, query_grad = gate_call(place, gate_grad, query, mixed)
    grad_next = along(grad_mixed, -1)
    long_sum, query_sum = long_grad_call(
        groups, short_taps, mixer_prev, mixer, grad_mixed, query_grad, tokens, rim
    )
    other_grads, key_sum, value_sum = unmix_call(
        lines, short_taps, grad_mixed, grad_next, key, value, tokens, rim
    )
    edge = along(jnp.concatenate([query_grad[None, :RIM], other_grads[:, :RIM]], axis=0), -1)
    grad_tokens = short_adjoint_call(query_grad[None], edge, short_filter, 0, None)
    grad_short, grad_long, grad_tokens = total_over_devices(
        spread_to, collect_from, query_sum, key_sum, value_sum, long_sum, short_taps, grad_tokens
    )
    grad_tokens = short_adjoint_call(other_grads, edge, short_filter, 1, grad_tokens)
    return output[None], grad_tokens[None], grad_short, grad_long, grad_weight


def solution(mesh):
    dp, seq = mesh.shape["dp"], mesh.shape["seq"]
    grid = jax.sharding.Mesh(mesh.devices.reshape(dp // 2, 2, 2, seq // 4, 2), ("y", "xl", "xh", "z", "c"))
    rows, line = ("y", "xl"), ("xh", "z", "c")
    return jax.shard_map(
        shards,
        mesh=grid,
        in_specs=(P(rows, line, None), P(), P(), P(rows, line), P(rows, None, line)),
        out_specs=(P(rows, None, line), P(rows, line, None), P(), P(), P(rows, line)),
        check_vma=False,
    )
```

```python
import functools
import itertools
import math

import jax
import jax.numpy as jnp
from jax import lax
from jax.experimental import pallas as pl
from jax.experimental.pallas import tpu as pltpu
from jax.sharding import PartitionSpec as P

LANES = 128
RIM = 8
MIB = 1024 * 1024
WIDTH = 1024
F32 = jnp.float32
BF16 = jnp.bfloat16


PLANE = ("y", "xl", "xh")
LINE = ("xh", "z", "c")


def along(x, by):
    size = math.prod(lax.axis_size(a) for a in LINE)
    pairs = [(i, i + by) for i in range(size) if 0 <= i + by < size]
    return lax.ppermute(x, LINE, pairs)


def move(x, **steps):
    axes = tuple(a for a in ("y", "xl", "xh", "z", "c") if steps.get(a, 0) % lax.axis_size(a))
    if not axes:
        return x
    sizes = [lax.axis_size(a) for a in axes]
    pairs = []
    for at in itertools.product(*(range(n) for n in sizes)):
        to = [(p + steps[a]) % n for p, a, n in zip(at, axes, sizes)]
        pairs.append((flat(at, sizes), flat(to, sizes)))
    return lax.ppermute(x, axes, pairs)


def flat(at, sizes):
    index = 0
    for p, n in zip(at, sizes):
        index = index * n + p
    return index


FLIPS = [(0, 0), (0, 1), (1, 0), (1, 1)]


def params(mib=16):
    return pltpu.CompilerParams(vmem_limit_bytes=mib * MIB)


def hbm_call(kernel, *, out_shape, loose=(), **options):
    single = not isinstance(out_shape, (list, tuple))
    shapes = [out_shape] if single else out_shape
    placed = [pltpu.HBM(x.shape, x.dtype) if x.size * x.dtype.itemsize > 256 * 1024 else x for x in shapes]
    call = pl.pallas_call(kernel, out_shape=placed[0] if single else placed, **options)

    def run(*args):
        held = [x if i in loose else pltpu.with_memory_space_constraint(x, pltpu.HBM) for i, x in enumerate(args)]
        return call(*held)

    return run


def cost(flops, moved):
    return pl.CostEstimate(flops=int(flops), bytes_accessed=int(moved), transcendentals=0)


def block_width(channels, most):
    width = min(channels, most)
    while channels % width:
        width //= 2
    return width


def extend(ext, rim, rows_of, at):
    ext[0:RIM, :] = rim[:, at].astype(F32)
    ext[RIM:, :] = rows_of.astype(F32)


def features_kernel(short_taps, tokens, rims, filters, query_ref, key_ref, value_ref, mixer_ref, ext):
    rows, width = tokens[0].shape

    def filtered(part, block, at):
        own = ext.at[(3 * block + part) % ext.shape[0]]
        extend(own, rims[part], tokens[part][:, at], at)
        taps = filters[part][:, at]
        total = taps[0:1] * own[RIM : RIM + rows, :]
        for tap in range(1, short_taps):
            total = total + taps[tap : tap + 1] * own[RIM - tap : RIM - tap + rows, :]
        return total

    for block in range(width // LANES):
        at = pl.ds(block * LANES, LANES)
        query_ref[:, at] = filtered(0, block, at).astype(BF16)
        key, value = filtered(1, block, at), filtered(2, block, at)
        key_ref[:, at] = key.astype(BF16)
        value_ref[:, at] = value.astype(BF16)
        mixer_ref[:, at] = (key * value).astype(BF16)


def features_call(tokens, rim, filters):
    rows, wide = tokens.shape
    channels = wide // 3
    taps = filters.shape[0]
    width = block_width(channels, WIDTH)
    steps = channels // width

    def spec(height, part):
        return pl.BlockSpec((height, width), lambda i, part=part: (0, i + part * steps))

    def body(*refs):
        features_kernel(taps, refs[0:3], refs[3:6], refs[6:9], *refs[9:])

    out = jax.ShapeDtypeStruct((rows, channels), BF16)
    return hbm_call(
        body,
        loose=(3, 4, 5),
        grid=(steps,),
        in_specs=[spec(rows, p) for p in range(3)]
        + [spec(RIM, p) for p in range(3)]
        + [spec(taps, p) for p in range(3)],
        out_specs=[pl.BlockSpec((rows, width), lambda i: (0, i))] * 4,
        out_shape=[out] * 4,
        scratch_shapes=[pltpu.VMEM((6, RIM + rows, LANES), F32)],
        compiler_params=params(),
        cost_estimate=cost(0, rows * wide),
        name="features",
    )(tokens, tokens, tokens, rim, rim, rim, filters, filters, filters)


def lane_row(shape):
    row = lax.broadcasted_iota(jnp.int32, shape, 0)
    lane = lax.broadcasted_iota(jnp.int32, shape, 1)
    return row, lane


def mirror(size):
    row, lane = lane_row((size, size))
    both = row + lane
    return jnp.where((both == 0) | (both == size), 1.0, 0.0)


def circulant(line, taps):
    wide = jnp.broadcast_to(line.astype(F32), (taps, taps))
    return pltpu.roll(wide, 0, 1, stride=1, stride_axis=0)


def pick_groups(product, rows, per_group):
    lane = lax.broadcasted_iota(jnp.int32, (rows, LANES), 1)
    total = product[0:rows]
    for g in range(1, LANES // per_group):
        total = jnp.where(lane >= g * per_group, product[g * rows : (g + 1) * rows], total)
    return total


def mix_kernel(per_group, lines_ref, prev_ref, cur_ref, query_ref, mixed_ref, gated_ref, table, lines):
    rows, width = cur_ref.shape
    row, lane = lane_row((rows, rows))
    above = lane > row
    packed = LANES // per_group
    lines[...] = jnp.dot(lines_ref[...].astype(BF16), mirror(rows).astype(BF16), preferred_element_type=F32)
    for block in range(width // LANES):
        at = pl.ds(block * LANES, LANES)
        own = table.at[block % 2]
        for g in range(packed):
            ring = circulant(lines[block * packed + g : block * packed + g + 1, :], rows)
            own[g * rows : (g + 1) * rows, 0:rows] = jnp.where(above, ring, 0.0).astype(BF16)
            own[g * rows : (g + 1) * rows, rows : 2 * rows] = jnp.where(above, 0.0, ring).astype(BF16)
        window = jnp.concatenate([prev_ref[:, at], cur_ref[:, at]], axis=0)
        product = jnp.dot(own[...], window, preferred_element_type=F32)
        mixed = pick_groups(product, rows, per_group)
        mixed_ref[:, at] = mixed.astype(BF16)
        gated_ref[:, at] = (query_ref[:, at].astype(F32) * mixed).astype(BF16)


def mix_call(lines, prev, cur, query):
    rows, channels = cur.shape
    groups, taps = lines.shape
    per_group = channels // groups
    width = block_width(channels, WIDTH)
    steps = channels // width
    wide = pl.BlockSpec((rows, width), lambda i: (0, i))
    out = jax.ShapeDtypeStruct((rows, channels), BF16)
    return hbm_call(
        functools.partial(mix_kernel, per_group),
        loose=(0, 1),
        grid=(steps,),
        in_specs=[pl.BlockSpec((width // per_group, taps), lambda i: (i, 0)), wide, wide, wide],
        out_specs=[wide, wide],
        out_shape=[out, out],
        scratch_shapes=[
            pltpu.VMEM((2, LANES // per_group * rows, 2 * rows), BF16),
            pltpu.VMEM((width // per_group, taps), F32),
        ],
        compiler_params=params(),
        cost_estimate=cost(0, 2 * rows * channels),
        name="mix",
    )(lines, prev, cur, query)


def gate_kernel(place, gate_grad_ref, query_ref, mixed_ref, grad_ref, feature_ref):
    width = query_ref.shape[1] // place.shape[0]
    for i in range(place.shape[0]):
        at = pl.ds(i * width, width)
        gate_grad = gate_grad_ref[:, pl.ds(pl.multiple_of(place[i] * width, width), width)].astype(F32)
        grad_ref[:, at] = (gate_grad * query_ref[:, at].astype(F32)).astype(BF16)
        feature_ref[:, at] = (gate_grad * mixed_ref[:, at].astype(F32)).astype(BF16)


def gate_call(place, gate_grad, query, mixed):
    rows, channels = query.shape
    out = jax.ShapeDtypeStruct((rows, channels), BF16)
    return hbm_call(
        gate_kernel,
        loose=(0,),
        grid_spec=pltpu.PrefetchScalarGridSpec(
            num_scalar_prefetch=1,
            grid=(2,),
            in_specs=[pl.BlockSpec((rows // 2, channels), lambda i, place: (i, 0))] * 3,
            out_specs=[pl.BlockSpec((rows // 2, channels), lambda i, place: (i, 0))] * 2,
        ),
        out_shape=[out, out],
        compiler_params=params(),
        cost_estimate=cost(2 * rows * channels, 10 * rows * channels),
        name="gate_back",
    )(place, gate_grad, query, mixed)


def tap_sums(short_taps, grad, tokens_ref, rim_ref, out_ref, at, ext):
    rows = tokens_ref.shape[0]
    extend(ext, rim_ref, tokens_ref[:, at], at)
    grad = grad.astype(F32)
    for tap in range(short_taps):
        out_ref[tap : tap + 1, at] = jnp.sum(grad * ext[RIM - tap : RIM - tap + rows, :], axis=0, keepdims=True)
    out_ref[short_taps:8, at] = jnp.zeros((8 - short_taps, LANES), F32)


def long_grad_kernel(
    per_group, short_taps, prev_ref, cur_ref, grad_ref, feature_ref, tokens_ref, rim_ref, long_ref, short_ref, fold, masked, ext
):
    rows, width = cur_ref.shape
    row, lane = lane_row((rows, rows))
    above = lane > row
    member = lax.broadcasted_iota(jnp.int32, (rows, LANES), 1)
    packed = LANES // per_group
    sums = []
    for block in range(width // LANES):
        at = pl.ds(block * LANES, LANES)
        window = jnp.concatenate([prev_ref[:, at], cur_ref[:, at]], axis=0)
        grad_wide = grad_ref[:, at].astype(F32)
        own = masked.at[block % 2]
        for g in range(packed):
            own[g * rows : (g + 1) * rows, :] = jnp.where((member >= g * per_group) & (member < (g + 1) * per_group), grad_wide, 0.0).astype(BF16)
        pairs = lax.dot_general(own[...], window, (((1,), (1,)), ((), ())), preferred_element_type=F32)
        for g in range(packed):
            pair = pairs[g * rows : (g + 1) * rows]
            ring = jnp.where(above, pair[:, 0:rows], pair[:, rows : 2 * rows])
            total = ring[0:8]
            for tile in range(1, rows // 8):
                total = total + pltpu.roll(ring[8 * tile : 8 * tile + 8], rows - 8 * tile, 1)
            fold[block % 2, g * 8 : (g + 1) * 8, :] = total
        total = fold[block % 2, pl.ds(0, packed, stride=8), :]
        for step in range(1, 8):
            total = total + pltpu.roll(fold[block % 2, pl.ds(step, packed, stride=8), :], rows - step, 1)
        sums.append(total)
        tap_sums(short_taps, feature_ref[:, at], tokens_ref, rim_ref, short_ref, at, ext.at[block % 2])
    long_ref[...] = jnp.dot(
        jnp.concatenate(sums, axis=0), mirror(rows), precision=lax.Precision.HIGHEST, preferred_element_type=F32
    )


def long_grad_call(groups, short_taps, prev, cur, grad, feature, tokens, rim):
    rows, channels = cur.shape
    per_group = channels // groups
    width = block_width(channels, WIDTH)
    steps = channels // width
    wide = pl.BlockSpec((rows, width), lambda i: (0, i))
    packed = LANES // per_group
    return hbm_call(
        functools.partial(long_grad_kernel, per_group, short_taps),
        grid=(steps,),
        in_specs=[wide] * 5 + [pl.BlockSpec((RIM, width), lambda i: (0, i))],
        out_specs=[
            pl.BlockSpec((width // per_group, rows), lambda i: (i, 0)),
            pl.BlockSpec((8, width), lambda i: (0, i)),
        ],
        out_shape=[
            jax.ShapeDtypeStruct((groups, rows), F32),
            jax.ShapeDtypeStruct((8, channels), F32),
        ],
        scratch_shapes=[
            pltpu.VMEM((2, packed * 8, LANES), F32),
            pltpu.VMEM((2, packed * rows, LANES), BF16),
            pltpu.VMEM((2, RIM + rows, LANES), F32),
        ],
        compiler_params=params(),
        cost_estimate=cost(2 * groups * rows * 2 * rows * LANES, 10 * rows * channels),
        name="long_grad",
    )(prev, cur, grad, feature, tokens, rim)


def unmix_kernel(
    per_group, short_taps, lines_ref, grad_ref, next_ref, key_ref, value_ref, key_tokens_ref, value_tokens_ref,
    key_rim_ref, value_rim_ref, query_grad_ref, feature_ref, key_sum_ref, value_sum_ref, edge_ref, table, ext,
):
    rows, width = grad_ref.shape
    row, lane = lane_row((rows, rows))
    below = lane < row
    packed = LANES // per_group
    edge_ref[0] = query_grad_ref[0:RIM, :]
    for block in range(width // LANES):
        at = pl.ds(block * LANES, LANES)
        own = table.at[block % 2]
        for g in range(packed):
            ring = circulant(lines_ref[block * packed + g : block * packed + g + 1, :], rows)
            own[g * rows : (g + 1) * rows, 0:rows] = jnp.where(below, 0.0, ring).astype(BF16)
            own[g * rows : (g + 1) * rows, rows : 2 * rows] = jnp.where(below, ring, 0.0).astype(BF16)
        window = jnp.concatenate([grad_ref[:, at], next_ref[:, at]], axis=0)
        product = jnp.dot(own[...], window, preferred_element_type=F32)
        grad_mixer = pick_groups(product, rows, per_group)
        key_grad = (grad_mixer * value_ref[:, at].astype(F32)).astype(BF16)
        value_grad = (grad_mixer * key_ref[:, at].astype(F32)).astype(BF16)
        feature_ref[0, :, at] = key_grad
        feature_ref[1, :, at] = value_grad
        edge_ref[1, :, at] = key_grad[0:RIM]
        edge_ref[2, :, at] = value_grad[0:RIM]
        slot = 2 * (block % 2)
        tap_sums(short_taps, key_grad, key_tokens_ref, key_rim_ref, key_sum_ref, at, ext.at[slot])
        tap_sums(short_taps, value_grad, value_tokens_ref, value_rim_ref, value_sum_ref, at, ext.at[slot + 1])


def unmix_call(lines, short_taps, grad, grad_next, key, value, tokens, rim, query_grad):
    rows, channels = grad.shape
    per_group = channels // lines.shape[0]
    width = block_width(channels, WIDTH)
    steps = channels // width

    def spec(height, part):
        return pl.BlockSpec((height, width), lambda i, part=part: (0, i + part * steps))

    wide = spec(rows, 0)
    sums = jax.ShapeDtypeStruct((8, channels), F32)
    return hbm_call(
        functools.partial(unmix_kernel, per_group, short_taps),
        loose=(0, 2),
        grid=(steps,),
        in_specs=[pl.BlockSpec((width // per_group, rows), lambda i: (i, 0))]
        + [wide] * 4
        + [spec(rows, 1), spec(rows, 2), spec(RIM, 1), spec(RIM, 2), spec(2 * RIM, 0)],
        out_specs=[
            pl.BlockSpec((2, rows, width), lambda i: (0, 0, i)),
            spec(8, 0),
            spec(8, 0),
            pl.BlockSpec((3, RIM, width), lambda i: (0, 0, i)),
        ],
        out_shape=[
            jax.ShapeDtypeStruct((2, rows, channels), BF16),
            sums,
            sums,
            jax.ShapeDtypeStruct((3, RIM, channels), BF16),
        ],
        scratch_shapes=[
            pltpu.VMEM((2, LANES // per_group * rows, 2 * rows), BF16),
            pltpu.VMEM((4, RIM + rows, LANES), F32),
        ],
        compiler_params=params(),
        cost_estimate=cost(2 * channels * rows * 2 * rows * LANES // per_group, 16 * rows * channels),
        name="unmix",
    )(lines, grad, grad_next, key, value, tokens, tokens, rim, rim, query_grad)


def short_adjoint_kernel(short_taps, grads_ref, rim_ref, filter_ref, *refs):
    out_ref, ext = refs[-2:]
    rows, width = out_ref.shape
    for block in range(width // LANES):
        at = pl.ds(block * LANES, LANES)
        own = ext.at[block % 2]
        own[0:rows, :] = grads_ref[0, :, at].astype(F32)
        own[rows:, :] = rim_ref[0, :, at].astype(F32)
        taps = filter_ref[:, at]
        total = taps[0:1] * own[0:rows, :]
        for tap in range(1, short_taps):
            total = total + taps[tap : tap + 1] * own[tap : tap + rows, :]
        out_ref[:, at] = total.astype(BF16)


def short_adjoint_call(grads, rim, filters, first, out):
    parts, rows, channels = grads.shape
    short_taps = filters.shape[0]
    width = block_width(channels, 2 * WIDTH)
    steps = channels // width
    result = pl.BlockSpec((rows, width), lambda p, i: (0, (p + first) * steps + i))
    given = [] if out is None else [out]
    return hbm_call(
        functools.partial(short_adjoint_kernel, short_taps),
        loose=(1,),
        grid=(parts, steps),
        in_specs=[
            pl.BlockSpec((1, rows, width), lambda p, i: (p, 0, i)),
            pl.BlockSpec((1, RIM, width), lambda p, i: (p + first, 0, i)),
            pl.BlockSpec((short_taps, width), lambda p, i: (0, (p + first) * steps + i)),
        ]
        + [pl.BlockSpec(memory_space=pl.ANY)] * len(given),
        out_specs=result,
        out_shape=jax.ShapeDtypeStruct((rows, 3 * channels), BF16),
        input_output_aliases={3: 0} if given else {},
        scratch_shapes=[pltpu.VMEM((2, rows + RIM, LANES), F32)],
        compiler_params=params(),
        cost_estimate=cost(2 * parts * short_taps * rows * channels, 4 * parts * rows * channels),
        name="short_adjoint",
    )(grads, rim, filters, *given)


def spread_kernel(place, query_ref, key_ref, value_ref, long_ref, own_ref, other_ref):
    steps = query_ref.shape[1] // LANES
    half = own_ref.shape[0]
    tiles = [ref[:, i * LANES : (i + 1) * LANES] for ref in (query_ref, key_ref, value_ref) for i in range(steps)]
    tiles += [long_ref[8 * i : 8 * i + 8, :] for i in range(long_ref.shape[0] // 8)]
    first = place[0] < half

    @pl.when(first)
    def _():
        for i in range(half):
            own_ref[place[i]] = tiles[i]
            other_ref[place[half + i] - half] = tiles[half + i]

    @pl.when(jnp.logical_not(first))
    def _():
        for i in range(half):
            other_ref[place[i] - half] = tiles[i]
            own_ref[place[half + i]] = tiles[half + i]


def collect_kernel(place, *refs):
    parts, short_ref, long_ref, tiles_ref = refs[:-3], refs[-3], refs[-2], refs[-1]
    short_taps, wide = short_ref.shape
    steps = wide // LANES
    size = parts[0].shape[0]
    for i, part in enumerate(parts):
        tiles_ref[i * size : (i + 1) * size] = part[...]
    for i in range(steps):
        short_ref[:, i * LANES : (i + 1) * LANES] = tiles_ref[place[i]][0:short_taps, :]
    for i in range(long_ref.shape[0] // 8):
        long_ref[8 * i : 8 * i + 8, :] = tiles_ref[place[steps + i]]


def in_vmem():
    return pl.BlockSpec(memory_space=pltpu.VMEM)


def total_over_devices(spread_to, collect_from, query_sum, key_sum, value_sum, long_sum, short_taps, beside):
    ny, nz = lax.axis_size("y"), lax.axis_size("z")
    channels = query_sum.shape[1]
    count = 3 * channels // LANES + long_sum.shape[0] // 8
    half = jax.ShapeDtypeStruct((count // 2, 8, LANES), F32)
    own, other = pl.pallas_call(
        spread_kernel,
        in_specs=[pl.BlockSpec(memory_space=pltpu.SMEM)] + [in_vmem()] * 4,
        out_specs=[in_vmem()] * 2,
        out_shape=[half] * 2,
        compiler_params=params(),
        name="spread",
    )(spread_to, query_sum, key_sum, value_sum, long_sum)
    part = own + move(other, c=1)
    size = count // 2 // nz
    part = sum([move(part[d * size : (d + 1) * size], z=d) for d in range(1, nz)], part[:size])
    terms, beside = lax.optimization_barrier(([part] + [move(part, y=d) for d in range(1, ny)], beside))
    whole = paired_sum(terms)
    whole = paired_sum([move(whole, xl=a, xh=b) for a, b in FLIPS])
    line = jnp.concatenate([whole, move(whole, c=1)], axis=0)
    lines = [move(line, z=-d) for d in range(nz)]
    groups, taps = long_sum.shape
    short, long = pl.pallas_call(
        collect_kernel,
        in_specs=[pl.BlockSpec(memory_space=pltpu.SMEM)] + [in_vmem()] * nz,
        out_specs=[in_vmem(), in_vmem()],
        scratch_shapes=[pltpu.VMEM((count, 8, LANES), F32)],
        out_shape=[
            jax.ShapeDtypeStruct((short_taps, 3 * channels), F32),
            jax.ShapeDtypeStruct((groups, taps), F32),
        ],
        compiler_params=params(),
        name="collect",
    )(collect_from, *lines)
    return short, long, beside


def paired_sum(terms):
    half = len(terms) // 2
    if half == 0:
        return terms[0]
    return paired_sum([terms[i] + terms[i + half] for i in range(half)])


def gather_tall(shard):
    return [move(shard[shard.shape[0] // 2 :], y=d) for d in range(lax.axis_size("y"))]


def gather_wide(shard):
    return [move(shard[: shard.shape[0] // 2], xl=a, xh=b) for a, b in FLIPS]


def gather_far(wide_top, tall_bottom):
    ny = lax.axis_size("y")
    wide_top, tall_bottom = jnp.stack(wide_top), jnp.stack(tall_bottom)
    return (
        [move(wide_top, y=d) for d in range(ny)],
        [move(tall_bottom, xl=a, xh=b) for a, b in FLIPS],
    )


def piece_rows(tops, bottoms, step):
    rows = []
    for a in range(2):
        rows.append(jnp.concatenate([tops[step][2 * a + b] for b in range(2)], axis=1))
        rows.append(jnp.concatenate([bottoms[2 * a + b][step] for b in range(2)], axis=1))
    return rows


def gate_matmul_kernel(ny, *refs):
    cotangent_ref, tops, bottoms, out_ref = refs[0], refs[1 : 1 + ny], refs[1 + ny : 5 + ny], refs[5 + ny]
    left = cotangent_ref[...]
    at = 0
    for step in range(ny):
        for right in piece_rows(tops, bottoms, step):
            size = right.shape[0]
            out_ref[:, at : at + size] = lax.dot_general(
                left, right, (((1,), (1,)), ((), ())), preferred_element_type=F32
            ).astype(BF16)
            at += size


def whole(x):
    return pl.BlockSpec(x.shape, lambda *_, n=x.ndim: (0,) * n)


def gate_matmul(cotangents, tops, bottoms):
    rows, depth = cotangents.shape
    ny = len(tops)
    channels = 4 * ny * tops[0].shape[1]
    height = rows // 2
    return hbm_call(
        functools.partial(gate_matmul_kernel, ny),
        loose=range(5 + ny),
        grid=(rows // height,),
        in_specs=[pl.BlockSpec((height, depth), lambda i: (i, 0))] + [whole(x) for x in (*tops, *bottoms)],
        out_specs=pl.BlockSpec((height, channels), lambda i: (i, 0)),
        out_shape=jax.ShapeDtypeStruct((rows, channels), BF16),
        compiler_params=params(32),
        cost_estimate=cost(2 * rows * depth * channels, 2 * (rows + depth) * channels),
        name="gate_matmul",
    )(cotangents, *tops, *bottoms)


def picked(origin, step, rows_ref):
    height = rows_ref.shape[1] // 2
    at = [pl.multiple_of(origin[2 * step + a] % 2 * height, height) for a in range(2)]
    return jnp.concatenate([rows_ref[:, pl.ds(x, height)] for x in at], axis=1)


def weight_grad_kernel(ny, origin, rows_ref, turned_ref, *refs):
    top_grads, bottom_grads = refs[:ny], refs[ny:]
    step = pl.program_id(0)
    size = bottom_grads[0].shape[2]
    width = bottom_grads[0].shape[1]
    rows = picked(origin, step, rows_ref)
    grads = jnp.dot(turned_ref[...], rows, preferred_element_type=F32).astype(BF16)
    for f in range(4):
        a, b = f // 2, f % 2
        at = (2 * a + 1) * size
        bottom_grads[f][step] = grads[b * width : (b + 1) * width, at : at + size]
    for d in range(ny):

        @pl.when(step == d)
        def _(d=d):
            for f in range(4):
                a, b = f // 2, f % 2
                at = 2 * a * size
                top_grads[d][f] = grads[b * width : (b + 1) * width, at : at + size]


def rows_of(origin, all_rows, ny):
    rows, channels = all_rows.shape
    return pl.BlockSpec((rows, channels // ny), lambda i, origin: (0, origin[2 * i] // 2))


def weight_grad(origin, all_rows, turned, ny):
    rows, channels = all_rows.shape
    size = channels // (4 * ny)
    width = turned.shape[0] // 2
    outs = [jax.ShapeDtypeStruct((4, width, size), BF16)] * ny + [jax.ShapeDtypeStruct((ny, width, size), BF16)] * 4
    results = hbm_call(
        functools.partial(weight_grad_kernel, ny),
        loose=(0, 2),
        grid_spec=pltpu.PrefetchScalarGridSpec(
            num_scalar_prefetch=1,
            grid=(ny,),
            in_specs=[rows_of(origin, all_rows, ny), whole(turned)],
            out_specs=[whole(x) for x in outs],
        ),
        out_shape=outs,
        compiler_params=params(40),
        cost_estimate=cost(4 * rows * width * channels, 2 * (rows + 2 * width) * channels),
        name="weight_grad",
    )(origin, all_rows, turned)
    return results[:ny], results[ny:]


def output_kernel(ny, origin, rows_ref, *refs):
    tops, bottoms, own_ref, other_ref, total = refs[:ny], refs[ny : ny + 4], refs[-3], refs[-2], refs[-1]
    step = pl.program_id(0)
    width = own_ref.shape[1]
    rows = picked(origin, step, rows_ref)
    for d in range(ny):

        @pl.when(step == d)
        def _(d=d):
            right = jnp.concatenate(piece_rows(tops, bottoms, d), axis=0)
            product = jnp.dot(rows, right, preferred_element_type=F32)
            if d == 0:
                total[...] = product
            else:
                total[...] += product

    @pl.when(step == ny - 1)
    def _():
        own_ref[...] = total[:, :width].astype(BF16)
        other_ref[...] = total[:, width:].astype(BF16)


def output_call(origin, all_rows, tops, bottoms):
    rows, channels = all_rows.shape
    ny = len(tops)
    width = tops[0].shape[2]
    half = jax.ShapeDtypeStruct((rows, width), BF16)
    return hbm_call(
        functools.partial(output_kernel, ny),
        loose=(0, *range(2, 6 + ny)),
        grid_spec=pltpu.PrefetchScalarGridSpec(
            num_scalar_prefetch=1,
            grid=(ny,),
            in_specs=[rows_of(origin, all_rows, ny)] + [whole(x) for x in (*tops, *bottoms)],
            out_specs=[whole(half)] * 2,
            scratch_shapes=[pltpu.VMEM((rows, 2 * width), F32)],
        ),
        out_shape=[half, half],
        compiler_params=params(32),
        cost_estimate=cost(4 * rows * width * channels, 2 * (rows + 2 * width) * channels),
        name="output",
    )(origin, all_rows, *tops, *bottoms)


def plane_scatter_sum(top_grads, bottom_grads):
    ny = len(top_grads)

    def added(terms):
        total = terms[0].astype(F32)
        for term in terms[1:]:
            total = total + term.astype(F32)
        return total

    top = added([move(top_grads[d], y=-d) for d in range(ny)]).astype(BF16)
    bottom = added([move(bottom_grads[f], xl=a, xh=b) for f, (a, b) in enumerate(FLIPS)]).astype(BF16)
    top = added([move(top[f], xl=a, xh=b) for f, (a, b) in enumerate(FLIPS)])
    bottom = added([move(bottom[d], y=-d) for d in range(ny)])
    return jnp.concatenate([top, bottom], axis=1).T


def shards(tokens_in, short_filter, long_filter, out_weight, cotangent):
    ny, nz = lax.axis_size("y"), lax.axis_size("z")
    y, xl, xh, z, c = (lax.axis_index(a) for a in ("y", "xl", "xh", "z", "c"))
    tokens = tokens_in[0]
    rows, wide = tokens.shape
    channels = wide // 3
    short_taps = short_filter.shape[0]
    groups = long_filter.shape[0]
    upstream = cotangent[0]
    length, columns = upstream.shape
    span = length // 2

    block = jnp.arange(2 * ny, dtype=jnp.int32)
    place = ((y - block // 2) % ny) * 2 + (block + xl) % 2
    origin = place
    size = 3 * channels // LANES + groups // 8
    each = size // (2 * nz)
    tile = jnp.arange(size, dtype=jnp.int32)
    core_step, z_step = (tile // (nz * each) + c) % 2, (tile // each - z) % nz
    spread_to = (core_step * nz + z_step) * each + tile % each
    collect_from = (z_step * 2 + core_step) * each + tile % each

    rim = along(tokens[rows - RIM :], 1)
    lines = long_filter.astype(F32)
    query, key, value, mixer = features_call(tokens, rim, short_filter)
    mixer, out_weight = lax.optimization_barrier((mixer, out_weight))
    mixer_prev = along(mixer, 1)
    tall_bottom = gather_tall(out_weight)
    mixer_prev, tall_bottom = lax.optimization_barrier((mixer_prev, tall_bottom))
    mixed, gated = mix_call(lines, mixer_prev, mixer, query)
    mixed, out_weight, tall_bottom, upstream = lax.optimization_barrier((mixed, out_weight, tall_bottom, upstream))
    wide_top = gather_wide(out_weight)
    all_rows = lax.all_gather(gated, ("z", "c"), axis=0, tiled=True)
    tops, bottoms = gather_far(wide_top, tall_bottom)
    mine = lax.dynamic_slice_in_dim(upstream, xh * span, span, 0)
    others = move(lax.dynamic_slice_in_dim(upstream, (1 - xh) * span, span, 0), xh=1)
    cotangents = jnp.concatenate([mine, others], axis=1)
    partial = gate_matmul(cotangents, tops, bottoms)
    partial, all_rows = lax.optimization_barrier((partial, all_rows))
    gate_grad = lax.psum_scatter(partial, ("z", "c"), scatter_dimension=0, tiled=True)

    top_grads, bottom_grads = weight_grad(origin, all_rows, cotangents.T, ny)
    own, other = output_call(origin, all_rows, tops, bottoms)
    grad_weight = plane_scatter_sum(top_grads, bottom_grads)
    theirs = move(other, xh=1)
    output = jnp.where(xh == 0, jnp.concatenate([own, theirs], axis=0), jnp.concatenate([theirs, own], axis=0))
    gate_grad, grad_weight, output = lax.optimization_barrier((gate_grad, grad_weight, output))

    grad_mixed, query_grad = gate_call(place, gate_grad, query, mixed)
    grad_next = along(grad_mixed, -1)
    long_sum, query_sum = long_grad_call(
        groups, short_taps, mixer_prev, mixer, grad_mixed, query_grad, tokens, rim
    )
    other_grads, key_sum, value_sum, edge = unmix_call(
        lines, short_taps, grad_mixed, grad_next, key, value, tokens, rim, query_grad
    )
    edge = along(edge, -1)
    grad_tokens = short_adjoint_call(query_grad[None], edge, short_filter, 0, None)
    grad_short, grad_long, grad_tokens = total_over_devices(
        spread_to, collect_from, query_sum, key_sum, value_sum, long_sum, short_taps, grad_tokens
    )
    grad_tokens = short_adjoint_call(other_grads, edge, short_filter, 1, grad_tokens)
    return output[None], grad_tokens[None], grad_short, grad_long, grad_weight


def solution(mesh):
    dp, seq = mesh.shape["dp"], mesh.shape["seq"]
    grid = jax.sharding.Mesh(mesh.devices.reshape(dp // 2, 2, 2, seq // 4, 2), ("y", "xl", "xh", "z", "c"))
    rows, line = ("y", "xl"), ("xh", "z", "c")
    return jax.shard_map(
        shards,
        mesh=grid,
        in_specs=(P(rows, line, None), P(), P(), P(rows, line), P(rows, None, line)),
        out_specs=(P(rows, None, line), P(rows, line, None), P(), P(), P(rows, line)),
        check_vma=False,
    )
```

```python
import functools
import itertools
import math

import jax
import jax.numpy as jnp
from jax import lax
from jax.experimental import pallas as pl
from jax.experimental.pallas import tpu as pltpu
from jax.sharding import PartitionSpec as P

LANES = 128
RIM = 8
MIB = 1024 * 1024
WIDTH = 1024
F32 = jnp.float32
BF16 = jnp.bfloat16


PLANE = ("y", "xl", "xh")
LINE = ("xh", "z", "c")


def along(x, by):
    size = math.prod(lax.axis_size(a) for a in LINE)
    pairs = [(i, i + by) for i in range(size) if 0 <= i + by < size]
    return lax.ppermute(x, LINE, pairs)


def move(x, **steps):
    axes = tuple(a for a in ("y", "xl", "xh", "z", "c") if steps.get(a, 0) % lax.axis_size(a))
    if not axes:
        return x
    sizes = [lax.axis_size(a) for a in axes]
    pairs = []
    for at in itertools.product(*(range(n) for n in sizes)):
        to = [(p + steps[a]) % n for p, a, n in zip(at, axes, sizes)]
        pairs.append((flat(at, sizes), flat(to, sizes)))
    return lax.ppermute(x, axes, pairs)


def flat(at, sizes):
    index = 0
    for p, n in zip(at, sizes):
        index = index * n + p
    return index


FLIPS = [(0, 0), (0, 1), (1, 0), (1, 1)]


def params(mib=16):
    return pltpu.CompilerParams(vmem_limit_bytes=mib * MIB)


def hbm_call(kernel, *, out_shape, loose=(), **options):
    single = not isinstance(out_shape, (list, tuple))
    shapes = [out_shape] if single else out_shape
    placed = [pltpu.HBM(x.shape, x.dtype) if x.size * x.dtype.itemsize > 256 * 1024 else x for x in shapes]
    call = pl.pallas_call(kernel, out_shape=placed[0] if single else placed, **options)

    def run(*args):
        held = [x if i in loose else pltpu.with_memory_space_constraint(x, pltpu.HBM) for i, x in enumerate(args)]
        return call(*held)

    return run


def cost(flops, moved):
    return pl.CostEstimate(flops=int(flops), bytes_accessed=int(moved), transcendentals=0)


def block_width(channels, most):
    width = min(channels, most)
    while channels % width:
        width //= 2
    return width


def extend(ext, rim, rows_of, at):
    ext[0:RIM, :] = rim[:, at].astype(F32)
    ext[RIM:, :] = rows_of.astype(F32)


def features_kernel(short_taps, tokens, rims, filters, query_ref, key_ref, value_ref, mixer_ref, ext):
    rows, width = tokens[0].shape

    def filtered(part, block, at):
        own = ext.at[(3 * block + part) % ext.shape[0]]
        extend(own, rims[part], tokens[part][:, at], at)
        taps = filters[part][:, at]
        total = taps[0:1] * own[RIM : RIM + rows, :]
        for tap in range(1, short_taps):
            total = total + taps[tap : tap + 1] * own[RIM - tap : RIM - tap + rows, :]
        return total

    for block in range(width // LANES):
        at = pl.ds(block * LANES, LANES)
        query_ref[:, at] = filtered(0, block, at).astype(BF16)
        key, value = filtered(1, block, at), filtered(2, block, at)
        key_ref[:, at] = key.astype(BF16)
        value_ref[:, at] = value.astype(BF16)
        mixer_ref[:, at] = (key * value).astype(BF16)


def features_call(tokens, rim, filters):
    rows, wide = tokens.shape
    channels = wide // 3
    taps = filters.shape[0]
    width = block_width(channels, WIDTH)
    steps = channels // width

    def spec(height, part):
        return pl.BlockSpec((height, width), lambda i, part=part: (0, i + part * steps))

    def body(*refs):
        features_kernel(taps, refs[0:3], refs[3:6], refs[6:9], *refs[9:])

    out = jax.ShapeDtypeStruct((rows, channels), BF16)
    return hbm_call(
        body,
        loose=(3, 4, 5),
        grid=(steps,),
        in_specs=[spec(rows, p) for p in range(3)]
        + [spec(RIM, p) for p in range(3)]
        + [spec(taps, p) for p in range(3)],
        out_specs=[pl.BlockSpec((rows, width), lambda i: (0, i))] * 4,
        out_shape=[out] * 4,
        scratch_shapes=[pltpu.VMEM((6, RIM + rows, LANES), F32)],
        compiler_params=params(),
        cost_estimate=cost(0, rows * wide),
        name="features",
    )(tokens, tokens, tokens, rim, rim, rim, filters, filters, filters)


def lane_row(shape):
    row = lax.broadcasted_iota(jnp.int32, shape, 0)
    lane = lax.broadcasted_iota(jnp.int32, shape, 1)
    return row, lane


def mirror(size):
    row, lane = lane_row((size, size))
    both = row + lane
    return jnp.where((both == 0) | (both == size), 1.0, 0.0)


def circulant(line, taps):
    wide = jnp.broadcast_to(line.astype(F32), (taps, taps))
    return pltpu.roll(wide, 0, 1, stride=1, stride_axis=0)


def pick_groups(product, rows, per_group):
    lane = lax.broadcasted_iota(jnp.int32, (rows, LANES), 1)
    total = product[0:rows]
    for g in range(1, LANES // per_group):
        total = jnp.where(lane >= g * per_group, product[g * rows : (g + 1) * rows], total)
    return total


def mix_kernel(per_group, lines_ref, prev_ref, cur_ref, query_ref, mixed_ref, gated_ref, table, lines):
    rows, width = cur_ref.shape
    row, lane = lane_row((rows, rows))
    above = lane > row
    packed = LANES // per_group
    lines[...] = jnp.dot(lines_ref[...].astype(BF16), mirror(rows).astype(BF16), preferred_element_type=F32)
    for block in range(width // LANES):
        at = pl.ds(block * LANES, LANES)
        own = table.at[block % 2]
        for g in range(packed):
            ring = circulant(lines[block * packed + g : block * packed + g + 1, :], rows)
            own[g * rows : (g + 1) * rows, 0:rows] = jnp.where(above, ring, 0.0).astype(BF16)
            own[g * rows : (g + 1) * rows, rows : 2 * rows] = jnp.where(above, 0.0, ring).astype(BF16)
        window = jnp.concatenate([prev_ref[:, at], cur_ref[:, at]], axis=0)
        product = jnp.dot(own[...], window, preferred_element_type=F32)
        mixed = pick_groups(product, rows, per_group)
        mixed_ref[:, at] = mixed.astype(BF16)
        gated_ref[:, at] = (query_ref[:, at].astype(F32) * mixed).astype(BF16)


def mix_call(lines, prev, cur, query):
    rows, channels = cur.shape
    groups, taps = lines.shape
    per_group = channels // groups
    width = block_width(channels, WIDTH)
    steps = channels // width
    wide = pl.BlockSpec((rows, width), lambda i: (0, i))
    out = jax.ShapeDtypeStruct((rows, channels), BF16)
    return hbm_call(
        functools.partial(mix_kernel, per_group),
        loose=(0, 1),
        grid=(steps,),
        in_specs=[pl.BlockSpec((width // per_group, taps), lambda i: (i, 0)), wide, wide, wide],
        out_specs=[wide, wide],
        out_shape=[out, out],
        scratch_shapes=[
            pltpu.VMEM((2, LANES // per_group * rows, 2 * rows), BF16),
            pltpu.VMEM((width // per_group, taps), F32),
        ],
        compiler_params=params(),
        cost_estimate=cost(0, 2 * rows * channels),
        name="mix",
    )(lines, prev, cur, query)


def gate_kernel(place, gate_grad_ref, query_ref, mixed_ref, grad_ref, feature_ref):
    width = query_ref.shape[1] // place.shape[0]
    for i in range(place.shape[0]):
        at = pl.ds(i * width, width)
        gate_grad = gate_grad_ref[:, pl.ds(pl.multiple_of(place[i] * width, width), width)].astype(F32)
        grad_ref[:, at] = (gate_grad * query_ref[:, at].astype(F32)).astype(BF16)
        feature_ref[:, at] = (gate_grad * mixed_ref[:, at].astype(F32)).astype(BF16)


def gate_call(place, gate_grad, query, mixed):
    rows, channels = query.shape
    out = jax.ShapeDtypeStruct((rows, channels), BF16)
    return hbm_call(
        gate_kernel,
        loose=(0,),
        grid_spec=pltpu.PrefetchScalarGridSpec(
            num_scalar_prefetch=1,
            grid=(2,),
            in_specs=[pl.BlockSpec((rows // 2, channels), lambda i, place: (i, 0))] * 3,
            out_specs=[pl.BlockSpec((rows // 2, channels), lambda i, place: (i, 0))] * 2,
        ),
        out_shape=[out, out],
        compiler_params=params(),
        cost_estimate=cost(2 * rows * channels, 10 * rows * channels),
        name="gate_back",
    )(place, gate_grad, query, mixed)


def tap_sums(short_taps, grad, tokens_ref, rim_ref, out_ref, at, ext):
    rows = tokens_ref.shape[0]
    extend(ext, rim_ref, tokens_ref[:, at], at)
    grad = grad.astype(F32)
    for tap in range(short_taps):
        out_ref[tap : tap + 1, at] = jnp.sum(grad * ext[RIM - tap : RIM - tap + rows, :], axis=0, keepdims=True)
    out_ref[short_taps:8, at] = jnp.zeros((8 - short_taps, LANES), F32)


def long_grad_kernel(
    per_group, short_taps, prev_ref, cur_ref, grad_ref, feature_ref, tokens_ref, rim_ref, long_ref, short_ref, fold, masked, ext
):
    rows, width = cur_ref.shape
    row, lane = lane_row((rows, rows))
    above = lane > row
    member = lax.broadcasted_iota(jnp.int32, (rows, LANES), 1)
    packed = LANES // per_group
    sums = []
    for block in range(width // LANES):
        at = pl.ds(block * LANES, LANES)
        window = jnp.concatenate([prev_ref[:, at], cur_ref[:, at]], axis=0)
        grad_wide = grad_ref[:, at].astype(F32)
        own = masked.at[block % 2]
        for g in range(packed):
            own[g * rows : (g + 1) * rows, :] = jnp.where((member >= g * per_group) & (member < (g + 1) * per_group), grad_wide, 0.0).astype(BF16)
        pairs = lax.dot_general(own[...], window, (((1,), (1,)), ((), ())), preferred_element_type=F32)
        for g in range(packed):
            pair = pairs[g * rows : (g + 1) * rows]
            ring = jnp.where(above, pair[:, 0:rows], pair[:, rows : 2 * rows])
            total = ring[0:8]
            for tile in range(1, rows // 8):
                total = total + pltpu.roll(ring[8 * tile : 8 * tile + 8], rows - 8 * tile, 1)
            fold[block % 2, g * 8 : (g + 1) * 8, :] = total
        total = fold[block % 2, pl.ds(0, packed, stride=8), :]
        for step in range(1, 8):
            total = total + pltpu.roll(fold[block % 2, pl.ds(step, packed, stride=8), :], rows - step, 1)
        sums.append(total)
        tap_sums(short_taps, feature_ref[:, at], tokens_ref, rim_ref, short_ref, at, ext.at[block % 2])
    long_ref[...] = jnp.dot(
        jnp.concatenate(sums, axis=0), mirror(rows), precision=lax.Precision.HIGHEST, preferred_element_type=F32
    )


def long_grad_call(groups, short_taps, prev, cur, grad, feature, tokens, rim):
    rows, channels = cur.shape
    per_group = channels // groups
    width = block_width(channels, WIDTH)
    steps = channels // width
    wide = pl.BlockSpec((rows, width), lambda i: (0, i))
    packed = LANES // per_group
    return hbm_call(
        functools.partial(long_grad_kernel, per_group, short_taps),
        grid=(steps,),
        in_specs=[wide] * 5 + [pl.BlockSpec((RIM, width), lambda i: (0, i))],
        out_specs=[
            pl.BlockSpec((width // per_group, rows), lambda i: (i, 0)),
            pl.BlockSpec((8, width), lambda i: (0, i)),
        ],
        out_shape=[
            jax.ShapeDtypeStruct((groups, rows), F32),
            jax.ShapeDtypeStruct((8, channels), F32),
        ],
        scratch_shapes=[
            pltpu.VMEM((2, packed * 8, LANES), F32),
            pltpu.VMEM((2, packed * rows, LANES), BF16),
            pltpu.VMEM((2, RIM + rows, LANES), F32),
        ],
        compiler_params=params(),
        cost_estimate=cost(2 * groups * rows * 2 * rows * LANES, 10 * rows * channels),
        name="long_grad",
    )(prev, cur, grad, feature, tokens, rim)


def unmix_kernel(
    per_group, short_taps, lines_ref, grad_ref, next_ref, key_ref, value_ref, key_tokens_ref, value_tokens_ref,
    key_rim_ref, value_rim_ref, query_grad_ref, feature_ref, key_sum_ref, value_sum_ref, edge_ref, table, ext,
):
    rows, width = grad_ref.shape
    row, lane = lane_row((rows, rows))
    below = lane < row
    packed = LANES // per_group
    edge_ref[0] = query_grad_ref[0:RIM, :]
    for block in range(width // LANES):
        at = pl.ds(block * LANES, LANES)
        own = table.at[block % 2]
        for g in range(packed):
            ring = circulant(lines_ref[block * packed + g : block * packed + g + 1, :], rows)
            own[g * rows : (g + 1) * rows, 0:rows] = jnp.where(below, 0.0, ring).astype(BF16)
            own[g * rows : (g + 1) * rows, rows : 2 * rows] = jnp.where(below, ring, 0.0).astype(BF16)
        window = jnp.concatenate([grad_ref[:, at], next_ref[:, at]], axis=0)
        product = jnp.dot(own[...], window, preferred_element_type=F32)
        grad_mixer = pick_groups(product, rows, per_group)
        key_grad = (grad_mixer * value_ref[:, at].astype(F32)).astype(BF16)
        value_grad = (grad_mixer * key_ref[:, at].astype(F32)).astype(BF16)
        feature_ref[0, :, at] = key_grad
        feature_ref[1, :, at] = value_grad
        edge_ref[1, :, at] = key_grad[0:RIM]
        edge_ref[2, :, at] = value_grad[0:RIM]
        slot = 2 * (block % 2)
        tap_sums(short_taps, key_grad, key_tokens_ref, key_rim_ref, key_sum_ref, at, ext.at[slot])
        tap_sums(short_taps, value_grad, value_tokens_ref, value_rim_ref, value_sum_ref, at, ext.at[slot + 1])


def unmix_call(lines, short_taps, grad, grad_next, key, value, tokens, rim, query_grad):
    rows, channels = grad.shape
    per_group = channels // lines.shape[0]
    width = block_width(channels, WIDTH)
    steps = channels // width

    def spec(height, part):
        return pl.BlockSpec((height, width), lambda i, part=part: (0, i + part * steps))

    wide = spec(rows, 0)
    sums = jax.ShapeDtypeStruct((8, channels), F32)
    return hbm_call(
        functools.partial(unmix_kernel, per_group, short_taps),
        loose=(0, 2),
        grid=(steps,),
        in_specs=[pl.BlockSpec((width // per_group, rows), lambda i: (i, 0))]
        + [wide] * 4
        + [spec(rows, 1), spec(rows, 2), spec(RIM, 1), spec(RIM, 2), spec(2 * RIM, 0)],
        out_specs=[
            pl.BlockSpec((2, rows, width), lambda i: (0, 0, i)),
            spec(8, 0),
            spec(8, 0),
            pl.BlockSpec((3, RIM, width), lambda i: (0, 0, i)),
        ],
        out_shape=[
            jax.ShapeDtypeStruct((2, rows, channels), BF16),
            sums,
            sums,
            jax.ShapeDtypeStruct((3, RIM, channels), BF16),
        ],
        scratch_shapes=[
            pltpu.VMEM((2, LANES // per_group * rows, 2 * rows), BF16),
            pltpu.VMEM((4, RIM + rows, LANES), F32),
        ],
        compiler_params=params(),
        cost_estimate=cost(2 * channels * rows * 2 * rows * LANES // per_group, 16 * rows * channels),
        name="unmix",
    )(lines, grad, grad_next, key, value, tokens, tokens, rim, rim, query_grad)


def short_adjoint_kernel(short_taps, grads_ref, rim_ref, filter_ref, *refs):
    out_ref, ext = refs[-2:]
    rows, width = out_ref.shape
    for block in range(width // LANES):
        at = pl.ds(block * LANES, LANES)
        own = ext.at[block % 2]
        own[0:rows, :] = grads_ref[0, :, at].astype(F32)
        own[rows:, :] = rim_ref[0, :, at].astype(F32)
        taps = filter_ref[:, at]
        total = taps[0:1] * own[0:rows, :]
        for tap in range(1, short_taps):
            total = total + taps[tap : tap + 1] * own[tap : tap + rows, :]
        out_ref[:, at] = total.astype(BF16)


def short_adjoint_call(grads, rim, filters, first, out):
    parts, rows, channels = grads.shape
    short_taps = filters.shape[0]
    width = block_width(channels, 2 * WIDTH)
    steps = channels // width
    result = pl.BlockSpec((rows, width), lambda p, i: (0, (p + first) * steps + i))
    given = [] if out is None else [out]
    return hbm_call(
        functools.partial(short_adjoint_kernel, short_taps),
        loose=(1,),
        grid=(parts, steps),
        in_specs=[
            pl.BlockSpec((1, rows, width), lambda p, i: (p, 0, i)),
            pl.BlockSpec((1, RIM, width), lambda p, i: (p + first, 0, i)),
            pl.BlockSpec((short_taps, width), lambda p, i: (0, (p + first) * steps + i)),
        ]
        + [pl.BlockSpec(memory_space=pl.ANY)] * len(given),
        out_specs=result,
        out_shape=jax.ShapeDtypeStruct((rows, 3 * channels), BF16),
        input_output_aliases={3: 0} if given else {},
        scratch_shapes=[pltpu.VMEM((2, rows + RIM, LANES), F32)],
        compiler_params=params(),
        cost_estimate=cost(2 * parts * short_taps * rows * channels, 4 * parts * rows * channels),
        name="short_adjoint",
    )(grads, rim, filters, *given)


def spread_kernel(place, query_ref, key_ref, value_ref, long_ref, own_ref, other_ref):
    steps = query_ref.shape[1] // LANES
    half = own_ref.shape[0]
    tiles = [ref[:, i * LANES : (i + 1) * LANES] for ref in (query_ref, key_ref, value_ref) for i in range(steps)]
    tiles += [long_ref[8 * i : 8 * i + 8, :] for i in range(long_ref.shape[0] // 8)]
    first = place[0] < half

    @pl.when(first)
    def _():
        for i in range(half):
            own_ref[place[i]] = tiles[i]
            other_ref[place[half + i] - half] = tiles[half + i]

    @pl.when(jnp.logical_not(first))
    def _():
        for i in range(half):
            other_ref[place[i] - half] = tiles[i]
            own_ref[place[half + i]] = tiles[half + i]


def collect_kernel(place, *refs):
    parts, short_ref, long_ref, tiles_ref = refs[:-3], refs[-3], refs[-2], refs[-1]
    short_taps, wide = short_ref.shape
    steps = wide // LANES
    size = parts[0].shape[0]
    for i, part in enumerate(parts):
        tiles_ref[i * size : (i + 1) * size] = part[...]
    for i in range(steps):
        short_ref[:, i * LANES : (i + 1) * LANES] = tiles_ref[place[i]][0:short_taps, :]
    for i in range(long_ref.shape[0] // 8):
        long_ref[8 * i : 8 * i + 8, :] = tiles_ref[place[steps + i]]


def in_vmem():
    return pl.BlockSpec(memory_space=pltpu.VMEM)


def total_over_devices(spread_to, collect_from, query_sum, key_sum, value_sum, long_sum, short_taps, beside):
    ny, nz = lax.axis_size("y"), lax.axis_size("z")
    channels = query_sum.shape[1]
    count = 3 * channels // LANES + long_sum.shape[0] // 8
    half = jax.ShapeDtypeStruct((count // 2, 8, LANES), F32)
    own, other = pl.pallas_call(
        spread_kernel,
        in_specs=[pl.BlockSpec(memory_space=pltpu.SMEM)] + [in_vmem()] * 4,
        out_specs=[in_vmem()] * 2,
        out_shape=[half] * 2,
        compiler_params=params(),
        name="spread",
    )(spread_to, query_sum, key_sum, value_sum, long_sum)
    part = own + move(other, c=1)
    size = count // 2 // nz
    part = sum([move(part[d * size : (d + 1) * size], z=d) for d in range(1, nz)], part[:size])
    terms, beside = lax.optimization_barrier(([part] + [move(part, y=d) for d in range(1, ny)], beside))
    whole = paired_sum(terms)
    whole = paired_sum([move(whole, xl=a, xh=b) for a, b in FLIPS])
    line = jnp.concatenate([whole, move(whole, c=1)], axis=0)
    lines = [move(line, z=-d) for d in range(nz)]
    groups, taps = long_sum.shape
    short, long = pl.pallas_call(
        collect_kernel,
        in_specs=[pl.BlockSpec(memory_space=pltpu.SMEM)] + [in_vmem()] * nz,
        out_specs=[in_vmem(), in_vmem()],
        scratch_shapes=[pltpu.VMEM((count, 8, LANES), F32)],
        out_shape=[
            jax.ShapeDtypeStruct((short_taps, 3 * channels), F32),
            jax.ShapeDtypeStruct((groups, taps), F32),
        ],
        compiler_params=params(),
        name="collect",
    )(collect_from, *lines)
    return short, long, beside


def paired_sum(terms):
    half = len(terms) // 2
    if half == 0:
        return terms[0]
    return paired_sum([terms[i] + terms[i + half] for i in range(half)])


def gather_tall(shard):
    return [move(shard[shard.shape[0] // 2 :], y=d) for d in range(lax.axis_size("y"))]


def gather_wide(shard):
    return [move(shard[: shard.shape[0] // 2], xl=a, xh=b) for a, b in FLIPS]


def gather_far(wide_top, tall_bottom):
    ny = lax.axis_size("y")
    wide_top, tall_bottom = jnp.stack(wide_top), jnp.stack(tall_bottom)
    return (
        [move(wide_top, y=d) for d in range(ny)],
        [move(tall_bottom, xl=a, xh=b) for a, b in FLIPS],
    )


def piece_rows(tops, bottoms, step):
    rows = []
    for a in range(2):
        rows.append(jnp.concatenate([tops[step][2 * a + b] for b in range(2)], axis=1))
        rows.append(jnp.concatenate([bottoms[2 * a + b][step] for b in range(2)], axis=1))
    return rows


def gate_matmul_kernel(ny, *refs):
    cotangent_ref, tops, bottoms, out_ref = refs[0], refs[1 : 1 + ny], refs[1 + ny : 5 + ny], refs[5 + ny]
    left = cotangent_ref[...]
    at = 0
    for step in range(ny):
        for right in piece_rows(tops, bottoms, step):
            size = right.shape[0]
            out_ref[:, at : at + size] = lax.dot_general(
                left, right, (((1,), (1,)), ((), ())), preferred_element_type=F32
            ).astype(BF16)
            at += size


def whole(x):
    return pl.BlockSpec(x.shape, lambda *_, n=x.ndim: (0,) * n)


def gate_matmul(cotangents, tops, bottoms):
    rows, depth = cotangents.shape
    ny = len(tops)
    channels = 4 * ny * tops[0].shape[1]
    height = rows // 2
    return hbm_call(
        functools.partial(gate_matmul_kernel, ny),
        loose=range(5 + ny),
        grid=(rows // height,),
        in_specs=[pl.BlockSpec((height, depth), lambda i: (i, 0))] + [whole(x) for x in (*tops, *bottoms)],
        out_specs=pl.BlockSpec((height, channels), lambda i: (i, 0)),
        out_shape=jax.ShapeDtypeStruct((rows, channels), BF16),
        compiler_params=params(32),
        cost_estimate=cost(2 * rows * depth * channels, 2 * (rows + depth) * channels),
        name="gate_matmul",
    )(cotangents, *tops, *bottoms)


def picked(origin, step, rows_ref):
    height = rows_ref.shape[1] // 2
    at = [pl.multiple_of(origin[2 * step + a] % 2 * height, height) for a in range(2)]
    return jnp.concatenate([rows_ref[:, pl.ds(x, height)] for x in at], axis=1)


def weight_grad_kernel(ny, origin, rows_ref, turned_ref, *refs):
    top_grads, bottom_grads = refs[:ny], refs[ny:]
    step = pl.program_id(0)
    size = bottom_grads[0].shape[2]
    width = bottom_grads[0].shape[1]
    rows = picked(origin, step, rows_ref)
    grads = jnp.dot(turned_ref[...], rows, preferred_element_type=F32).astype(BF16)
    for f in range(4):
        a, b = f // 2, f % 2
        at = (2 * a + 1) * size
        bottom_grads[f][step] = grads[b * width : (b + 1) * width, at : at + size]
    for d in range(ny):

        @pl.when(step == d)
        def _(d=d):
            for f in range(4):
                a, b = f // 2, f % 2
                at = 2 * a * size
                top_grads[d][f] = grads[b * width : (b + 1) * width, at : at + size]


def rows_of(origin, all_rows, ny):
    rows, channels = all_rows.shape
    return pl.BlockSpec((rows, channels // ny), lambda i, origin: (0, origin[2 * i] // 2))


def weight_grad(origin, all_rows, turned, ny):
    rows, channels = all_rows.shape
    size = channels // (4 * ny)
    width = turned.shape[0] // 2
    outs = [jax.ShapeDtypeStruct((4, width, size), BF16)] * ny + [jax.ShapeDtypeStruct((ny, width, size), BF16)] * 4
    results = hbm_call(
        functools.partial(weight_grad_kernel, ny),
        loose=(0, 2),
        grid_spec=pltpu.PrefetchScalarGridSpec(
            num_scalar_prefetch=1,
            grid=(ny,),
            in_specs=[rows_of(origin, all_rows, ny), whole(turned)],
            out_specs=[whole(x) for x in outs],
        ),
        out_shape=outs,
        compiler_params=params(40),
        cost_estimate=cost(4 * rows * width * channels, 2 * (rows + 2 * width) * channels),
        name="weight_grad",
    )(origin, all_rows, turned)
    return results[:ny], results[ny:]


def output_kernel(ny, origin, rows_ref, *refs):
    tops, bottoms, own_ref, other_ref, total = refs[:ny], refs[ny : ny + 4], refs[-3], refs[-2], refs[-1]
    step = pl.program_id(0)
    width = own_ref.shape[1]
    rows = picked(origin, step, rows_ref)
    for d in range(ny):

        @pl.when(step == d)
        def _(d=d):
            right = jnp.concatenate(piece_rows(tops, bottoms, d), axis=0)
            product = jnp.dot(rows, right, preferred_element_type=F32)
            if d == 0:
                total[...] = product
            else:
                total[...] += product

    @pl.when(step == ny - 1)
    def _():
        own_ref[...] = total[:, :width].astype(BF16)
        other_ref[...] = total[:, width:].astype(BF16)


def output_call(origin, all_rows, tops, bottoms):
    rows, channels = all_rows.shape
    ny = len(tops)
    width = tops[0].shape[2]
    half = jax.ShapeDtypeStruct((rows, width), BF16)
    return hbm_call(
        functools.partial(output_kernel, ny),
        loose=(0, *range(2, 6 + ny)),
        grid_spec=pltpu.PrefetchScalarGridSpec(
            num_scalar_prefetch=1,
            grid=(ny,),
            in_specs=[rows_of(origin, all_rows, ny)] + [whole(x) for x in (*tops, *bottoms)],
            out_specs=[whole(half)] * 2,
            scratch_shapes=[pltpu.VMEM((rows, 2 * width), F32)],
        ),
        out_shape=[half, half],
        compiler_params=params(32),
        cost_estimate=cost(4 * rows * width * channels, 2 * (rows + 2 * width) * channels),
        name="output",
    )(origin, all_rows, *tops, *bottoms)


def added(terms):
    total = terms[0].astype(F32)
    for term in terms[1:]:
        total = total + term.astype(F32)
    return total


def plane_scatter(top_grads, bottom_grads, beside):
    ny = len(top_grads)
    top = added([move(top_grads[d], y=-d) for d in range(ny)]).astype(BF16)
    bottom = added([move(bottom_grads[f], xl=a, xh=b) for f, (a, b) in enumerate(FLIPS)]).astype(BF16)
    top, bottom, beside = lax.optimization_barrier((top, bottom, beside))
    top = [move(top[f], xl=a, xh=b) for f, (a, b) in enumerate(FLIPS)]
    bottom = [move(bottom[d], y=-d) for d in range(ny)]
    return top, bottom, beside


def shards(tokens_in, short_filter, long_filter, out_weight, cotangent):
    ny, nz = lax.axis_size("y"), lax.axis_size("z")
    y, xl, xh, z, c = (lax.axis_index(a) for a in ("y", "xl", "xh", "z", "c"))
    tokens = tokens_in[0]
    rows, wide = tokens.shape
    channels = wide // 3
    short_taps = short_filter.shape[0]
    groups = long_filter.shape[0]
    upstream = cotangent[0]
    length, columns = upstream.shape
    span = length // 2

    block = jnp.arange(2 * ny, dtype=jnp.int32)
    place = ((y - block // 2) % ny) * 2 + (block + xl) % 2
    origin = place
    size = 3 * channels // LANES + groups // 8
    each = size // (2 * nz)
    tile = jnp.arange(size, dtype=jnp.int32)
    core_step, z_step = (tile // (nz * each) + c) % 2, (tile // each - z) % nz
    spread_to = (core_step * nz + z_step) * each + tile % each
    collect_from = (z_step * 2 + core_step) * each + tile % each

    rim = along(tokens[rows - RIM :], 1)
    lines = long_filter.astype(F32)
    query, key, value, mixer = features_call(tokens, rim, short_filter)
    mixer, out_weight = lax.optimization_barrier((mixer, out_weight))
    mixer_prev = along(mixer, 1)
    wide_top = gather_wide(out_weight)
    mixer_prev, wide_top = lax.optimization_barrier((mixer_prev, wide_top))
    mixed, gated = mix_call(lines, mixer_prev, mixer, query)
    mixed, out_weight, wide_top, upstream = lax.optimization_barrier((mixed, out_weight, wide_top, upstream))
    tall_bottom = gather_tall(out_weight)
    all_rows = lax.all_gather(gated, ("z", "c"), axis=0, tiled=True)
    tops, bottoms = gather_far(wide_top, tall_bottom)
    mine = lax.dynamic_slice_in_dim(upstream, xh * span, span, 0)
    others = move(lax.dynamic_slice_in_dim(upstream, (1 - xh) * span, span, 0), xh=1)
    cotangents = jnp.concatenate([mine, others], axis=1)
    partial = gate_matmul(cotangents, tops, bottoms)
    partial, all_rows = lax.optimization_barrier((partial, all_rows))
    gate_grad = lax.psum_scatter(partial, ("z", "c"), scatter_dimension=0, tiled=True)

    top_grads, bottom_grads = weight_grad(origin, all_rows, cotangents.T, ny)
    own, other = output_call(origin, all_rows, tops, bottoms)
    top, bottom, other = plane_scatter(top_grads, bottom_grads, other)
    gate_grad, top, bottom, other = lax.optimization_barrier((gate_grad, top, bottom, other))

    grad_mixed, query_grad = gate_call(place, gate_grad, query, mixed)
    grad_next = along(grad_mixed, -1)
    long_sum, query_sum = long_grad_call(
        groups, short_taps, mixer_prev, mixer, grad_mixed, query_grad, tokens, rim
    )
    grad_weight = jnp.concatenate([added(top), added(bottom)], axis=1).T
    theirs = move(other, xh=1)
    grad_next, grad_weight, theirs = lax.optimization_barrier((grad_next, grad_weight, theirs))
    output = jnp.where(xh == 0, jnp.concatenate([own, theirs], axis=0), jnp.concatenate([theirs, own], axis=0))
    other_grads, key_sum, value_sum, edge = unmix_call(
        lines, short_taps, grad_mixed, grad_next, key, value, tokens, rim, query_grad
    )
    edge = along(edge, -1)
    grad_tokens = short_adjoint_call(query_grad[None], edge, short_filter, 0, None)
    grad_short, grad_long, grad_tokens = total_over_devices(
        spread_to, collect_from, query_sum, key_sum, value_sum, long_sum, short_taps, grad_tokens
    )
    grad_tokens = short_adjoint_call(other_grads, edge, short_filter, 1, grad_tokens)
    return output[None], grad_tokens[None], grad_short, grad_long, grad_weight


def solution(mesh):
    dp, seq = mesh.shape["dp"], mesh.shape["seq"]
    grid = jax.sharding.Mesh(mesh.devices.reshape(dp // 2, 2, 2, seq // 4, 2), ("y", "xl", "xh", "z", "c"))
    rows, line = ("y", "xl"), ("xh", "z", "c")
    return jax.shard_map(
        shards,
        mesh=grid,
        in_specs=(P(rows, line, None), P(), P(), P(rows, line), P(rows, None, line)),
        out_specs=(P(rows, None, line), P(rows, line, None), P(), P(), P(rows, line)),
        check_vma=False,
    )
```

```python
import functools
import itertools
import math

import jax
import jax.numpy as jnp
from jax import lax
from jax.experimental import pallas as pl
from jax.experimental.pallas import tpu as pltpu
from jax.sharding import PartitionSpec as P

LANES = 128
RIM = 8
MIB = 1024 * 1024
WIDTH = 1024
F32 = jnp.float32
BF16 = jnp.bfloat16


PLANE = ("y", "xl", "xh")
LINE = ("xh", "z", "c")


def along(x, by):
    size = math.prod(lax.axis_size(a) for a in LINE)
    pairs = [(i, i + by) for i in range(size) if 0 <= i + by < size]
    return lax.ppermute(x, LINE, pairs)


def move(x, **steps):
    axes = tuple(a for a in ("y", "xl", "xh", "z", "c") if steps.get(a, 0) % lax.axis_size(a))
    if not axes:
        return x
    sizes = [lax.axis_size(a) for a in axes]
    pairs = []
    for at in itertools.product(*(range(n) for n in sizes)):
        to = [(p + steps[a]) % n for p, a, n in zip(at, axes, sizes)]
        pairs.append((flat(at, sizes), flat(to, sizes)))
    return lax.ppermute(x, axes, pairs)


def flat(at, sizes):
    index = 0
    for p, n in zip(at, sizes):
        index = index * n + p
    return index


FLIPS = [(0, 0), (0, 1), (1, 0), (1, 1)]


def params(mib=16):
    return pltpu.CompilerParams(vmem_limit_bytes=mib * MIB)


def hbm_call(kernel, *, out_shape, loose=(), **options):
    single = not isinstance(out_shape, (list, tuple))
    shapes = [out_shape] if single else out_shape
    placed = [pltpu.HBM(x.shape, x.dtype) if x.size * x.dtype.itemsize > 256 * 1024 else x for x in shapes]
    call = pl.pallas_call(kernel, out_shape=placed[0] if single else placed, **options)

    def run(*args):
        held = [x if i in loose else pltpu.with_memory_space_constraint(x, pltpu.HBM) for i, x in enumerate(args)]
        return call(*held)

    return run


def cost(flops, moved):
    return pl.CostEstimate(flops=int(flops), bytes_accessed=int(moved), transcendentals=0)


def block_width(channels, most):
    width = min(channels, most)
    while channels % width:
        width //= 2
    return width


def extend(ext, rim, rows_of, at):
    ext[0:RIM, :] = jnp.zeros((RIM, LANES), F32) if rim is None else rim[:, at].astype(F32)
    ext[RIM:, :] = rows_of.astype(F32)


def features_kernel(short_taps, tokens, rims, filters, query_ref, key_ref, value_ref, mixer_ref, ext):
    rows, width = tokens[0].shape

    def filtered(part, block, at):
        own = ext.at[(3 * block + part) % ext.shape[0]]
        extend(own, rims and rims[part], tokens[part][:, at], at)
        taps = filters[part][:, at]
        total = taps[0:1] * own[RIM : RIM + rows, :]
        for tap in range(1, short_taps):
            total = total + taps[tap : tap + 1] * own[RIM - tap : RIM - tap + rows, :]
        return total

    for block in range(width // LANES):
        at = pl.ds(block * LANES, LANES)
        query_ref[:, at] = filtered(0, block, at).astype(BF16)
        key, value = filtered(1, block, at), filtered(2, block, at)
        key_ref[:, at] = key.astype(BF16)
        value_ref[:, at] = value.astype(BF16)
        mixer_ref[:, at] = (key * value).astype(BF16)


def features_call(tokens, filters, rim=None, given=None):
    rows, wide = tokens.shape
    channels = wide // 3
    taps = filters.shape[0]
    rows = rows if given is None else 2 * RIM
    width = channels if given else block_width(channels, WIDTH)
    steps = channels // width

    def spec(height, part):
        return pl.BlockSpec((height, width), lambda i, part=part: (0, i + part * steps))

    held = [] if given is None else [rim] * 3
    olds = [] if given is None else list(given)

    def body(*refs):
        n = 3 + len(held)
        rims = refs[3:n] if held else None
        features_kernel(taps, refs[0:3], rims, refs[n : n + 3], *refs[n + 3 + len(olds) :])

    out = jax.ShapeDtypeStruct((tokens.shape[0], channels), BF16)
    return hbm_call(
        body,
        loose=(3, 4, 5) if held else (),
        grid=(steps,),
        in_specs=[spec(rows, p) for p in range(3)]
        + [spec(RIM, p) for p in range(len(held))]
        + [spec(taps, p) for p in range(3)]
        + [pl.BlockSpec(memory_space=pl.ANY)] * len(olds),
        out_specs=[pl.BlockSpec((rows, width), lambda i: (0, i))] * 4,
        out_shape=[out] * 4,
        input_output_aliases={9 + i: i for i in range(len(olds))},
        scratch_shapes=[pltpu.VMEM((6, RIM + rows, LANES), F32)],
        compiler_params=params(),
        cost_estimate=cost(0, rows * wide),
        name="features" if given is None else "first_rows",
    )(*[tokens] * 3, *held, *[filters] * 3, *olds)


def lane_row(shape):
    row = lax.broadcasted_iota(jnp.int32, shape, 0)
    lane = lax.broadcasted_iota(jnp.int32, shape, 1)
    return row, lane


def mirror(size):
    row, lane = lane_row((size, size))
    both = row + lane
    return jnp.where((both == 0) | (both == size), 1.0, 0.0)


def circulant(line, taps):
    wide = jnp.broadcast_to(line.astype(F32), (taps, taps))
    return pltpu.roll(wide, 0, 1, stride=1, stride_axis=0)


def pick_groups(product, rows, per_group):
    lane = lax.broadcasted_iota(jnp.int32, (rows, LANES), 1)
    total = product[0:rows]
    for g in range(1, LANES // per_group):
        total = jnp.where(lane >= g * per_group, product[g * rows : (g + 1) * rows], total)
    return total


def mix_kernel(per_group, lines_ref, prev_ref, cur_ref, query_ref, mixed_ref, gated_ref, table, lines):
    rows, width = cur_ref.shape
    row, lane = lane_row((rows, rows))
    above = lane > row
    packed = LANES // per_group
    lines[...] = jnp.dot(lines_ref[...].astype(BF16), mirror(rows).astype(BF16), preferred_element_type=F32)
    for block in range(width // LANES):
        at = pl.ds(block * LANES, LANES)
        own = table.at[block % 2]
        for g in range(packed):
            ring = circulant(lines[block * packed + g : block * packed + g + 1, :], rows)
            own[g * rows : (g + 1) * rows, 0:rows] = jnp.where(above, ring, 0.0).astype(BF16)
            own[g * rows : (g + 1) * rows, rows : 2 * rows] = jnp.where(above, 0.0, ring).astype(BF16)
        window = jnp.concatenate([prev_ref[:, at], cur_ref[:, at]], axis=0)
        product = jnp.dot(own[...], window, preferred_element_type=F32)
        mixed = pick_groups(product, rows, per_group)
        mixed_ref[:, at] = mixed.astype(BF16)
        gated_ref[:, at] = (query_ref[:, at].astype(F32) * mixed).astype(BF16)


def mix_call(lines, prev, cur, query):
    rows, channels = cur.shape
    groups, taps = lines.shape
    per_group = channels // groups
    width = block_width(channels, WIDTH)
    steps = channels // width
    wide = pl.BlockSpec((rows, width), lambda i: (0, i))
    out = jax.ShapeDtypeStruct((rows, channels), BF16)
    return hbm_call(
        functools.partial(mix_kernel, per_group),
        loose=(0, 1),
        grid=(steps,),
        in_specs=[pl.BlockSpec((width // per_group, taps), lambda i: (i, 0)), wide, wide, wide],
        out_specs=[wide, wide],
        out_shape=[out, out],
        scratch_shapes=[
            pltpu.VMEM((2, LANES // per_group * rows, 2 * rows), BF16),
            pltpu.VMEM((width // per_group, taps), F32),
        ],
        compiler_params=params(),
        cost_estimate=cost(0, 2 * rows * channels),
        name="mix",
    )(lines, prev, cur, query)


def gate_kernel(place, gate_grad_ref, query_ref, mixed_ref, grad_ref, feature_ref):
    width = query_ref.shape[1] // place.shape[0]
    for i in range(place.shape[0]):
        at = pl.ds(i * width, width)
        gate_grad = gate_grad_ref[:, pl.ds(pl.multiple_of(place[i] * width, width), width)].astype(F32)
        grad_ref[:, at] = (gate_grad * query_ref[:, at].astype(F32)).astype(BF16)
        feature_ref[:, at] = (gate_grad * mixed_ref[:, at].astype(F32)).astype(BF16)


def gate_call(place, gate_grad, query, mixed):
    rows, channels = query.shape
    out = jax.ShapeDtypeStruct((rows, channels), BF16)
    return hbm_call(
        gate_kernel,
        loose=(0,),
        grid_spec=pltpu.PrefetchScalarGridSpec(
            num_scalar_prefetch=1,
            grid=(2,),
            in_specs=[pl.BlockSpec((rows // 2, channels), lambda i, place: (i, 0))] * 3,
            out_specs=[pl.BlockSpec((rows // 2, channels), lambda i, place: (i, 0))] * 2,
        ),
        out_shape=[out, out],
        compiler_params=params(),
        cost_estimate=cost(2 * rows * channels, 10 * rows * channels),
        name="gate_back",
    )(place, gate_grad, query, mixed)


def tap_sums(short_taps, grad, tokens_ref, rim_ref, out_ref, at, ext):
    rows = tokens_ref.shape[0]
    extend(ext, rim_ref, tokens_ref[:, at], at)
    grad = grad.astype(F32)
    for tap in range(short_taps):
        out_ref[tap : tap + 1, at] = jnp.sum(grad * ext[RIM - tap : RIM - tap + rows, :], axis=0, keepdims=True)
    out_ref[short_taps:8, at] = jnp.zeros((8 - short_taps, LANES), F32)


def long_grad_kernel(
    per_group, short_taps, prev_ref, cur_ref, grad_ref, feature_ref, tokens_ref, rim_ref, long_ref, short_ref, fold, masked, ext
):
    rows, width = cur_ref.shape
    row, lane = lane_row((rows, rows))
    above = lane > row
    member = lax.broadcasted_iota(jnp.int32, (rows, LANES), 1)
    packed = LANES // per_group
    sums = []
    for block in range(width // LANES):
        at = pl.ds(block * LANES, LANES)
        window = jnp.concatenate([prev_ref[:, at], cur_ref[:, at]], axis=0)
        grad_wide = grad_ref[:, at].astype(F32)
        own = masked.at[block % 2]
        for g in range(packed):
            own[g * rows : (g + 1) * rows, :] = jnp.where((member >= g * per_group) & (member < (g + 1) * per_group), grad_wide, 0.0).astype(BF16)
        pairs = lax.dot_general(own[...], window, (((1,), (1,)), ((), ())), preferred_element_type=F32)
        for g in range(packed):
            pair = pairs[g * rows : (g + 1) * rows]
            ring = jnp.where(above, pair[:, 0:rows], pair[:, rows : 2 * rows])
            total = ring[0:8]
            for tile in range(1, rows // 8):
                total = total + pltpu.roll(ring[8 * tile : 8 * tile + 8], rows - 8 * tile, 1)
            fold[block % 2, g * 8 : (g + 1) * 8, :] = total
        total = fold[block % 2, pl.ds(0, packed, stride=8), :]
        for step in range(1, 8):
            total = total + pltpu.roll(fold[block % 2, pl.ds(step, packed, stride=8), :], rows - step, 1)
        sums.append(total)
        tap_sums(short_taps, feature_ref[:, at], tokens_ref, rim_ref, short_ref, at, ext.at[block % 2])
    long_ref[...] = jnp.dot(
        jnp.concatenate(sums, axis=0), mirror(rows), precision=lax.Precision.HIGHEST, preferred_element_type=F32
    )


def long_grad_call(groups, short_taps, prev, cur, grad, feature, tokens, rim):
    rows, channels = cur.shape
    per_group = channels // groups
    width = block_width(channels, WIDTH)
    steps = channels // width
    wide = pl.BlockSpec((rows, width), lambda i: (0, i))
    packed = LANES // per_group
    return hbm_call(
        functools.partial(long_grad_kernel, per_group, short_taps),
        grid=(steps,),
        in_specs=[wide] * 5 + [pl.BlockSpec((RIM, width), lambda i: (0, i))],
        out_specs=[
            pl.BlockSpec((width // per_group, rows), lambda i: (i, 0)),
            pl.BlockSpec((8, width), lambda i: (0, i)),
        ],
        out_shape=[
            jax.ShapeDtypeStruct((groups, rows), F32),
            jax.ShapeDtypeStruct((8, channels), F32),
        ],
        scratch_shapes=[
            pltpu.VMEM((2, packed * 8, LANES), F32),
            pltpu.VMEM((2, packed * rows, LANES), BF16),
            pltpu.VMEM((2, RIM + rows, LANES), F32),
        ],
        compiler_params=params(),
        cost_estimate=cost(2 * groups * rows * 2 * rows * LANES, 10 * rows * channels),
        name="long_grad",
    )(prev, cur, grad, feature, tokens, rim)


def unmix_kernel(
    per_group, short_taps, lines_ref, grad_ref, next_ref, key_ref, value_ref, key_tokens_ref, value_tokens_ref,
    key_rim_ref, value_rim_ref, query_grad_ref, feature_ref, key_sum_ref, value_sum_ref, edge_ref, table, ext,
):
    rows, width = grad_ref.shape
    row, lane = lane_row((rows, rows))
    below = lane < row
    packed = LANES // per_group
    edge_ref[0] = query_grad_ref[0:RIM, :]
    for block in range(width // LANES):
        at = pl.ds(block * LANES, LANES)
        own = table.at[block % 2]
        for g in range(packed):
            ring = circulant(lines_ref[block * packed + g : block * packed + g + 1, :], rows)
            own[g * rows : (g + 1) * rows, 0:rows] = jnp.where(below, 0.0, ring).astype(BF16)
            own[g * rows : (g + 1) * rows, rows : 2 * rows] = jnp.where(below, ring, 0.0).astype(BF16)
        window = jnp.concatenate([grad_ref[:, at], next_ref[:, at]], axis=0)
        product = jnp.dot(own[...], window, preferred_element_type=F32)
        grad_mixer = pick_groups(product, rows, per_group)
        key_grad = (grad_mixer * value_ref[:, at].astype(F32)).astype(BF16)
        value_grad = (grad_mixer * key_ref[:, at].astype(F32)).astype(BF16)
        feature_ref[0, :, at] = key_grad
        feature_ref[1, :, at] = value_grad
        edge_ref[1, :, at] = key_grad[0:RIM]
        edge_ref[2, :, at] = value_grad[0:RIM]
        slot = 2 * (block % 2)
        tap_sums(short_taps, key_grad, key_tokens_ref, key_rim_ref, key_sum_ref, at, ext.at[slot])
        tap_sums(short_taps, value_grad, value_tokens_ref, value_rim_ref, value_sum_ref, at, ext.at[slot + 1])


def unmix_call(lines, short_taps, grad, grad_next, key, value, tokens, rim, query_grad):
    rows, channels = grad.shape
    per_group = channels // lines.shape[0]
    width = block_width(channels, WIDTH)
    steps = channels // width

    def spec(height, part):
        return pl.BlockSpec((height, width), lambda i, part=part: (0, i + part * steps))

    wide = spec(rows, 0)
    sums = jax.ShapeDtypeStruct((8, channels), F32)
    return hbm_call(
        functools.partial(unmix_kernel, per_group, short_taps),
        loose=(0, 2),
        grid=(steps,),
        in_specs=[pl.BlockSpec((width // per_group, rows), lambda i: (i, 0))]
        + [wide] * 4
        + [spec(rows, 1), spec(rows, 2), spec(RIM, 1), spec(RIM, 2), spec(2 * RIM, 0)],
        out_specs=[
            pl.BlockSpec((2, rows, width), lambda i: (0, 0, i)),
            spec(8, 0),
            spec(8, 0),
            pl.BlockSpec((3, RIM, width), lambda i: (0, 0, i)),
        ],
        out_shape=[
            jax.ShapeDtypeStruct((2, rows, channels), BF16),
            sums,
            sums,
            jax.ShapeDtypeStruct((3, RIM, channels), BF16),
        ],
        scratch_shapes=[
            pltpu.VMEM((2, LANES // per_group * rows, 2 * rows), BF16),
            pltpu.VMEM((4, RIM + rows, LANES), F32),
        ],
        compiler_params=params(),
        cost_estimate=cost(2 * channels * rows * 2 * rows * LANES // per_group, 16 * rows * channels),
        name="unmix",
    )(lines, grad, grad_next, key, value, tokens, tokens, rim, rim, query_grad)


def short_adjoint_kernel(short_taps, grads_ref, rim_ref, filter_ref, *refs):
    out_ref, ext = refs[-2:]
    rows, width = out_ref.shape
    for block in range(width // LANES):
        at = pl.ds(block * LANES, LANES)
        own = ext.at[block % 2]
        own[0:rows, :] = grads_ref[0, :, at].astype(F32)
        own[rows:, :] = rim_ref[0, :, at].astype(F32)
        taps = filter_ref[:, at]
        total = taps[0:1] * own[0:rows, :]
        for tap in range(1, short_taps):
            total = total + taps[tap : tap + 1] * own[tap : tap + rows, :]
        out_ref[:, at] = total.astype(BF16)


def short_adjoint_call(grads, rim, filters, first, out):
    parts, rows, channels = grads.shape
    short_taps = filters.shape[0]
    width = block_width(channels, 2 * WIDTH)
    steps = channels // width
    result = pl.BlockSpec((rows, width), lambda p, i: (0, (p + first) * steps + i))
    given = [] if out is None else [out]
    return hbm_call(
        functools.partial(short_adjoint_kernel, short_taps),
        loose=(1,),
        grid=(parts, steps),
        in_specs=[
            pl.BlockSpec((1, rows, width), lambda p, i: (p, 0, i)),
            pl.BlockSpec((1, RIM, width), lambda p, i: (p + first, 0, i)),
            pl.BlockSpec((short_taps, width), lambda p, i: (0, (p + first) * steps + i)),
        ]
        + [pl.BlockSpec(memory_space=pl.ANY)] * len(given),
        out_specs=result,
        out_shape=jax.ShapeDtypeStruct((rows, 3 * channels), BF16),
        input_output_aliases={3: 0} if given else {},
        scratch_shapes=[pltpu.VMEM((2, rows + RIM, LANES), F32)],
        compiler_params=params(),
        cost_estimate=cost(2 * parts * short_taps * rows * channels, 4 * parts * rows * channels),
        name="short_adjoint",
    )(grads, rim, filters, *given)


def spread_kernel(place, query_ref, key_ref, value_ref, long_ref, own_ref, other_ref):
    steps = query_ref.shape[1] // LANES
    half = own_ref.shape[0]
    tiles = [ref[:, i * LANES : (i + 1) * LANES] for ref in (query_ref, key_ref, value_ref) for i in range(steps)]
    tiles += [long_ref[8 * i : 8 * i + 8, :] for i in range(long_ref.shape[0] // 8)]
    first = place[0] < half

    @pl.when(first)
    def _():
        for i in range(half):
            own_ref[place[i]] = tiles[i]
            other_ref[place[half + i] - half] = tiles[half + i]

    @pl.when(jnp.logical_not(first))
    def _():
        for i in range(half):
            other_ref[place[i] - half] = tiles[i]
            own_ref[place[half + i]] = tiles[half + i]


def collect_kernel(place, *refs):
    parts, short_ref, long_ref, tiles_ref = refs[:-3], refs[-3], refs[-2], refs[-1]
    short_taps, wide = short_ref.shape
    steps = wide // LANES
    size = parts[0].shape[0]
    for i, part in enumerate(parts):
        tiles_ref[i * size : (i + 1) * size] = part[...]
    for i in range(steps):
        short_ref[:, i * LANES : (i + 1) * LANES] = tiles_ref[place[i]][0:short_taps, :]
    for i in range(long_ref.shape[0] // 8):
        long_ref[8 * i : 8 * i + 8, :] = tiles_ref[place[steps + i]]


def in_vmem():
    return pl.BlockSpec(memory_space=pltpu.VMEM)


def total_over_devices(spread_to, collect_from, query_sum, key_sum, value_sum, long_sum, short_taps, beside):
    ny, nz = lax.axis_size("y"), lax.axis_size("z")
    channels = query_sum.shape[1]
    count = 3 * channels // LANES + long_sum.shape[0] // 8
    half = jax.ShapeDtypeStruct((count // 2, 8, LANES), F32)
    own, other = pl.pallas_call(
        spread_kernel,
        in_specs=[pl.BlockSpec(memory_space=pltpu.SMEM)] + [in_vmem()] * 4,
        out_specs=[in_vmem()] * 2,
        out_shape=[half] * 2,
        compiler_params=params(),
        name="spread",
    )(spread_to, query_sum, key_sum, value_sum, long_sum)
    part = own + move(other, c=1)
    size = count // 2 // nz
    part = sum([move(part[d * size : (d + 1) * size], z=d) for d in range(1, nz)], part[:size])
    terms, beside = lax.optimization_barrier(([part] + [move(part, y=d) for d in range(1, ny)], beside))
    whole = paired_sum(terms)
    whole = paired_sum([move(whole, xl=a, xh=b) for a, b in FLIPS])
    line = jnp.concatenate([whole, move(whole, c=1)], axis=0)
    lines = [move(line, z=-d) for d in range(nz)]
    groups, taps = long_sum.shape
    short, long = pl.pallas_call(
        collect_kernel,
        in_specs=[pl.BlockSpec(memory_space=pltpu.SMEM)] + [in_vmem()] * nz,
        out_specs=[in_vmem(), in_vmem()],
        scratch_shapes=[pltpu.VMEM((count, 8, LANES), F32)],
        out_shape=[
            jax.ShapeDtypeStruct((short_taps, 3 * channels), F32),
            jax.ShapeDtypeStruct((groups, taps), F32),
        ],
        compiler_params=params(),
        name="collect",
    )(collect_from, *lines)
    return short, long, beside


def paired_sum(terms):
    half = len(terms) // 2
    if half == 0:
        return terms[0]
    return paired_sum([terms[i] + terms[i + half] for i in range(half)])


def gather_tall(shard):
    return [move(shard[shard.shape[0] // 2 :], y=d) for d in range(lax.axis_size("y"))]


def gather_wide(shard):
    return [move(shard[: shard.shape[0] // 2], xl=a, xh=b) for a, b in FLIPS]


def gather_far(wide_top, tall_bottom):
    ny = lax.axis_size("y")
    wide_top, tall_bottom = jnp.stack(wide_top), jnp.stack(tall_bottom)
    return (
        [move(wide_top, y=d) for d in range(ny)],
        [move(tall_bottom, xl=a, xh=b) for a, b in FLIPS],
    )


def piece_rows(tops, bottoms, step):
    rows = []
    for a in range(2):
        rows.append(jnp.concatenate([tops[step][2 * a + b] for b in range(2)], axis=1))
        rows.append(jnp.concatenate([bottoms[2 * a + b][step] for b in range(2)], axis=1))
    return rows


def gate_matmul_kernel(ny, *refs):
    cotangent_ref, tops, bottoms, out_ref = refs[0], refs[1 : 1 + ny], refs[1 + ny : 5 + ny], refs[5 + ny]
    left = cotangent_ref[...]
    at = 0
    for step in range(ny):
        for right in piece_rows(tops, bottoms, step):
            size = right.shape[0]
            out_ref[:, at : at + size] = lax.dot_general(
                left, right, (((1,), (1,)), ((), ())), preferred_element_type=F32
            ).astype(BF16)
            at += size


def whole(x):
    return pl.BlockSpec(x.shape, lambda *_, n=x.ndim: (0,) * n)


def gate_matmul(cotangents, tops, bottoms):
    rows, depth = cotangents.shape
    ny = len(tops)
    channels = 4 * ny * tops[0].shape[1]
    height = rows // 2
    return hbm_call(
        functools.partial(gate_matmul_kernel, ny),
        loose=range(5 + ny),
        grid=(rows // height,),
        in_specs=[pl.BlockSpec((height, depth), lambda i: (i, 0))] + [whole(x) for x in (*tops, *bottoms)],
        out_specs=pl.BlockSpec((height, channels), lambda i: (i, 0)),
        out_shape=jax.ShapeDtypeStruct((rows, channels), BF16),
        compiler_params=params(32),
        cost_estimate=cost(2 * rows * depth * channels, 2 * (rows + depth) * channels),
        name="gate_matmul",
    )(cotangents, *tops, *bottoms)


def picked(origin, step, rows_ref):
    height = rows_ref.shape[1] // 2
    at = [pl.multiple_of(origin[2 * step + a] % 2 * height, height) for a in range(2)]
    return jnp.concatenate([rows_ref[:, pl.ds(x, height)] for x in at], axis=1)


def weight_grad_kernel(ny, origin, rows_ref, turned_ref, *refs):
    top_grads, bottom_grads = refs[:ny], refs[ny:]
    step = pl.program_id(0)
    size = bottom_grads[0].shape[2]
    width = bottom_grads[0].shape[1]
    rows = picked(origin, step, rows_ref)
    grads = jnp.dot(turned_ref[...], rows, preferred_element_type=F32).astype(BF16)
    for f in range(4):
        a, b = f // 2, f % 2
        at = (2 * a + 1) * size
        bottom_grads[f][step] = grads[b * width : (b + 1) * width, at : at + size]
    for d in range(ny):

        @pl.when(step == d)
        def _(d=d):
            for f in range(4):
                a, b = f // 2, f % 2
                at = 2 * a * size
                top_grads[d][f] = grads[b * width : (b + 1) * width, at : at + size]


def rows_of(origin, all_rows, ny):
    rows, channels = all_rows.shape
    return pl.BlockSpec((rows, channels // ny), lambda i, origin: (0, origin[2 * i] // 2))


def weight_grad(origin, all_rows, turned, ny):
    rows, channels = all_rows.shape
    size = channels // (4 * ny)
    width = turned.shape[0] // 2
    outs = [jax.ShapeDtypeStruct((4, width, size), BF16)] * ny + [jax.ShapeDtypeStruct((ny, width, size), BF16)] * 4
    results = hbm_call(
        functools.partial(weight_grad_kernel, ny),
        loose=(0, 2),
        grid_spec=pltpu.PrefetchScalarGridSpec(
            num_scalar_prefetch=1,
            grid=(ny,),
            in_specs=[rows_of(origin, all_rows, ny), whole(turned)],
            out_specs=[whole(x) for x in outs],
        ),
        out_shape=outs,
        compiler_params=params(40),
        cost_estimate=cost(4 * rows * width * channels, 2 * (rows + 2 * width) * channels),
        name="weight_grad",
    )(origin, all_rows, turned)
    return results[:ny], results[ny:]


def output_kernel(ny, origin, rows_ref, *refs):
    tops, bottoms, own_ref, other_ref, total = refs[:ny], refs[ny : ny + 4], refs[-3], refs[-2], refs[-1]
    step = pl.program_id(0)
    width = own_ref.shape[1]
    rows = picked(origin, step, rows_ref)
    for d in range(ny):

        @pl.when(step == d)
        def _(d=d):
            right = jnp.concatenate(piece_rows(tops, bottoms, d), axis=0)
            product = jnp.dot(rows, right, preferred_element_type=F32)
            if d == 0:
                total[...] = product
            else:
                total[...] += product

    @pl.when(step == ny - 1)
    def _():
        own_ref[...] = total[:, :width].astype(BF16)
        other_ref[...] = total[:, width:].astype(BF16)


def output_call(origin, all_rows, tops, bottoms):
    rows, channels = all_rows.shape
    ny = len(tops)
    width = tops[0].shape[2]
    half = jax.ShapeDtypeStruct((rows, width), BF16)
    return hbm_call(
        functools.partial(output_kernel, ny),
        loose=(0, *range(2, 6 + ny)),
        grid_spec=pltpu.PrefetchScalarGridSpec(
            num_scalar_prefetch=1,
            grid=(ny,),
            in_specs=[rows_of(origin, all_rows, ny)] + [whole(x) for x in (*tops, *bottoms)],
            out_specs=[whole(half)] * 2,
            scratch_shapes=[pltpu.VMEM((rows, 2 * width), F32)],
        ),
        out_shape=[half, half],
        compiler_params=params(32),
        cost_estimate=cost(4 * rows * width * channels, 2 * (rows + 2 * width) * channels),
        name="output",
    )(origin, all_rows, *tops, *bottoms)


def added(terms):
    total = terms[0].astype(F32)
    for term in terms[1:]:
        total = total + term.astype(F32)
    return total


def plane_scatter(top_grads, bottom_grads, beside):
    ny = len(top_grads)
    top = added([move(top_grads[d], y=-d) for d in range(ny)]).astype(BF16)
    bottom = added([move(bottom_grads[f], xl=a, xh=b) for f, (a, b) in enumerate(FLIPS)]).astype(BF16)
    top, bottom, beside = lax.optimization_barrier((top, bottom, beside))
    top = [move(top[f], xl=a, xh=b) for f, (a, b) in enumerate(FLIPS)]
    bottom = [move(bottom[d], y=-d) for d in range(ny)]
    return top, bottom, beside


def shards(tokens_in, short_filter, long_filter, out_weight, cotangent):
    ny, nz = lax.axis_size("y"), lax.axis_size("z")
    y, xl, xh, z, c = (lax.axis_index(a) for a in ("y", "xl", "xh", "z", "c"))
    tokens = tokens_in[0]
    rows, wide = tokens.shape
    channels = wide // 3
    short_taps = short_filter.shape[0]
    groups = long_filter.shape[0]
    upstream = cotangent[0]
    length, columns = upstream.shape
    span = length // 2

    block = jnp.arange(2 * ny, dtype=jnp.int32)
    place = ((y - block // 2) % ny) * 2 + (block + xl) % 2
    origin = place
    size = 3 * channels // LANES + groups // 8
    each = size // (2 * nz)
    tile = jnp.arange(size, dtype=jnp.int32)
    core_step, z_step = (tile // (nz * each) + c) % 2, (tile // each - z) % nz
    spread_to = (core_step * nz + z_step) * each + tile % each
    collect_from = (z_step * 2 + core_step) * each + tile % each

    rim = along(tokens[rows - RIM :], 1)
    lines = long_filter.astype(F32)
    parts = features_call(tokens, short_filter)
    parts, rim = lax.optimization_barrier((parts, rim))
    query, key, value, mixer = features_call(tokens, short_filter, rim, parts)
    mixer, out_weight = lax.optimization_barrier((mixer, out_weight))
    mixer_prev = along(mixer, 1)
    wide_top = gather_wide(out_weight)
    mixer_prev, wide_top = lax.optimization_barrier((mixer_prev, wide_top))
    mixed, gated = mix_call(lines, mixer_prev, mixer, query)
    mixed, out_weight, wide_top, upstream = lax.optimization_barrier((mixed, out_weight, wide_top, upstream))
    tall_bottom = gather_tall(out_weight)
    all_rows = lax.all_gather(gated, ("z", "c"), axis=0, tiled=True)
    tops, bottoms = gather_far(wide_top, tall_bottom)
    mine = lax.dynamic_slice_in_dim(upstream, xh * span, span, 0)
    others = move(lax.dynamic_slice_in_dim(upstream, (1 - xh) * span, span, 0), xh=1)
    cotangents = jnp.concatenate([mine, others], axis=1)
    partial = gate_matmul(cotangents, tops, bottoms)
    partial, all_rows = lax.optimization_barrier((partial, all_rows))
    gate_grad = lax.psum_scatter(partial, ("z", "c"), scatter_dimension=0, tiled=True)

    top_grads, bottom_grads = weight_grad(origin, all_rows, cotangents.T, ny)
    own, other = output_call(origin, all_rows, tops, bottoms)
    top, bottom, other = plane_scatter(top_grads, bottom_grads, other)
    gate_grad, top, bottom, other = lax.optimization_barrier((gate_grad, top, bottom, other))

    grad_mixed, query_grad = gate_call(place, gate_grad, query, mixed)
    grad_next = along(grad_mixed, -1)
    long_sum, query_sum = long_grad_call(
        groups, short_taps, mixer_prev, mixer, grad_mixed, query_grad, tokens, rim
    )
    grad_weight = jnp.concatenate([added(top), added(bottom)], axis=1).T
    theirs = move(other, xh=1)
    grad_next, grad_weight = lax.optimization_barrier((grad_next, grad_weight))
    other_grads, key_sum, value_sum, edge = unmix_call(
        lines, short_taps, grad_mixed, grad_next, key, value, tokens, rim, query_grad
    )
    edge, key_sum, theirs = lax.optimization_barrier((edge, key_sum, theirs))
    edge = along(edge, -1)
    output = jnp.where(xh == 0, jnp.concatenate([own, theirs], axis=0), jnp.concatenate([theirs, own], axis=0))
    grad_tokens = short_adjoint_call(query_grad[None], edge, short_filter, 0, None)
    grad_short, grad_long, grad_tokens = total_over_devices(
        spread_to, collect_from, query_sum, key_sum, value_sum, long_sum, short_taps, grad_tokens
    )
    grad_tokens = short_adjoint_call(other_grads, edge, short_filter, 1, grad_tokens)
    return output[None], grad_tokens[None], grad_short, grad_long, grad_weight


def solution(mesh):
    dp, seq = mesh.shape["dp"], mesh.shape["seq"]
    grid = jax.sharding.Mesh(mesh.devices.reshape(dp // 2, 2, 2, seq // 4, 2), ("y", "xl", "xh", "z", "c"))
    rows, line = ("y", "xl"), ("xh", "z", "c")
    return jax.shard_map(
        shards,
        mesh=grid,
        in_specs=(P(rows, line, None), P(), P(), P(rows, line), P(rows, None, line)),
        out_specs=(P(rows, None, line), P(rows, line, None), P(), P(), P(rows, line)),
        check_vma=False,
    )
```

```python
import functools
import itertools
import math

import jax
import jax.numpy as jnp
from jax import lax
from jax.experimental import pallas as pl
from jax.experimental.pallas import tpu as pltpu
from jax.sharding import PartitionSpec as P

LANES = 128
RIM = 8
MIB = 1024 * 1024
WIDTH = 1024
F32 = jnp.float32
BF16 = jnp.bfloat16


PLANE = ("y", "xl", "xh")
LINE = ("xh", "z", "c")


def along(x, by):
    size = math.prod(lax.axis_size(a) for a in LINE)
    pairs = [(i, i + by) for i in range(size) if 0 <= i + by < size]
    return lax.ppermute(x, LINE, pairs)


def move(x, **steps):
    axes = tuple(a for a in ("y", "xl", "xh", "z", "c") if steps.get(a, 0) % lax.axis_size(a))
    if not axes:
        return x
    sizes = [lax.axis_size(a) for a in axes]
    pairs = []
    for at in itertools.product(*(range(n) for n in sizes)):
        to = [(p + steps[a]) % n for p, a, n in zip(at, axes, sizes)]
        pairs.append((flat(at, sizes), flat(to, sizes)))
    return lax.ppermute(x, axes, pairs)


def flat(at, sizes):
    index = 0
    for p, n in zip(at, sizes):
        index = index * n + p
    return index


FLIPS = [(0, 0), (0, 1), (1, 0), (1, 1)]


def params(mib=16):
    return pltpu.CompilerParams(vmem_limit_bytes=mib * MIB)


def hbm_call(kernel, *, out_shape, loose=(), **options):
    single = not isinstance(out_shape, (list, tuple))
    shapes = [out_shape] if single else out_shape
    placed = [pltpu.HBM(x.shape, x.dtype) if x.size * x.dtype.itemsize > 256 * 1024 else x for x in shapes]
    call = pl.pallas_call(kernel, out_shape=placed[0] if single else placed, **options)

    def run(*args):
        held = [x if i in loose else pltpu.with_memory_space_constraint(x, pltpu.HBM) for i, x in enumerate(args)]
        return call(*held)

    return run


def cost(flops, moved):
    return pl.CostEstimate(flops=int(flops), bytes_accessed=int(moved), transcendentals=0)


def block_width(channels, most):
    width = min(channels, most)
    while channels % width:
        width //= 2
    return width


def extend(ext, rim, rows_of, at):
    ext[0:RIM, :] = jnp.zeros((RIM, LANES), F32) if rim is None else rim[:, at].astype(F32)
    ext[RIM:, :] = rows_of.astype(F32)


def features_kernel(short_taps, tokens, rims, filters, query_ref, key_ref, value_ref, mixer_ref, ext):
    rows, width = tokens[0].shape

    def filtered(part, block, at):
        own = ext.at[(3 * block + part) % ext.shape[0]]
        extend(own, rims and rims[part], tokens[part][:, at], at)
        taps = filters[part][:, at]
        total = taps[0:1] * own[RIM : RIM + rows, :]
        for tap in range(1, short_taps):
            total = total + taps[tap : tap + 1] * own[RIM - tap : RIM - tap + rows, :]
        return total

    for block in range(width // LANES):
        at = pl.ds(block * LANES, LANES)
        query_ref[:, at] = filtered(0, block, at).astype(BF16)
        key, value = filtered(1, block, at), filtered(2, block, at)
        key_ref[:, at] = key.astype(BF16)
        value_ref[:, at] = value.astype(BF16)
        mixer_ref[:, at] = (key * value).astype(BF16)


def features_call(tokens, filters, rim=None, given=None):
    rows, wide = tokens.shape
    channels = wide // 3
    taps = filters.shape[0]
    rows = rows if given is None else 2 * RIM
    width = channels if given else block_width(channels, WIDTH)
    steps = channels // width

    def spec(height, part):
        return pl.BlockSpec((height, width), lambda i, part=part: (0, i + part * steps))

    held = [] if given is None else [rim] * 3
    olds = [] if given is None else list(given)

    def body(*refs):
        n = 3 + len(held)
        rims = refs[3:n] if held else None
        features_kernel(taps, refs[0:3], rims, refs[n : n + 3], *refs[n + 3 + len(olds) :])

    out = jax.ShapeDtypeStruct((tokens.shape[0], channels), BF16)
    return hbm_call(
        body,
        loose=(3, 4, 5) if held else (),
        grid=(steps,),
        in_specs=[spec(rows, p) for p in range(3)]
        + [spec(RIM, p) for p in range(len(held))]
        + [spec(taps, p) for p in range(3)]
        + [pl.BlockSpec(memory_space=pl.ANY)] * len(olds),
        out_specs=[pl.BlockSpec((rows, width), lambda i: (0, i))] * 4,
        out_shape=[out] * 4,
        input_output_aliases={9 + i: i for i in range(len(olds))},
        scratch_shapes=[pltpu.VMEM((6, RIM + rows, LANES), F32)],
        compiler_params=params(),
        cost_estimate=cost(0, rows * wide),
        name="features" if given is None else "first_rows",
    )(*[tokens] * 3, *held, *[filters] * 3, *olds)


def lane_row(shape):
    row = lax.broadcasted_iota(jnp.int32, shape, 0)
    lane = lax.broadcasted_iota(jnp.int32, shape, 1)
    return row, lane


def mirror(size):
    row, lane = lane_row((size, size))
    both = row + lane
    return jnp.where((both == 0) | (both == size), 1.0, 0.0)


def circulant(line, taps):
    wide = jnp.broadcast_to(line.astype(F32), (taps, taps))
    return pltpu.roll(wide, 0, 1, stride=1, stride_axis=0)


def pick_groups(product, rows, per_group):
    lane = lax.broadcasted_iota(jnp.int32, (rows, LANES), 1)
    total = product[0:rows]
    for g in range(1, LANES // per_group):
        total = jnp.where(lane >= g * per_group, product[g * rows : (g + 1) * rows], total)
    return total


def mix_kernel(per_group, lines_ref, prev_ref, cur_ref, query_ref, mixed_ref, gated_ref, table, lines):
    rows, width = cur_ref.shape
    row, lane = lane_row((rows, rows))
    above = lane > row
    packed = LANES // per_group
    lines[...] = jnp.dot(lines_ref[...].astype(BF16), mirror(rows).astype(BF16), preferred_element_type=F32)
    for block in range(width // LANES):
        at = pl.ds(block * LANES, LANES)
        own = table.at[block % 2]
        for g in range(packed):
            ring = circulant(lines[block * packed + g : block * packed + g + 1, :], rows)
            own[g * rows : (g + 1) * rows, 0:rows] = jnp.where(above, ring, 0.0).astype(BF16)
            own[g * rows : (g + 1) * rows, rows : 2 * rows] = jnp.where(above, 0.0, ring).astype(BF16)
        window = jnp.concatenate([prev_ref[:, at], cur_ref[:, at]], axis=0)
        product = jnp.dot(own[...], window, preferred_element_type=F32)
        mixed = pick_groups(product, rows, per_group)
        mixed_ref[:, at] = mixed.astype(BF16)
        gated_ref[:, at] = (query_ref[:, at].astype(F32) * mixed).astype(BF16)


def mix_call(lines, prev, cur, query):
    rows, channels = cur.shape
    groups, taps = lines.shape
    per_group = channels // groups
    width = block_width(channels, WIDTH)
    steps = channels // width
    wide = pl.BlockSpec((rows, width), lambda i: (0, i))
    out = jax.ShapeDtypeStruct((rows, channels), BF16)
    return hbm_call(
        functools.partial(mix_kernel, per_group),
        loose=(0, 1),
        grid=(steps,),
        in_specs=[pl.BlockSpec((width // per_group, taps), lambda i: (i, 0)), wide, wide, wide],
        out_specs=[wide, wide],
        out_shape=[out, out],
        scratch_shapes=[
            pltpu.VMEM((2, LANES // per_group * rows, 2 * rows), BF16),
            pltpu.VMEM((width // per_group, taps), F32),
        ],
        compiler_params=params(),
        cost_estimate=cost(0, 2 * rows * channels),
        name="mix",
    )(lines, prev, cur, query)


def gate_kernel(place, gate_grad_ref, query_ref, mixed_ref, grad_ref, feature_ref):
    width = query_ref.shape[1] // place.shape[0]
    for i in range(place.shape[0]):
        at = pl.ds(i * width, width)
        gate_grad = gate_grad_ref[:, pl.ds(pl.multiple_of(place[i] * width, width), width)].astype(F32)
        grad_ref[:, at] = (gate_grad * query_ref[:, at].astype(F32)).astype(BF16)
        feature_ref[:, at] = (gate_grad * mixed_ref[:, at].astype(F32)).astype(BF16)


def gate_call(place, gate_grad, query, mixed):
    rows, channels = query.shape
    out = jax.ShapeDtypeStruct((rows, channels), BF16)
    return hbm_call(
        gate_kernel,
        loose=(0,),
        grid_spec=pltpu.PrefetchScalarGridSpec(
            num_scalar_prefetch=1,
            grid=(2,),
            in_specs=[pl.BlockSpec((rows // 2, channels), lambda i, place: (i, 0))] * 3,
            out_specs=[pl.BlockSpec((rows // 2, channels), lambda i, place: (i, 0))] * 2,
        ),
        out_shape=[out, out],
        compiler_params=params(),
        cost_estimate=cost(2 * rows * channels, 10 * rows * channels),
        name="gate_back",
    )(place, gate_grad, query, mixed)


def tap_sums(short_taps, grad, tokens_ref, rim_ref, out_ref, at, ext):
    rows = tokens_ref.shape[0]
    extend(ext, rim_ref, tokens_ref[:, at], at)
    grad = grad.astype(F32)
    for tap in range(short_taps):
        out_ref[tap : tap + 1, at] = jnp.sum(grad * ext[RIM - tap : RIM - tap + rows, :], axis=0, keepdims=True)
    out_ref[short_taps:8, at] = jnp.zeros((8 - short_taps, LANES), F32)


def long_grad_kernel(
    per_group, short_taps, prev_ref, cur_ref, grad_ref, feature_ref, tokens_ref, rim_ref, long_ref, short_ref, fold, masked, ext
):
    rows, width = cur_ref.shape
    row, lane = lane_row((rows, rows))
    above = lane > row
    member = lax.broadcasted_iota(jnp.int32, (rows, LANES), 1)
    packed = LANES // per_group
    sums = []
    for block in range(width // LANES):
        at = pl.ds(block * LANES, LANES)
        window = jnp.concatenate([prev_ref[:, at], cur_ref[:, at]], axis=0)
        grad_wide = grad_ref[:, at].astype(F32)
        own = masked.at[block % 2]
        for g in range(packed):
            own[g * rows : (g + 1) * rows, :] = jnp.where((member >= g * per_group) & (member < (g + 1) * per_group), grad_wide, 0.0).astype(BF16)
        pairs = lax.dot_general(own[...], window, (((1,), (1,)), ((), ())), preferred_element_type=F32)
        for g in range(packed):
            pair = pairs[g * rows : (g + 1) * rows]
            ring = jnp.where(above, pair[:, 0:rows], pair[:, rows : 2 * rows])
            total = ring[0:8]
            for tile in range(1, rows // 8):
                total = total + pltpu.roll(ring[8 * tile : 8 * tile + 8], rows - 8 * tile, 1)
            fold[block % 2, g * 8 : (g + 1) * 8, :] = total
        total = fold[block % 2, pl.ds(0, packed, stride=8), :]
        for step in range(1, 8):
            total = total + pltpu.roll(fold[block % 2, pl.ds(step, packed, stride=8), :], rows - step, 1)
        sums.append(total)
        tap_sums(short_taps, feature_ref[:, at], tokens_ref, rim_ref, short_ref, at, ext.at[block % 2])
    long_ref[...] = jnp.dot(
        jnp.concatenate(sums, axis=0), mirror(rows), precision=lax.Precision.HIGHEST, preferred_element_type=F32
    )


def long_grad_call(groups, short_taps, prev, cur, grad, feature, tokens, rim):
    rows, channels = cur.shape
    per_group = channels // groups
    width = block_width(channels, WIDTH)
    steps = channels // width
    wide = pl.BlockSpec((rows, width), lambda i: (0, i))
    packed = LANES // per_group
    return hbm_call(
        functools.partial(long_grad_kernel, per_group, short_taps),
        grid=(steps,),
        in_specs=[wide] * 5 + [pl.BlockSpec((RIM, width), lambda i: (0, i))],
        out_specs=[
            pl.BlockSpec((width // per_group, rows), lambda i: (i, 0)),
            pl.BlockSpec((8, width), lambda i: (0, i)),
        ],
        out_shape=[
            jax.ShapeDtypeStruct((groups, rows), F32),
            jax.ShapeDtypeStruct((8, channels), F32),
        ],
        scratch_shapes=[
            pltpu.VMEM((2, packed * 8, LANES), F32),
            pltpu.VMEM((2, packed * rows, LANES), BF16),
            pltpu.VMEM((2, RIM + rows, LANES), F32),
        ],
        compiler_params=params(),
        cost_estimate=cost(2 * groups * rows * 2 * rows * LANES, 10 * rows * channels),
        name="long_grad",
    )(prev, cur, grad, feature, tokens, rim)


def unmix_kernel(
    per_group, short_taps, lines_ref, grad_ref, next_ref, key_ref, value_ref, key_tokens_ref, value_tokens_ref,
    key_rim_ref, value_rim_ref, query_grad_ref, feature_ref, key_sum_ref, value_sum_ref, edge_ref, table, ext,
):
    rows, width = grad_ref.shape
    row, lane = lane_row((rows, rows))
    below = lane < row
    packed = LANES // per_group
    edge_ref[0] = query_grad_ref[0:RIM, :]
    for block in range(width // LANES):
        at = pl.ds(block * LANES, LANES)
        own = table.at[block % 2]
        for g in range(packed):
            ring = circulant(lines_ref[block * packed + g : block * packed + g + 1, :], rows)
            own[g * rows : (g + 1) * rows, 0:rows] = jnp.where(below, 0.0, ring).astype(BF16)
            own[g * rows : (g + 1) * rows, rows : 2 * rows] = jnp.where(below, ring, 0.0).astype(BF16)
        window = jnp.concatenate([grad_ref[:, at], next_ref[:, at]], axis=0)
        product = jnp.dot(own[...], window, preferred_element_type=F32)
        grad_mixer = pick_groups(product, rows, per_group)
        key_grad = (grad_mixer * value_ref[:, at].astype(F32)).astype(BF16)
        value_grad = (grad_mixer * key_ref[:, at].astype(F32)).astype(BF16)
        feature_ref[0, :, at] = key_grad
        feature_ref[1, :, at] = value_grad
        edge_ref[1, :, at] = key_grad[0:RIM]
        edge_ref[2, :, at] = value_grad[0:RIM]
        slot = 2 * (block % 2)
        tap_sums(short_taps, key_grad, key_tokens_ref, key_rim_ref, key_sum_ref, at, ext.at[slot])
        tap_sums(short_taps, value_grad, value_tokens_ref, value_rim_ref, value_sum_ref, at, ext.at[slot + 1])


def unmix_call(lines, short_taps, grad, grad_next, key, value, tokens, rim, query_grad):
    rows, channels = grad.shape
    per_group = channels // lines.shape[0]
    width = block_width(channels, WIDTH)
    steps = channels // width

    def spec(height, part):
        return pl.BlockSpec((height, width), lambda i, part=part: (0, i + part * steps))

    wide = spec(rows, 0)
    sums = jax.ShapeDtypeStruct((8, channels), F32)
    return hbm_call(
        functools.partial(unmix_kernel, per_group, short_taps),
        loose=(0, 2),
        grid=(steps,),
        in_specs=[pl.BlockSpec((width // per_group, rows), lambda i: (i, 0))]
        + [wide] * 4
        + [spec(rows, 1), spec(rows, 2), spec(RIM, 1), spec(RIM, 2), spec(2 * RIM, 0)],
        out_specs=[
            pl.BlockSpec((2, rows, width), lambda i: (0, 0, i)),
            spec(8, 0),
            spec(8, 0),
            pl.BlockSpec((3, RIM, width), lambda i: (0, 0, i)),
        ],
        out_shape=[
            jax.ShapeDtypeStruct((2, rows, channels), BF16),
            sums,
            sums,
            jax.ShapeDtypeStruct((3, RIM, channels), BF16),
        ],
        scratch_shapes=[
            pltpu.VMEM((2, LANES // per_group * rows, 2 * rows), BF16),
            pltpu.VMEM((4, RIM + rows, LANES), F32),
        ],
        compiler_params=params(),
        cost_estimate=cost(2 * channels * rows * 2 * rows * LANES // per_group, 16 * rows * channels),
        name="unmix",
    )(lines, grad, grad_next, key, value, tokens, tokens, rim, rim, query_grad)


def short_adjoint_kernel(short_taps, grads_ref, rim_ref, filter_ref, *refs):
    out_ref, ext = refs[-2:]
    rows, width = out_ref.shape
    for block in range(width // LANES):
        at = pl.ds(block * LANES, LANES)
        own = ext.at[block % 2]
        own[0:rows, :] = grads_ref[0, :, at].astype(F32)
        own[rows:, :] = rim_ref[0, :, at].astype(F32)
        taps = filter_ref[:, at]
        total = taps[0:1] * own[0:rows, :]
        for tap in range(1, short_taps):
            total = total + taps[tap : tap + 1] * own[tap : tap + rows, :]
        out_ref[:, at] = total.astype(BF16)


def short_adjoint_call(grads, rim, filters, given, part, out):
    _, rows, channels = grads.shape
    short_taps = filters.shape[0]
    width = block_width(channels, 2 * WIDTH)
    steps = channels // width
    result = pl.BlockSpec((rows, width), lambda i: (0, part * steps + i))
    olds = [] if out is None else [out]
    return hbm_call(
        functools.partial(short_adjoint_kernel, short_taps),
        loose=(1,),
        grid=(steps,),
        in_specs=[
            pl.BlockSpec((1, rows, width), lambda i: (given, 0, i)),
            pl.BlockSpec((1, RIM, width), lambda i: (part, 0, i)),
            pl.BlockSpec((short_taps, width), lambda i: (0, part * steps + i)),
        ]
        + [pl.BlockSpec(memory_space=pl.ANY)] * len(olds),
        out_specs=result,
        out_shape=jax.ShapeDtypeStruct((rows, 3 * channels), BF16),
        input_output_aliases={3: 0} if olds else {},
        scratch_shapes=[pltpu.VMEM((2, rows + RIM, LANES), F32)],
        compiler_params=params(),
        cost_estimate=cost(2 * short_taps * rows * channels, 4 * rows * channels),
        name="short_adjoint",
    )(grads, rim, filters, *olds)


def spread_kernel(place, query_ref, key_ref, value_ref, long_ref, own_ref, other_ref):
    steps = query_ref.shape[1] // LANES
    half = own_ref.shape[0]
    tiles = [ref[:, i * LANES : (i + 1) * LANES] for ref in (query_ref, key_ref, value_ref) for i in range(steps)]
    tiles += [long_ref[8 * i : 8 * i + 8, :] for i in range(long_ref.shape[0] // 8)]
    first = place[0] < half

    @pl.when(first)
    def _():
        for i in range(half):
            own_ref[place[i]] = tiles[i]
            other_ref[place[half + i] - half] = tiles[half + i]

    @pl.when(jnp.logical_not(first))
    def _():
        for i in range(half):
            other_ref[place[i] - half] = tiles[i]
            own_ref[place[half + i]] = tiles[half + i]


def collect_kernel(place, *refs):
    parts, short_ref, long_ref, tiles_ref = refs[:-3], refs[-3], refs[-2], refs[-1]
    short_taps, wide = short_ref.shape
    steps = wide // LANES
    size = parts[0].shape[0]
    for i, part in enumerate(parts):
        tiles_ref[i * size : (i + 1) * size] = part[...]
    for i in range(steps):
        short_ref[:, i * LANES : (i + 1) * LANES] = tiles_ref[place[i]][0:short_taps, :]
    for i in range(long_ref.shape[0] // 8):
        long_ref[8 * i : 8 * i + 8, :] = tiles_ref[place[steps + i]]


def in_vmem():
    return pl.BlockSpec(memory_space=pltpu.VMEM)


def total_over_devices(spread_to, collect_from, query_sum, key_sum, value_sum, long_sum, short_taps, first, after, last):
    ny, nz = lax.axis_size("y"), lax.axis_size("z")
    channels = query_sum.shape[1]
    count = 3 * channels // LANES + long_sum.shape[0] // 8
    half = jax.ShapeDtypeStruct((count // 2, 8, LANES), F32)
    own, other = pl.pallas_call(
        spread_kernel,
        in_specs=[pl.BlockSpec(memory_space=pltpu.SMEM)] + [in_vmem()] * 4,
        out_specs=[in_vmem()] * 2,
        out_shape=[half] * 2,
        compiler_params=params(),
        name="spread",
    )(spread_to, query_sum, key_sum, value_sum, long_sum)
    part = own + move(other, c=1)
    size = count // 2 // nz
    part = sum([move(part[d * size : (d + 1) * size], z=d) for d in range(1, nz)], part[:size])
    terms, first = lax.optimization_barrier(([part] + [move(part, y=d) for d in range(1, ny)], first))
    whole = paired_sum(terms)
    terms = [move(whole, xl=a, xh=b) for a, b in FLIPS]
    terms, beside, last = lax.optimization_barrier((terms, after(first), last))
    whole = paired_sum(terms)
    line = jnp.concatenate([whole, move(whole, c=1)], axis=0)
    lines = [move(line, z=-d) for d in range(nz)]
    groups, taps = long_sum.shape
    short, long = pl.pallas_call(
        collect_kernel,
        in_specs=[pl.BlockSpec(memory_space=pltpu.SMEM)] + [in_vmem()] * nz,
        out_specs=[in_vmem(), in_vmem()],
        scratch_shapes=[pltpu.VMEM((count, 8, LANES), F32)],
        out_shape=[
            jax.ShapeDtypeStruct((short_taps, 3 * channels), F32),
            jax.ShapeDtypeStruct((groups, taps), F32),
        ],
        compiler_params=params(),
        name="collect",
    )(collect_from, *lines)
    return short, long, beside, last


def paired_sum(terms):
    half = len(terms) // 2
    if half == 0:
        return terms[0]
    return paired_sum([terms[i] + terms[i + half] for i in range(half)])


def gather_tall(shard):
    return [move(shard[shard.shape[0] // 2 :], y=d) for d in range(lax.axis_size("y"))]


def gather_wide(shard):
    return [move(shard[: shard.shape[0] // 2], xl=a, xh=b) for a, b in FLIPS]


def gather_far(wide_top, tall_bottom):
    ny = lax.axis_size("y")
    wide_top, tall_bottom = jnp.stack(wide_top), jnp.stack(tall_bottom)
    return (
        [move(wide_top, y=d) for d in range(ny)],
        [move(tall_bottom, xl=a, xh=b) for a, b in FLIPS],
    )


def piece_rows(tops, bottoms, step):
    rows = []
    for a in range(2):
        rows.append(jnp.concatenate([tops[step][2 * a + b] for b in range(2)], axis=1))
        rows.append(jnp.concatenate([bottoms[2 * a + b][step] for b in range(2)], axis=1))
    return rows


def gate_matmul_kernel(ny, *refs):
    cotangent_ref, tops, bottoms, out_ref = refs[0], refs[1 : 1 + ny], refs[1 + ny : 5 + ny], refs[5 + ny]
    left = cotangent_ref[...]
    at = 0
    for step in range(ny):
        for right in piece_rows(tops, bottoms, step):
            size = right.shape[0]
            out_ref[:, at : at + size] = lax.dot_general(
                left, right, (((1,), (1,)), ((), ())), preferred_element_type=F32
            ).astype(BF16)
            at += size


def whole(x):
    return pl.BlockSpec(x.shape, lambda *_, n=x.ndim: (0,) * n)


def gate_matmul(cotangents, tops, bottoms):
    rows, depth = cotangents.shape
    ny = len(tops)
    channels = 4 * ny * tops[0].shape[1]
    height = rows // 2
    return hbm_call(
        functools.partial(gate_matmul_kernel, ny),
        loose=range(5 + ny),
        grid=(rows // height,),
        in_specs=[pl.BlockSpec((height, depth), lambda i: (i, 0))] + [whole(x) for x in (*tops, *bottoms)],
        out_specs=pl.BlockSpec((height, channels), lambda i: (i, 0)),
        out_shape=jax.ShapeDtypeStruct((rows, channels), BF16),
        compiler_params=params(32),
        cost_estimate=cost(2 * rows * depth * channels, 2 * (rows + depth) * channels),
        name="gate_matmul",
    )(cotangents, *tops, *bottoms)


def picked(origin, step, rows_ref):
    height = rows_ref.shape[1] // 2
    at = [pl.multiple_of(origin[2 * step + a] % 2 * height, height) for a in range(2)]
    return jnp.concatenate([rows_ref[:, pl.ds(x, height)] for x in at], axis=1)


def weight_grad_kernel(ny, origin, rows_ref, turned_ref, *refs):
    top_grads, bottom_grads = refs[:ny], refs[ny:]
    step = pl.program_id(0)
    size = bottom_grads[0].shape[2]
    width = bottom_grads[0].shape[1]
    rows = picked(origin, step, rows_ref)
    grads = jnp.dot(turned_ref[...], rows, preferred_element_type=F32).astype(BF16)
    for f in range(4):
        a, b = f // 2, f % 2
        at = (2 * a + 1) * size
        bottom_grads[f][step] = grads[b * width : (b + 1) * width, at : at + size]
    for d in range(ny):

        @pl.when(step == d)
        def _(d=d):
            for f in range(4):
                a, b = f // 2, f % 2
                at = 2 * a * size
                top_grads[d][f] = grads[b * width : (b + 1) * width, at : at + size]


def rows_of(origin, all_rows, ny):
    rows, channels = all_rows.shape
    return pl.BlockSpec((rows, channels // ny), lambda i, origin: (0, origin[2 * i] // 2))


def weight_grad(origin, all_rows, turned, ny):
    rows, channels = all_rows.shape
    size = channels // (4 * ny)
    width = turned.shape[0] // 2
    outs = [jax.ShapeDtypeStruct((4, width, size), BF16)] * ny + [jax.ShapeDtypeStruct((ny, width, size), BF16)] * 4
    results = hbm_call(
        functools.partial(weight_grad_kernel, ny),
        loose=(0, 2),
        grid_spec=pltpu.PrefetchScalarGridSpec(
            num_scalar_prefetch=1,
            grid=(ny,),
            in_specs=[rows_of(origin, all_rows, ny), whole(turned)],
            out_specs=[whole(x) for x in outs],
        ),
        out_shape=outs,
        compiler_params=params(40),
        cost_estimate=cost(4 * rows * width * channels, 2 * (rows + 2 * width) * channels),
        name="weight_grad",
    )(origin, all_rows, turned)
    return results[:ny], results[ny:]


def output_kernel(ny, origin, rows_ref, *refs):
    tops, bottoms, own_ref, other_ref, total = refs[:ny], refs[ny : ny + 4], refs[-3], refs[-2], refs[-1]
    step = pl.program_id(0)
    width = own_ref.shape[1]
    rows = picked(origin, step, rows_ref)
    for d in range(ny):

        @pl.when(step == d)
        def _(d=d):
            right = jnp.concatenate(piece_rows(tops, bottoms, d), axis=0)
            product = jnp.dot(rows, right, preferred_element_type=F32)
            if d == 0:
                total[...] = product
            else:
                total[...] += product

    @pl.when(step == ny - 1)
    def _():
        own_ref[...] = total[:, :width].astype(BF16)
        other_ref[...] = total[:, width:].astype(BF16)


def output_call(origin, all_rows, tops, bottoms):
    rows, channels = all_rows.shape
    ny = len(tops)
    width = tops[0].shape[2]
    half = jax.ShapeDtypeStruct((rows, width), BF16)
    return hbm_call(
        functools.partial(output_kernel, ny),
        loose=(0, *range(2, 6 + ny)),
        grid_spec=pltpu.PrefetchScalarGridSpec(
            num_scalar_prefetch=1,
            grid=(ny,),
            in_specs=[rows_of(origin, all_rows, ny)] + [whole(x) for x in (*tops, *bottoms)],
            out_specs=[whole(half)] * 2,
            scratch_shapes=[pltpu.VMEM((rows, 2 * width), F32)],
        ),
        out_shape=[half, half],
        compiler_params=params(32),
        cost_estimate=cost(4 * rows * width * channels, 2 * (rows + 2 * width) * channels),
        name="output",
    )(origin, all_rows, *tops, *bottoms)


def added(terms):
    total = terms[0].astype(F32)
    for term in terms[1:]:
        total = total + term.astype(F32)
    return total


def plane_scatter(top_grads, bottom_grads, beside):
    ny = len(top_grads)
    top = added([move(top_grads[d], y=-d) for d in range(ny)]).astype(BF16)
    bottom = added([move(bottom_grads[f], xl=a, xh=b) for f, (a, b) in enumerate(FLIPS)]).astype(BF16)
    top, bottom, beside = lax.optimization_barrier((top, bottom, beside))
    top = [move(top[f], xl=a, xh=b) for f, (a, b) in enumerate(FLIPS)]
    bottom = [move(bottom[d], y=-d) for d in range(ny)]
    return top, bottom, beside


def shards(tokens_in, short_filter, long_filter, out_weight, cotangent):
    ny, nz = lax.axis_size("y"), lax.axis_size("z")
    y, xl, xh, z, c = (lax.axis_index(a) for a in ("y", "xl", "xh", "z", "c"))
    tokens = tokens_in[0]
    rows, wide = tokens.shape
    channels = wide // 3
    short_taps = short_filter.shape[0]
    groups = long_filter.shape[0]
    upstream = cotangent[0]
    length, columns = upstream.shape
    span = length // 2

    block = jnp.arange(2 * ny, dtype=jnp.int32)
    place = ((y - block // 2) % ny) * 2 + (block + xl) % 2
    origin = place
    size = 3 * channels // LANES + groups // 8
    each = size // (2 * nz)
    tile = jnp.arange(size, dtype=jnp.int32)
    core_step, z_step = (tile // (nz * each) + c) % 2, (tile // each - z) % nz
    spread_to = (core_step * nz + z_step) * each + tile % each
    collect_from = (z_step * 2 + core_step) * each + tile % each

    rim = along(tokens[rows - RIM :], 1)
    lines = long_filter.astype(F32)
    parts = features_call(tokens, short_filter)
    parts, rim = lax.optimization_barrier((parts, rim))
    query, key, value, mixer = features_call(tokens, short_filter, rim, parts)
    mixer, out_weight, half = lax.optimization_barrier((mixer, out_weight, xh))
    mixer_prev = along(mixer, 1)
    others = move(lax.dynamic_slice_in_dim(upstream, (1 - half) * span, span, 0), xh=1)
    tall_bottom = gather_tall(out_weight)
    mixer_prev, tall_bottom, others = lax.optimization_barrier((mixer_prev, tall_bottom, others))
    mixed, gated = mix_call(lines, mixer_prev, mixer, query)
    mixed, out_weight, half = lax.optimization_barrier((mixed, out_weight, half))
    wide_top = gather_wide(out_weight)
    wide_top, tall_bottom = lax.optimization_barrier((wide_top, tall_bottom))
    all_rows = lax.all_gather(gated, ("z", "c"), axis=0, tiled=True)
    tops, bottoms = gather_far(wide_top, tall_bottom)
    mine = lax.dynamic_slice_in_dim(upstream, half * span, span, 0)
    cotangents = jnp.concatenate([mine, others], axis=1)
    partial = gate_matmul(cotangents, tops, bottoms)
    partial, all_rows = lax.optimization_barrier((partial, all_rows))
    gate_grad = lax.psum_scatter(partial, ("z", "c"), scatter_dimension=0, tiled=True)

    top_grads, bottom_grads = weight_grad(origin, all_rows, cotangents.T, ny)
    own, other = output_call(origin, all_rows, tops, bottoms)
    top, bottom, other = plane_scatter(top_grads, bottom_grads, other)
    gate_grad, top, bottom, other = lax.optimization_barrier((gate_grad, top, bottom, other))

    grad_mixed, query_grad = gate_call(place, gate_grad, query, mixed)
    grad_next = along(grad_mixed, -1)
    long_sum, query_sum = long_grad_call(
        groups, short_taps, mixer_prev, mixer, grad_mixed, query_grad, tokens, rim
    )
    grad_weight = jnp.concatenate([added(top), added(bottom)], axis=1).T
    theirs = move(other, xh=1)
    grad_next, grad_weight = lax.optimization_barrier((grad_next, grad_weight))
    other_grads, key_sum, value_sum, edge = unmix_call(
        lines, short_taps, grad_mixed, grad_next, key, value, tokens, rim, query_grad
    )
    edge, key_sum, theirs = lax.optimization_barrier((edge, key_sum, theirs))
    edge = along(edge, -1)
    output = jnp.where(xh == 0, jnp.concatenate([own, theirs], axis=0), jnp.concatenate([theirs, own], axis=0))
    query_part = short_adjoint_call(query_grad[None], edge, short_filter, 0, 0, None)

    def key_part(query_part):
        return short_adjoint_call(other_grads, edge, short_filter, 0, 1, query_part)

    grad_short, grad_long, grad_tokens, output = total_over_devices(
        spread_to, collect_from, query_sum, key_sum, value_sum, long_sum, short_taps, query_part, key_part, output
    )
    grad_tokens = short_adjoint_call(other_grads, edge, short_filter, 1, 2, grad_tokens)
    return output[None], grad_tokens[None], grad_short, grad_long, grad_weight


def solution(mesh):
    dp, seq = mesh.shape["dp"], mesh.shape["seq"]
    grid = jax.sharding.Mesh(mesh.devices.reshape(dp // 2, 2, 2, seq // 4, 2), ("y", "xl", "xh", "z", "c"))
    rows, line = ("y", "xl"), ("xh", "z", "c")
    return jax.shard_map(
        shards,
        mesh=grid,
        in_specs=(P(rows, line, None), P(), P(), P(rows, line), P(rows, None, line)),
        out_specs=(P(rows, None, line), P(rows, line, None), P(), P(), P(rows, line)),
        check_vma=False,
    )
```

```python
import functools
import itertools
import math

import jax
import jax.numpy as jnp
from jax import lax
from jax.experimental import pallas as pl
from jax.experimental.pallas import tpu as pltpu
from jax.sharding import PartitionSpec as P

LANES = 128
RIM = 8
MIB = 1024 * 1024
WIDTH = 1024
F32 = jnp.float32
BF16 = jnp.bfloat16


PLANE = ("y", "xl", "xh")
LINE = ("xh", "z", "c")


def along(x, by):
    size = math.prod(lax.axis_size(a) for a in LINE)
    pairs = [(i, i + by) for i in range(size) if 0 <= i + by < size]
    return lax.ppermute(x, LINE, pairs)


def move(x, **steps):
    axes = tuple(a for a in ("y", "xl", "xh", "z", "c") if steps.get(a, 0) % lax.axis_size(a))
    if not axes:
        return x
    sizes = [lax.axis_size(a) for a in axes]
    pairs = []
    for at in itertools.product(*(range(n) for n in sizes)):
        to = [(p + steps[a]) % n for p, a, n in zip(at, axes, sizes)]
        pairs.append((flat(at, sizes), flat(to, sizes)))
    return lax.ppermute(x, axes, pairs)


def flat(at, sizes):
    index = 0
    for p, n in zip(at, sizes):
        index = index * n + p
    return index


FLIPS = [(0, 0), (0, 1), (1, 0), (1, 1)]


def params(mib=16):
    return pltpu.CompilerParams(vmem_limit_bytes=mib * MIB)


def hbm_call(kernel, *, out_shape, loose=(), **options):
    single = not isinstance(out_shape, (list, tuple))
    shapes = [out_shape] if single else out_shape
    placed = [pltpu.HBM(x.shape, x.dtype) if x.size * x.dtype.itemsize > 256 * 1024 else x for x in shapes]
    call = pl.pallas_call(kernel, out_shape=placed[0] if single else placed, **options)

    def run(*args):
        held = [x if i in loose else pltpu.with_memory_space_constraint(x, pltpu.HBM) for i, x in enumerate(args)]
        return call(*held)

    return run


def cost(flops, moved):
    return pl.CostEstimate(flops=int(flops), bytes_accessed=int(moved), transcendentals=0)


def block_width(channels, most):
    width = min(channels, most)
    while channels % width:
        width //= 2
    return width


def extend(ext, rim, rows_of, at):
    ext[0:RIM, :] = jnp.zeros((RIM, LANES), F32) if rim is None else rim[:, at].astype(F32)
    ext[RIM:, :] = rows_of.astype(F32)


def features_kernel(short_taps, tokens, rims, filters, query_ref, key_ref, value_ref, mixer_ref, ext):
    rows, width = tokens[0].shape

    def filtered(part, block, at):
        own = ext.at[(3 * block + part) % ext.shape[0]]
        extend(own, rims and rims[part], tokens[part][:, at], at)
        taps = filters[part][:, at]
        total = taps[0:1] * own[RIM : RIM + rows, :]
        for tap in range(1, short_taps):
            total = total + taps[tap : tap + 1] * own[RIM - tap : RIM - tap + rows, :]
        return total

    for block in range(width // LANES):
        at = pl.ds(block * LANES, LANES)
        query_ref[:, at] = filtered(0, block, at).astype(BF16)
        key, value = filtered(1, block, at), filtered(2, block, at)
        key_ref[:, at] = key.astype(BF16)
        value_ref[:, at] = value.astype(BF16)
        mixer_ref[:, at] = (key * value).astype(BF16)


def features_call(tokens, filters, rim=None, given=None):
    rows, wide = tokens.shape
    channels = wide // 3
    taps = filters.shape[0]
    rows = rows if given is None else 2 * RIM
    width = channels if given else block_width(channels, WIDTH)
    steps = channels // width

    def spec(height, part):
        return pl.BlockSpec((height, width), lambda i, part=part: (0, i + part * steps))

    held = [] if given is None else [rim] * 3
    olds = [] if given is None else list(given)

    def body(*refs):
        n = 3 + len(held)
        rims = refs[3:n] if held else None
        features_kernel(taps, refs[0:3], rims, refs[n : n + 3], *refs[n + 3 + len(olds) :])

    out = jax.ShapeDtypeStruct((tokens.shape[0], channels), BF16)
    return hbm_call(
        body,
        loose=(3, 4, 5) if held else (),
        grid=(steps,),
        in_specs=[spec(rows, p) for p in range(3)]
        + [spec(RIM, p) for p in range(len(held))]
        + [spec(taps, p) for p in range(3)]
        + [pl.BlockSpec(memory_space=pl.ANY)] * len(olds),
        out_specs=[pl.BlockSpec((rows, width), lambda i: (0, i))] * 4,
        out_shape=[out] * 4,
        input_output_aliases={9 + i: i for i in range(len(olds))},
        scratch_shapes=[pltpu.VMEM((6, RIM + rows, LANES), F32)],
        compiler_params=params(),
        cost_estimate=cost(0, rows * wide),
        name="features" if given is None else "first_rows",
    )(*[tokens] * 3, *held, *[filters] * 3, *olds)


def lane_row(shape):
    row = lax.broadcasted_iota(jnp.int32, shape, 0)
    lane = lax.broadcasted_iota(jnp.int32, shape, 1)
    return row, lane


def mirror(size):
    row, lane = lane_row((size, size))
    both = row + lane
    return jnp.where((both == 0) | (both == size), 1.0, 0.0)


def circulant(line, taps):
    wide = jnp.broadcast_to(line.astype(F32), (taps, taps))
    return pltpu.roll(wide, 0, 1, stride=1, stride_axis=0)


def pick_groups(product, rows, per_group):
    lane = lax.broadcasted_iota(jnp.int32, (rows, LANES), 1)
    total = product[0:rows]
    for g in range(1, LANES // per_group):
        total = jnp.where(lane >= g * per_group, product[g * rows : (g + 1) * rows], total)
    return total


def mix_kernel(per_group, lines_ref, prev_ref, cur_ref, query_ref, mixed_ref, gated_ref, table, lines):
    rows, width = cur_ref.shape
    row, lane = lane_row((rows, rows))
    above = lane > row
    packed = LANES // per_group
    lines[...] = jnp.dot(lines_ref[...].astype(BF16), mirror(rows).astype(BF16), preferred_element_type=F32)
    for block in range(width // LANES):
        at = pl.ds(block * LANES, LANES)
        own = table.at[block % 2]
        for g in range(packed):
            ring = circulant(lines[block * packed + g : block * packed + g + 1, :], rows)
            own[g * rows : (g + 1) * rows, 0:rows] = jnp.where(above, ring, 0.0).astype(BF16)
            own[g * rows : (g + 1) * rows, rows : 2 * rows] = jnp.where(above, 0.0, ring).astype(BF16)
        window = jnp.concatenate([prev_ref[:, at], cur_ref[:, at]], axis=0)
        product = jnp.dot(own[...], window, preferred_element_type=F32)
        mixed = pick_groups(product, rows, per_group)
        mixed_ref[:, at] = mixed.astype(BF16)
        gated_ref[:, at] = (query_ref[:, at].astype(F32) * mixed).astype(BF16)


def mix_call(lines, prev, cur, query):
    rows, channels = cur.shape
    groups, taps = lines.shape
    per_group = channels // groups
    width = block_width(channels, WIDTH)
    steps = channels // width
    wide = pl.BlockSpec((rows, width), lambda i: (0, i))
    out = jax.ShapeDtypeStruct((rows, channels), BF16)
    return hbm_call(
        functools.partial(mix_kernel, per_group),
        loose=(0, 1),
        grid=(steps,),
        in_specs=[pl.BlockSpec((width // per_group, taps), lambda i: (i, 0)), wide, wide, wide],
        out_specs=[wide, wide],
        out_shape=[out, out],
        scratch_shapes=[
            pltpu.VMEM((2, LANES // per_group * rows, 2 * rows), BF16),
            pltpu.VMEM((width // per_group, taps), F32),
        ],
        compiler_params=params(),
        cost_estimate=cost(0, 2 * rows * channels),
        name="mix",
    )(lines, prev, cur, query)


def gate_kernel(place, gate_grad_ref, query_ref, mixed_ref, grad_ref, feature_ref):
    width = query_ref.shape[1] // place.shape[0]
    for i in range(place.shape[0]):
        at = pl.ds(i * width, width)
        gate_grad = gate_grad_ref[:, pl.ds(pl.multiple_of(place[i] * width, width), width)].astype(F32)
        grad_ref[:, at] = (gate_grad * query_ref[:, at].astype(F32)).astype(BF16)
        feature_ref[:, at] = (gate_grad * mixed_ref[:, at].astype(F32)).astype(BF16)


def gate_call(place, gate_grad, query, mixed):
    rows, channels = query.shape
    out = jax.ShapeDtypeStruct((rows, channels), BF16)
    return hbm_call(
        gate_kernel,
        loose=(0,),
        grid_spec=pltpu.PrefetchScalarGridSpec(
            num_scalar_prefetch=1,
            grid=(2,),
            in_specs=[pl.BlockSpec((rows // 2, channels), lambda i, place: (i, 0))] * 3,
            out_specs=[pl.BlockSpec((rows // 2, channels), lambda i, place: (i, 0))] * 2,
        ),
        out_shape=[out, out],
        compiler_params=params(),
        cost_estimate=cost(2 * rows * channels, 10 * rows * channels),
        name="gate_back",
    )(place, gate_grad, query, mixed)


def tap_sums(short_taps, grad, tokens_ref, rim_ref, out_ref, at, ext):
    rows = tokens_ref.shape[0]
    extend(ext, rim_ref, tokens_ref[:, at], at)
    grad = grad.astype(F32)
    for tap in range(short_taps):
        out_ref[tap : tap + 1, at] = jnp.sum(grad * ext[RIM - tap : RIM - tap + rows, :], axis=0, keepdims=True)
    out_ref[short_taps:8, at] = jnp.zeros((8 - short_taps, LANES), F32)


def long_grad_kernel(
    per_group, short_taps, prev_ref, cur_ref, grad_ref, feature_ref, tokens_ref, rim_ref, long_ref, short_ref, fold, masked, ext
):
    rows, width = cur_ref.shape
    row, lane = lane_row((rows, rows))
    above = lane > row
    member = lax.broadcasted_iota(jnp.int32, (rows, LANES), 1)
    packed = LANES // per_group
    sums = []
    for block in range(width // LANES):
        at = pl.ds(block * LANES, LANES)
        window = jnp.concatenate([prev_ref[:, at], cur_ref[:, at]], axis=0)
        grad_wide = grad_ref[:, at].astype(F32)
        own = masked.at[block % 2]
        for g in range(packed):
            own[g * rows : (g + 1) * rows, :] = jnp.where((member >= g * per_group) & (member < (g + 1) * per_group), grad_wide, 0.0).astype(BF16)
        pairs = lax.dot_general(own[...], window, (((1,), (1,)), ((), ())), preferred_element_type=F32)
        for g in range(packed):
            pair = pairs[g * rows : (g + 1) * rows]
            ring = jnp.where(above, pair[:, 0:rows], pair[:, rows : 2 * rows])
            total = ring[0:8]
            for tile in range(1, rows // 8):
                total = total + pltpu.roll(ring[8 * tile : 8 * tile + 8], rows - 8 * tile, 1)
            fold[block % 2, g * 8 : (g + 1) * 8, :] = total
        total = fold[block % 2, pl.ds(0, packed, stride=8), :]
        for step in range(1, 8):
            total = total + pltpu.roll(fold[block % 2, pl.ds(step, packed, stride=8), :], rows - step, 1)
        sums.append(total)
        tap_sums(short_taps, feature_ref[:, at], tokens_ref, rim_ref, short_ref, at, ext.at[block % 2])
    long_ref[...] = jnp.dot(
        jnp.concatenate(sums, axis=0), mirror(rows), precision=lax.Precision.HIGHEST, preferred_element_type=F32
    )


def long_grad_call(groups, short_taps, prev, cur, grad, feature, tokens, rim):
    rows, channels = cur.shape
    per_group = channels // groups
    width = block_width(channels, WIDTH)
    steps = channels // width
    wide = pl.BlockSpec((rows, width), lambda i: (0, i))
    packed = LANES // per_group
    return hbm_call(
        functools.partial(long_grad_kernel, per_group, short_taps),
        grid=(steps,),
        in_specs=[wide] * 5 + [pl.BlockSpec((RIM, width), lambda i: (0, i))],
        out_specs=[
            pl.BlockSpec((width // per_group, rows), lambda i: (i, 0)),
            pl.BlockSpec((8, width), lambda i: (0, i)),
        ],
        out_shape=[
            jax.ShapeDtypeStruct((groups, rows), F32),
            jax.ShapeDtypeStruct((8, channels), F32),
        ],
        scratch_shapes=[
            pltpu.VMEM((2, packed * 8, LANES), F32),
            pltpu.VMEM((2, packed * rows, LANES), BF16),
            pltpu.VMEM((2, RIM + rows, LANES), F32),
        ],
        compiler_params=params(),
        cost_estimate=cost(2 * groups * rows * 2 * rows * LANES, 10 * rows * channels),
        name="long_grad",
    )(prev, cur, grad, feature, tokens, rim)


def unmix_kernel(
    per_group, short_taps, lines_ref, grad_ref, next_ref, key_ref, value_ref, key_tokens_ref, value_tokens_ref,
    key_rim_ref, value_rim_ref, query_grad_ref, feature_ref, key_sum_ref, value_sum_ref, edge_ref, table, ext,
):
    rows, width = grad_ref.shape
    row, lane = lane_row((rows, rows))
    below = lane < row
    packed = LANES // per_group
    edge_ref[0] = query_grad_ref[0:RIM, :]
    for block in range(width // LANES):
        at = pl.ds(block * LANES, LANES)
        own = table.at[block % 2]
        for g in range(packed):
            ring = circulant(lines_ref[block * packed + g : block * packed + g + 1, :], rows)
            own[g * rows : (g + 1) * rows, 0:rows] = jnp.where(below, 0.0, ring).astype(BF16)
            own[g * rows : (g + 1) * rows, rows : 2 * rows] = jnp.where(below, ring, 0.0).astype(BF16)
        window = jnp.concatenate([grad_ref[:, at], next_ref[:, at]], axis=0)
        product = jnp.dot(own[...], window, preferred_element_type=F32)
        grad_mixer = pick_groups(product, rows, per_group)
        key_grad = (grad_mixer * value_ref[:, at].astype(F32)).astype(BF16)
        value_grad = (grad_mixer * key_ref[:, at].astype(F32)).astype(BF16)
        feature_ref[0, :, at] = key_grad
        feature_ref[1, :, at] = value_grad
        edge_ref[1, :, at] = key_grad[0:RIM]
        edge_ref[2, :, at] = value_grad[0:RIM]
        slot = 2 * (block % 2)
        tap_sums(short_taps, key_grad, key_tokens_ref, key_rim_ref, key_sum_ref, at, ext.at[slot])
        tap_sums(short_taps, value_grad, value_tokens_ref, value_rim_ref, value_sum_ref, at, ext.at[slot + 1])


def unmix_call(lines, short_taps, grad, grad_next, key, value, tokens, rim, query_grad):
    rows, channels = grad.shape
    per_group = channels // lines.shape[0]
    width = block_width(channels, WIDTH)
    steps = channels // width

    def spec(height, part):
        return pl.BlockSpec((height, width), lambda i, part=part: (0, i + part * steps))

    wide = spec(rows, 0)
    sums = jax.ShapeDtypeStruct((8, channels), F32)
    return hbm_call(
        functools.partial(unmix_kernel, per_group, short_taps),
        loose=(0, 2),
        grid=(steps,),
        in_specs=[pl.BlockSpec((width // per_group, rows), lambda i: (i, 0))]
        + [wide] * 4
        + [spec(rows, 1), spec(rows, 2), spec(RIM, 1), spec(RIM, 2), spec(2 * RIM, 0)],
        out_specs=[
            pl.BlockSpec((2, rows, width), lambda i: (0, 0, i)),
            spec(8, 0),
            spec(8, 0),
            pl.BlockSpec((3, RIM, width), lambda i: (0, 0, i)),
        ],
        out_shape=[
            jax.ShapeDtypeStruct((2, rows, channels), BF16),
            sums,
            sums,
            jax.ShapeDtypeStruct((3, RIM, channels), BF16),
        ],
        scratch_shapes=[
            pltpu.VMEM((2, LANES // per_group * rows, 2 * rows), BF16),
            pltpu.VMEM((4, RIM + rows, LANES), F32),
        ],
        compiler_params=params(),
        cost_estimate=cost(2 * channels * rows * 2 * rows * LANES // per_group, 16 * rows * channels),
        name="unmix",
    )(lines, grad, grad_next, key, value, tokens, tokens, rim, rim, query_grad)


def short_adjoint_kernel(short_taps, grads_ref, rim_ref, filter_ref, *refs):
    out_ref, ext = refs[-2:]
    rows, width = out_ref.shape
    for block in range(width // LANES):
        at = pl.ds(block * LANES, LANES)
        own = ext.at[block % 2]
        own[0:rows, :] = grads_ref[0, :, at].astype(F32)
        own[rows:, :] = rim_ref[0, :, at].astype(F32)
        taps = filter_ref[:, at]
        total = taps[0:1] * own[0:rows, :]
        for tap in range(1, short_taps):
            total = total + taps[tap : tap + 1] * own[tap : tap + rows, :]
        out_ref[:, at] = total.astype(BF16)


def short_adjoint_call(grads, rim, filters, given, part, out):
    _, rows, channels = grads.shape
    short_taps = filters.shape[0]
    width = block_width(channels, 2 * WIDTH)
    steps = channels // width
    result = pl.BlockSpec((rows, width), lambda i: (0, part * steps + i))
    olds = [] if out is None else [out]
    return hbm_call(
        functools.partial(short_adjoint_kernel, short_taps),
        loose=(1,),
        grid=(steps,),
        in_specs=[
            pl.BlockSpec((1, rows, width), lambda i: (given, 0, i)),
            pl.BlockSpec((1, RIM, width), lambda i: (part, 0, i)),
            pl.BlockSpec((short_taps, width), lambda i: (0, part * steps + i)),
        ]
        + [pl.BlockSpec(memory_space=pl.ANY)] * len(olds),
        out_specs=result,
        out_shape=jax.ShapeDtypeStruct((rows, 3 * channels), BF16),
        input_output_aliases={3: 0} if olds else {},
        scratch_shapes=[pltpu.VMEM((2, rows + RIM, LANES), F32)],
        compiler_params=params(),
        cost_estimate=cost(2 * short_taps * rows * channels, 4 * rows * channels),
        name="short_adjoint",
    )(grads, rim, filters, *olds)


def spread_kernel(place, query_ref, key_ref, value_ref, long_ref, own_ref, other_ref):
    steps = query_ref.shape[1] // LANES
    half = own_ref.shape[0]
    tiles = [ref[:, i * LANES : (i + 1) * LANES] for ref in (query_ref, key_ref, value_ref) for i in range(steps)]
    tiles += [long_ref[8 * i : 8 * i + 8, :] for i in range(long_ref.shape[0] // 8)]
    first = place[0] < half

    @pl.when(first)
    def _():
        for i in range(half):
            own_ref[place[i]] = tiles[i]
            other_ref[place[half + i] - half] = tiles[half + i]

    @pl.when(jnp.logical_not(first))
    def _():
        for i in range(half):
            other_ref[place[i] - half] = tiles[i]
            own_ref[place[half + i]] = tiles[half + i]


def collect_kernel(place, *refs):
    parts, short_ref, long_ref, tiles_ref = refs[:-3], refs[-3], refs[-2], refs[-1]
    short_taps, wide = short_ref.shape
    steps = wide // LANES
    size = parts[0].shape[0]
    for i, part in enumerate(parts):
        tiles_ref[i * size : (i + 1) * size] = part[...]
    for i in range(steps):
        short_ref[:, i * LANES : (i + 1) * LANES] = tiles_ref[place[i]][0:short_taps, :]
    for i in range(long_ref.shape[0] // 8):
        long_ref[8 * i : 8 * i + 8, :] = tiles_ref[place[steps + i]]


def in_vmem():
    return pl.BlockSpec(memory_space=pltpu.VMEM)


def total_over_devices(spread_to, collect_from, query_sum, key_sum, value_sum, long_sum, short_taps, first, after):
    ny, nz = lax.axis_size("y"), lax.axis_size("z")
    channels = query_sum.shape[1]
    count = 3 * channels // LANES + long_sum.shape[0] // 8
    half = jax.ShapeDtypeStruct((count // 2, 8, LANES), F32)
    own, other = pl.pallas_call(
        spread_kernel,
        in_specs=[pl.BlockSpec(memory_space=pltpu.SMEM)] + [in_vmem()] * 4,
        out_specs=[in_vmem()] * 2,
        out_shape=[half] * 2,
        compiler_params=params(),
        name="spread",
    )(spread_to, query_sum, key_sum, value_sum, long_sum)
    part = own + move(other, c=1)
    size = count // 2 // nz
    part = sum([move(part[d * size : (d + 1) * size], z=d) for d in range(1, nz)], part[:size])
    terms, first = lax.optimization_barrier(([part] + [move(part, y=d) for d in range(1, ny)], first))
    whole = paired_sum(terms)
    terms = [move(whole, xl=a, xh=b) for a, b in FLIPS]
    terms, beside = lax.optimization_barrier((terms, after(first)))
    whole = paired_sum(terms)
    line = jnp.concatenate([whole, move(whole, c=1)], axis=0)
    lines = [move(line, z=-d) for d in range(nz)]
    groups, taps = long_sum.shape
    short, long = pl.pallas_call(
        collect_kernel,
        in_specs=[pl.BlockSpec(memory_space=pltpu.SMEM)] + [in_vmem()] * nz,
        out_specs=[in_vmem(), in_vmem()],
        scratch_shapes=[pltpu.VMEM((count, 8, LANES), F32)],
        out_shape=[
            jax.ShapeDtypeStruct((short_taps, 3 * channels), F32),
            jax.ShapeDtypeStruct((groups, taps), F32),
        ],
        compiler_params=params(),
        name="collect",
    )(collect_from, *lines)
    return short, long, beside


def paired_sum(terms):
    half = len(terms) // 2
    if half == 0:
        return terms[0]
    return paired_sum([terms[i] + terms[i + half] for i in range(half)])


def gather_tall(shard):
    return [move(shard[shard.shape[0] // 2 :], y=d) for d in range(lax.axis_size("y"))]


def gather_wide(shard):
    return [move(shard[: shard.shape[0] // 2], xl=a, xh=b) for a, b in FLIPS]


def gather_far(wide_top, tall_bottom):
    ny = lax.axis_size("y")
    wide_top, tall_bottom = jnp.stack(wide_top), jnp.stack(tall_bottom)
    return (
        [move(wide_top, y=d) for d in range(ny)],
        [move(tall_bottom, xl=a, xh=b) for a, b in FLIPS],
    )


def piece_rows(tops, bottoms, step):
    rows = []
    for a in range(2):
        rows.append(jnp.concatenate([tops[step][2 * a + b] for b in range(2)], axis=1))
        rows.append(jnp.concatenate([bottoms[2 * a + b][step] for b in range(2)], axis=1))
    return rows


def gate_matmul_kernel(ny, *refs):
    cotangent_ref, tops, bottoms, out_ref = refs[0], refs[1 : 1 + ny], refs[1 + ny : 5 + ny], refs[5 + ny]
    left = cotangent_ref[...]
    at = 0
    for step in range(ny):
        for right in piece_rows(tops, bottoms, step):
            size = right.shape[0]
            out_ref[:, at : at + size] = lax.dot_general(
                left, right, (((1,), (1,)), ((), ())), preferred_element_type=F32
            ).astype(BF16)
            at += size


def whole(x):
    return pl.BlockSpec(x.shape, lambda *_, n=x.ndim: (0,) * n)


def gate_matmul(cotangents, tops, bottoms):
    rows, depth = cotangents.shape
    ny = len(tops)
    channels = 4 * ny * tops[0].shape[1]
    height = rows // 2
    return hbm_call(
        functools.partial(gate_matmul_kernel, ny),
        loose=range(5 + ny),
        grid=(rows // height,),
        in_specs=[pl.BlockSpec((height, depth), lambda i: (i, 0))] + [whole(x) for x in (*tops, *bottoms)],
        out_specs=pl.BlockSpec((height, channels), lambda i: (i, 0)),
        out_shape=jax.ShapeDtypeStruct((rows, channels), BF16),
        compiler_params=params(32),
        cost_estimate=cost(2 * rows * depth * channels, 2 * (rows + depth) * channels),
        name="gate_matmul",
    )(cotangents, *tops, *bottoms)


def picked(origin, step, rows_ref):
    height = rows_ref.shape[1] // 2
    at = [pl.multiple_of(origin[2 * step + a] % 2 * height, height) for a in range(2)]
    return jnp.concatenate([rows_ref[:, pl.ds(x, height)] for x in at], axis=1)


def weight_grad_kernel(ny, origin, rows_ref, turned_ref, *refs):
    top_grads, bottom_grads = refs[:ny], refs[ny:]
    step = pl.program_id(0)
    size = bottom_grads[0].shape[2]
    width = bottom_grads[0].shape[1]
    rows = picked(origin, step, rows_ref)
    grads = jnp.dot(turned_ref[...], rows, preferred_element_type=F32).astype(BF16)
    for f in range(4):
        a, b = f // 2, f % 2
        at = (2 * a + 1) * size
        bottom_grads[f][step] = grads[b * width : (b + 1) * width, at : at + size]
    for d in range(ny):

        @pl.when(step == d)
        def _(d=d):
            for f in range(4):
                a, b = f // 2, f % 2
                at = 2 * a * size
                top_grads[d][f] = grads[b * width : (b + 1) * width, at : at + size]


def rows_of(origin, all_rows, ny):
    rows, channels = all_rows.shape
    return pl.BlockSpec((rows, channels // ny), lambda i, origin: (0, origin[2 * i] // 2))


def weight_grad(origin, all_rows, turned, ny):
    rows, channels = all_rows.shape
    size = channels // (4 * ny)
    width = turned.shape[0] // 2
    outs = [jax.ShapeDtypeStruct((4, width, size), BF16)] * ny + [jax.ShapeDtypeStruct((ny, width, size), BF16)] * 4
    results = hbm_call(
        functools.partial(weight_grad_kernel, ny),
        loose=(0, 2),
        grid_spec=pltpu.PrefetchScalarGridSpec(
            num_scalar_prefetch=1,
            grid=(ny,),
            in_specs=[rows_of(origin, all_rows, ny), whole(turned)],
            out_specs=[whole(x) for x in outs],
        ),
        out_shape=outs,
        compiler_params=params(40),
        cost_estimate=cost(4 * rows * width * channels, 2 * (rows + 2 * width) * channels),
        name="weight_grad",
    )(origin, all_rows, turned)
    return results[:ny], results[ny:]


def output_kernel(ny, origin, rows_ref, *refs):
    tops, bottoms, own_ref, other_ref, total = refs[:ny], refs[ny : ny + 4], refs[-3], refs[-2], refs[-1]
    step = pl.program_id(0)
    width = own_ref.shape[1]
    rows = picked(origin, step, rows_ref)
    for d in range(ny):

        @pl.when(step == d)
        def _(d=d):
            right = jnp.concatenate(piece_rows(tops, bottoms, d), axis=0)
            product = jnp.dot(rows, right, preferred_element_type=F32)
            if d == 0:
                total[...] = product
            else:
                total[...] += product

    @pl.when(step == ny - 1)
    def _():
        own_ref[...] = total[:, :width].astype(BF16)
        other_ref[...] = total[:, width:].astype(BF16)


def output_call(origin, all_rows, tops, bottoms):
    rows, channels = all_rows.shape
    ny = len(tops)
    width = tops[0].shape[2]
    half = jax.ShapeDtypeStruct((rows, width), BF16)
    return hbm_call(
        functools.partial(output_kernel, ny),
        loose=(0, *range(2, 6 + ny)),
        grid_spec=pltpu.PrefetchScalarGridSpec(
            num_scalar_prefetch=1,
            grid=(ny,),
            in_specs=[rows_of(origin, all_rows, ny)] + [whole(x) for x in (*tops, *bottoms)],
            out_specs=[whole(half)] * 2,
            scratch_shapes=[pltpu.VMEM((rows, 2 * width), F32)],
        ),
        out_shape=[half, half],
        compiler_params=params(32),
        cost_estimate=cost(4 * rows * width * channels, 2 * (rows + 2 * width) * channels),
        name="output",
    )(origin, all_rows, *tops, *bottoms)


def added(terms):
    total = terms[0].astype(F32)
    for term in terms[1:]:
        total = total + term.astype(F32)
    return total


def plane_scatter(top_grads, bottom_grads):
    ny = len(top_grads)
    top = added([move(top_grads[d], y=-d) for d in range(ny)]).astype(BF16)
    bottom = added([move(bottom_grads[f], xl=a, xh=b) for f, (a, b) in enumerate(FLIPS)]).astype(BF16)
    top = [move(top[f], xl=a, xh=b) for f, (a, b) in enumerate(FLIPS)]
    bottom = [move(bottom[d], y=-d) for d in range(ny)]
    return top, bottom


def shards(tokens_in, short_filter, long_filter, out_weight, cotangent):
    ny, nz = lax.axis_size("y"), lax.axis_size("z")
    y, xl, xh, z, c = (lax.axis_index(a) for a in ("y", "xl", "xh", "z", "c"))
    tokens = tokens_in[0]
    rows, wide = tokens.shape
    channels = wide // 3
    short_taps = short_filter.shape[0]
    groups = long_filter.shape[0]
    upstream = cotangent[0]
    length, columns = upstream.shape
    span = length // 2

    block = jnp.arange(2 * ny, dtype=jnp.int32)
    place = ((y - block // 2) % ny) * 2 + (block + xl) % 2
    origin = place
    size = 3 * channels // LANES + groups // 8
    each = size // (2 * nz)
    tile = jnp.arange(size, dtype=jnp.int32)
    core_step, z_step = (tile // (nz * each) + c) % 2, (tile // each - z) % nz
    spread_to = (core_step * nz + z_step) * each + tile % each
    collect_from = (z_step * 2 + core_step) * each + tile % each

    rim = along(tokens[rows - RIM :], 1)
    lines = long_filter.astype(F32)
    parts = features_call(tokens, short_filter)
    parts, rim = lax.optimization_barrier((parts, rim))
    query, key, value, mixer = features_call(tokens, short_filter, rim, parts)
    mixer, out_weight = lax.optimization_barrier((mixer, out_weight))
    mixer_prev = along(mixer, 1)
    tall_bottom = gather_tall(out_weight)
    mixer_prev, tall_bottom = lax.optimization_barrier((mixer_prev, tall_bottom))
    mixed, gated = mix_call(lines, mixer_prev, mixer, query)
    mixed, out_weight, half = lax.optimization_barrier((mixed, out_weight, xh))
    wide_top = gather_wide(out_weight)
    wide_top, tall_bottom, half = lax.optimization_barrier((wide_top, tall_bottom, half))
    all_rows = lax.all_gather(gated, ("z", "c"), axis=0, tiled=True)
    tops, bottoms = gather_far(wide_top, tall_bottom)
    others = move(lax.dynamic_slice_in_dim(upstream, (1 - half) * span, span, 0), xh=1)
    mine = lax.dynamic_slice_in_dim(upstream, half * span, span, 0)
    cotangents = jnp.concatenate([mine, others], axis=1)
    partial = gate_matmul(cotangents, tops, bottoms)
    partial, all_rows = lax.optimization_barrier((partial, all_rows))
    gate_grad = lax.psum_scatter(partial, ("z", "c"), scatter_dimension=0, tiled=True)

    top_grads, bottom_grads = weight_grad(origin, all_rows, cotangents.T, ny)
    own, other = output_call(origin, all_rows, tops, bottoms)
    top, bottom = plane_scatter(top_grads, bottom_grads)
    theirs = move(other, xh=1)
    output = jnp.where(xh == 0, jnp.concatenate([own, theirs], axis=0), jnp.concatenate([theirs, own], axis=0))
    gate_grad, top, bottom, output = lax.optimization_barrier((gate_grad, top, bottom, output))

    grad_mixed, query_grad = gate_call(place, gate_grad, query, mixed)
    grad_next = along(grad_mixed, -1)
    long_sum, query_sum = long_grad_call(
        groups, short_taps, mixer_prev, mixer, grad_mixed, query_grad, tokens, rim
    )
    grad_weight = jnp.concatenate([added(top), added(bottom)], axis=1).T
    grad_next, grad_weight = lax.optimization_barrier((grad_next, grad_weight))
    other_grads, key_sum, value_sum, edge = unmix_call(
        lines, short_taps, grad_mixed, grad_next, key, value, tokens, rim, query_grad
    )
    edge = along(edge, -1)
    query_part = short_adjoint_call(query_grad[None], edge, short_filter, 0, 0, None)

    def key_part(query_part):
        return short_adjoint_call(other_grads, edge, short_filter, 0, 1, query_part)

    grad_short, grad_long, grad_tokens = total_over_devices(
        spread_to, collect_from, query_sum, key_sum, value_sum, long_sum, short_taps, query_part, key_part
    )
    grad_tokens = short_adjoint_call(other_grads, edge, short_filter, 1, 2, grad_tokens)
    return output[None], grad_tokens[None], grad_short, grad_long, grad_weight


def solution(mesh):
    dp, seq = mesh.shape["dp"], mesh.shape["seq"]
    grid = jax.sharding.Mesh(mesh.devices.reshape(dp // 2, 2, 2, seq // 4, 2), ("y", "xl", "xh", "z", "c"))
    rows, line = ("y", "xl"), ("xh", "z", "c")
    return jax.shard_map(
        shards,
        mesh=grid,
        in_specs=(P(rows, line, None), P(), P(), P(rows, line), P(rows, None, line)),
        out_specs=(P(rows, None, line), P(rows, line, None), P(), P(), P(rows, line)),
        check_vma=False,
    )
```

```python
import functools
import itertools
import math

import jax
import jax.numpy as jnp
from jax import lax
from jax.experimental import pallas as pl
from jax.experimental.pallas import tpu as pltpu
from jax.sharding import PartitionSpec as P

LANES = 128
RIM = 8
MIB = 1024 * 1024
WIDTH = 1024
F32 = jnp.float32
BF16 = jnp.bfloat16


PLANE = ("y", "xl", "xh")
LINE = ("xh", "z", "c")


def along(x, by):
    size = math.prod(lax.axis_size(a) for a in LINE)
    pairs = [(i, i + by) for i in range(size) if 0 <= i + by < size]
    return lax.ppermute(x, LINE, pairs)


def move(x, **steps):
    axes = tuple(a for a in ("y", "xl", "xh", "z", "c") if steps.get(a, 0) % lax.axis_size(a))
    if not axes:
        return x
    sizes = [lax.axis_size(a) for a in axes]
    pairs = []
    for at in itertools.product(*(range(n) for n in sizes)):
        to = [(p + steps[a]) % n for p, a, n in zip(at, axes, sizes)]
        pairs.append((flat(at, sizes), flat(to, sizes)))
    return lax.ppermute(x, axes, pairs)


def flat(at, sizes):
    index = 0
    for p, n in zip(at, sizes):
        index = index * n + p
    return index


FLIPS = [(0, 0), (0, 1), (1, 0), (1, 1)]


def params(mib=16):
    return pltpu.CompilerParams(vmem_limit_bytes=mib * MIB)


def hbm_call(kernel, *, out_shape, loose=(), **options):
    single = not isinstance(out_shape, (list, tuple))
    shapes = [out_shape] if single else out_shape
    placed = [pltpu.HBM(x.shape, x.dtype) if x.size * x.dtype.itemsize > 256 * 1024 else x for x in shapes]
    call = pl.pallas_call(kernel, out_shape=placed[0] if single else placed, **options)

    def run(*args):
        held = [x if i in loose else pltpu.with_memory_space_constraint(x, pltpu.HBM) for i, x in enumerate(args)]
        return call(*held)

    return run


def cost(flops, moved):
    return pl.CostEstimate(flops=int(flops), bytes_accessed=int(moved), transcendentals=0)


def block_width(channels, most):
    width = min(channels, most)
    while channels % width:
        width //= 2
    return width


def extend(ext, rim, rows_of, at):
    ext[0:RIM, :] = jnp.zeros((RIM, LANES), F32) if rim is None else rim[:, at].astype(F32)
    ext[RIM:, :] = rows_of.astype(F32)


def features_kernel(short_taps, tokens, rims, filters, query_ref, key_ref, value_ref, mixer_ref, ext):
    rows, width = tokens[0].shape

    def filtered(part, block, at):
        own = ext.at[(3 * block + part) % ext.shape[0]]
        extend(own, rims and rims[part], tokens[part][:, at], at)
        taps = filters[part][:, at]
        total = taps[0:1] * own[RIM : RIM + rows, :]
        for tap in range(1, short_taps):
            total = total + taps[tap : tap + 1] * own[RIM - tap : RIM - tap + rows, :]
        return total

    for block in range(width // LANES):
        at = pl.ds(block * LANES, LANES)
        query_ref[:, at] = filtered(0, block, at).astype(BF16)
        key, value = filtered(1, block, at), filtered(2, block, at)
        key_ref[:, at] = key.astype(BF16)
        value_ref[:, at] = value.astype(BF16)
        mixer_ref[:, at] = (key * value).astype(BF16)


def features_call(tokens, filters, rim=None, given=None):
    rows, wide = tokens.shape
    channels = wide // 3
    taps = filters.shape[0]
    rows = rows if given is None else 2 * RIM
    width = channels if given else block_width(channels, WIDTH)
    steps = channels // width

    def spec(height, part):
        return pl.BlockSpec((height, width), lambda i, part=part: (0, i + part * steps))

    held = [] if given is None else [rim] * 3
    olds = [] if given is None else list(given)

    def body(*refs):
        n = 3 + len(held)
        rims = refs[3:n] if held else None
        features_kernel(taps, refs[0:3], rims, refs[n : n + 3], *refs[n + 3 + len(olds) :])

    out = jax.ShapeDtypeStruct((tokens.shape[0], channels), BF16)
    return hbm_call(
        body,
        loose=(3, 4, 5) if held else (),
        grid=(steps,),
        in_specs=[spec(rows, p) for p in range(3)]
        + [spec(RIM, p) for p in range(len(held))]
        + [spec(taps, p) for p in range(3)]
        + [pl.BlockSpec(memory_space=pl.ANY)] * len(olds),
        out_specs=[pl.BlockSpec((rows, width), lambda i: (0, i))] * 4,
        out_shape=[out] * 4,
        input_output_aliases={9 + i: i for i in range(len(olds))},
        scratch_shapes=[pltpu.VMEM((6, RIM + rows, LANES), F32)],
        compiler_params=params(),
        cost_estimate=cost(0, rows * wide),
        name="features" if given is None else "first_rows",
    )(*[tokens] * 3, *held, *[filters] * 3, *olds)


def lane_row(shape):
    row = lax.broadcasted_iota(jnp.int32, shape, 0)
    lane = lax.broadcasted_iota(jnp.int32, shape, 1)
    return row, lane


def mirror(size):
    row, lane = lane_row((size, size))
    both = row + lane
    return jnp.where((both == 0) | (both == size), 1.0, 0.0)


def circulant(line, taps):
    wide = jnp.broadcast_to(line.astype(F32), (taps, taps))
    return pltpu.roll(wide, 0, 1, stride=1, stride_axis=0)


def pick_groups(product, rows, per_group):
    lane = lax.broadcasted_iota(jnp.int32, (rows, LANES), 1)
    total = product[0:rows]
    for g in range(1, LANES // per_group):
        total = jnp.where(lane >= g * per_group, product[g * rows : (g + 1) * rows], total)
    return total


def mix_kernel(per_group, lines_ref, prev_ref, cur_ref, query_ref, mixed_ref, gated_ref, table, lines):
    rows, width = cur_ref.shape
    row, lane = lane_row((rows, rows))
    above = lane > row
    packed = LANES // per_group
    lines[...] = jnp.dot(lines_ref[...].astype(BF16), mirror(rows).astype(BF16), preferred_element_type=F32)
    for block in range(width // LANES):
        at = pl.ds(block * LANES, LANES)
        own = table.at[block % 2]
        for g in range(packed):
            ring = circulant(lines[block * packed + g : block * packed + g + 1, :], rows)
            own[g * rows : (g + 1) * rows, 0:rows] = jnp.where(above, ring, 0.0).astype(BF16)
            own[g * rows : (g + 1) * rows, rows : 2 * rows] = jnp.where(above, 0.0, ring).astype(BF16)
        window = jnp.concatenate([prev_ref[:, at], cur_ref[:, at]], axis=0)
        product = jnp.dot(own[...], window, preferred_element_type=F32)
        mixed = pick_groups(product, rows, per_group)
        mixed_ref[:, at] = mixed.astype(BF16)
        gated_ref[:, at] = (query_ref[:, at].astype(F32) * mixed).astype(BF16)


def mix_call(lines, prev, cur, query):
    rows, channels = cur.shape
    groups, taps = lines.shape
    per_group = channels // groups
    width = block_width(channels, WIDTH)
    steps = channels // width
    wide = pl.BlockSpec((rows, width), lambda i: (0, i))
    out = jax.ShapeDtypeStruct((rows, channels), BF16)
    return hbm_call(
        functools.partial(mix_kernel, per_group),
        loose=(0, 1),
        grid=(steps,),
        in_specs=[pl.BlockSpec((width // per_group, taps), lambda i: (i, 0)), wide, wide, wide],
        out_specs=[wide, wide],
        out_shape=[out, out],
        scratch_shapes=[
            pltpu.VMEM((2, LANES // per_group * rows, 2 * rows), BF16),
            pltpu.VMEM((width // per_group, taps), F32),
        ],
        compiler_params=params(),
        cost_estimate=cost(0, 2 * rows * channels),
        name="mix",
    )(lines, prev, cur, query)


def gate_kernel(place, gate_grad_ref, query_ref, mixed_ref, grad_ref, feature_ref):
    width = query_ref.shape[1] // place.shape[0]
    for i in range(place.shape[0]):
        at = pl.ds(i * width, width)
        gate_grad = gate_grad_ref[:, pl.ds(pl.multiple_of(place[i] * width, width), width)].astype(F32)
        grad_ref[:, at] = (gate_grad * query_ref[:, at].astype(F32)).astype(BF16)
        feature_ref[:, at] = (gate_grad * mixed_ref[:, at].astype(F32)).astype(BF16)


def gate_call(place, gate_grad, query, mixed):
    rows, channels = query.shape
    out = jax.ShapeDtypeStruct((rows, channels), BF16)
    return hbm_call(
        gate_kernel,
        loose=(0,),
        grid_spec=pltpu.PrefetchScalarGridSpec(
            num_scalar_prefetch=1,
            grid=(2,),
            in_specs=[pl.BlockSpec((rows // 2, channels), lambda i, place: (i, 0))] * 3,
            out_specs=[pl.BlockSpec((rows // 2, channels), lambda i, place: (i, 0))] * 2,
        ),
        out_shape=[out, out],
        compiler_params=params(),
        cost_estimate=cost(2 * rows * channels, 10 * rows * channels),
        name="gate_back",
    )(place, gate_grad, query, mixed)


def tap_sums(short_taps, grad, tokens_ref, rim_ref, out_ref, at, ext):
    rows = tokens_ref.shape[0]
    extend(ext, rim_ref, tokens_ref[:, at], at)
    grad = grad.astype(F32)
    for tap in range(short_taps):
        out_ref[tap : tap + 1, at] = jnp.sum(grad * ext[RIM - tap : RIM - tap + rows, :], axis=0, keepdims=True)
    out_ref[short_taps:8, at] = jnp.zeros((8 - short_taps, LANES), F32)


def long_grad_kernel(
    per_group, short_taps, prev_ref, cur_ref, grad_ref, feature_ref, tokens_ref, rim_ref, long_ref, short_ref, fold, masked, ext
):
    rows, width = cur_ref.shape
    row, lane = lane_row((rows, rows))
    above = lane > row
    member = lax.broadcasted_iota(jnp.int32, (rows, LANES), 1)
    packed = LANES // per_group
    sums = []
    for block in range(width // LANES):
        at = pl.ds(block * LANES, LANES)
        window = jnp.concatenate([prev_ref[:, at], cur_ref[:, at]], axis=0)
        grad_wide = grad_ref[:, at].astype(F32)
        own = masked.at[block % 2]
        for g in range(packed):
            own[g * rows : (g + 1) * rows, :] = jnp.where((member >= g * per_group) & (member < (g + 1) * per_group), grad_wide, 0.0).astype(BF16)
        pairs = lax.dot_general(own[...], window, (((1,), (1,)), ((), ())), preferred_element_type=F32)
        for g in range(packed):
            pair = pairs[g * rows : (g + 1) * rows]
            ring = jnp.where(above, pair[:, 0:rows], pair[:, rows : 2 * rows])
            total = ring[0:8]
            for tile in range(1, rows // 8):
                total = total + pltpu.roll(ring[8 * tile : 8 * tile + 8], rows - 8 * tile, 1)
            fold[block % 2, g * 8 : (g + 1) * 8, :] = total
        total = fold[block % 2, pl.ds(0, packed, stride=8), :]
        for step in range(1, 8):
            total = total + pltpu.roll(fold[block % 2, pl.ds(step, packed, stride=8), :], rows - step, 1)
        sums.append(total)
        tap_sums(short_taps, feature_ref[:, at], tokens_ref, rim_ref, short_ref, at, ext.at[block % 2])
    long_ref[...] = jnp.dot(
        jnp.concatenate(sums, axis=0), mirror(rows), precision=lax.Precision.HIGHEST, preferred_element_type=F32
    )


def long_grad_call(groups, short_taps, prev, cur, grad, feature, tokens, rim):
    rows, channels = cur.shape
    per_group = channels // groups
    width = block_width(channels, WIDTH)
    steps = channels // width
    wide = pl.BlockSpec((rows, width), lambda i: (0, i))
    packed = LANES // per_group
    return hbm_call(
        functools.partial(long_grad_kernel, per_group, short_taps),
        grid=(steps,),
        in_specs=[wide] * 5 + [pl.BlockSpec((RIM, width), lambda i: (0, i))],
        out_specs=[
            pl.BlockSpec((width // per_group, rows), lambda i: (i, 0)),
            pl.BlockSpec((8, width), lambda i: (0, i)),
        ],
        out_shape=[
            jax.ShapeDtypeStruct((groups, rows), F32),
            jax.ShapeDtypeStruct((8, channels), F32),
        ],
        scratch_shapes=[
            pltpu.VMEM((2, packed * 8, LANES), F32),
            pltpu.VMEM((2, packed * rows, LANES), BF16),
            pltpu.VMEM((2, RIM + rows, LANES), F32),
        ],
        compiler_params=params(),
        cost_estimate=cost(2 * groups * rows * 2 * rows * LANES, 10 * rows * channels),
        name="long_grad",
    )(prev, cur, grad, feature, tokens, rim)


def unmix_kernel(
    per_group, short_taps, lines_ref, grad_ref, next_ref, key_ref, value_ref, key_tokens_ref, value_tokens_ref,
    key_rim_ref, value_rim_ref, query_grad_ref, feature_ref, key_sum_ref, value_sum_ref, edge_ref, table, ext,
):
    rows, width = grad_ref.shape
    row, lane = lane_row((rows, rows))
    below = lane < row
    packed = LANES // per_group
    edge_ref[0] = query_grad_ref[0:RIM, :]
    for block in range(width // LANES):
        at = pl.ds(block * LANES, LANES)
        own = table.at[block % 2]
        for g in range(packed):
            ring = circulant(lines_ref[block * packed + g : block * packed + g + 1, :], rows)
            own[g * rows : (g + 1) * rows, 0:rows] = jnp.where(below, 0.0, ring).astype(BF16)
            own[g * rows : (g + 1) * rows, rows : 2 * rows] = jnp.where(below, ring, 0.0).astype(BF16)
        window = jnp.concatenate([grad_ref[:, at], next_ref[:, at]], axis=0)
        product = jnp.dot(own[...], window, preferred_element_type=F32)
        grad_mixer = pick_groups(product, rows, per_group)
        key_grad = (grad_mixer * value_ref[:, at].astype(F32)).astype(BF16)
        value_grad = (grad_mixer * key_ref[:, at].astype(F32)).astype(BF16)
        feature_ref[0, :, at] = key_grad
        feature_ref[1, :, at] = value_grad
        edge_ref[1, :, at] = key_grad[0:RIM]
        edge_ref[2, :, at] = value_grad[0:RIM]
        slot = 2 * (block % 2)
        tap_sums(short_taps, key_grad, key_tokens_ref, key_rim_ref, key_sum_ref, at, ext.at[slot])
        tap_sums(short_taps, value_grad, value_tokens_ref, value_rim_ref, value_sum_ref, at, ext.at[slot + 1])


def unmix_call(lines, short_taps, grad, grad_next, key, value, tokens, rim, query_grad):
    rows, channels = grad.shape
    per_group = channels // lines.shape[0]
    width = block_width(channels, WIDTH)
    steps = channels // width

    def spec(height, part):
        return pl.BlockSpec((height, width), lambda i, part=part: (0, i + part * steps))

    wide = spec(rows, 0)
    sums = jax.ShapeDtypeStruct((8, channels), F32)
    return hbm_call(
        functools.partial(unmix_kernel, per_group, short_taps),
        loose=(0, 2),
        grid=(steps,),
        in_specs=[pl.BlockSpec((width // per_group, rows), lambda i: (i, 0))]
        + [wide] * 4
        + [spec(rows, 1), spec(rows, 2), spec(RIM, 1), spec(RIM, 2), spec(2 * RIM, 0)],
        out_specs=[
            pl.BlockSpec((2, rows, width), lambda i: (0, 0, i)),
            spec(8, 0),
            spec(8, 0),
            pl.BlockSpec((3, RIM, width), lambda i: (0, 0, i)),
        ],
        out_shape=[
            jax.ShapeDtypeStruct((2, rows, channels), BF16),
            sums,
            sums,
            jax.ShapeDtypeStruct((3, RIM, channels), BF16),
        ],
        scratch_shapes=[
            pltpu.VMEM((2, LANES // per_group * rows, 2 * rows), BF16),
            pltpu.VMEM((4, RIM + rows, LANES), F32),
        ],
        compiler_params=params(),
        cost_estimate=cost(2 * channels * rows * 2 * rows * LANES // per_group, 16 * rows * channels),
        name="unmix",
    )(lines, grad, grad_next, key, value, tokens, tokens, rim, rim, query_grad)


def short_adjoint_kernel(short_taps, grads_ref, rim_ref, filter_ref, *refs):
    out_ref, ext = refs[-2:]
    rows, width = out_ref.shape
    for block in range(width // LANES):
        at = pl.ds(block * LANES, LANES)
        own = ext.at[block % 2]
        own[0:rows, :] = grads_ref[0, :, at].astype(F32)
        own[rows:, :] = rim_ref[0, :, at].astype(F32)
        taps = filter_ref[:, at]
        total = taps[0:1] * own[0:rows, :]
        for tap in range(1, short_taps):
            total = total + taps[tap : tap + 1] * own[tap : tap + rows, :]
        out_ref[:, at] = total.astype(BF16)


def short_adjoint_call(grads, rim, filters, given, part, out):
    _, rows, channels = grads.shape
    short_taps = filters.shape[0]
    width = block_width(channels, 2 * WIDTH)
    steps = channels // width
    result = pl.BlockSpec((rows, width), lambda i: (0, part * steps + i))
    olds = [] if out is None else [out]
    return hbm_call(
        functools.partial(short_adjoint_kernel, short_taps),
        loose=(1,),
        grid=(steps,),
        in_specs=[
            pl.BlockSpec((1, rows, width), lambda i: (given, 0, i)),
            pl.BlockSpec((1, RIM, width), lambda i: (part, 0, i)),
            pl.BlockSpec((short_taps, width), lambda i: (0, part * steps + i)),
        ]
        + [pl.BlockSpec(memory_space=pl.ANY)] * len(olds),
        out_specs=result,
        out_shape=jax.ShapeDtypeStruct((rows, 3 * channels), BF16),
        input_output_aliases={3: 0} if olds else {},
        scratch_shapes=[pltpu.VMEM((2, rows + RIM, LANES), F32)],
        compiler_params=params(),
        cost_estimate=cost(2 * short_taps * rows * channels, 4 * rows * channels),
        name="short_adjoint",
    )(grads, rim, filters, *olds)


def spread_kernel(place, query_ref, key_ref, value_ref, long_ref, own_ref, other_ref):
    steps = query_ref.shape[1] // LANES
    half = own_ref.shape[0]
    tiles = [ref[:, i * LANES : (i + 1) * LANES] for ref in (query_ref, key_ref, value_ref) for i in range(steps)]
    tiles += [long_ref[8 * i : 8 * i + 8, :] for i in range(long_ref.shape[0] // 8)]
    first = place[0] < half

    @pl.when(first)
    def _():
        for i in range(half):
            own_ref[place[i]] = tiles[i]
            other_ref[place[half + i] - half] = tiles[half + i]

    @pl.when(jnp.logical_not(first))
    def _():
        for i in range(half):
            other_ref[place[i] - half] = tiles[i]
            own_ref[place[half + i]] = tiles[half + i]


def collect_kernel(place, *refs):
    parts, short_ref, long_ref, tiles_ref = refs[:-3], refs[-3], refs[-2], refs[-1]
    short_taps, wide = short_ref.shape
    steps = wide // LANES
    size = parts[0].shape[0]
    for i, part in enumerate(parts):
        tiles_ref[i * size : (i + 1) * size] = part[...]
    for i in range(steps):
        short_ref[:, i * LANES : (i + 1) * LANES] = tiles_ref[place[i]][0:short_taps, :]
    for i in range(long_ref.shape[0] // 8):
        long_ref[8 * i : 8 * i + 8, :] = tiles_ref[place[steps + i]]


def in_vmem():
    return pl.BlockSpec(memory_space=pltpu.VMEM)


def total_over_devices(spread_to, collect_from, query_sum, key_sum, value_sum, long_sum, short_taps, first, after):
    ny, nz = lax.axis_size("y"), lax.axis_size("z")
    channels = query_sum.shape[1]
    count = 3 * channels // LANES + long_sum.shape[0] // 8
    half = jax.ShapeDtypeStruct((count // 2, 8, LANES), F32)
    own, other = pl.pallas_call(
        spread_kernel,
        in_specs=[pl.BlockSpec(memory_space=pltpu.SMEM)] + [in_vmem()] * 4,
        out_specs=[in_vmem()] * 2,
        out_shape=[half] * 2,
        compiler_params=params(),
        name="spread",
    )(spread_to, query_sum, key_sum, value_sum, long_sum)
    part = own + move(other, c=1)
    size = count // 2 // nz
    part = sum([move(part[d * size : (d + 1) * size], z=d) for d in range(1, nz)], part[:size])
    terms, first = lax.optimization_barrier(([part] + [move(part, y=d) for d in range(1, ny)], first))
    whole = paired_sum(terms)
    terms = [move(whole, xl=a, xh=b) for a, b in FLIPS]
    terms, beside = lax.optimization_barrier((terms, after(first)))
    whole = paired_sum(terms)
    line = jnp.concatenate([whole, move(whole, c=1)], axis=0)
    lines = [move(line, z=-d) for d in range(nz)]
    groups, taps = long_sum.shape
    short, long = pl.pallas_call(
        collect_kernel,
        in_specs=[pl.BlockSpec(memory_space=pltpu.SMEM)] + [in_vmem()] * nz,
        out_specs=[in_vmem(), in_vmem()],
        scratch_shapes=[pltpu.VMEM((count, 8, LANES), F32)],
        out_shape=[
            jax.ShapeDtypeStruct((short_taps, 3 * channels), F32),
            jax.ShapeDtypeStruct((groups, taps), F32),
        ],
        compiler_params=params(),
        name="collect",
    )(collect_from, *lines)
    return short, long, beside


def paired_sum(terms):
    half = len(terms) // 2
    if half == 0:
        return terms[0]
    return paired_sum([terms[i] + terms[i + half] for i in range(half)])


def gather_tall(shard):
    return [move(shard[shard.shape[0] // 2 :], y=d) for d in range(lax.axis_size("y"))]


def gather_wide(shard):
    return [move(shard[: shard.shape[0] // 2], xl=a, xh=b) for a, b in FLIPS]


def gather_far(wide_top, tall_bottom):
    ny = lax.axis_size("y")
    wide_top, tall_bottom = jnp.stack(wide_top), jnp.stack(tall_bottom)
    return (
        [move(wide_top, y=d) for d in range(ny)],
        [move(tall_bottom, xl=a, xh=b) for a, b in FLIPS],
    )


def piece_rows(tops, bottoms, step):
    rows = []
    for a in range(2):
        rows.append(jnp.concatenate([tops[step][2 * a + b] for b in range(2)], axis=1))
        rows.append(jnp.concatenate([bottoms[2 * a + b][step] for b in range(2)], axis=1))
    return rows


def gate_matmul_kernel(ny, *refs):
    cotangent_ref, tops, bottoms, out_ref = refs[0], refs[1 : 1 + ny], refs[1 + ny : 5 + ny], refs[5 + ny]
    left = cotangent_ref[...]
    at = 0
    for step in range(ny):
        for right in piece_rows(tops, bottoms, step):
            size = right.shape[0]
            out_ref[:, at : at + size] = lax.dot_general(
                left, right, (((1,), (1,)), ((), ())), preferred_element_type=F32
            ).astype(BF16)
            at += size


def whole(x):
    return pl.BlockSpec(x.shape, lambda *_, n=x.ndim: (0,) * n)


def gate_matmul(cotangents, tops, bottoms):
    rows, depth = cotangents.shape
    ny = len(tops)
    channels = 4 * ny * tops[0].shape[1]
    height = rows // 2
    return hbm_call(
        functools.partial(gate_matmul_kernel, ny),
        loose=range(5 + ny),
        grid=(rows // height,),
        in_specs=[pl.BlockSpec((height, depth), lambda i: (i, 0))] + [whole(x) for x in (*tops, *bottoms)],
        out_specs=pl.BlockSpec((height, channels), lambda i: (i, 0)),
        out_shape=jax.ShapeDtypeStruct((rows, channels), BF16),
        compiler_params=params(32),
        cost_estimate=cost(2 * rows * depth * channels, 2 * (rows + depth) * channels),
        name="gate_matmul",
    )(cotangents, *tops, *bottoms)


def picked(origin, step, rows_ref):
    height = rows_ref.shape[1] // 2
    at = [pl.multiple_of(origin[2 * step + a] % 2 * height, height) for a in range(2)]
    return jnp.concatenate([rows_ref[:, pl.ds(x, height)] for x in at], axis=1)


def weight_grad_kernel(ny, origin, rows_ref, turned_ref, *refs):
    top_grads, bottom_grads = refs[:ny], refs[ny:]
    step = pl.program_id(0)
    size = bottom_grads[0].shape[2]
    width = bottom_grads[0].shape[1]
    rows = picked(origin, step, rows_ref)
    grads = jnp.dot(turned_ref[...], rows, preferred_element_type=F32).astype(BF16)
    for f in range(4):
        a, b = f // 2, f % 2
        at = (2 * a + 1) * size
        bottom_grads[f][step] = grads[b * width : (b + 1) * width, at : at + size]
    for d in range(ny):

        @pl.when(step == d)
        def _(d=d):
            for f in range(4):
                a, b = f // 2, f % 2
                at = 2 * a * size
                top_grads[d][f] = grads[b * width : (b + 1) * width, at : at + size]


def rows_of(origin, all_rows, ny):
    rows, channels = all_rows.shape
    return pl.BlockSpec((rows, channels // ny), lambda i, origin: (0, origin[2 * i] // 2))


def weight_grad(origin, all_rows, turned, ny):
    rows, channels = all_rows.shape
    size = channels // (4 * ny)
    width = turned.shape[0] // 2
    outs = [jax.ShapeDtypeStruct((4, width, size), BF16)] * ny + [jax.ShapeDtypeStruct((ny, width, size), BF16)] * 4
    results = hbm_call(
        functools.partial(weight_grad_kernel, ny),
        loose=(0, 2),
        grid_spec=pltpu.PrefetchScalarGridSpec(
            num_scalar_prefetch=1,
            grid=(ny,),
            in_specs=[rows_of(origin, all_rows, ny), whole(turned)],
            out_specs=[whole(x) for x in outs],
        ),
        out_shape=outs,
        compiler_params=params(40),
        cost_estimate=cost(4 * rows * width * channels, 2 * (rows + 2 * width) * channels),
        name="weight_grad",
    )(origin, all_rows, turned)
    return results[:ny], results[ny:]


def output_kernel(ny, origin, rows_ref, *refs):
    tops, bottoms, own_ref, other_ref, total = refs[:ny], refs[ny : ny + 4], refs[-3], refs[-2], refs[-1]
    step = pl.program_id(0)
    width = own_ref.shape[1]
    rows = picked(origin, step, rows_ref)
    for d in range(ny):

        @pl.when(step == d)
        def _(d=d):
            right = jnp.concatenate(piece_rows(tops, bottoms, d), axis=0)
            product = jnp.dot(rows, right, preferred_element_type=F32)
            if d == 0:
                total[...] = product
            else:
                total[...] += product

    @pl.when(step == ny - 1)
    def _():
        own_ref[...] = total[:, :width].astype(BF16)
        other_ref[...] = total[:, width:].astype(BF16)


def output_call(origin, all_rows, tops, bottoms):
    rows, channels = all_rows.shape
    ny = len(tops)
    width = tops[0].shape[2]
    half = jax.ShapeDtypeStruct((rows, width), BF16)
    return hbm_call(
        functools.partial(output_kernel, ny),
        loose=(0, *range(2, 6 + ny)),
        grid_spec=pltpu.PrefetchScalarGridSpec(
            num_scalar_prefetch=1,
            grid=(ny,),
            in_specs=[rows_of(origin, all_rows, ny)] + [whole(x) for x in (*tops, *bottoms)],
            out_specs=[whole(half)] * 2,
            scratch_shapes=[pltpu.VMEM((rows, 2 * width), F32)],
        ),
        out_shape=[half, half],
        compiler_params=params(32),
        cost_estimate=cost(4 * rows * width * channels, 2 * (rows + 2 * width) * channels),
        name="output",
    )(origin, all_rows, *tops, *bottoms)


def added(terms):
    total = terms[0].astype(F32)
    for term in terms[1:]:
        total = total + term.astype(F32)
    return total


def plane_scatter(top_grads, bottom_grads, beside):
    ny = len(top_grads)
    top = added([move(top_grads[d], y=-d) for d in range(ny)]).astype(BF16)
    bottom = added([move(bottom_grads[f], xl=a, xh=b) for f, (a, b) in enumerate(FLIPS)]).astype(BF16)
    top, bottom, beside = lax.optimization_barrier((top, bottom, beside))
    top = [move(top[f], xl=a, xh=b) for f, (a, b) in enumerate(FLIPS)]
    bottom = [move(bottom[d], y=-d) for d in range(ny)]
    return top, bottom, beside


def shards(tokens_in, short_filter, long_filter, out_weight, cotangent):
    ny, nz = lax.axis_size("y"), lax.axis_size("z")
    y, xl, xh, z, c = (lax.axis_index(a) for a in ("y", "xl", "xh", "z", "c"))
    tokens = tokens_in[0]
    rows, wide = tokens.shape
    channels = wide // 3
    short_taps = short_filter.shape[0]
    groups = long_filter.shape[0]
    upstream = cotangent[0]
    length, columns = upstream.shape
    span = length // 2

    block = jnp.arange(2 * ny, dtype=jnp.int32)
    place = ((y - block // 2) % ny) * 2 + (block + xl) % 2
    origin = place
    size = 3 * channels // LANES + groups // 8
    each = size // (2 * nz)
    tile = jnp.arange(size, dtype=jnp.int32)
    core_step, z_step = (tile // (nz * each) + c) % 2, (tile // each - z) % nz
    spread_to = (core_step * nz + z_step) * each + tile % each
    collect_from = (z_step * 2 + core_step) * each + tile % each

    rim = along(tokens[rows - RIM :], 1)
    lines = long_filter.astype(F32)
    parts = features_call(tokens, short_filter)
    parts, rim = lax.optimization_barrier((parts, rim))
    query, key, value, mixer = features_call(tokens, short_filter, rim, parts)
    mixer, out_weight = lax.optimization_barrier((mixer, out_weight))
    mixer_prev = along(mixer, 1)
    tall_bottom = gather_tall(out_weight)
    mixer_prev, tall_bottom = lax.optimization_barrier((mixer_prev, tall_bottom))
    mixed, gated = mix_call(lines, mixer_prev, mixer, query)
    mixed, out_weight, half = lax.optimization_barrier((mixed, out_weight, xh))
    wide_top = gather_wide(out_weight)
    wide_top, tall_bottom, half = lax.optimization_barrier((wide_top, tall_bottom, half))
    all_rows = lax.all_gather(gated, ("z", "c"), axis=0, tiled=True)
    tops, bottoms = gather_far(wide_top, tall_bottom)
    others = move(lax.dynamic_slice_in_dim(upstream, (1 - half) * span, span, 0), xh=1)
    mine = lax.dynamic_slice_in_dim(upstream, half * span, span, 0)
    cotangents = jnp.concatenate([mine, others], axis=1)
    partial = gate_matmul(cotangents, tops, bottoms)
    partial, all_rows = lax.optimization_barrier((partial, all_rows))
    gate_grad = lax.psum_scatter(partial, ("z", "c"), scatter_dimension=0, tiled=True)

    top_grads, bottom_grads = weight_grad(origin, all_rows, cotangents.T, ny)
    own, other = output_call(origin, all_rows, tops, bottoms)
    top, bottom, other = plane_scatter(top_grads, bottom_grads, other)
    gate_grad, top, bottom, other = lax.optimization_barrier((gate_grad, top, bottom, other))

    grad_mixed, query_grad = gate_call(place, gate_grad, query, mixed)
    grad_next = along(grad_mixed, -1)
    long_sum, query_sum = long_grad_call(
        groups, short_taps, mixer_prev, mixer, grad_mixed, query_grad, tokens, rim
    )
    grad_weight = jnp.concatenate([added(top), added(bottom)], axis=1).T
    grad_next, grad_weight, other, long_sum, query_sum = lax.optimization_barrier(
        (grad_next, grad_weight, other, long_sum, query_sum)
    )
    theirs = move(other, xh=1)
    other_grads, key_sum, value_sum, edge = unmix_call(
        lines, short_taps, grad_mixed, grad_next, key, value, tokens, rim, query_grad
    )
    edge, key_sum, theirs = lax.optimization_barrier((edge, key_sum, theirs))
    output = jnp.where(xh == 0, jnp.concatenate([own, theirs], axis=0), jnp.concatenate([theirs, own], axis=0))
    edge = along(edge, -1)
    query_part = short_adjoint_call(query_grad[None], edge, short_filter, 0, 0, None)

    def key_part(query_part):
        return short_adjoint_call(other_grads, edge, short_filter, 0, 1, query_part)

    grad_short, grad_long, grad_tokens = total_over_devices(
        spread_to, collect_from, query_sum, key_sum, value_sum, long_sum, short_taps, query_part, key_part
    )
    grad_tokens = short_adjoint_call(other_grads, edge, short_filter, 1, 2, grad_tokens)
    return output[None], grad_tokens[None], grad_short, grad_long, grad_weight


def solution(mesh):
    dp, seq = mesh.shape["dp"], mesh.shape["seq"]
    grid = jax.sharding.Mesh(mesh.devices.reshape(dp // 2, 2, 2, seq // 4, 2), ("y", "xl", "xh", "z", "c"))
    rows, line = ("y", "xl"), ("xh", "z", "c")
    return jax.shard_map(
        shards,
        mesh=grid,
        in_specs=(P(rows, line, None), P(), P(), P(rows, line), P(rows, None, line)),
        out_specs=(P(rows, None, line), P(rows, line, None), P(), P(), P(rows, line)),
        check_vma=False,
    )
```

```python
import functools
import itertools
import math

import jax
import jax.numpy as jnp
from jax import lax
from jax.experimental import pallas as pl
from jax.experimental.pallas import tpu as pltpu
from jax.sharding import PartitionSpec as P

LANES = 128
RIM = 8
MIB = 1024 * 1024
WIDTH = 1024
F32 = jnp.float32
BF16 = jnp.bfloat16


PLANE = ("y", "xl", "xh")
LINE = ("xh", "z", "c")


def along(x, by):
    size = math.prod(lax.axis_size(a) for a in LINE)
    pairs = [(i, i + by) for i in range(size) if 0 <= i + by < size]
    return lax.ppermute(x, LINE, pairs)


def move(x, **steps):
    axes = tuple(a for a in ("y", "xl", "xh", "z", "c") if steps.get(a, 0) % lax.axis_size(a))
    if not axes:
        return x
    sizes = [lax.axis_size(a) for a in axes]
    pairs = []
    for at in itertools.product(*(range(n) for n in sizes)):
        to = [(p + steps[a]) % n for p, a, n in zip(at, axes, sizes)]
        pairs.append((flat(at, sizes), flat(to, sizes)))
    return lax.ppermute(x, axes, pairs)


def flat(at, sizes):
    index = 0
    for p, n in zip(at, sizes):
        index = index * n + p
    return index


FLIPS = [(0, 0), (0, 1), (1, 0), (1, 1)]


def params(mib=16):
    return pltpu.CompilerParams(vmem_limit_bytes=mib * MIB)


def hbm_call(kernel, *, out_shape, loose=(), **options):
    single = not isinstance(out_shape, (list, tuple))
    shapes = [out_shape] if single else out_shape
    placed = [pltpu.HBM(x.shape, x.dtype) if x.size * x.dtype.itemsize > 256 * 1024 else x for x in shapes]
    call = pl.pallas_call(kernel, out_shape=placed[0] if single else placed, **options)

    def run(*args):
        held = [x if i in loose else pltpu.with_memory_space_constraint(x, pltpu.HBM) for i, x in enumerate(args)]
        return call(*held)

    return run


def cost(flops, moved):
    return pl.CostEstimate(flops=int(flops), bytes_accessed=int(moved), transcendentals=0)


def block_width(channels, most):
    width = min(channels, most)
    while channels % width:
        width //= 2
    return width


def extend(ext, rim, rows_of, at):
    ext[0:RIM, :] = jnp.zeros((RIM, LANES), F32) if rim is None else rim[:, at].astype(F32)
    ext[RIM:, :] = rows_of.astype(F32)


def features_kernel(short_taps, tokens, rims, filters, query_ref, key_ref, value_ref, mixer_ref, ext):
    rows, width = tokens[0].shape

    def filtered(part, block, at):
        own = ext.at[(3 * block + part) % ext.shape[0]]
        extend(own, rims and rims[part], tokens[part][:, at], at)
        taps = filters[part][:, at]
        total = taps[0:1] * own[RIM : RIM + rows, :]
        for tap in range(1, short_taps):
            total = total + taps[tap : tap + 1] * own[RIM - tap : RIM - tap + rows, :]
        return total

    for block in range(width // LANES):
        at = pl.ds(block * LANES, LANES)
        query_ref[:, at] = filtered(0, block, at).astype(BF16)
        key, value = filtered(1, block, at), filtered(2, block, at)
        key_ref[:, at] = key.astype(BF16)
        value_ref[:, at] = value.astype(BF16)
        mixer_ref[:, at] = (key * value).astype(BF16)


def features_call(tokens, filters, rim=None, given=None):
    rows, wide = tokens.shape
    channels = wide // 3
    taps = filters.shape[0]
    rows = rows if given is None else 2 * RIM
    width = channels if given else block_width(channels, WIDTH)
    steps = channels // width

    def spec(height, part):
        return pl.BlockSpec((height, width), lambda i, part=part: (0, i + part * steps))

    held = [] if given is None else [rim] * 3
    olds = [] if given is None else list(given)

    def body(*refs):
        n = 3 + len(held)
        rims = refs[3:n] if held else None
        features_kernel(taps, refs[0:3], rims, refs[n : n + 3], *refs[n + 3 + len(olds) :])

    out = jax.ShapeDtypeStruct((tokens.shape[0], channels), BF16)
    return hbm_call(
        body,
        loose=(3, 4, 5) if held else (),
        grid=(steps,),
        in_specs=[spec(rows, p) for p in range(3)]
        + [spec(RIM, p) for p in range(len(held))]
        + [spec(taps, p) for p in range(3)]
        + [pl.BlockSpec(memory_space=pl.ANY)] * len(olds),
        out_specs=[pl.BlockSpec((rows, width), lambda i: (0, i))] * 4,
        out_shape=[out] * 4,
        input_output_aliases={9 + i: i for i in range(len(olds))},
        scratch_shapes=[pltpu.VMEM((6, RIM + rows, LANES), F32)],
        compiler_params=params(),
        cost_estimate=cost(0, rows * wide),
        name="features" if given is None else "first_rows",
    )(*[tokens] * 3, *held, *[filters] * 3, *olds)


def lane_row(shape):
    row = lax.broadcasted_iota(jnp.int32, shape, 0)
    lane = lax.broadcasted_iota(jnp.int32, shape, 1)
    return row, lane


def mirror(size):
    row, lane = lane_row((size, size))
    both = row + lane
    return jnp.where((both == 0) | (both == size), 1.0, 0.0)


def circulant(line, taps):
    wide = jnp.broadcast_to(line.astype(F32), (taps, taps))
    return pltpu.roll(wide, 0, 1, stride=1, stride_axis=0)


def pick_groups(product, rows, per_group):
    lane = lax.broadcasted_iota(jnp.int32, (rows, LANES), 1)
    total = product[0:rows]
    for g in range(1, LANES // per_group):
        total = jnp.where(lane >= g * per_group, product[g * rows : (g + 1) * rows], total)
    return total


def mix_kernel(per_group, lines_ref, prev_ref, cur_ref, query_ref, mixed_ref, gated_ref, table, lines):
    rows, width = cur_ref.shape
    row, lane = lane_row((rows, rows))
    above = lane > row
    packed = LANES // per_group
    lines[...] = jnp.dot(lines_ref[...].astype(BF16), mirror(rows).astype(BF16), preferred_element_type=F32)
    for block in range(width // LANES):
        at = pl.ds(block * LANES, LANES)
        own = table.at[block % 2]
        for g in range(packed):
            ring = circulant(lines[block * packed + g : block * packed + g + 1, :], rows)
            own[g * rows : (g + 1) * rows, 0:rows] = jnp.where(above, ring, 0.0).astype(BF16)
            own[g * rows : (g + 1) * rows, rows : 2 * rows] = jnp.where(above, 0.0, ring).astype(BF16)
        window = jnp.concatenate([prev_ref[:, at], cur_ref[:, at]], axis=0)
        product = jnp.dot(own[...], window, preferred_element_type=F32)
        mixed = pick_groups(product, rows, per_group)
        mixed_ref[:, at] = mixed.astype(BF16)
        gated_ref[:, at] = (query_ref[:, at].astype(F32) * mixed).astype(BF16)


def mix_call(lines, prev, cur, query):
    rows, channels = cur.shape
    groups, taps = lines.shape
    per_group = channels // groups
    width = block_width(channels, WIDTH)
    steps = channels // width
    wide = pl.BlockSpec((rows, width), lambda i: (0, i))
    out = jax.ShapeDtypeStruct((rows, channels), BF16)
    return hbm_call(
        functools.partial(mix_kernel, per_group),
        loose=(0, 1),
        grid=(steps,),
        in_specs=[pl.BlockSpec((width // per_group, taps), lambda i: (i, 0)), wide, wide, wide],
        out_specs=[wide, wide],
        out_shape=[out, out],
        scratch_shapes=[
            pltpu.VMEM((2, LANES // per_group * rows, 2 * rows), BF16),
            pltpu.VMEM((width // per_group, taps), F32),
        ],
        compiler_params=params(),
        cost_estimate=cost(0, 2 * rows * channels),
        name="mix",
    )(lines, prev, cur, query)


def gate_kernel(place, gate_grad_ref, query_ref, grad_ref):
    width = query_ref.shape[1] // place.shape[0]
    for i in range(place.shape[0]):
        at = pl.ds(i * width, width)
        gate_grad = gate_grad_ref[:, pl.ds(pl.multiple_of(place[i] * width, width), width)].astype(F32)
        grad_ref[:, at] = (gate_grad * query_ref[:, at].astype(F32)).astype(BF16)


def gate_call(place, gate_grad, query):
    rows, channels = query.shape
    half = pl.BlockSpec((rows // 2, channels), lambda i, place: (i, 0))
    return hbm_call(
        gate_kernel,
        loose=(0,),
        grid_spec=pltpu.PrefetchScalarGridSpec(
            num_scalar_prefetch=1, grid=(2,), in_specs=[half, half], out_specs=half
        ),
        out_shape=jax.ShapeDtypeStruct((rows, channels), BF16),
        compiler_params=params(),
        cost_estimate=cost(rows * channels, 6 * rows * channels),
        name="gate_back",
    )(place, gate_grad, query)


def tap_sums(short_taps, grad, tokens_ref, rim_ref, out_ref, at, ext):
    rows = tokens_ref.shape[0]
    extend(ext, rim_ref, tokens_ref[:, at], at)
    grad = grad.astype(F32)
    for tap in range(short_taps):
        out_ref[tap : tap + 1, at] = jnp.sum(grad * ext[RIM - tap : RIM - tap + rows, :], axis=0, keepdims=True)
    out_ref[short_taps:8, at] = jnp.zeros((8 - short_taps, LANES), F32)


def long_grad_kernel(
    per_group, short_taps, place, prev_ref, cur_ref, grad_ref, gate_grad_ref, mixed_ref, tokens_ref, rim_ref,
    long_ref, short_ref, feature_ref, fold, masked, ext,
):
    step = pl.program_id(0)
    rows, width = cur_ref.shape
    row, lane = lane_row((rows, rows))
    above = lane > row
    member = lax.broadcasted_iota(jnp.int32, (rows, LANES), 1)
    packed = LANES // per_group
    sums = []
    for block in range(width // LANES):
        at = pl.ds(block * LANES, LANES)
        window = jnp.concatenate([prev_ref[:, at], cur_ref[:, at]], axis=0)
        grad_wide = grad_ref[:, at].astype(F32)
        own = masked.at[block % 2]
        for g in range(packed):
            own[g * rows : (g + 1) * rows, :] = jnp.where((member >= g * per_group) & (member < (g + 1) * per_group), grad_wide, 0.0).astype(BF16)
        pairs = lax.dot_general(own[...], window, (((1,), (1,)), ((), ())), preferred_element_type=F32)
        for g in range(packed):
            pair = pairs[g * rows : (g + 1) * rows]
            ring = jnp.where(above, pair[:, 0:rows], pair[:, rows : 2 * rows])
            total = ring[0:8]
            for tile in range(1, rows // 8):
                total = total + pltpu.roll(ring[8 * tile : 8 * tile + 8], rows - 8 * tile, 1)
            fold[block % 2, g * 8 : (g + 1) * 8, :] = total
        total = fold[block % 2, pl.ds(0, packed, stride=8), :]
        for step in range(1, 8):
            total = total + pltpu.roll(fold[block % 2, pl.ds(step, packed, stride=8), :], rows - step, 1)
        sums.append(total)
        side, inner = divmod(block * LANES, width // 2)
        gate_at = pl.multiple_of(place[2 * step + side] % 2 * (width // 2) + inner, LANES)
        gate_grad = gate_grad_ref[:, pl.ds(gate_at, LANES)].astype(F32)
        feature = (gate_grad * mixed_ref[:, at].astype(F32)).astype(BF16)
        feature_ref[:, at] = feature
        tap_sums(short_taps, feature, tokens_ref, rim_ref, short_ref, at, ext.at[block % 2])
    long_ref[...] = jnp.dot(
        jnp.concatenate(sums, axis=0), mirror(rows), precision=lax.Precision.HIGHEST, preferred_element_type=F32
    )


def long_grad_call(place, groups, short_taps, prev, cur, grad, gate_grad, mixed, tokens, rim):
    rows, channels = cur.shape
    per_group = channels // groups
    steps = place.shape[0] // 2
    width = channels // steps
    wide = pl.BlockSpec((rows, width), lambda i, place: (0, i))
    packed = LANES // per_group
    return hbm_call(
        functools.partial(long_grad_kernel, per_group, short_taps),
        loose=(0,),
        grid_spec=pltpu.PrefetchScalarGridSpec(
            num_scalar_prefetch=1,
            grid=(steps,),
            in_specs=[
                wide,
                wide,
                wide,
                pl.BlockSpec((rows, width), lambda i, place: (0, place[2 * i] // 2)),
                wide,
                wide,
                pl.BlockSpec((RIM, width), lambda i, place: (0, i)),
            ],
            out_specs=[
                pl.BlockSpec((width // per_group, rows), lambda i, place: (i, 0)),
                pl.BlockSpec((8, width), lambda i, place: (0, i)),
                wide,
            ],
            scratch_shapes=[
                pltpu.VMEM((2, packed * 8, LANES), F32),
                pltpu.VMEM((2, packed * rows, LANES), BF16),
                pltpu.VMEM((2, RIM + rows, LANES), F32),
            ],
        ),
        out_shape=[
            jax.ShapeDtypeStruct((groups, rows), F32),
            jax.ShapeDtypeStruct((8, channels), F32),
            jax.ShapeDtypeStruct((rows, channels), BF16),
        ],
        compiler_params=params(),
        cost_estimate=cost(2 * groups * rows * 2 * rows * LANES, 14 * rows * channels),
        name="long_grad",
    )(place, prev, cur, grad, gate_grad, mixed, tokens, rim)


def unmix_kernel(
    per_group, short_taps, lines_ref, grad_ref, next_ref, key_ref, value_ref, key_tokens_ref, value_tokens_ref,
    key_rim_ref, value_rim_ref, query_grad_ref, feature_ref, key_sum_ref, value_sum_ref, edge_ref, table, ext,
):
    rows, width = grad_ref.shape
    row, lane = lane_row((rows, rows))
    below = lane < row
    packed = LANES // per_group
    edge_ref[0] = query_grad_ref[0:RIM, :]
    for block in range(width // LANES):
        at = pl.ds(block * LANES, LANES)
        own = table.at[block % 2]
        for g in range(packed):
            ring = circulant(lines_ref[block * packed + g : block * packed + g + 1, :], rows)
            own[g * rows : (g + 1) * rows, 0:rows] = jnp.where(below, 0.0, ring).astype(BF16)
            own[g * rows : (g + 1) * rows, rows : 2 * rows] = jnp.where(below, ring, 0.0).astype(BF16)
        window = jnp.concatenate([grad_ref[:, at], next_ref[:, at]], axis=0)
        product = jnp.dot(own[...], window, preferred_element_type=F32)
        grad_mixer = pick_groups(product, rows, per_group)
        key_grad = (grad_mixer * value_ref[:, at].astype(F32)).astype(BF16)
        value_grad = (grad_mixer * key_ref[:, at].astype(F32)).astype(BF16)
        feature_ref[0, :, at] = key_grad
        feature_ref[1, :, at] = value_grad
        edge_ref[1, :, at] = key_grad[0:RIM]
        edge_ref[2, :, at] = value_grad[0:RIM]
        slot = 2 * (block % 2)
        tap_sums(short_taps, key_grad, key_tokens_ref, key_rim_ref, key_sum_ref, at, ext.at[slot])
        tap_sums(short_taps, value_grad, value_tokens_ref, value_rim_ref, value_sum_ref, at, ext.at[slot + 1])


def unmix_call(lines, short_taps, grad, grad_next, key, value, tokens, rim, query_grad):
    rows, channels = grad.shape
    per_group = channels // lines.shape[0]
    width = block_width(channels, WIDTH)
    steps = channels // width

    def spec(height, part):
        return pl.BlockSpec((height, width), lambda i, part=part: (0, i + part * steps))

    wide = spec(rows, 0)
    sums = jax.ShapeDtypeStruct((8, channels), F32)
    return hbm_call(
        functools.partial(unmix_kernel, per_group, short_taps),
        loose=(0, 2),
        grid=(steps,),
        in_specs=[pl.BlockSpec((width // per_group, rows), lambda i: (i, 0))]
        + [wide] * 4
        + [spec(rows, 1), spec(rows, 2), spec(RIM, 1), spec(RIM, 2), spec(2 * RIM, 0)],
        out_specs=[
            pl.BlockSpec((2, rows, width), lambda i: (0, 0, i)),
            spec(8, 0),
            spec(8, 0),
            pl.BlockSpec((3, RIM, width), lambda i: (0, 0, i)),
        ],
        out_shape=[
            jax.ShapeDtypeStruct((2, rows, channels), BF16),
            sums,
            sums,
            jax.ShapeDtypeStruct((3, RIM, channels), BF16),
        ],
        scratch_shapes=[
            pltpu.VMEM((2, LANES // per_group * rows, 2 * rows), BF16),
            pltpu.VMEM((4, RIM + rows, LANES), F32),
        ],
        compiler_params=params(),
        cost_estimate=cost(2 * channels * rows * 2 * rows * LANES // per_group, 16 * rows * channels),
        name="unmix",
    )(lines, grad, grad_next, key, value, tokens, tokens, rim, rim, query_grad)


def short_adjoint_kernel(short_taps, grads_ref, rim_ref, filter_ref, *refs):
    out_ref, ext = refs[-2:]
    rows, width = out_ref.shape
    for block in range(width // LANES):
        at = pl.ds(block * LANES, LANES)
        own = ext.at[block % 2]
        own[0:rows, :] = grads_ref[0, :, at].astype(F32)
        own[rows:, :] = rim_ref[0, :, at].astype(F32)
        taps = filter_ref[:, at]
        total = taps[0:1] * own[0:rows, :]
        for tap in range(1, short_taps):
            total = total + taps[tap : tap + 1] * own[tap : tap + rows, :]
        out_ref[:, at] = total.astype(BF16)


def short_adjoint_call(grads, rim, filters, given, part, out):
    _, rows, channels = grads.shape
    short_taps = filters.shape[0]
    width = block_width(channels, 2 * WIDTH)
    steps = channels // width
    result = pl.BlockSpec((rows, width), lambda i: (0, part * steps + i))
    olds = [] if out is None else [out]
    return hbm_call(
        functools.partial(short_adjoint_kernel, short_taps),
        loose=(1,),
        grid=(steps,),
        in_specs=[
            pl.BlockSpec((1, rows, width), lambda i: (given, 0, i)),
            pl.BlockSpec((1, RIM, width), lambda i: (part, 0, i)),
            pl.BlockSpec((short_taps, width), lambda i: (0, part * steps + i)),
        ]
        + [pl.BlockSpec(memory_space=pl.ANY)] * len(olds),
        out_specs=result,
        out_shape=jax.ShapeDtypeStruct((rows, 3 * channels), BF16),
        input_output_aliases={3: 0} if olds else {},
        scratch_shapes=[pltpu.VMEM((2, rows + RIM, LANES), F32)],
        compiler_params=params(),
        cost_estimate=cost(2 * short_taps * rows * channels, 4 * rows * channels),
        name="short_adjoint",
    )(grads, rim, filters, *olds)


def spread_kernel(place, query_ref, key_ref, value_ref, long_ref, own_ref, other_ref):
    steps = query_ref.shape[1] // LANES
    half = own_ref.shape[0]
    tiles = [ref[:, i * LANES : (i + 1) * LANES] for ref in (query_ref, key_ref, value_ref) for i in range(steps)]
    tiles += [long_ref[8 * i : 8 * i + 8, :] for i in range(long_ref.shape[0] // 8)]
    first = place[0] < half

    @pl.when(first)
    def _():
        for i in range(half):
            own_ref[place[i]] = tiles[i]
            other_ref[place[half + i] - half] = tiles[half + i]

    @pl.when(jnp.logical_not(first))
    def _():
        for i in range(half):
            other_ref[place[i] - half] = tiles[i]
            own_ref[place[half + i]] = tiles[half + i]


def collect_kernel(place, *refs):
    parts, short_ref, long_ref, tiles_ref = refs[:-3], refs[-3], refs[-2], refs[-1]
    short_taps, wide = short_ref.shape
    steps = wide // LANES
    size = parts[0].shape[0]
    for i, part in enumerate(parts):
        tiles_ref[i * size : (i + 1) * size] = part[...]
    for i in range(steps):
        short_ref[:, i * LANES : (i + 1) * LANES] = tiles_ref[place[i]][0:short_taps, :]
    for i in range(long_ref.shape[0] // 8):
        long_ref[8 * i : 8 * i + 8, :] = tiles_ref[place[steps + i]]


def in_vmem():
    return pl.BlockSpec(memory_space=pltpu.VMEM)


def total_over_devices(spread_to, collect_from, query_sum, key_sum, value_sum, long_sum, short_taps, first, after):
    ny, nz = lax.axis_size("y"), lax.axis_size("z")
    channels = query_sum.shape[1]
    count = 3 * channels // LANES + long_sum.shape[0] // 8
    half = jax.ShapeDtypeStruct((count // 2, 8, LANES), F32)
    own, other = pl.pallas_call(
        spread_kernel,
        in_specs=[pl.BlockSpec(memory_space=pltpu.SMEM)] + [in_vmem()] * 4,
        out_specs=[in_vmem()] * 2,
        out_shape=[half] * 2,
        compiler_params=params(),
        name="spread",
    )(spread_to, query_sum, key_sum, value_sum, long_sum)
    part = own + move(other, c=1)
    size = count // 2 // nz
    part = sum([move(part[d * size : (d + 1) * size], z=d) for d in range(1, nz)], part[:size])
    terms, first = lax.optimization_barrier(([part] + [move(part, y=d) for d in range(1, ny)], first))
    whole = paired_sum(terms)
    terms = [move(whole, xl=a, xh=b) for a, b in FLIPS]
    terms, beside = lax.optimization_barrier((terms, after(first)))
    whole = paired_sum(terms)
    line = jnp.concatenate([whole, move(whole, c=1)], axis=0)
    lines = [move(line, z=-d) for d in range(nz)]
    groups, taps = long_sum.shape
    short, long = pl.pallas_call(
        collect_kernel,
        in_specs=[pl.BlockSpec(memory_space=pltpu.SMEM)] + [in_vmem()] * nz,
        out_specs=[in_vmem(), in_vmem()],
        scratch_shapes=[pltpu.VMEM((count, 8, LANES), F32)],
        out_shape=[
            jax.ShapeDtypeStruct((short_taps, 3 * channels), F32),
            jax.ShapeDtypeStruct((groups, taps), F32),
        ],
        compiler_params=params(),
        name="collect",
    )(collect_from, *lines)
    return short, long, beside


def paired_sum(terms):
    half = len(terms) // 2
    if half == 0:
        return terms[0]
    return paired_sum([terms[i] + terms[i + half] for i in range(half)])


def gather_tall(shard):
    return [move(shard[shard.shape[0] // 2 :], y=d) for d in range(lax.axis_size("y"))]


def gather_wide(shard):
    return [move(shard[: shard.shape[0] // 2], xl=a, xh=b) for a, b in FLIPS]


def gather_far(wide_top, tall_bottom):
    ny = lax.axis_size("y")
    wide_top, tall_bottom = jnp.stack(wide_top), jnp.stack(tall_bottom)
    return (
        [move(wide_top, y=d) for d in range(ny)],
        [move(tall_bottom, xl=a, xh=b) for a, b in FLIPS],
    )


def piece_rows(tops, bottoms, step):
    rows = []
    for a in range(2):
        rows.append(jnp.concatenate([tops[step][2 * a + b] for b in range(2)], axis=1))
        rows.append(jnp.concatenate([bottoms[2 * a + b][step] for b in range(2)], axis=1))
    return rows


def gate_matmul_kernel(ny, *refs):
    cotangent_ref, tops, bottoms, out_ref = refs[0], refs[1 : 1 + ny], refs[1 + ny : 5 + ny], refs[5 + ny]
    left = cotangent_ref[...]
    at = 0
    for step in range(ny):
        for right in piece_rows(tops, bottoms, step):
            size = right.shape[0]
            out_ref[:, at : at + size] = lax.dot_general(
                left, right, (((1,), (1,)), ((), ())), preferred_element_type=F32
            ).astype(BF16)
            at += size


def whole(x):
    return pl.BlockSpec(x.shape, lambda *_, n=x.ndim: (0,) * n)


def gate_matmul(cotangents, tops, bottoms):
    rows, depth = cotangents.shape
    ny = len(tops)
    channels = 4 * ny * tops[0].shape[1]
    height = rows // 2
    return hbm_call(
        functools.partial(gate_matmul_kernel, ny),
        loose=range(5 + ny),
        grid=(rows // height,),
        in_specs=[pl.BlockSpec((height, depth), lambda i: (i, 0))] + [whole(x) for x in (*tops, *bottoms)],
        out_specs=pl.BlockSpec((height, channels), lambda i: (i, 0)),
        out_shape=jax.ShapeDtypeStruct((rows, channels), BF16),
        compiler_params=params(32),
        cost_estimate=cost(2 * rows * depth * channels, 2 * (rows + depth) * channels),
        name="gate_matmul",
    )(cotangents, *tops, *bottoms)


def picked(origin, step, rows_ref):
    height = rows_ref.shape[1] // 2
    at = [pl.multiple_of(origin[2 * step + a] % 2 * height, height) for a in range(2)]
    return jnp.concatenate([rows_ref[:, pl.ds(x, height)] for x in at], axis=1)


def weight_grad_kernel(ny, origin, rows_ref, turned_ref, *refs):
    top_grads, bottom_grads = refs[:ny], refs[ny:]
    step = pl.program_id(0)
    size = bottom_grads[0].shape[2]
    width = bottom_grads[0].shape[1]
    rows = picked(origin, step, rows_ref)
    grads = jnp.dot(turned_ref[...], rows, preferred_element_type=F32).astype(BF16)
    for f in range(4):
        a, b = f // 2, f % 2
        at = (2 * a + 1) * size
        bottom_grads[f][step] = grads[b * width : (b + 1) * width, at : at + size]
    for d in range(ny):

        @pl.when(step == d)
        def _(d=d):
            for f in range(4):
                a, b = f // 2, f % 2
                at = 2 * a * size
                top_grads[d][f] = grads[b * width : (b + 1) * width, at : at + size]


def rows_of(origin, all_rows, ny):
    rows, channels = all_rows.shape
    return pl.BlockSpec((rows, channels // ny), lambda i, origin: (0, origin[2 * i] // 2))


def weight_grad(origin, all_rows, turned, ny):
    rows, channels = all_rows.shape
    size = channels // (4 * ny)
    width = turned.shape[0] // 2
    outs = [jax.ShapeDtypeStruct((4, width, size), BF16)] * ny + [jax.ShapeDtypeStruct((ny, width, size), BF16)] * 4
    results = hbm_call(
        functools.partial(weight_grad_kernel, ny),
        loose=(0, 2),
        grid_spec=pltpu.PrefetchScalarGridSpec(
            num_scalar_prefetch=1,
            grid=(ny,),
            in_specs=[rows_of(origin, all_rows, ny), whole(turned)],
            out_specs=[whole(x) for x in outs],
        ),
        out_shape=outs,
        compiler_params=params(40),
        cost_estimate=cost(4 * rows * width * channels, 2 * (rows + 2 * width) * channels),
        name="weight_grad",
    )(origin, all_rows, turned)
    return results[:ny], results[ny:]


def output_kernel(ny, origin, rows_ref, *refs):
    tops, bottoms, own_ref, other_ref, total = refs[:ny], refs[ny : ny + 4], refs[-3], refs[-2], refs[-1]
    step = pl.program_id(0)
    width = own_ref.shape[1]
    rows = picked(origin, step, rows_ref)
    for d in range(ny):

        @pl.when(step == d)
        def _(d=d):
            right = jnp.concatenate(piece_rows(tops, bottoms, d), axis=0)
            product = jnp.dot(rows, right, preferred_element_type=F32)
            if d == 0:
                total[...] = product
            else:
                total[...] += product

    @pl.when(step == ny - 1)
    def _():
        own_ref[...] = total[:, :width].astype(BF16)
        other_ref[...] = total[:, width:].astype(BF16)


def output_call(origin, all_rows, tops, bottoms):
    rows, channels = all_rows.shape
    ny = len(tops)
    width = tops[0].shape[2]
    half = jax.ShapeDtypeStruct((rows, width), BF16)
    return hbm_call(
        functools.partial(output_kernel, ny),
        loose=(0, *range(2, 6 + ny)),
        grid_spec=pltpu.PrefetchScalarGridSpec(
            num_scalar_prefetch=1,
            grid=(ny,),
            in_specs=[rows_of(origin, all_rows, ny)] + [whole(x) for x in (*tops, *bottoms)],
            out_specs=[whole(half)] * 2,
            scratch_shapes=[pltpu.VMEM((rows, 2 * width), F32)],
        ),
        out_shape=[half, half],
        compiler_params=params(32),
        cost_estimate=cost(4 * rows * width * channels, 2 * (rows + 2 * width) * channels),
        name="output",
    )(origin, all_rows, *tops, *bottoms)


def added(terms):
    total = terms[0].astype(F32)
    for term in terms[1:]:
        total = total + term.astype(F32)
    return total


def plane_scatter(top_grads, bottom_grads, beside):
    ny = len(top_grads)
    top = added([move(top_grads[d], y=-d) for d in range(ny)]).astype(BF16)
    bottom = added([move(bottom_grads[f], xl=a, xh=b) for f, (a, b) in enumerate(FLIPS)]).astype(BF16)
    top, bottom, beside = lax.optimization_barrier((top, bottom, beside))
    top = [move(top[f], xl=a, xh=b) for f, (a, b) in enumerate(FLIPS)]
    bottom = [move(bottom[d], y=-d) for d in range(ny)]
    return top, bottom, beside


def shards(tokens_in, short_filter, long_filter, out_weight, cotangent):
    ny, nz = lax.axis_size("y"), lax.axis_size("z")
    y, xl, xh, z, c = (lax.axis_index(a) for a in ("y", "xl", "xh", "z", "c"))
    tokens = tokens_in[0]
    rows, wide = tokens.shape
    channels = wide // 3
    short_taps = short_filter.shape[0]
    groups = long_filter.shape[0]
    upstream = cotangent[0]
    length, columns = upstream.shape
    span = length // 2

    block = jnp.arange(2 * ny, dtype=jnp.int32)
    place = ((y - block // 2) % ny) * 2 + (block + xl) % 2
    origin = place
    size = 3 * channels // LANES + groups // 8
    each = size // (2 * nz)
    tile = jnp.arange(size, dtype=jnp.int32)
    core_step, z_step = (tile // (nz * each) + c) % 2, (tile // each - z) % nz
    spread_to = (core_step * nz + z_step) * each + tile % each
    collect_from = (z_step * 2 + core_step) * each + tile % each

    rim = along(tokens[rows - RIM :], 1)
    lines = long_filter.astype(F32)
    parts = features_call(tokens, short_filter)
    parts, rim = lax.optimization_barrier((parts, rim))
    query, key, value, mixer = features_call(tokens, short_filter, rim, parts)
    mixer, out_weight = lax.optimization_barrier((mixer, out_weight))
    mixer_prev = along(mixer, 1)
    tall_bottom = gather_tall(out_weight)
    mixer_prev, tall_bottom = lax.optimization_barrier((mixer_prev, tall_bottom))
    mixed, gated = mix_call(lines, mixer_prev, mixer, query)
    mixed, out_weight, half = lax.optimization_barrier((mixed, out_weight, xh))
    wide_top = gather_wide(out_weight)
    wide_top, tall_bottom, half = lax.optimization_barrier((wide_top, tall_bottom, half))
    all_rows = lax.all_gather(gated, ("z", "c"), axis=0, tiled=True)
    tops, bottoms = gather_far(wide_top, tall_bottom)
    others = move(lax.dynamic_slice_in_dim(upstream, (1 - half) * span, span, 0), xh=1)
    mine = lax.dynamic_slice_in_dim(upstream, half * span, span, 0)
    cotangents = jnp.concatenate([mine, others], axis=1)
    partial = gate_matmul(cotangents, tops, bottoms)
    partial, all_rows = lax.optimization_barrier((partial, all_rows))
    gate_grad = lax.psum_scatter(partial, ("z", "c"), scatter_dimension=0, tiled=True)

    top_grads, bottom_grads = weight_grad(origin, all_rows, cotangents.T, ny)
    own, other = output_call(origin, all_rows, tops, bottoms)
    top, bottom, other = plane_scatter(top_grads, bottom_grads, other)
    gate_grad, top, bottom, other = lax.optimization_barrier((gate_grad, top, bottom, other))

    grad_mixed = gate_call(place, gate_grad, query)
    grad_next = along(grad_mixed, -1)
    long_sum, query_sum, query_grad = long_grad_call(
        place, groups, short_taps, mixer_prev, mixer, grad_mixed, gate_grad, mixed, tokens, rim
    )
    grad_weight = jnp.concatenate([added(top), added(bottom)], axis=1).T
    other, long_sum, query_sum = lax.optimization_barrier((other, long_sum, query_sum))
    grad_next, grad_weight, long_sum = lax.optimization_barrier((grad_next, grad_weight, long_sum))
    theirs = move(other, xh=1)
    other_grads, key_sum, value_sum, edge = unmix_call(
        lines, short_taps, grad_mixed, grad_next, key, value, tokens, rim, query_grad
    )
    edge, key_sum, theirs = lax.optimization_barrier((edge, key_sum, theirs))
    output = jnp.where(xh == 0, jnp.concatenate([own, theirs], axis=0), jnp.concatenate([theirs, own], axis=0))
    edge = along(edge, -1)
    query_part = short_adjoint_call(query_grad[None], edge, short_filter, 0, 0, None)

    def key_part(query_part):
        return short_adjoint_call(other_grads, edge, short_filter, 0, 1, query_part)

    grad_short, grad_long, grad_tokens = total_over_devices(
        spread_to, collect_from, query_sum, key_sum, value_sum, long_sum, short_taps, query_part, key_part
    )
    grad_tokens = short_adjoint_call(other_grads, edge, short_filter, 1, 2, grad_tokens)
    return output[None], grad_tokens[None], grad_short, grad_long, grad_weight


def solution(mesh):
    dp, seq = mesh.shape["dp"], mesh.shape["seq"]
    grid = jax.sharding.Mesh(mesh.devices.reshape(dp // 2, 2, 2, seq // 4, 2), ("y", "xl", "xh", "z", "c"))
    rows, line = ("y", "xl"), ("xh", "z", "c")
    return jax.shard_map(
        shards,
        mesh=grid,
        in_specs=(P(rows, line, None), P(), P(), P(rows, line), P(rows, None, line)),
        out_specs=(P(rows, None, line), P(rows, line, None), P(), P(), P(rows, line)),
        check_vma=False,
    )
```

```python
import functools
import itertools
import math

import jax
import jax.numpy as jnp
from jax import lax
from jax.experimental import pallas as pl
from jax.experimental.pallas import tpu as pltpu
from jax.sharding import PartitionSpec as P

LANES = 128
RIM = 16
MIB = 1024 * 1024
WIDTH = 1024
F32 = jnp.float32
BF16 = jnp.bfloat16


PLANE = ("y", "xl", "xh")
LINE = ("xh", "z", "c")


def along(x, by):
    size = math.prod(lax.axis_size(a) for a in LINE)
    pairs = [(i, i + by) for i in range(size) if 0 <= i + by < size]
    return lax.ppermute(x, LINE, pairs)


def move(x, **steps):
    axes = tuple(a for a in ("y", "xl", "xh", "z", "c") if steps.get(a, 0) % lax.axis_size(a))
    if not axes:
        return x
    sizes = [lax.axis_size(a) for a in axes]
    pairs = []
    for at in itertools.product(*(range(n) for n in sizes)):
        to = [(p + steps[a]) % n for p, a, n in zip(at, axes, sizes)]
        pairs.append((flat(at, sizes), flat(to, sizes)))
    return lax.ppermute(x, axes, pairs)


def flat(at, sizes):
    index = 0
    for p, n in zip(at, sizes):
        index = index * n + p
    return index


FLIPS = [(0, 0), (0, 1), (1, 0), (1, 1)]


def params(mib=16):
    return pltpu.CompilerParams(vmem_limit_bytes=mib * MIB)


def hbm_call(kernel, *, out_shape, loose=(), **options):
    single = not isinstance(out_shape, (list, tuple))
    shapes = [out_shape] if single else out_shape
    placed = [pltpu.HBM(x.shape, x.dtype) if x.size * x.dtype.itemsize > 256 * 1024 else x for x in shapes]
    call = pl.pallas_call(kernel, out_shape=placed[0] if single else placed, **options)

    def run(*args):
        held = [x if i in loose else pltpu.with_memory_space_constraint(x, pltpu.HBM) for i, x in enumerate(args)]
        return call(*held)

    return run


def cost(flops, moved):
    return pl.CostEstimate(flops=int(flops), bytes_accessed=int(moved), transcendentals=0)


def block_width(channels, most):
    width = min(channels, most)
    while channels % width:
        width //= 2
    return width


def extend(ext, rim, rows_of, at):
    ext[0:RIM, :] = jnp.zeros((RIM, LANES), F32) if rim is None else rim[:, at].astype(F32)
    ext[RIM:, :] = rows_of.astype(F32)


def features_kernel(short_taps, tokens, rims, filters, query_ref, key_ref, value_ref, mixer_ref, ext):
    rows, width = tokens[0].shape

    def filtered(part, block, at):
        own = ext.at[(3 * block + part) % ext.shape[0]]
        extend(own, rims and rims[part], tokens[part][:, at], at)
        taps = filters[part][:, at]
        total = taps[0:1] * own[RIM : RIM + rows, :]
        for tap in range(1, short_taps):
            total = total + taps[tap : tap + 1] * own[RIM - tap : RIM - tap + rows, :]
        return total

    for block in range(width // LANES):
        at = pl.ds(block * LANES, LANES)
        query_ref[:, at] = filtered(0, block, at).astype(BF16)
        key, value = filtered(1, block, at), filtered(2, block, at)
        key_ref[:, at] = key.astype(BF16)
        value_ref[:, at] = value.astype(BF16)
        mixer_ref[:, at] = (key * value).astype(BF16)


def features_call(tokens, filters, rim=None, given=None):
    rows, wide = tokens.shape
    channels = wide // 3
    taps = filters.shape[0]
    rows = rows if given is None else 2 * RIM
    width = channels if given else block_width(channels, WIDTH)
    steps = channels // width

    def spec(height, part):
        return pl.BlockSpec((height, width), lambda i, part=part: (0, i + part * steps))

    held = [] if given is None else [rim] * 3
    olds = [] if given is None else list(given)

    def body(*refs):
        n = 3 + len(held)
        rims = refs[3:n] if held else None
        features_kernel(taps, refs[0:3], rims, refs[n : n + 3], *refs[n + 3 + len(olds) :])

    out = jax.ShapeDtypeStruct((tokens.shape[0], channels), BF16)
    return hbm_call(
        body,
        loose=(3, 4, 5) if held else (),
        grid=(steps,),
        in_specs=[spec(rows, p) for p in range(3)]
        + [spec(RIM, p) for p in range(len(held))]
        + [spec(taps, p) for p in range(3)]
        + [pl.BlockSpec(memory_space=pl.ANY)] * len(olds),
        out_specs=[pl.BlockSpec((rows, width), lambda i: (0, i))] * 4,
        out_shape=[out] * 4,
        input_output_aliases={9 + i: i for i in range(len(olds))},
        scratch_shapes=[pltpu.VMEM((6, RIM + rows, LANES), F32)],
        compiler_params=params(),
        cost_estimate=cost(0, rows * wide),
        name="features" if given is None else "first_rows",
    )(*[tokens] * 3, *held, *[filters] * 3, *olds)


def lane_row(shape):
    row = lax.broadcasted_iota(jnp.int32, shape, 0)
    lane = lax.broadcasted_iota(jnp.int32, shape, 1)
    return row, lane


def mirror(size):
    row, lane = lane_row((size, size))
    both = row + lane
    return jnp.where((both == 0) | (both == size), 1.0, 0.0)


def circulant(line, taps):
    wide = jnp.broadcast_to(line.astype(F32), (taps, taps))
    return pltpu.roll(wide, 0, 1, stride=1, stride_axis=0)


def pick_groups(product, rows, per_group):
    lane = lax.broadcasted_iota(jnp.int32, (rows, LANES), 1)
    total = product[0:rows]
    for g in range(1, LANES // per_group):
        total = jnp.where(lane >= g * per_group, product[g * rows : (g + 1) * rows], total)
    return total


def mix_kernel(per_group, lines_ref, prev_ref, cur_ref, query_ref, mixed_ref, gated_ref, table, lines):
    rows, width = cur_ref.shape
    row, lane = lane_row((rows, rows))
    above = lane > row
    packed = LANES // per_group
    lines[...] = jnp.dot(lines_ref[...].astype(BF16), mirror(rows).astype(BF16), preferred_element_type=F32)
    for block in range(width // LANES):
        at = pl.ds(block * LANES, LANES)
        own = table.at[block % 2]
        for g in range(packed):
            ring = circulant(lines[block * packed + g : block * packed + g + 1, :], rows)
            own[g * rows : (g + 1) * rows, 0:rows] = jnp.where(above, ring, 0.0).astype(BF16)
            own[g * rows : (g + 1) * rows, rows : 2 * rows] = jnp.where(above, 0.0, ring).astype(BF16)
        window = jnp.concatenate([prev_ref[:, at], cur_ref[:, at]], axis=0)
        product = jnp.dot(own[...], window, preferred_element_type=F32)
        mixed = pick_groups(product, rows, per_group)
        mixed_ref[:, at] = mixed.astype(BF16)
        gated_ref[:, at] = (query_ref[:, at].astype(F32) * mixed).astype(BF16)


def mix_call(lines, prev, cur, query):
    rows, channels = cur.shape
    groups, taps = lines.shape
    per_group = channels // groups
    width = block_width(channels, WIDTH)
    steps = channels // width
    wide = pl.BlockSpec((rows, width), lambda i: (0, i))
    out = jax.ShapeDtypeStruct((rows, channels), BF16)
    return hbm_call(
        functools.partial(mix_kernel, per_group),
        loose=(0, 1),
        grid=(steps,),
        in_specs=[pl.BlockSpec((width // per_group, taps), lambda i: (i, 0)), wide, wide, wide],
        out_specs=[wide, wide],
        out_shape=[out, out],
        scratch_shapes=[
            pltpu.VMEM((2, LANES // per_group * rows, 2 * rows), BF16),
            pltpu.VMEM((width // per_group, taps), F32),
        ],
        compiler_params=params(),
        cost_estimate=cost(0, 2 * rows * channels),
        name="mix",
    )(lines, prev, cur, query)


def gate_kernel(place, gate_grad_ref, query_ref, grad_ref):
    width = query_ref.shape[1] // place.shape[0]
    for i in range(place.shape[0]):
        at = pl.ds(i * width, width)
        gate_grad = gate_grad_ref[:, pl.ds(pl.multiple_of(place[i] * width, width), width)].astype(F32)
        grad_ref[:, at] = (gate_grad * query_ref[:, at].astype(F32)).astype(BF16)


def gate_call(place, gate_grad, query):
    rows, channels = query.shape
    half = pl.BlockSpec((rows // 2, channels), lambda i, place: (i, 0))
    return hbm_call(
        gate_kernel,
        loose=(0,),
        grid_spec=pltpu.PrefetchScalarGridSpec(
            num_scalar_prefetch=1, grid=(2,), in_specs=[half, half], out_specs=half
        ),
        out_shape=jax.ShapeDtypeStruct((rows, channels), BF16),
        compiler_params=params(),
        cost_estimate=cost(rows * channels, 6 * rows * channels),
        name="gate_back",
    )(place, gate_grad, query)


def tap_sums(short_taps, grad, tokens_ref, rim_ref, out_ref, at, ext):
    rows = tokens_ref.shape[0]
    extend(ext, rim_ref, tokens_ref[:, at], at)
    grad = grad.astype(F32)
    for tap in range(short_taps):
        out_ref[tap : tap + 1, at] = jnp.sum(grad * ext[RIM - tap : RIM - tap + rows, :], axis=0, keepdims=True)
    out_ref[short_taps:8, at] = jnp.zeros((8 - short_taps, LANES), F32)


def long_grad_kernel(
    per_group, short_taps, place, prev_ref, cur_ref, grad_ref, gate_grad_ref, mixed_ref, tokens_ref, rim_ref,
    long_ref, short_ref, feature_ref, fold, masked, ext,
):
    step = pl.program_id(0)
    rows, width = cur_ref.shape
    row, lane = lane_row((rows, rows))
    above = lane > row
    member = lax.broadcasted_iota(jnp.int32, (rows, LANES), 1)
    packed = LANES // per_group
    sums = []
    for block in range(width // LANES):
        at = pl.ds(block * LANES, LANES)
        window = jnp.concatenate([prev_ref[:, at], cur_ref[:, at]], axis=0)
        grad_wide = grad_ref[:, at].astype(F32)
        own = masked.at[block % 2]
        for g in range(packed):
            own[g * rows : (g + 1) * rows, :] = jnp.where((member >= g * per_group) & (member < (g + 1) * per_group), grad_wide, 0.0).astype(BF16)
        pairs = lax.dot_general(own[...], window, (((1,), (1,)), ((), ())), preferred_element_type=F32)
        for g in range(packed):
            pair = pairs[g * rows : (g + 1) * rows]
            ring = jnp.where(above, pair[:, 0:rows], pair[:, rows : 2 * rows])
            total = ring[0:8]
            for tile in range(1, rows // 8):
                total = total + pltpu.roll(ring[8 * tile : 8 * tile + 8], rows - 8 * tile, 1)
            fold[block % 2, g * 8 : (g + 1) * 8, :] = total
        total = fold[block % 2, pl.ds(0, packed, stride=8), :]
        for step in range(1, 8):
            total = total + pltpu.roll(fold[block % 2, pl.ds(step, packed, stride=8), :], rows - step, 1)
        sums.append(total)
        side, inner = divmod(block * LANES, width // 2)
        gate_at = pl.multiple_of(place[2 * step + side] % 2 * (width // 2) + inner, LANES)
        gate_grad = gate_grad_ref[:, pl.ds(gate_at, LANES)].astype(F32)
        feature = (gate_grad * mixed_ref[:, at].astype(F32)).astype(BF16)
        feature_ref[:, at] = feature
        tap_sums(short_taps, feature, tokens_ref, rim_ref, short_ref, at, ext.at[block % 2])
    long_ref[...] = jnp.dot(
        jnp.concatenate(sums, axis=0), mirror(rows), precision=lax.Precision.HIGHEST, preferred_element_type=F32
    )


def long_grad_call(place, groups, short_taps, prev, cur, grad, gate_grad, mixed, tokens, rim):
    rows, channels = cur.shape
    per_group = channels // groups
    steps = place.shape[0] // 2
    width = channels // steps
    wide = pl.BlockSpec((rows, width), lambda i, place: (0, i))
    packed = LANES // per_group
    return hbm_call(
        functools.partial(long_grad_kernel, per_group, short_taps),
        loose=(0,),
        grid_spec=pltpu.PrefetchScalarGridSpec(
            num_scalar_prefetch=1,
            grid=(steps,),
            in_specs=[
                wide,
                wide,
                wide,
                pl.BlockSpec((rows, width), lambda i, place: (0, place[2 * i] // 2)),
                wide,
                wide,
                pl.BlockSpec((RIM, width), lambda i, place: (0, i)),
            ],
            out_specs=[
                pl.BlockSpec((width // per_group, rows), lambda i, place: (i, 0)),
                pl.BlockSpec((8, width), lambda i, place: (0, i)),
                wide,
            ],
            scratch_shapes=[
                pltpu.VMEM((2, packed * 8, LANES), F32),
                pltpu.VMEM((2, packed * rows, LANES), BF16),
                pltpu.VMEM((2, RIM + rows, LANES), F32),
            ],
        ),
        out_shape=[
            jax.ShapeDtypeStruct((groups, rows), F32),
            jax.ShapeDtypeStruct((8, channels), F32),
            jax.ShapeDtypeStruct((rows, channels), BF16),
        ],
        compiler_params=params(),
        cost_estimate=cost(2 * groups * rows * 2 * rows * LANES, 14 * rows * channels),
        name="long_grad",
    )(place, prev, cur, grad, gate_grad, mixed, tokens, rim)


def unmix_kernel(
    per_group, short_taps, lines_ref, grad_ref, next_ref, key_ref, value_ref, key_tokens_ref, value_tokens_ref,
    key_rim_ref, value_rim_ref, query_grad_ref, feature_ref, key_sum_ref, value_sum_ref, edge_ref, table, ext,
):
    rows, width = grad_ref.shape
    row, lane = lane_row((rows, rows))
    below = lane < row
    packed = LANES // per_group
    edge_ref[0] = query_grad_ref[0:RIM, :]
    for block in range(width // LANES):
        at = pl.ds(block * LANES, LANES)
        own = table.at[block % 2]
        for g in range(packed):
            ring = circulant(lines_ref[block * packed + g : block * packed + g + 1, :], rows)
            own[g * rows : (g + 1) * rows, 0:rows] = jnp.where(below, 0.0, ring).astype(BF16)
            own[g * rows : (g + 1) * rows, rows : 2 * rows] = jnp.where(below, ring, 0.0).astype(BF16)
        window = jnp.concatenate([grad_ref[:, at], next_ref[:, at]], axis=0)
        product = jnp.dot(own[...], window, preferred_element_type=F32)
        grad_mixer = pick_groups(product, rows, per_group)
        key_grad = (grad_mixer * value_ref[:, at].astype(F32)).astype(BF16)
        value_grad = (grad_mixer * key_ref[:, at].astype(F32)).astype(BF16)
        feature_ref[0, :, at] = key_grad
        feature_ref[1, :, at] = value_grad
        edge_ref[1, :, at] = key_grad[0:RIM]
        edge_ref[2, :, at] = value_grad[0:RIM]
        slot = 2 * (block % 2)
        tap_sums(short_taps, key_grad, key_tokens_ref, key_rim_ref, key_sum_ref, at, ext.at[slot])
        tap_sums(short_taps, value_grad, value_tokens_ref, value_rim_ref, value_sum_ref, at, ext.at[slot + 1])


def unmix_call(lines, short_taps, grad, grad_next, key, value, tokens, rim, query_grad):
    rows, channels = grad.shape
    per_group = channels // lines.shape[0]
    width = block_width(channels, WIDTH)
    steps = channels // width

    def spec(height, part):
        return pl.BlockSpec((height, width), lambda i, part=part: (0, i + part * steps))

    wide = spec(rows, 0)
    sums = jax.ShapeDtypeStruct((8, channels), F32)
    return hbm_call(
        functools.partial(unmix_kernel, per_group, short_taps),
        loose=(0, 2),
        grid=(steps,),
        in_specs=[pl.BlockSpec((width // per_group, rows), lambda i: (i, 0))]
        + [wide] * 4
        + [spec(rows, 1), spec(rows, 2), spec(RIM, 1), spec(RIM, 2), spec(2 * RIM, 0)],
        out_specs=[
            pl.BlockSpec((2, rows, width), lambda i: (0, 0, i)),
            spec(8, 0),
            spec(8, 0),
            pl.BlockSpec((3, RIM, width), lambda i: (0, 0, i)),
        ],
        out_shape=[
            jax.ShapeDtypeStruct((2, rows, channels), BF16),
            sums,
            sums,
            jax.ShapeDtypeStruct((3, RIM, channels), BF16),
        ],
        scratch_shapes=[
            pltpu.VMEM((2, LANES // per_group * rows, 2 * rows), BF16),
            pltpu.VMEM((4, RIM + rows, LANES), F32),
        ],
        compiler_params=params(),
        cost_estimate=cost(2 * channels * rows * 2 * rows * LANES // per_group, 16 * rows * channels),
        name="unmix",
    )(lines, grad, grad_next, key, value, tokens, tokens, rim, rim, query_grad)


def short_adjoint_kernel(short_taps, grads_ref, rim_ref, filter_ref, *refs):
    out_ref, ext = refs[-2:]
    rows, width = out_ref.shape
    for block in range(width // LANES):
        at = pl.ds(block * LANES, LANES)
        own = ext.at[block % 2]
        own[0:rows, :] = grads_ref[0, :, at].astype(F32)
        own[rows:, :] = rim_ref[0, :, at].astype(F32)
        taps = filter_ref[:, at]
        total = taps[0:1] * own[0:rows, :]
        for tap in range(1, short_taps):
            total = total + taps[tap : tap + 1] * own[tap : tap + rows, :]
        out_ref[:, at] = total.astype(BF16)


def short_adjoint_call(grads, rim, filters, given, part, out):
    _, rows, channels = grads.shape
    short_taps = filters.shape[0]
    width = block_width(channels, 2 * WIDTH)
    steps = channels // width
    result = pl.BlockSpec((rows, width), lambda i: (0, part * steps + i))
    olds = [] if out is None else [out]
    return hbm_call(
        functools.partial(short_adjoint_kernel, short_taps),
        loose=(1,),
        grid=(steps,),
        in_specs=[
            pl.BlockSpec((1, rows, width), lambda i: (given, 0, i)),
            pl.BlockSpec((1, RIM, width), lambda i: (part, 0, i)),
            pl.BlockSpec((short_taps, width), lambda i: (0, part * steps + i)),
        ]
        + [pl.BlockSpec(memory_space=pl.ANY)] * len(olds),
        out_specs=result,
        out_shape=jax.ShapeDtypeStruct((rows, 3 * channels), BF16),
        input_output_aliases={3: 0} if olds else {},
        scratch_shapes=[pltpu.VMEM((2, rows + RIM, LANES), F32)],
        compiler_params=params(),
        cost_estimate=cost(2 * short_taps * rows * channels, 4 * rows * channels),
        name="short_adjoint",
    )(grads, rim, filters, *olds)


def spread_kernel(place, query_ref, key_ref, value_ref, long_ref, own_ref, other_ref):
    steps = query_ref.shape[1] // LANES
    half = own_ref.shape[0]
    tiles = [ref[:, i * LANES : (i + 1) * LANES] for ref in (query_ref, key_ref, value_ref) for i in range(steps)]
    tiles += [long_ref[8 * i : 8 * i + 8, :] for i in range(long_ref.shape[0] // 8)]
    first = place[0] < half

    @pl.when(first)
    def _():
        for i in range(half):
            own_ref[place[i]] = tiles[i]
            other_ref[place[half + i] - half] = tiles[half + i]

    @pl.when(jnp.logical_not(first))
    def _():
        for i in range(half):
            other_ref[place[i] - half] = tiles[i]
            own_ref[place[half + i]] = tiles[half + i]


def collect_kernel(place, *refs):
    parts, short_ref, long_ref, tiles_ref = refs[:-3], refs[-3], refs[-2], refs[-1]
    short_taps, wide = short_ref.shape
    steps = wide // LANES
    size = parts[0].shape[0]
    for i, part in enumerate(parts):
        tiles_ref[i * size : (i + 1) * size] = part[...]
    for i in range(steps):
        short_ref[:, i * LANES : (i + 1) * LANES] = tiles_ref[place[i]][0:short_taps, :]
    for i in range(long_ref.shape[0] // 8):
        long_ref[8 * i : 8 * i + 8, :] = tiles_ref[place[steps + i]]


def in_vmem():
    return pl.BlockSpec(memory_space=pltpu.VMEM)


def total_over_devices(spread_to, collect_from, query_sum, key_sum, value_sum, long_sum, short_taps, first, after):
    ny, nz = lax.axis_size("y"), lax.axis_size("z")
    channels = query_sum.shape[1]
    count = 3 * channels // LANES + long_sum.shape[0] // 8
    half = jax.ShapeDtypeStruct((count // 2, 8, LANES), F32)
    own, other = pl.pallas_call(
        spread_kernel,
        in_specs=[pl.BlockSpec(memory_space=pltpu.SMEM)] + [in_vmem()] * 4,
        out_specs=[in_vmem()] * 2,
        out_shape=[half] * 2,
        compiler_params=params(),
        name="spread",
    )(spread_to, query_sum, key_sum, value_sum, long_sum)
    part = own + move(other, c=1)
    size = count // 2 // nz
    part = sum([move(part[d * size : (d + 1) * size], z=d) for d in range(1, nz)], part[:size])
    terms, first = lax.optimization_barrier(([part] + [move(part, y=d) for d in range(1, ny)], first))
    whole = paired_sum(terms)
    terms = [move(whole, xl=a, xh=b) for a, b in FLIPS]
    terms, beside = lax.optimization_barrier((terms, after(first)))
    whole = paired_sum(terms)
    line = jnp.concatenate([whole, move(whole, c=1)], axis=0)
    lines = [move(line, z=-d) for d in range(nz)]
    groups, taps = long_sum.shape
    short, long = pl.pallas_call(
        collect_kernel,
        in_specs=[pl.BlockSpec(memory_space=pltpu.SMEM)] + [in_vmem()] * nz,
        out_specs=[in_vmem(), in_vmem()],
        scratch_shapes=[pltpu.VMEM((count, 8, LANES), F32)],
        out_shape=[
            jax.ShapeDtypeStruct((short_taps, 3 * channels), F32),
            jax.ShapeDtypeStruct((groups, taps), F32),
        ],
        compiler_params=params(),
        name="collect",
    )(collect_from, *lines)
    return short, long, beside


def paired_sum(terms):
    half = len(terms) // 2
    if half == 0:
        return terms[0]
    return paired_sum([terms[i] + terms[i + half] for i in range(half)])


def gather_tall(shard):
    return [move(shard[shard.shape[0] // 2 :], y=d) for d in range(lax.axis_size("y"))]


def gather_wide(shard):
    return [move(shard[: shard.shape[0] // 2], xl=a, xh=b) for a, b in FLIPS]


def gather_far(wide_top, tall_bottom):
    ny = lax.axis_size("y")
    wide_top, tall_bottom = jnp.stack(wide_top), jnp.stack(tall_bottom)
    return (
        [move(wide_top, y=d) for d in range(ny)],
        [move(tall_bottom, xl=a, xh=b) for a, b in FLIPS],
    )


def piece_rows(tops, bottoms, step):
    rows = []
    for a in range(2):
        rows.append(jnp.concatenate([tops[step][2 * a + b] for b in range(2)], axis=1))
        rows.append(jnp.concatenate([bottoms[2 * a + b][step] for b in range(2)], axis=1))
    return rows


def gate_matmul_kernel(ny, *refs):
    cotangent_ref, tops, bottoms, out_ref = refs[0], refs[1 : 1 + ny], refs[1 + ny : 5 + ny], refs[5 + ny]
    left = cotangent_ref[...]
    at = 0
    for step in range(ny):
        for right in piece_rows(tops, bottoms, step):
            size = right.shape[0]
            out_ref[:, at : at + size] = lax.dot_general(
                left, right, (((1,), (1,)), ((), ())), preferred_element_type=F32
            ).astype(BF16)
            at += size


def whole(x):
    return pl.BlockSpec(x.shape, lambda *_, n=x.ndim: (0,) * n)


def gate_matmul(cotangents, tops, bottoms):
    rows, depth = cotangents.shape
    ny = len(tops)
    channels = 4 * ny * tops[0].shape[1]
    height = rows // 2
    return hbm_call(
        functools.partial(gate_matmul_kernel, ny),
        loose=range(5 + ny),
        grid=(rows // height,),
        in_specs=[pl.BlockSpec((height, depth), lambda i: (i, 0))] + [whole(x) for x in (*tops, *bottoms)],
        out_specs=pl.BlockSpec((height, channels), lambda i: (i, 0)),
        out_shape=jax.ShapeDtypeStruct((rows, channels), BF16),
        compiler_params=params(32),
        cost_estimate=cost(2 * rows * depth * channels, 2 * (rows + depth) * channels),
        name="gate_matmul",
    )(cotangents, *tops, *bottoms)


def picked(origin, step, rows_ref):
    height = rows_ref.shape[1] // 2
    at = [pl.multiple_of(origin[2 * step + a] % 2 * height, height) for a in range(2)]
    return jnp.concatenate([rows_ref[:, pl.ds(x, height)] for x in at], axis=1)


def weight_grad_kernel(ny, origin, rows_ref, turned_ref, *refs):
    top_grads, bottom_grads = refs[:ny], refs[ny:]
    step = pl.program_id(0)
    size = bottom_grads[0].shape[2]
    width = bottom_grads[0].shape[1]
    rows = picked(origin, step, rows_ref)
    grads = jnp.dot(turned_ref[...], rows, preferred_element_type=F32).astype(BF16)
    for f in range(4):
        a, b = f // 2, f % 2
        at = (2 * a + 1) * size
        bottom_grads[f][step] = grads[b * width : (b + 1) * width, at : at + size]
    for d in range(ny):

        @pl.when(step == d)
        def _(d=d):
            for f in range(4):
                a, b = f // 2, f % 2
                at = 2 * a * size
                top_grads[d][f] = grads[b * width : (b + 1) * width, at : at + size]


def rows_of(origin, all_rows, ny):
    rows, channels = all_rows.shape
    return pl.BlockSpec((rows, channels // ny), lambda i, origin: (0, origin[2 * i] // 2))


def weight_grad(origin, all_rows, turned, ny):
    rows, channels = all_rows.shape
    size = channels // (4 * ny)
    width = turned.shape[0] // 2
    outs = [jax.ShapeDtypeStruct((4, width, size), BF16)] * ny + [jax.ShapeDtypeStruct((ny, width, size), BF16)] * 4
    results = hbm_call(
        functools.partial(weight_grad_kernel, ny),
        loose=(0, 2),
        grid_spec=pltpu.PrefetchScalarGridSpec(
            num_scalar_prefetch=1,
            grid=(ny,),
            in_specs=[rows_of(origin, all_rows, ny), whole(turned)],
            out_specs=[whole(x) for x in outs],
        ),
        out_shape=outs,
        compiler_params=params(40),
        cost_estimate=cost(4 * rows * width * channels, 2 * (rows + 2 * width) * channels),
        name="weight_grad",
    )(origin, all_rows, turned)
    return results[:ny], results[ny:]


def output_kernel(ny, origin, rows_ref, *refs):
    tops, bottoms, own_ref, other_ref, total = refs[:ny], refs[ny : ny + 4], refs[-3], refs[-2], refs[-1]
    step = pl.program_id(0)
    width = own_ref.shape[1]
    rows = picked(origin, step, rows_ref)
    for d in range(ny):

        @pl.when(step == d)
        def _(d=d):
            right = jnp.concatenate(piece_rows(tops, bottoms, d), axis=0)
            product = jnp.dot(rows, right, preferred_element_type=F32)
            if d == 0:
                total[...] = product
            else:
                total[...] += product

    @pl.when(step == ny - 1)
    def _():
        own_ref[...] = total[:, :width].astype(BF16)
        other_ref[...] = total[:, width:].astype(BF16)


def output_call(origin, all_rows, tops, bottoms):
    rows, channels = all_rows.shape
    ny = len(tops)
    width = tops[0].shape[2]
    half = jax.ShapeDtypeStruct((rows, width), BF16)
    return hbm_call(
        functools.partial(output_kernel, ny),
        loose=(0, *range(2, 6 + ny)),
        grid_spec=pltpu.PrefetchScalarGridSpec(
            num_scalar_prefetch=1,
            grid=(ny,),
            in_specs=[rows_of(origin, all_rows, ny)] + [whole(x) for x in (*tops, *bottoms)],
            out_specs=[whole(half)] * 2,
            scratch_shapes=[pltpu.VMEM((rows, 2 * width), F32)],
        ),
        out_shape=[half, half],
        compiler_params=params(32),
        cost_estimate=cost(4 * rows * width * channels, 2 * (rows + 2 * width) * channels),
        name="output",
    )(origin, all_rows, *tops, *bottoms)


def added(terms):
    total = terms[0].astype(F32)
    for term in terms[1:]:
        total = total + term.astype(F32)
    return total


def plane_scatter(top_grads, bottom_grads, beside):
    ny = len(top_grads)
    top = added([move(top_grads[d], y=-d) for d in range(ny)]).astype(BF16)
    bottom = added([move(bottom_grads[f], xl=a, xh=b) for f, (a, b) in enumerate(FLIPS)]).astype(BF16)
    top, bottom, beside = lax.optimization_barrier((top, bottom, beside))
    top = [move(top[f], xl=a, xh=b) for f, (a, b) in enumerate(FLIPS)]
    bottom = [move(bottom[d], y=-d) for d in range(ny)]
    return top, bottom, beside


def shards(tokens_in, short_filter, long_filter, out_weight, cotangent):
    ny, nz = lax.axis_size("y"), lax.axis_size("z")
    y, xl, xh, z, c = (lax.axis_index(a) for a in ("y", "xl", "xh", "z", "c"))
    tokens = tokens_in[0]
    rows, wide = tokens.shape
    channels = wide // 3
    short_taps = short_filter.shape[0]
    groups = long_filter.shape[0]
    upstream = cotangent[0]
    length, columns = upstream.shape
    span = length // 2

    block = jnp.arange(2 * ny, dtype=jnp.int32)
    place = ((y - block // 2) % ny) * 2 + (block + xl) % 2
    origin = place
    size = 3 * channels // LANES + groups // 8
    each = size // (2 * nz)
    tile = jnp.arange(size, dtype=jnp.int32)
    core_step, z_step = (tile // (nz * each) + c) % 2, (tile // each - z) % nz
    spread_to = (core_step * nz + z_step) * each + tile % each
    collect_from = (z_step * 2 + core_step) * each + tile % each

    rim = along(tokens[rows - RIM :], 1)
    lines = long_filter.astype(F32)
    parts = features_call(tokens, short_filter)
    parts, rim = lax.optimization_barrier((parts, rim))
    query, key, value, mixer = features_call(tokens, short_filter, rim, parts)
    mixer, out_weight = lax.optimization_barrier((mixer, out_weight))
    mixer_prev = along(mixer, 1)
    tall_bottom = gather_tall(out_weight)
    mixer_prev, tall_bottom = lax.optimization_barrier((mixer_prev, tall_bottom))
    mixed, gated = mix_call(lines, mixer_prev, mixer, query)
    mixed, out_weight, half = lax.optimization_barrier((mixed, out_weight, xh))
    wide_top = gather_wide(out_weight)
    wide_top, tall_bottom, half = lax.optimization_barrier((wide_top, tall_bottom, half))
    all_rows = lax.all_gather(gated, ("z", "c"), axis=0, tiled=True)
    tops, bottoms = gather_far(wide_top, tall_bottom)
    others = move(lax.dynamic_slice_in_dim(upstream, (1 - half) * span, span, 0), xh=1)
    mine = lax.dynamic_slice_in_dim(upstream, half * span, span, 0)
    cotangents = jnp.concatenate([mine, others], axis=1)
    partial = gate_matmul(cotangents, tops, bottoms)
    partial, all_rows = lax.optimization_barrier((partial, all_rows))
    gate_grad = lax.psum_scatter(partial, ("z", "c"), scatter_dimension=0, tiled=True)

    top_grads, bottom_grads = weight_grad(origin, all_rows, cotangents.T, ny)
    own, other = output_call(origin, all_rows, tops, bottoms)
    top, bottom, other = plane_scatter(top_grads, bottom_grads, other)
    gate_grad, top, bottom, other = lax.optimization_barrier((gate_grad, top, bottom, other))

    grad_mixed = gate_call(place, gate_grad, query)
    grad_next = along(grad_mixed, -1)
    long_sum, query_sum, query_grad = long_grad_call(
        place, groups, short_taps, mixer_prev, mixer, grad_mixed, gate_grad, mixed, tokens, rim
    )
    grad_weight = jnp.concatenate([added(top), added(bottom)], axis=1).T
    other, long_sum, query_sum = lax.optimization_barrier((other, long_sum, query_sum))
    grad_next, grad_weight, long_sum = lax.optimization_barrier((grad_next, grad_weight, long_sum))
    theirs = move(other, xh=1)
    other_grads, key_sum, value_sum, edge = unmix_call(
        lines, short_taps, grad_mixed, grad_next, key, value, tokens, rim, query_grad
    )
    edge, key_sum, theirs = lax.optimization_barrier((edge, key_sum, theirs))
    output = jnp.where(xh == 0, jnp.concatenate([own, theirs], axis=0), jnp.concatenate([theirs, own], axis=0))
    edge = along(edge, -1)
    query_part = short_adjoint_call(query_grad[None], edge, short_filter, 0, 0, None)

    def key_part(query_part):
        return short_adjoint_call(other_grads, edge, short_filter, 0, 1, query_part)

    grad_short, grad_long, grad_tokens = total_over_devices(
        spread_to, collect_from, query_sum, key_sum, value_sum, long_sum, short_taps, query_part, key_part
    )
    grad_tokens = short_adjoint_call(other_grads, edge, short_filter, 1, 2, grad_tokens)
    return output[None], grad_tokens[None], grad_short, grad_long, grad_weight


def solution(mesh):
    dp, seq = mesh.shape["dp"], mesh.shape["seq"]
    grid = jax.sharding.Mesh(mesh.devices.reshape(dp // 2, 2, 2, seq // 4, 2), ("y", "xl", "xh", "z", "c"))
    rows, line = ("y", "xl"), ("xh", "z", "c")
    return jax.shard_map(
        shards,
        mesh=grid,
        in_specs=(P(rows, line, None), P(), P(), P(rows, line), P(rows, None, line)),
        out_specs=(P(rows, None, line), P(rows, line, None), P(), P(), P(rows, line)),
        check_vma=False,
    )
```

```python
import functools
import itertools
import math

import jax
import jax.numpy as jnp
from jax import lax
from jax.experimental import pallas as pl
from jax.experimental.pallas import tpu as pltpu
from jax.sharding import PartitionSpec as P

LANES = 128
RIM = 8
MIB = 1024 * 1024
WIDTH = 1024
F32 = jnp.float32
BF16 = jnp.bfloat16


PLANE = ("y", "xl", "xh")
LINE = ("xh", "z", "c")


def along(x, by):
    size = math.prod(lax.axis_size(a) for a in LINE)
    pairs = [(i, i + by) for i in range(size) if 0 <= i + by < size]
    return lax.ppermute(x, LINE, pairs)


def move(x, **steps):
    axes = tuple(a for a in ("y", "xl", "xh", "z", "c") if steps.get(a, 0) % lax.axis_size(a))
    if not axes:
        return x
    sizes = [lax.axis_size(a) for a in axes]
    pairs = []
    for at in itertools.product(*(range(n) for n in sizes)):
        to = [(p + steps[a]) % n for p, a, n in zip(at, axes, sizes)]
        pairs.append((flat(at, sizes), flat(to, sizes)))
    return lax.ppermute(x, axes, pairs)


def flat(at, sizes):
    index = 0
    for p, n in zip(at, sizes):
        index = index * n + p
    return index


FLIPS = [(0, 0), (0, 1), (1, 0), (1, 1)]


def params(mib=16):
    return pltpu.CompilerParams(vmem_limit_bytes=mib * MIB)


def hbm_call(kernel, *, out_shape, loose=(), **options):
    single = not isinstance(out_shape, (list, tuple))
    shapes = [out_shape] if single else out_shape
    placed = [pltpu.HBM(x.shape, x.dtype) if x.size * x.dtype.itemsize > 256 * 1024 else x for x in shapes]
    call = pl.pallas_call(kernel, out_shape=placed[0] if single else placed, **options)

    def run(*args):
        held = [x if i in loose else pltpu.with_memory_space_constraint(x, pltpu.HBM) for i, x in enumerate(args)]
        return call(*held)

    return run


def cost(flops, moved):
    return pl.CostEstimate(flops=int(flops), bytes_accessed=int(moved), transcendentals=0)


def block_width(channels, most):
    width = min(channels, most)
    while channels % width:
        width //= 2
    return width


def extend(ext, rim, rows_of, at):
    ext[0:RIM, :] = jnp.zeros((RIM, LANES), F32) if rim is None else rim[:, at].astype(F32)
    ext[RIM:, :] = rows_of.astype(F32)


def features_kernel(short_taps, tokens, rims, filters, query_ref, key_ref, value_ref, mixer_ref, ext):
    rows, width = tokens[0].shape

    def filtered(part, block, at):
        own = ext.at[(3 * block + part) % ext.shape[0]]
        extend(own, rims and rims[part], tokens[part][:, at], at)
        taps = filters[part][:, at]
        total = taps[0:1] * own[RIM : RIM + rows, :]
        for tap in range(1, short_taps):
            total = total + taps[tap : tap + 1] * own[RIM - tap : RIM - tap + rows, :]
        return total

    for block in range(width // LANES):
        at = pl.ds(block * LANES, LANES)
        query_ref[:, at] = filtered(0, block, at).astype(BF16)
        key, value = filtered(1, block, at), filtered(2, block, at)
        key_ref[:, at] = key.astype(BF16)
        value_ref[:, at] = value.astype(BF16)
        mixer_ref[:, at] = (key * value).astype(BF16)


def features_call(tokens, filters, rim=None, given=None):
    rows, wide = tokens.shape
    channels = wide // 3
    taps = filters.shape[0]
    rows = rows if given is None else 2 * RIM
    width = channels if given else block_width(channels, WIDTH)
    steps = channels // width

    def spec(height, part):
        return pl.BlockSpec((height, width), lambda i, part=part: (0, i + part * steps))

    held = [] if given is None else [rim] * 3
    olds = [] if given is None else list(given)

    def body(*refs):
        n = 3 + len(held)
        rims = refs[3:n] if held else None
        features_kernel(taps, refs[0:3], rims, refs[n : n + 3], *refs[n + 3 + len(olds) :])

    out = jax.ShapeDtypeStruct((tokens.shape[0], channels), BF16)
    return hbm_call(
        body,
        loose=(3, 4, 5) if held else (),
        grid=(steps,),
        in_specs=[spec(rows, p) for p in range(3)]
        + [spec(RIM, p) for p in range(len(held))]
        + [spec(taps, p) for p in range(3)]
        + [pl.BlockSpec(memory_space=pl.ANY)] * len(olds),
        out_specs=[pl.BlockSpec((rows, width), lambda i: (0, i))] * 4,
        out_shape=[out] * 4,
        input_output_aliases={9 + i: i for i in range(len(olds))},
        scratch_shapes=[pltpu.VMEM((6, RIM + rows, LANES), F32)],
        compiler_params=params(),
        cost_estimate=cost(0, rows * wide),
        name="features" if given is None else "first_rows",
    )(*[tokens] * 3, *held, *[filters] * 3, *olds)


def lane_row(shape):
    row = lax.broadcasted_iota(jnp.int32, shape, 0)
    lane = lax.broadcasted_iota(jnp.int32, shape, 1)
    return row, lane


def mirror(size):
    row, lane = lane_row((size, size))
    both = row + lane
    return jnp.where((both == 0) | (both == size), 1.0, 0.0)


def circulant(line, taps):
    wide = jnp.broadcast_to(line.astype(F32), (taps, taps))
    return pltpu.roll(wide, 0, 1, stride=1, stride_axis=0)


def pick_groups(product, rows, per_group):
    lane = lax.broadcasted_iota(jnp.int32, (rows, LANES), 1)
    total = product[0:rows]
    for g in range(1, LANES // per_group):
        total = jnp.where(lane >= g * per_group, product[g * rows : (g + 1) * rows], total)
    return total


def mix_kernel(per_group, lines_ref, prev_ref, cur_ref, query_ref, mixed_ref, gated_ref, table, lines):
    rows, width = cur_ref.shape
    row, lane = lane_row((rows, rows))
    above = lane > row
    packed = LANES // per_group
    lines[...] = jnp.dot(lines_ref[...].astype(BF16), mirror(rows).astype(BF16), preferred_element_type=F32)
    for block in range(width // LANES):
        at = pl.ds(block * LANES, LANES)
        own = table.at[block % 2]
        for g in range(packed):
            ring = circulant(lines[block * packed + g : block * packed + g + 1, :], rows)
            own[g * rows : (g + 1) * rows, 0:rows] = jnp.where(above, ring, 0.0).astype(BF16)
            own[g * rows : (g + 1) * rows, rows : 2 * rows] = jnp.where(above, 0.0, ring).astype(BF16)
        window = jnp.concatenate([prev_ref[:, at], cur_ref[:, at]], axis=0)
        product = jnp.dot(own[...], window, preferred_element_type=F32)
        mixed = pick_groups(product, rows, per_group)
        mixed_ref[:, at] = mixed.astype(BF16)
        gated_ref[:, at] = (query_ref[:, at].astype(F32) * mixed).astype(BF16)


def mix_call(lines, prev, cur, query):
    rows, channels = cur.shape
    groups, taps = lines.shape
    per_group = channels // groups
    width = block_width(channels, WIDTH)
    steps = channels // width
    wide = pl.BlockSpec((rows, width), lambda i: (0, i))
    out = jax.ShapeDtypeStruct((rows, channels), BF16)
    return hbm_call(
        functools.partial(mix_kernel, per_group),
        loose=(0, 1),
        grid=(steps,),
        in_specs=[pl.BlockSpec((width // per_group, taps), lambda i: (i, 0)), wide, wide, wide],
        out_specs=[wide, wide],
        out_shape=[out, out],
        scratch_shapes=[
            pltpu.VMEM((2, LANES // per_group * rows, 2 * rows), BF16),
            pltpu.VMEM((width // per_group, taps), F32),
        ],
        compiler_params=params(),
        cost_estimate=cost(0, 2 * rows * channels),
        name="mix",
    )(lines, prev, cur, query)


def gate_kernel(place, gate_grad_ref, query_ref, grad_ref):
    width = query_ref.shape[1] // place.shape[0]
    for i in range(place.shape[0]):
        at = pl.ds(i * width, width)
        gate_grad = gate_grad_ref[:, pl.ds(pl.multiple_of(place[i] * width, width), width)].astype(F32)
        grad_ref[:, at] = (gate_grad * query_ref[:, at].astype(F32)).astype(BF16)


def gate_call(place, gate_grad, query):
    rows, channels = query.shape
    half = pl.BlockSpec((rows // 2, channels), lambda i, place: (i, 0))
    return hbm_call(
        gate_kernel,
        loose=(0,),
        grid_spec=pltpu.PrefetchScalarGridSpec(
            num_scalar_prefetch=1, grid=(2,), in_specs=[half, half], out_specs=half
        ),
        out_shape=jax.ShapeDtypeStruct((rows, channels), BF16),
        compiler_params=params(),
        cost_estimate=cost(rows * channels, 6 * rows * channels),
        name="gate_back",
    )(place, gate_grad, query)


def tap_sums(short_taps, grad, tokens_ref, rim_ref, out_ref, at, ext):
    rows = tokens_ref.shape[0]
    extend(ext, rim_ref, tokens_ref[:, at], at)
    grad = grad.astype(F32)
    for tap in range(short_taps):
        out_ref[tap : tap + 1, at] = jnp.sum(grad * ext[RIM - tap : RIM - tap + rows, :], axis=0, keepdims=True)
    out_ref[short_taps:8, at] = jnp.zeros((8 - short_taps, LANES), F32)


def long_grad_kernel(
    per_group, short_taps, place, prev_ref, cur_ref, grad_ref, gate_grad_ref, mixed_ref, tokens_ref, rim_ref,
    long_ref, short_ref, feature_ref, fold, masked, ext,
):
    step = pl.program_id(0)
    rows, width = cur_ref.shape
    row, lane = lane_row((rows, rows))
    above = lane > row
    member = lax.broadcasted_iota(jnp.int32, (rows, LANES), 1)
    packed = LANES // per_group
    sums = []
    for block in range(width // LANES):
        at = pl.ds(block * LANES, LANES)
        window = jnp.concatenate([prev_ref[:, at], cur_ref[:, at]], axis=0)
        grad_wide = grad_ref[:, at].astype(F32)
        own = masked.at[block % 2]
        for g in range(packed):
            own[g * rows : (g + 1) * rows, :] = jnp.where((member >= g * per_group) & (member < (g + 1) * per_group), grad_wide, 0.0).astype(BF16)
        pairs = lax.dot_general(own[...], window, (((1,), (1,)), ((), ())), preferred_element_type=F32)
        for g in range(packed):
            pair = pairs[g * rows : (g + 1) * rows]
            ring = jnp.where(above, pair[:, 0:rows], pair[:, rows : 2 * rows])
            total = ring[0:8]
            for tile in range(1, rows // 8):
                total = total + pltpu.roll(ring[8 * tile : 8 * tile + 8], rows - 8 * tile, 1)
            fold[block % 2, g * 8 : (g + 1) * 8, :] = total
        total = fold[block % 2, pl.ds(0, packed, stride=8), :]
        for step in range(1, 8):
            total = total + pltpu.roll(fold[block % 2, pl.ds(step, packed, stride=8), :], rows - step, 1)
        sums.append(total)
        side, inner = divmod(block * LANES, width // 2)
        gate_at = pl.multiple_of(place[2 * step + side] % 2 * (width // 2) + inner, LANES)
        gate_grad = gate_grad_ref[:, pl.ds(gate_at, LANES)].astype(F32)
        feature = (gate_grad * mixed_ref[:, at].astype(F32)).astype(BF16)
        feature_ref[:, at] = feature
        tap_sums(short_taps, feature, tokens_ref, rim_ref, short_ref, at, ext.at[block % 2])
    long_ref[...] = jnp.dot(
        jnp.concatenate(sums, axis=0), mirror(rows), precision=lax.Precision.HIGHEST, preferred_element_type=F32
    )


def long_grad_call(place, groups, short_taps, prev, cur, grad, gate_grad, mixed, tokens, rim):
    rows, channels = cur.shape
    per_group = channels // groups
    steps = place.shape[0] // 2
    width = channels // steps
    wide = pl.BlockSpec((rows, width), lambda i, place: (0, i))
    packed = LANES // per_group
    return hbm_call(
        functools.partial(long_grad_kernel, per_group, short_taps),
        loose=(0,),
        grid_spec=pltpu.PrefetchScalarGridSpec(
            num_scalar_prefetch=1,
            grid=(steps,),
            in_specs=[
                wide,
                wide,
                wide,
                pl.BlockSpec((rows, width), lambda i, place: (0, place[2 * i] // 2)),
                wide,
                wide,
                pl.BlockSpec((RIM, width), lambda i, place: (0, i)),
            ],
            out_specs=[
                pl.BlockSpec((width // per_group, rows), lambda i, place: (i, 0)),
                pl.BlockSpec((8, width), lambda i, place: (0, i)),
                wide,
            ],
            scratch_shapes=[
                pltpu.VMEM((2, packed * 8, LANES), F32),
                pltpu.VMEM((2, packed * rows, LANES), BF16),
                pltpu.VMEM((2, RIM + rows, LANES), F32),
            ],
        ),
        out_shape=[
            jax.ShapeDtypeStruct((groups, rows), F32),
            jax.ShapeDtypeStruct((8, channels), F32),
            jax.ShapeDtypeStruct((rows, channels), BF16),
        ],
        compiler_params=params(),
        cost_estimate=cost(2 * groups * rows * 2 * rows * LANES, 14 * rows * channels),
        name="long_grad",
    )(place, prev, cur, grad, gate_grad, mixed, tokens, rim)


def unmix_kernel(
    per_group, short_taps, lines_ref, grad_ref, next_ref, key_ref, value_ref, key_tokens_ref, value_tokens_ref,
    key_rim_ref, value_rim_ref, query_grad_ref, feature_ref, key_sum_ref, value_sum_ref, edge_ref, table, ext,
):
    rows, width = grad_ref.shape
    row, lane = lane_row((rows, rows))
    below = lane < row
    packed = LANES // per_group
    edge_ref[0] = query_grad_ref[0:RIM, :]
    for block in range(width // LANES):
        at = pl.ds(block * LANES, LANES)
        own = table.at[block % 2]
        for g in range(packed):
            ring = circulant(lines_ref[block * packed + g : block * packed + g + 1, :], rows)
            own[g * rows : (g + 1) * rows, 0:rows] = jnp.where(below, 0.0, ring).astype(BF16)
            own[g * rows : (g + 1) * rows, rows : 2 * rows] = jnp.where(below, ring, 0.0).astype(BF16)
        window = jnp.concatenate([grad_ref[:, at], next_ref[:, at]], axis=0)
        product = jnp.dot(own[...], window, preferred_element_type=F32)
        grad_mixer = pick_groups(product, rows, per_group)
        key_grad = (grad_mixer * value_ref[:, at].astype(F32)).astype(BF16)
        value_grad = (grad_mixer * key_ref[:, at].astype(F32)).astype(BF16)
        feature_ref[0, :, at] = key_grad
        feature_ref[1, :, at] = value_grad
        edge_ref[1, :, at] = key_grad[0:RIM]
        edge_ref[2, :, at] = value_grad[0:RIM]
        slot = 2 * (block % 2)
        tap_sums(short_taps, key_grad, key_tokens_ref, key_rim_ref, key_sum_ref, at, ext.at[slot])
        tap_sums(short_taps, value_grad, value_tokens_ref, value_rim_ref, value_sum_ref, at, ext.at[slot + 1])


def unmix_call(lines, short_taps, grad, grad_next, key, value, tokens, rim, query_grad):
    rows, channels = grad.shape
    per_group = channels // lines.shape[0]
    width = block_width(channels, WIDTH)
    steps = channels // width

    def spec(height, part):
        return pl.BlockSpec((height, width), lambda i, part=part: (0, i + part * steps))

    wide = spec(rows, 0)
    sums = jax.ShapeDtypeStruct((8, channels), F32)
    return hbm_call(
        functools.partial(unmix_kernel, per_group, short_taps),
        loose=(0, 2),
        grid=(steps,),
        in_specs=[pl.BlockSpec((width // per_group, rows), lambda i: (i, 0))]
        + [wide] * 4
        + [spec(rows, 1), spec(rows, 2), spec(RIM, 1), spec(RIM, 2), spec(2 * RIM, 0)],
        out_specs=[
            pl.BlockSpec((2, rows, width), lambda i: (0, 0, i)),
            spec(8, 0),
            spec(8, 0),
            pl.BlockSpec((3, RIM, width), lambda i: (0, 0, i)),
        ],
        out_shape=[
            jax.ShapeDtypeStruct((2, rows, channels), BF16),
            sums,
            sums,
            jax.ShapeDtypeStruct((3, RIM, channels), BF16),
        ],
        scratch_shapes=[
            pltpu.VMEM((2, LANES // per_group * rows, 2 * rows), BF16),
            pltpu.VMEM((4, RIM + rows, LANES), F32),
        ],
        compiler_params=params(),
        cost_estimate=cost(2 * channels * rows * 2 * rows * LANES // per_group, 16 * rows * channels),
        name="unmix",
    )(lines, grad, grad_next, key, value, tokens, tokens, rim, rim, query_grad)


def short_adjoint_kernel(short_taps, grads_ref, rim_ref, filter_ref, *refs):
    out_ref, ext = refs[-2:]
    rows, width = out_ref.shape
    for block in range(width // LANES):
        at = pl.ds(block * LANES, LANES)
        own = ext.at[block % 2]
        own[0:rows, :] = grads_ref[0, :, at].astype(F32)
        own[rows:, :] = rim_ref[0, :, at].astype(F32)
        taps = filter_ref[:, at]
        total = taps[0:1] * own[0:rows, :]
        for tap in range(1, short_taps):
            total = total + taps[tap : tap + 1] * own[tap : tap + rows, :]
        out_ref[:, at] = total.astype(BF16)


def short_adjoint_call(grads, rim, filters, given, part, out):
    _, rows, channels = grads.shape
    short_taps = filters.shape[0]
    width = block_width(channels, 2 * WIDTH)
    steps = channels // width
    result = pl.BlockSpec((rows, width), lambda i: (0, part * steps + i))
    olds = [] if out is None else [out]
    return hbm_call(
        functools.partial(short_adjoint_kernel, short_taps),
        loose=(1,),
        grid=(steps,),
        in_specs=[
            pl.BlockSpec((1, rows, width), lambda i: (given, 0, i)),
            pl.BlockSpec((1, RIM, width), lambda i: (part, 0, i)),
            pl.BlockSpec((short_taps, width), lambda i: (0, part * steps + i)),
        ]
        + [pl.BlockSpec(memory_space=pl.ANY)] * len(olds),
        out_specs=result,
        out_shape=jax.ShapeDtypeStruct((rows, 3 * channels), BF16),
        input_output_aliases={3: 0} if olds else {},
        scratch_shapes=[pltpu.VMEM((2, rows + RIM, LANES), F32)],
        compiler_params=params(),
        cost_estimate=cost(2 * short_taps * rows * channels, 4 * rows * channels),
        name="short_adjoint",
    )(grads, rim, filters, *olds)


def spread_kernel(place, query_ref, key_ref, value_ref, long_ref, own_ref, other_ref):
    steps = query_ref.shape[1] // LANES
    half = own_ref.shape[0]
    tiles = [ref[:, i * LANES : (i + 1) * LANES] for ref in (query_ref, key_ref, value_ref) for i in range(steps)]
    tiles += [long_ref[8 * i : 8 * i + 8, :] for i in range(long_ref.shape[0] // 8)]
    first = place[0] < half

    @pl.when(first)
    def _():
        for i in range(half):
            own_ref[place[i]] = tiles[i]
            other_ref[place[half + i] - half] = tiles[half + i]

    @pl.when(jnp.logical_not(first))
    def _():
        for i in range(half):
            other_ref[place[i] - half] = tiles[i]
            own_ref[place[half + i]] = tiles[half + i]


def collect_kernel(place, *refs):
    parts, short_ref, long_ref, tiles_ref = refs[:-3], refs[-3], refs[-2], refs[-1]
    short_taps, wide = short_ref.shape
    steps = wide // LANES
    size = parts[0].shape[0]
    for i, part in enumerate(parts):
        tiles_ref[i * size : (i + 1) * size] = part[...]
    for i in range(steps):
        short_ref[:, i * LANES : (i + 1) * LANES] = tiles_ref[place[i]][0:short_taps, :]
    for i in range(long_ref.shape[0] // 8):
        long_ref[8 * i : 8 * i + 8, :] = tiles_ref[place[steps + i]]


def in_vmem():
    return pl.BlockSpec(memory_space=pltpu.VMEM)


def total_over_devices(spread_to, collect_from, query_sum, key_sum, value_sum, long_sum, short_taps, first, after):
    ny, nz = lax.axis_size("y"), lax.axis_size("z")
    channels = query_sum.shape[1]
    count = 3 * channels // LANES + long_sum.shape[0] // 8
    half = jax.ShapeDtypeStruct((count // 2, 8, LANES), F32)
    own, other = pl.pallas_call(
        spread_kernel,
        in_specs=[pl.BlockSpec(memory_space=pltpu.SMEM)] + [in_vmem()] * 4,
        out_specs=[in_vmem()] * 2,
        out_shape=[half] * 2,
        compiler_params=params(),
        name="spread",
    )(spread_to, query_sum, key_sum, value_sum, long_sum)
    part = own + move(other, c=1)
    size = count // 2 // nz
    part = sum([move(part[d * size : (d + 1) * size], z=d) for d in range(1, nz)], part[:size])
    terms, first = lax.optimization_barrier(([part] + [move(part, y=d) for d in range(1, ny)], first))
    whole = paired_sum(terms)
    terms = [move(whole, xl=a, xh=b) for a, b in FLIPS]
    terms, beside = lax.optimization_barrier((terms, after(first)))
    whole = paired_sum(terms)
    line = jnp.concatenate([whole, move(whole, c=1)], axis=0)
    lines = [move(line, z=-d) for d in range(nz)]
    groups, taps = long_sum.shape
    short, long = pl.pallas_call(
        collect_kernel,
        in_specs=[pl.BlockSpec(memory_space=pltpu.SMEM)] + [in_vmem()] * nz,
        out_specs=[in_vmem(), in_vmem()],
        scratch_shapes=[pltpu.VMEM((count, 8, LANES), F32)],
        out_shape=[
            jax.ShapeDtypeStruct((short_taps, 3 * channels), F32),
            jax.ShapeDtypeStruct((groups, taps), F32),
        ],
        compiler_params=params(),
        name="collect",
    )(collect_from, *lines)
    return short, long, beside


def paired_sum(terms):
    half = len(terms) // 2
    if half == 0:
        return terms[0]
    return paired_sum([terms[i] + terms[i + half] for i in range(half)])


def gather_tall(shard):
    return [move(shard[shard.shape[0] // 2 :], y=d) for d in range(lax.axis_size("y"))]


def gather_wide(shard):
    return [move(shard[: shard.shape[0] // 2], xl=a, xh=b) for a, b in FLIPS]


def gather_far(wide_top, tall_bottom):
    ny = lax.axis_size("y")
    wide_top, tall_bottom = jnp.stack(wide_top), jnp.stack(tall_bottom)
    return (
        [move(wide_top, y=d) for d in range(ny)],
        [move(tall_bottom, xl=a, xh=b) for a, b in FLIPS],
    )


def piece_rows(tops, bottoms, step):
    rows = []
    for a in range(2):
        rows.append(jnp.concatenate([tops[step][2 * a + b] for b in range(2)], axis=1))
        rows.append(jnp.concatenate([bottoms[2 * a + b][step] for b in range(2)], axis=1))
    return rows


def gate_matmul_kernel(ny, *refs):
    cotangent_ref, tops, bottoms, out_ref = refs[0], refs[1 : 1 + ny], refs[1 + ny : 5 + ny], refs[5 + ny]
    left = cotangent_ref[...]
    at = 0
    for step in range(ny):
        for right in piece_rows(tops, bottoms, step):
            size = right.shape[0]
            out_ref[:, at : at + size] = lax.dot_general(
                left, right, (((1,), (1,)), ((), ())), preferred_element_type=F32
            ).astype(BF16)
            at += size


def whole(x):
    return pl.BlockSpec(x.shape, lambda *_, n=x.ndim: (0,) * n)


def gate_matmul(cotangents, tops, bottoms):
    rows, depth = cotangents.shape
    ny = len(tops)
    channels = 4 * ny * tops[0].shape[1]
    height = rows // 4
    return hbm_call(
        functools.partial(gate_matmul_kernel, ny),
        loose=range(5 + ny),
        grid=(rows // height,),
        in_specs=[pl.BlockSpec((height, depth), lambda i: (i, 0))] + [whole(x) for x in (*tops, *bottoms)],
        out_specs=pl.BlockSpec((height, channels), lambda i: (i, 0)),
        out_shape=jax.ShapeDtypeStruct((rows, channels), BF16),
        compiler_params=params(32),
        cost_estimate=cost(2 * rows * depth * channels, 2 * (rows + depth) * channels),
        name="gate_matmul",
    )(cotangents, *tops, *bottoms)


def picked(origin, step, rows_ref):
    height = rows_ref.shape[1] // 2
    at = [pl.multiple_of(origin[2 * step + a] % 2 * height, height) for a in range(2)]
    return jnp.concatenate([rows_ref[:, pl.ds(x, height)] for x in at], axis=1)


def weight_grad_kernel(ny, origin, rows_ref, turned_ref, *refs):
    top_grads, bottom_grads = refs[:ny], refs[ny:]
    step = pl.program_id(0)
    size = bottom_grads[0].shape[2]
    width = bottom_grads[0].shape[1]
    rows = picked(origin, step, rows_ref)
    grads = jnp.dot(turned_ref[...], rows, preferred_element_type=F32).astype(BF16)
    for f in range(4):
        a, b = f // 2, f % 2
        at = (2 * a + 1) * size
        bottom_grads[f][step] = grads[b * width : (b + 1) * width, at : at + size]
    for d in range(ny):

        @pl.when(step == d)
        def _(d=d):
            for f in range(4):
                a, b = f // 2, f % 2
                at = 2 * a * size
                top_grads[d][f] = grads[b * width : (b + 1) * width, at : at + size]


def rows_of(origin, all_rows, ny):
    rows, channels = all_rows.shape
    return pl.BlockSpec((rows, channels // ny), lambda i, origin: (0, origin[2 * i] // 2))


def weight_grad(origin, all_rows, turned, ny):
    rows, channels = all_rows.shape
    size = channels // (4 * ny)
    width = turned.shape[0] // 2
    outs = [jax.ShapeDtypeStruct((4, width, size), BF16)] * ny + [jax.ShapeDtypeStruct((ny, width, size), BF16)] * 4
    results = hbm_call(
        functools.partial(weight_grad_kernel, ny),
        loose=(0, 2),
        grid_spec=pltpu.PrefetchScalarGridSpec(
            num_scalar_prefetch=1,
            grid=(ny,),
            in_specs=[rows_of(origin, all_rows, ny), whole(turned)],
            out_specs=[whole(x) for x in outs],
        ),
        out_shape=outs,
        compiler_params=params(40),
        cost_estimate=cost(4 * rows * width * channels, 2 * (rows + 2 * width) * channels),
        name="weight_grad",
    )(origin, all_rows, turned)
    return results[:ny], results[ny:]


def output_kernel(ny, origin, rows_ref, *refs):
    tops, bottoms, own_ref, other_ref, total = refs[:ny], refs[ny : ny + 4], refs[-3], refs[-2], refs[-1]
    step = pl.program_id(0)
    width = own_ref.shape[1]
    rows = picked(origin, step, rows_ref)
    for d in range(ny):

        @pl.when(step == d)
        def _(d=d):
            right = jnp.concatenate(piece_rows(tops, bottoms, d), axis=0)
            product = jnp.dot(rows, right, preferred_element_type=F32)
            if d == 0:
                total[...] = product
            else:
                total[...] += product

    @pl.when(step == ny - 1)
    def _():
        own_ref[...] = total[:, :width].astype(BF16)
        other_ref[...] = total[:, width:].astype(BF16)


def output_call(origin, all_rows, tops, bottoms):
    rows, channels = all_rows.shape
    ny = len(tops)
    width = tops[0].shape[2]
    half = jax.ShapeDtypeStruct((rows, width), BF16)
    return hbm_call(
        functools.partial(output_kernel, ny),
        loose=(0, *range(2, 6 + ny)),
        grid_spec=pltpu.PrefetchScalarGridSpec(
            num_scalar_prefetch=1,
            grid=(ny,),
            in_specs=[rows_of(origin, all_rows, ny)] + [whole(x) for x in (*tops, *bottoms)],
            out_specs=[whole(half)] * 2,
            scratch_shapes=[pltpu.VMEM((rows, 2 * width), F32)],
        ),
        out_shape=[half, half],
        compiler_params=params(32),
        cost_estimate=cost(4 * rows * width * channels, 2 * (rows + 2 * width) * channels),
        name="output",
    )(origin, all_rows, *tops, *bottoms)


def added(terms):
    total = terms[0].astype(F32)
    for term in terms[1:]:
        total = total + term.astype(F32)
    return total


def plane_scatter(top_grads, bottom_grads, beside):
    ny = len(top_grads)
    top = added([move(top_grads[d], y=-d) for d in range(ny)]).astype(BF16)
    bottom = added([move(bottom_grads[f], xl=a, xh=b) for f, (a, b) in enumerate(FLIPS)]).astype(BF16)
    top, bottom, beside = lax.optimization_barrier((top, bottom, beside))
    top = [move(top[f], xl=a, xh=b) for f, (a, b) in enumerate(FLIPS)]
    bottom = [move(bottom[d], y=-d) for d in range(ny)]
    return top, bottom, beside


def shards(tokens_in, short_filter, long_filter, out_weight, cotangent):
    ny, nz = lax.axis_size("y"), lax.axis_size("z")
    y, xl, xh, z, c = (lax.axis_index(a) for a in ("y", "xl", "xh", "z", "c"))
    tokens = tokens_in[0]
    rows, wide = tokens.shape
    channels = wide // 3
    short_taps = short_filter.shape[0]
    groups = long_filter.shape[0]
    upstream = cotangent[0]
    length, columns = upstream.shape
    span = length // 2

    block = jnp.arange(2 * ny, dtype=jnp.int32)
    place = ((y - block // 2) % ny) * 2 + (block + xl) % 2
    origin = place
    size = 3 * channels // LANES + groups // 8
    each = size // (2 * nz)
    tile = jnp.arange(size, dtype=jnp.int32)
    core_step, z_step = (tile // (nz * each) + c) % 2, (tile // each - z) % nz
    spread_to = (core_step * nz + z_step) * each + tile % each
    collect_from = (z_step * 2 + core_step) * each + tile % each

    rim = along(tokens[rows - RIM :], 1)
    lines = long_filter.astype(F32)
    parts = features_call(tokens, short_filter)
    parts, rim = lax.optimization_barrier((parts, rim))
    query, key, value, mixer = features_call(tokens, short_filter, rim, parts)
    mixer, out_weight = lax.optimization_barrier((mixer, out_weight))
    mixer_prev = along(mixer, 1)
    tall_bottom = gather_tall(out_weight)
    mixer_prev, tall_bottom = lax.optimization_barrier((mixer_prev, tall_bottom))
    mixed, gated = mix_call(lines, mixer_prev, mixer, query)
    mixed, out_weight, half = lax.optimization_barrier((mixed, out_weight, xh))
    wide_top = gather_wide(out_weight)
    wide_top, tall_bottom, half = lax.optimization_barrier((wide_top, tall_bottom, half))
    all_rows = lax.all_gather(gated, ("z", "c"), axis=0, tiled=True)
    tops, bottoms = gather_far(wide_top, tall_bottom)
    others = move(lax.dynamic_slice_in_dim(upstream, (1 - half) * span, span, 0), xh=1)
    mine = lax.dynamic_slice_in_dim(upstream, half * span, span, 0)
    cotangents = jnp.concatenate([mine, others], axis=1)
    partial = gate_matmul(cotangents, tops, bottoms)
    partial, all_rows = lax.optimization_barrier((partial, all_rows))
    gate_grad = lax.psum_scatter(partial, ("z", "c"), scatter_dimension=0, tiled=True)

    top_grads, bottom_grads = weight_grad(origin, all_rows, cotangents.T, ny)
    own, other = output_call(origin, all_rows, tops, bottoms)
    top, bottom, other = plane_scatter(top_grads, bottom_grads, other)
    gate_grad, top, bottom, other = lax.optimization_barrier((gate_grad, top, bottom, other))

    grad_mixed = gate_call(place, gate_grad, query)
    grad_next = along(grad_mixed, -1)
    long_sum, query_sum, query_grad = long_grad_call(
        place, groups, short_taps, mixer_prev, mixer, grad_mixed, gate_grad, mixed, tokens, rim
    )
    grad_weight = jnp.concatenate([added(top), added(bottom)], axis=1).T
    other, long_sum, query_sum = lax.optimization_barrier((other, long_sum, query_sum))
    grad_next, grad_weight, long_sum = lax.optimization_barrier((grad_next, grad_weight, long_sum))
    theirs = move(other, xh=1)
    other_grads, key_sum, value_sum, edge = unmix_call(
        lines, short_taps, grad_mixed, grad_next, key, value, tokens, rim, query_grad
    )
    edge, key_sum, theirs = lax.optimization_barrier((edge, key_sum, theirs))
    output = jnp.where(xh == 0, jnp.concatenate([own, theirs], axis=0), jnp.concatenate([theirs, own], axis=0))
    edge = along(edge, -1)
    query_part = short_adjoint_call(query_grad[None], edge, short_filter, 0, 0, None)

    def key_part(query_part):
        return short_adjoint_call(other_grads, edge, short_filter, 0, 1, query_part)

    grad_short, grad_long, grad_tokens = total_over_devices(
        spread_to, collect_from, query_sum, key_sum, value_sum, long_sum, short_taps, query_part, key_part
    )
    grad_tokens = short_adjoint_call(other_grads, edge, short_filter, 1, 2, grad_tokens)
    return output[None], grad_tokens[None], grad_short, grad_long, grad_weight


def solution(mesh):
    dp, seq = mesh.shape["dp"], mesh.shape["seq"]
    grid = jax.sharding.Mesh(mesh.devices.reshape(dp // 2, 2, 2, seq // 4, 2), ("y", "xl", "xh", "z", "c"))
    rows, line = ("y", "xl"), ("xh", "z", "c")
    return jax.shard_map(
        shards,
        mesh=grid,
        in_specs=(P(rows, line, None), P(), P(), P(rows, line), P(rows, None, line)),
        out_specs=(P(rows, None, line), P(rows, line, None), P(), P(), P(rows, line)),
        check_vma=False,
    )
```
